32 devices in a mesh: gz: 4 (over y, core), gy: 8 (over z, x).
Axes of the slice: x: 2, y: 2, z: 4, core: 2. Of those that a mesh axis runs over, the one named last changes fastest.
Arguments:
- displacement: float32 [9, 128, 128, 128], P(None, 'gy', 'gz'), may hold values from -0.8 to 0.8
- density: float32 [128, 128, 128], P('gy', 'gz'), may hold values from 0.01 to 1
- passive: int32 [128, 128, 128], P('gy', 'gz'), may hold values 0 or 1
- solid: int32 [128, 128, 128], P('gy', 'gz'), may hold values 0 or 1
- stiffness: float32 [24, 24], replicated, may hold values from -0.06 to 2.5, as said below
Outputs:
- new_density: float32 [128, 128, 128], P('gy', 'gz')
- log_multiplier: float32 [], replicated
The draws below stay inside these ranges and needn't reach their ends.
Inputs may be any that keep to these rules, and one draw needn't show every extreme that they name: `stiffness`: symmetric.
All inputs are finite; a program needn't handle non-finite values. No bound on the sum of `passive` or of `solid` on one device may be relied on, other than what follows from the above.
Results may differ from the reference program's by a relative error of at most 0.0003.
Values sent between devices are 32-bit elements; how exact they have to be, the bound alone decides.
No kernel may reach another device: no remote copies, remote signals or barrier semaphores. Data moves between devices by JAX's collectives and lax.ppermute only.
A program may use at most 64 MiB of HBM per device.

```python
import jax
import jax.numpy as jnp
from jax import lax

NX = 128
ITERS = 8
NY = 128
NZ = 128


def draw_density(key, part):
    key = jax.random.fold_in(key, 11)
    first_key = jax.random.fold_in(key, 0)
    ramp = (1.0 + 2.0 * jnp.arange(NZ, dtype=jnp.float32) / (NZ - 1)) / 3.0
    values = jax.random.uniform(first_key, (NY, NZ, NX), jnp.float32)
    return 0.01 + 0.99 * values * ramp[None, :, None]


def draw_stiffness(key, part):
    key = jax.random.fold_in(key, 23)
    first_key, second_key = jax.random.split(key)
    offdiag = jax.random.uniform(first_key, (24, 24), jnp.float32, -0.06, 0.06)
    offdiag = 0.5 * (offdiag + offdiag.T)
    identity = jnp.eye(24, dtype=jnp.float32)
    diagonal = jax.random.uniform(second_key, (24,), jnp.float32, 1.5, 2.5)
    return offdiag * (1.0 - identity) + jnp.diag(diagonal)


def set_ends(values, rng, smallest, top_value):
    longest = values.shape.index(max(values.shape))
    spots = []
    for shift in (0, 1):
        where = [jax.random.randint(jax.random.fold_in(rng, axis), (), 0, length) for axis, length in enumerate(values.shape)]
        where[longest] = (where[longest] + shift) % values.shape[longest]
        spots.append(tuple(where))
    return values.at[spots[0]].set(smallest).at[spots[1]].set(top_value)


def block_scale(own_key, dims, pieces, least, largest):
    level = 1.0
    for axis_at, parts in pieces:
        draws = jax.random.uniform(jax.random.fold_in(jax.random.fold_in(own_key, 6), axis_at), (parts,), jnp.float32, least / len(pieces), largest / len(pieces))
        level = level * jnp.repeat(jnp.exp(draws), dims[axis_at] // parts).reshape((-1,) + (1,) * (len(dims) - 1 - axis_at))
    return level


def centred(own_key, shape, scale, reach, cuts=(), held_as=jnp.bfloat16):
    drawn = jax.random.normal(own_key, shape, jnp.float32) * scale
    if len(cuts) > 0:
        drawn = block_scale(own_key, shape, cuts, -0.22, 0.18) * drawn
    return jnp.clip(drawn, min=-reach, max=reach).astype(held_as)


def setup_inputs(seed: int = 0) -> dict:
    splits = jax.random.split(jax.random.key(seed), 6)
    displacement = centred(splits[0], (9, NY, NZ, NX), 0.1, 0.8, ((1, 8), (2, 4)), jnp.float32)
    density = draw_density(jax.random.fold_in(splits[5], 71), 0)
    passive = set_ends((jax.random.randint(splits[2], (NY, NZ, NX), 0, 16) < 1).astype(jnp.int32), jax.random.fold_in(splits[2], 1), 0, 1)
    solid = set_ends((jax.random.randint(splits[3], (NY, NZ, NX), 0, 16) < 1).astype(jnp.int32), jax.random.fold_in(splits[3], 1), 0, 1)
    stiffness = draw_stiffness(jax.random.fold_in(splits[5], 71), 0)
    return dict(displacement=displacement, density=density, passive=passive, solid=solid, stiffness=stiffness)


smoothing = 0.52
move_limit = 0.2
floor_density = 0.001
bracket_end = 12.0

def cheb_weights():
    spectrum_top = 1.0 + 12.0 * smoothing
    centre_value = (spectrum_top + 1.0) / 2.0
    half_width = (spectrum_top - 1.0) / 2.0
    ratio_value = centre_value / half_width
    first_rho = 1.0 / ratio_value
    second_rho = 1.0 / (2.0 * ratio_value - first_rho)
    third_rho = 1.0 / (2.0 * ratio_value - second_rho)
    return (centre_value, second_rho * first_rho, 2.0 * second_rho / half_width, third_rho * second_rho, 2.0 * third_rho / half_width)

def stencil(field):
    centre = field[1:-1, 1:-1]
    xpadded = jnp.pad(centre, ((0, 0), (0, 0), (1, 1)))
    beside = field[2:, 1:-1] + field[:-2, 1:-1] + field[1:-1, 2:] + field[1:-1, :-2]
    beside = beside + xpadded[:, :, 2:] + xpadded[:, :, :-2]
    return (1.0 + 6.0 * smoothing) * centre - smoothing * beside

def energy(lower, upper, stiffness):
    zcount = lower.shape[1] - 1
    xcount = lower.shape[2]
    planes = (jnp.pad(lower, ((0, 0), (0, 0), (0, 1))), jnp.pad(upper, ((0, 0), (0, 0), (0, 1))))
    corners = []
    for ylift in (0, 1):
        for zlift in (0, 1):
            for xlift in (0, 1):
                corners.append(planes[ylift][:, zlift:zlift + zcount, xlift:xlift + xcount])
    stacked = jnp.stack(corners).reshape(8, 3, 3, zcount * xcount)
    dofs = jnp.transpose(stacked, (0, 2, 1, 3)).reshape(24, 3 * zcount * xcount)
    forces = jnp.dot(stiffness, dofs, precision=lax.Precision.HIGHEST, preferred_element_type=jnp.float32)
    return lax.optimization_barrier(jnp.sum(dofs * forces, axis=0)).reshape(3, zcount, xcount).sum(axis=0)

def update(density, drive, passive, solid, loglam):
    candidate = density * jnp.sqrt(drive * jnp.exp(-loglam))
    lower = jnp.maximum(density - move_limit, floor_density)
    upper = jnp.minimum(density + move_limit, 1.0)
    candidate = jnp.clip(candidate, lower, upper)
    return jnp.where(solid == 1, 1.0, jnp.where(passive == 1, floor_density, candidate))

def operate(field):
    return stencil(jnp.pad(field, ((1, 1), (1, 1), (0, 0))))

def reference(displacement, density, passive, solid, stiffness):
    rows_total = displacement.shape[1]

    def one_row(index):
        index = index.astype(jnp.int32)
        nxt = jnp.minimum(index + 1, rows_total - 1).astype(jnp.int32)
        lower = lax.dynamic_index_in_dim(displacement, index, 1, keepdims=False)
        upper = lax.dynamic_index_in_dim(displacement, nxt, 1, keepdims=False)
        upper = upper * (index + 1 < rows_total).astype(displacement.dtype)
        lower = jnp.pad(lower, ((0, 0), (0, 1), (0, 0)))
        upper = jnp.pad(upper, ((0, 0), (0, 1), (0, 0)))
        return energy(lower, upper, stiffness)
    work = lax.map(one_row, jnp.arange(rows_total, dtype=jnp.int32))
    source = density * (-3.0 * density * density * work)
    centre_value, weight_one, weight_two, weight_three, weight_four = cheb_weights()
    first = source / centre_value
    resid = source - operate(first)
    second = weight_one * first + weight_two * resid
    iterate = first + second
    resid = resid - operate(second)
    iterate = iterate + weight_three * second + weight_four * resid
    drive = jnp.maximum(-iterate / density, 0.0)
    masked = jnp.where(solid == 1, 1.0, jnp.where(passive == 1, floor_density, density))
    target = jnp.sum(masked)
    lower_log = jnp.asarray(-bracket_end, jnp.float32)
    upper_log = jnp.asarray(bracket_end, jnp.float32)
    for step in range(ITERS):
        middle = 0.5 * (lower_log + upper_log)
        volume = jnp.sum(update(density, drive, passive, solid, middle))
        above = volume > target
        lower_log = jnp.where(above, middle, lower_log)
        upper_log = jnp.where(above, upper_log, middle)
    log_multiplier = 0.5 * (lower_log + upper_log)
    return (update(density, drive, passive, solid, log_multiplier), log_multiplier)
```

```python
import functools

import jax
import jax.numpy as jnp
from jax import lax
from jax.experimental import pallas as pl
from jax.experimental.pallas import tpu as pltpu
from jax.sharding import PartitionSpec as P

ITERS = 8
POINTS = 2**ITERS

smoothing = 0.52
move_limit = 0.2
floor_density = 0.001
bracket_end = 12.0

f32 = jnp.float32
bf16 = jnp.bfloat16


def cheb_weights():
    spectrum_top = 1.0 + 12.0 * smoothing
    centre_value = (spectrum_top + 1.0) / 2.0
    half_width = (spectrum_top - 1.0) / 2.0
    ratio_value = centre_value / half_width
    first_rho = 1.0 / ratio_value
    second_rho = 1.0 / (2.0 * ratio_value - first_rho)
    third_rho = 1.0 / (2.0 * ratio_value - second_rho)
    return (
        centre_value,
        second_rho * first_rho,
        2.0 * second_rho / half_width,
        third_rho * second_rho,
        2.0 * third_rho / half_width,
    )


def filter_weights():
    t, w1, w2, w3, w4 = cheb_weights()
    diag = 1.0 + 6.0 * smoothing
    alpha = w1 / t + w2 * (1.0 - diag / t)
    beta = w2 * smoothing / t
    gamma = 1.0 / t - w4 * w1 / (t * w2)
    delta = 1.0 + w3 + w4 / w2 - w4 * diag
    eps = w4 * smoothing
    return alpha, beta, gamma, delta, eps


def lane_up(v):
    n = v.shape[-1]
    lane = lax.broadcasted_iota(jnp.int32, v.shape, v.ndim - 1)
    return jnp.where(lane < n - 1, pltpu.roll(v, n - 1, v.ndim - 1), 0.0)


def lane_down(v):
    n = v.shape[-1]
    lane = lax.broadcasted_iota(jnp.int32, v.shape, v.ndim - 1)
    return jnp.where(lane > 0, pltpu.roll(v, 1, v.ndim - 1), 0.0)


def build_matrix(stiff, mat):
    shape = (24, 112)
    col = lax.broadcasted_iota(jnp.int32, shape, 1)
    row = lax.broadcasted_iota(jnp.int32, shape, 0)
    main = col < 96
    dy = jnp.where(main, jnp.where(col >= 48, 1, 0), jnp.where(col >= 104, 1, 0))
    q = col - 48 * dy
    e = col - 96 - 8 * dy
    c = jnp.where(main, q >> 4, e >> 1)
    dx = jnp.where(main, (q >> 3) & 1, e & 1)
    valid = main | (e < 6)
    dof0 = 3 * (4 * dy + dx) + c
    pick0 = jnp.where(main & (row == dof0), 1.0, 0.0)
    pick1 = jnp.where(valid & (row == dof0 + 6), 1.0, 0.0)
    k = stiff[...]
    hp = lax.Precision.HIGHEST
    k0 = jnp.dot(k, pick0, precision=hp, preferred_element_type=f32)
    k1 = jnp.dot(k, pick1, precision=hp, preferred_element_type=f32)
    col8 = lax.broadcasted_iota(jnp.int32, (8, 112), 1)
    row8 = lax.broadcasted_iota(jnp.int32, (8, 112), 0)
    main8 = col8 < 96
    zc = col8 & 7
    m0 = main8 & (zc == row8)
    m1 = jnp.where(main8, zc, 8) == row8 + 1
    rows = []
    for dz in range(2):
        for dy_ in range(2):
            for c_ in range(3):
                for dx_ in range(2):
                    r = 3 * (4 * dy_ + 2 * dz + dx_) + c_
                    rows.append(jnp.where(m0, k0[r : r + 1], 0.0) + jnp.where(m1, k1[r : r + 1], 0.0))
    full = jnp.concatenate(rows, axis=0)
    hi = full.astype(bf16)
    lo = (full - hi.astype(f32)).astype(bf16)
    mat[:, 0:112] = hi
    mat[:, 112:224] = lo


def prepare(plane, ext, p, main_s, ext_s, mul_s):
    for l in range(3):
        for c in range(3):
            u = plane(3 * l + c)
            x = ext(3 * l + c)
            nz, nx = u.shape
            last = lax.broadcasted_iota(jnp.int32, u.shape, 0) == nz - 1
            both = (u, lane_up(u))
            bothx = (x, lane_up(x))
            for w in range(nz // 8):
                sl = slice(8 * w, 8 * w + 8)
                main_s[p, l, 16 * c : 16 * c + 16, w * nx : (w + 1) * nx] = jnp.concatenate(
                    [both[0][sl], both[1][sl]], axis=0
                ).astype(bf16)
            for dx in range(2):
                v, vx = both[dx], bothx[dx]
                k = 2 * c + dx
                for w in range(nz // 8):
                    nxt = v[8 * w + 8 : 8 * w + 9] if 8 * w + 8 < nz else vx
                    ext_s[p, l, k : k + 1, w * nx : (w + 1) * nx] = nxt
                m = 2.0 * v - v.astype(bf16).astype(f32)
                mx = 2.0 * vx - vx.astype(bf16).astype(f32)
                mul_s[p, l, k, 0] = m
                mul_s[p, l, k, 1] = jnp.where(last, jnp.broadcast_to(mx, v.shape), pltpu.roll(m, nz - 1, 0))


def energy_kernel(disp, fy, fz, fc, dens, stiff, src, zlow, zhigh, mat, main_s, ext_s, mul_s):
    _, ny, nz, nx = disp.shape
    build_matrix(stiff, mat)
    ext_s[...] = jnp.zeros_like(ext_s)

    prepare(lambda i: fy[i], lambda i: fc[i : i + 1], ny, main_s, ext_s, mul_s)

    def prep_body(y, _):
        prepare(lambda i: disp[i, y], lambda i: fz[i, pl.ds(y, 1)], y, main_s, ext_s, mul_s)
        return 0

    lax.fori_loop(0, ny, prep_body, 0)

    def body(y, _):
        acc = [None] * (nz // 8)
        for l in range(3):
            ext = jnp.concatenate([ext_s[y, l], ext_s[y + 1, l]], axis=0).astype(bf16)
            one = jnp.concatenate([main_s[y, l], main_s[y + 1, l], ext], axis=0)
            rhs = jnp.concatenate([one, one], axis=0)
            force = jnp.dot(mat[...], rhs, preferred_element_type=f32)
            i = 0
            for dz in range(2):
                for dy in range(2):
                    for k in range(6):
                        for w in range(nz // 8):
                            term = (
                                force[8 * i : 8 * i + 8, w * nx : (w + 1) * nx]
                                * mul_s[y + dy, l, k, dz, 8 * w : 8 * w + 8]
                            )
                            acc[w] = term if acc[w] is None else acc[w] + term
                        i += 1
        d = dens[y]
        s = d * (-3.0 * d * d * jnp.concatenate(acc, axis=0))
        src[y] = s
        for layer in range(2):
            zlow[layer, pl.ds(y, 1)] = s[layer : layer + 1]
            zhigh[layer, pl.ds(y, 1)] = s[nz - 2 + layer : nz - 1 + layer]
        return 0

    lax.fori_loop(0, ny, body, 0)


def energy_call(disp, fy, fz, fc, dens, stiff):
    _, ny, nz, nx = disp.shape
    return pl.pallas_call(
        energy_kernel,
        out_shape=(
            jax.ShapeDtypeStruct((ny, nz, nx), f32),
            jax.ShapeDtypeStruct((2, ny, nx), f32),
            jax.ShapeDtypeStruct((2, ny, nx), f32),
        ),
        scratch_shapes=[
            pltpu.VMEM((192, 224), bf16),
            pltpu.VMEM((ny + 1, 3, 48, nx * (nz // 8)), bf16),
            pltpu.VMEM((ny + 1, 3, 8, nx * (nz // 8)), f32),
            pltpu.VMEM((ny + 1, 3, 6, 2, nz, nx), f32),
        ],
        compiler_params=pltpu.CompilerParams(vmem_limit_bytes=48 * 2**20),
        name="energy",
    )(disp, fy, fz, fc, dens, stiff)


def filter_kernel(flags, src, yl, yh, zl, zh, dens, passive, solid, amp, low, high, vols, s_s, d_s, acc_s):
    ny, nz, nx = src.shape
    alpha, beta, gamma, delta, eps = filter_weights()
    off = 8
    s_s[2 : ny + 2, off : off + nz] = src[...]
    s_s[0:2, off : off + nz] = yl[...]
    s_s[ny + 2 : ny + 4, off : off + nz] = yh[...]
    for y in range(ny + 4):
        s_s[y, off - 2 : off] = jnp.concatenate([zl[0, y : y + 1], zl[1, y : y + 1]], axis=0)
        s_s[y, off + nz : off + nz + 2] = jnp.concatenate([zh[0, y : y + 1], zh[1, y : y + 1]], axis=0)

    rows = s_s.shape[1]

    def beside(v):
        return pltpu.roll(v, 1, 0) + pltpu.roll(v, rows - 1, 0) + lane_up(v) + lane_down(v)

    row = lax.broadcasted_iota(jnp.int32, (rows, nx), 0)
    keep = jnp.where(row < off, flags[2], jnp.where(row >= off + nz, flags[3], 1)) == 1

    def second(y, _):
        c = s_s[y + 1]
        d2 = alpha * c + beta * (beside(c) + s_s[y] + s_s[y + 2])
        inside = jnp.where(y == 0, flags[0], jnp.where(y == ny + 1, flags[1], 1)) == 1
        d_s[y] = jnp.where(keep & inside, d2, 0.0)
        return 0

    lax.fori_loop(0, ny + 2, second, 0)

    def third(y, total):
        d2 = d_s[y + 1]
        p3 = gamma * s_s[y + 2] + delta * d2 + eps * (beside(d2) + d_s[y] + d_s[y + 2])
        p3 = p3[off : off + nz]
        d = dens[y]
        amp[y] = jnp.sqrt(jnp.maximum(-p3 * d, 0.0))
        sol = solid[y] == 1
        pas = passive[y] == 1
        lower = jnp.maximum(d - move_limit, floor_density)
        upper = jnp.minimum(d + move_limit, 1.0)
        low[y] = jnp.where(sol, 1.0, jnp.where(pas, floor_density, lower))
        high[y] = jnp.where(sol, 1.0, jnp.where(pas, floor_density, upper))
        masked = jnp.where(sol, 1.0, jnp.where(pas, floor_density, d))
        return total + masked

    total = lax.fori_loop(0, ny, third, jnp.zeros((nz, nx), f32))
    target = jnp.sum(total, axis=0, keepdims=True)

    groups = POINTS // 8
    half = groups // 2
    sub = lax.broadcasted_iota(jnp.int32, (8, nx), 0)
    for part in range(2):
        scale = []
        for g in range(half):
            k = sub + 8 * (part * half + g)
            mid = -bracket_end + (2.0 * bracket_end / POINTS) * k.astype(f32)
            scale.append(jnp.exp(-0.5 * mid))

        def volume(y, acc):
            acc = list(acc)
            for z in range(nz):
                a = jnp.broadcast_to(amp[y, z : z + 1], (8, nx))
                lo = jnp.broadcast_to(low[y, z : z + 1], (8, nx))
                hi = jnp.broadcast_to(high[y, z : z + 1], (8, nx))
                for g in range(half):
                    acc[g] = acc[g] + jnp.minimum(jnp.maximum(a * scale[g], lo), hi)
            return tuple(acc)

        acc = lax.fori_loop(0, ny, volume, tuple(jnp.zeros((8, nx), f32) for _ in range(half)))
        for g in range(half):
            value = acc[g]
            if part == 0 and g == 0:
                value = jnp.where(sub == 0, jnp.broadcast_to(target, (8, nx)), value)
            acc_s[8 * (part * half + g) : 8 * (part * half + g) + 8] = value
    vols[...] = jnp.sum(jnp.transpose(acc_s[...]), axis=0, keepdims=True)


def filter_call(flags, src, yl, yh, zl, zh, dens, passive, solid):
    ny, nz, nx = src.shape
    field = jax.ShapeDtypeStruct((ny, nz, nx), f32)
    vmem = pl.BlockSpec(memory_space=pltpu.VMEM)
    return pl.pallas_call(
        filter_kernel,
        in_specs=[pl.BlockSpec(memory_space=pltpu.SMEM)] + [vmem] * 8,
        out_shape=(field, field, field, jax.ShapeDtypeStruct((1, POINTS), f32)),
        scratch_shapes=[
            pltpu.VMEM((ny + 4, nz + 16, nx), f32),
            pltpu.VMEM((ny + 2, nz + 16, nx), f32),
            pltpu.VMEM((POINTS, nx), f32),
        ],
        compiler_params=pltpu.CompilerParams(vmem_limit_bytes=32 * 2**20),
        name="filter",
    )(flags, src, yl, yh, zl, zh, dens, passive, solid)


def update_kernel(vols, amp, low, high, new, logm):
    target = vols[0, 0]
    k = jnp.int32(0)
    step = POINTS // 2
    while step >= 1:
        k = jnp.where(vols[0, k + step] > target, k + step, k)
        step //= 2
    middle = -bracket_end + (2.0 * bracket_end / POINTS) * (k.astype(f32) + 0.5)
    logm[0] = middle
    scale = jnp.exp(jnp.full((1, amp.shape[-1]), -0.5 * middle, f32))

    def body(y, _):
        new[y] = jnp.minimum(jnp.maximum(amp[y] * scale, low[y]), high[y])
        return 0

    lax.fori_loop(0, amp.shape[0], body, 0)


def update_call(vols, amp, low, high):
    vmem = pl.BlockSpec(memory_space=pltpu.VMEM)
    return pl.pallas_call(
        update_kernel,
        in_specs=[pl.BlockSpec(memory_space=pltpu.SMEM), vmem, vmem, vmem],
        out_specs=(vmem, pl.BlockSpec(memory_space=pltpu.SMEM)),
        out_shape=(jax.ShapeDtypeStruct(amp.shape, f32), jax.ShapeDtypeStruct((1,), f32)),
        name="update",
    )(vols, amp, low, high)


def to_lower(value, axis):
    count = lax.axis_size(axis)
    return lax.ppermute(value, axis, [(i + 1, i) for i in range(count - 1)])


def to_upper(value, axis):
    count = lax.axis_size(axis)
    return lax.ppermute(value, axis, [(i, i + 1) for i in range(count - 1)])


def on_device(displacement, density, passive, solid, stiffness):
    ny, nz, nx = density.shape
    gy, gz = lax.axis_size("gy"), lax.axis_size("gz")
    iy, iz = lax.axis_index("gy"), lax.axis_index("gz")

    fy = to_lower(displacement[:, 0], "gy")
    fz = to_lower(displacement[:, :, 0], "gz")
    pairs = [((z + 1) * gy + y + 1, z * gy + y) for z in range(gz - 1) for y in range(gy - 1)]
    fc = lax.ppermute(displacement[:, 0, 0], ("gz", "gy"), pairs)
    src, zlow, zhigh = energy_call(displacement, fy, fz, fc, density, stiffness)

    yl = to_upper(src[ny - 2 :], "gy")
    yh = to_lower(src[:2], "gy")
    own_low = jnp.concatenate([yl[:, 0:2].swapaxes(0, 1), zlow, yh[:, 0:2].swapaxes(0, 1)], axis=1)
    own_high = jnp.concatenate([yl[:, nz - 2 :].swapaxes(0, 1), zhigh, yh[:, nz - 2 :].swapaxes(0, 1)], axis=1)
    zl = to_upper(own_high, "gz")
    zh = to_lower(own_low, "gz")
    flags = jnp.stack([iy > 0, iy < gy - 1, iz > 0, iz < gz - 1]).astype(jnp.int32)
    amp, low, high, vols = filter_call(flags, src, yl, yh, zl, zh, density, passive, solid)

    vols = lax.psum(vols, ("gz", "gy"))
    new, logm = update_call(vols, amp, low, high)
    return new, logm.reshape(())


def solution(mesh):
    placed = (
        P(None, "gy", "gz", None),
        P("gy", "gz", None),
        P("gy", "gz", None),
        P("gy", "gz", None),
        P(),
    )
    return jax.shard_map(
        on_device, mesh=mesh, in_specs=placed, out_specs=(P("gy", "gz", None), P()), check_vma=False
    )
```

```python
import functools

import jax
import jax.numpy as jnp
from jax import lax
from jax.experimental import pallas as pl
from jax.experimental.pallas import tpu as pltpu
from jax.sharding import PartitionSpec as P

ITERS = 8
POINTS = 2**ITERS

smoothing = 0.52
move_limit = 0.2
floor_density = 0.001
bracket_end = 12.0

f32 = jnp.float32
bf16 = jnp.bfloat16


def cheb_weights():
    spectrum_top = 1.0 + 12.0 * smoothing
    centre_value = (spectrum_top + 1.0) / 2.0
    half_width = (spectrum_top - 1.0) / 2.0
    ratio_value = centre_value / half_width
    first_rho = 1.0 / ratio_value
    second_rho = 1.0 / (2.0 * ratio_value - first_rho)
    third_rho = 1.0 / (2.0 * ratio_value - second_rho)
    return (
        centre_value,
        second_rho * first_rho,
        2.0 * second_rho / half_width,
        third_rho * second_rho,
        2.0 * third_rho / half_width,
    )


def filter_weights():
    t, w1, w2, w3, w4 = cheb_weights()
    diag = 1.0 + 6.0 * smoothing
    alpha = w1 / t + w2 * (1.0 - diag / t)
    beta = w2 * smoothing / t
    gamma = 1.0 / t - w4 * w1 / (t * w2)
    delta = 1.0 + w3 + w4 / w2 - w4 * diag
    eps = w4 * smoothing
    return alpha, beta, gamma, delta, eps


def lane_up(v):
    n = v.shape[-1]
    lane = lax.broadcasted_iota(jnp.int32, v.shape, v.ndim - 1)
    return jnp.where(lane < n - 1, pltpu.roll(v, n - 1, v.ndim - 1), 0.0)


def lane_down(v):
    n = v.shape[-1]
    lane = lax.broadcasted_iota(jnp.int32, v.shape, v.ndim - 1)
    return jnp.where(lane > 0, pltpu.roll(v, 1, v.ndim - 1), 0.0)


def build_matrix(stiff, mat):
    shape = (24, 112)
    col = lax.broadcasted_iota(jnp.int32, shape, 1)
    row = lax.broadcasted_iota(jnp.int32, shape, 0)
    main = col < 96
    dy = jnp.where(main, jnp.where(col >= 48, 1, 0), jnp.where(col >= 104, 1, 0))
    q = col - 48 * dy
    e = col - 96 - 8 * dy
    c = jnp.where(main, q >> 4, e >> 1)
    dx = jnp.where(main, (q >> 3) & 1, e & 1)
    valid = main | (e < 6)
    dof0 = 3 * (4 * dy + dx) + c
    pick0 = jnp.where(main & (row == dof0), 1.0, 0.0)
    pick1 = jnp.where(valid & (row == dof0 + 6), 1.0, 0.0)
    k = stiff[...]
    hp = lax.Precision.HIGHEST
    k0 = jnp.dot(k, pick0, precision=hp, preferred_element_type=f32)
    k1 = jnp.dot(k, pick1, precision=hp, preferred_element_type=f32)
    col8 = lax.broadcasted_iota(jnp.int32, (8, 112), 1)
    row8 = lax.broadcasted_iota(jnp.int32, (8, 112), 0)
    main8 = col8 < 96
    zc = col8 & 7
    m0 = main8 & (zc == row8)
    m1 = jnp.where(main8, zc, 8) == row8 + 1
    rows = []
    for dz in range(2):
        for dy_ in range(2):
            for c_ in range(3):
                for dx_ in range(2):
                    r = 3 * (4 * dy_ + 2 * dz + dx_) + c_
                    rows.append(jnp.where(m0, k0[r : r + 1], 0.0) + jnp.where(m1, k1[r : r + 1], 0.0))
    full = jnp.concatenate(rows, axis=0)
    hi = full.astype(bf16)
    lo = (full - hi.astype(f32)).astype(bf16)
    mat[:, 0:112] = hi
    mat[:, 112:224] = lo


def prepare(plane, ext, p, main_s, ext_s, mul_s):
    for l in range(3):
        for c in range(3):
            u = plane(3 * l + c)
            x = ext(3 * l + c)
            nz, nx = u.shape
            last = lax.broadcasted_iota(jnp.int32, u.shape, 0) == nz - 1
            both = (u, lane_up(u))
            bothx = (x, lane_up(x))
            for w in range(nz // 8):
                sl = slice(8 * w, 8 * w + 8)
                main_s[p, l, 16 * c : 16 * c + 16, w * nx : (w + 1) * nx] = jnp.concatenate(
                    [both[0][sl], both[1][sl]], axis=0
                ).astype(bf16)
            for dx in range(2):
                v, vx = both[dx], bothx[dx]
                k = 2 * c + dx
                for w in range(nz // 8):
                    nxt = v[8 * w + 8 : 8 * w + 9] if 8 * w + 8 < nz else vx
                    ext_s[p, l, k : k + 1, w * nx : (w + 1) * nx] = nxt
                m = 2.0 * v - v.astype(bf16).astype(f32)
                mx = 2.0 * vx - vx.astype(bf16).astype(f32)
                mul_s[p, l, k, 0] = m
                mul_s[p, l, k, 1] = jnp.where(last, jnp.broadcast_to(mx, v.shape), pltpu.roll(m, nz - 1, 0))


def energy_kernel(disp, fy, fz, fc, dens, stiff, src, zlow, zhigh, mat, main_s, ext_s, mul_s):
    _, ny, nz, nx = disp.shape
    build_matrix(stiff, mat)
    ext_s[...] = jnp.zeros_like(ext_s)

    prepare(lambda i: fy[i], lambda i: fc[i : i + 1], ny, main_s, ext_s, mul_s)

    def prep_body(y, _):
        prepare(lambda i: disp[i, y], lambda i: fz[i, pl.ds(y, 1)], y, main_s, ext_s, mul_s)
        return 0

    lax.fori_loop(0, ny, prep_body, 0)

    def body(y, _):
        acc = [None] * (nz // 8)
        for l in range(3):
            ext = jnp.concatenate([ext_s[y, l], ext_s[y + 1, l]], axis=0).astype(bf16)
            one = jnp.concatenate([main_s[y, l], main_s[y + 1, l], ext], axis=0)
            rhs = jnp.concatenate([one, one], axis=0)
            force = jnp.dot(mat[...], rhs, preferred_element_type=f32)
            i = 0
            for dz in range(2):
                for dy in range(2):
                    for k in range(6):
                        for w in range(nz // 8):
                            term = (
                                force[8 * i : 8 * i + 8, w * nx : (w + 1) * nx]
                                * mul_s[y + dy, l, k, dz, 8 * w : 8 * w + 8]
                            )
                            acc[w] = term if acc[w] is None else acc[w] + term
                        i += 1
        d = dens[y]
        s = d * (-3.0 * d * d * jnp.concatenate(acc, axis=0))
        src[y] = s
        for layer in range(2):
            zlow[layer, pl.ds(y, 1)] = s[layer : layer + 1]
            zhigh[layer, pl.ds(y, 1)] = s[nz - 2 + layer : nz - 1 + layer]
        return 0

    lax.fori_loop(0, ny, body, 0)


def energy_call(disp, fy, fz, fc, dens, stiff):
    _, ny, nz, nx = disp.shape
    return pl.pallas_call(
        energy_kernel,
        out_shape=(
            jax.ShapeDtypeStruct((ny, nz, nx), f32),
            jax.ShapeDtypeStruct((2, ny, nx), f32),
            jax.ShapeDtypeStruct((2, ny, nx), f32),
        ),
        scratch_shapes=[
            pltpu.VMEM((192, 224), bf16),
            pltpu.VMEM((ny + 1, 3, 48, nx * (nz // 8)), bf16),
            pltpu.VMEM((ny + 1, 3, 8, nx * (nz // 8)), f32),
            pltpu.VMEM((ny + 1, 3, 6, 2, nz, nx), f32),
        ],
        compiler_params=pltpu.CompilerParams(vmem_limit_bytes=48 * 2**20),
        name="energy",
    )(disp, fy, fz, fc, dens, stiff)


def filter_kernel(flags, src, yl, yh, zl, zh, dens, passive, solid, amp, low, high, vols, s_s, d_s, acc_s):
    ny, nz, nx = src.shape
    alpha, beta, gamma, delta, eps = filter_weights()
    off = 8
    s_s[2 : ny + 2, off : off + nz] = src[...]
    s_s[0:2, off : off + nz] = yl[...]
    s_s[ny + 2 : ny + 4, off : off + nz] = yh[...]
    for y in range(ny + 4):
        s_s[y, off - 2 : off] = jnp.concatenate([zl[0, y : y + 1], zl[1, y : y + 1]], axis=0)
        s_s[y, off + nz : off + nz + 2] = jnp.concatenate([zh[0, y : y + 1], zh[1, y : y + 1]], axis=0)

    rows = s_s.shape[1]

    def beside(v):
        return pltpu.roll(v, 1, 0) + pltpu.roll(v, rows - 1, 0) + lane_up(v) + lane_down(v)

    row = lax.broadcasted_iota(jnp.int32, (rows, nx), 0)
    keep = jnp.where(row < off, flags[2], jnp.where(row >= off + nz, flags[3], 1)) == 1

    def second(y, _):
        c = s_s[y + 1]
        d2 = alpha * c + beta * (beside(c) + s_s[y] + s_s[y + 2])
        inside = jnp.where(y == 0, flags[0], jnp.where(y == ny + 1, flags[1], 1)) == 1
        d_s[y] = jnp.where(keep & inside, d2, 0.0)
        return 0

    lax.fori_loop(0, ny + 2, second, 0)

    def third(y, total):
        d2 = d_s[y + 1]
        p3 = gamma * s_s[y + 2] + delta * d2 + eps * (beside(d2) + d_s[y] + d_s[y + 2])
        p3 = p3[off : off + nz]
        d = dens[y]
        amp[y] = jnp.sqrt(jnp.maximum(-p3 * d, 0.0))
        sol = solid[y] == 1
        pas = passive[y] == 1
        lower = jnp.maximum(d - move_limit, floor_density)
        upper = jnp.minimum(d + move_limit, 1.0)
        low[y] = jnp.where(sol, 1.0, jnp.where(pas, floor_density, lower))
        high[y] = jnp.where(sol, 1.0, jnp.where(pas, floor_density, upper))
        masked = jnp.where(sol, 1.0, jnp.where(pas, floor_density, d))
        return total + masked

    total = lax.fori_loop(0, ny, third, jnp.zeros((nz, nx), f32))
    target = jnp.sum(total, axis=0, keepdims=True)

    groups = POINTS // 8
    half = groups // 2
    sub = lax.broadcasted_iota(jnp.int32, (8, nx), 0)
    for part in range(2):
        scale = []
        for g in range(half):
            k = sub + 8 * (part * half + g)
            mid = -bracket_end + (2.0 * bracket_end / POINTS) * k.astype(f32)
            scale.append(jnp.exp(-0.5 * mid))

        def volume(y, acc):
            acc = list(acc)
            for z in range(nz):
                a = jnp.broadcast_to(amp[y, z : z + 1], (8, nx))
                lo = jnp.broadcast_to(low[y, z : z + 1], (8, nx))
                hi = jnp.broadcast_to(high[y, z : z + 1], (8, nx))
                for g in range(half):
                    acc[g] = acc[g] + jnp.minimum(jnp.maximum(a * scale[g], lo), hi)
            return tuple(acc)

        acc = lax.fori_loop(0, ny, volume, tuple(jnp.zeros((8, nx), f32) for _ in range(half)))
        for g in range(half):
            value = acc[g]
            if part == 0 and g == 0:
                value = jnp.where(sub == 0, jnp.broadcast_to(target, (8, nx)), value)
            acc_s[8 * (part * half + g) : 8 * (part * half + g) + 8] = value
    vols[...] = jnp.sum(jnp.transpose(acc_s[...]), axis=0, keepdims=True)


def filter_call(flags, src, yl, yh, zl, zh, dens, passive, solid):
    ny, nz, nx = src.shape
    field = jax.ShapeDtypeStruct((ny, nz, nx), f32)
    vmem = pl.BlockSpec(memory_space=pltpu.VMEM)
    return pl.pallas_call(
        filter_kernel,
        in_specs=[pl.BlockSpec(memory_space=pltpu.SMEM)] + [vmem] * 8,
        out_shape=(field, field, field, jax.ShapeDtypeStruct((1, POINTS), f32)),
        scratch_shapes=[
            pltpu.VMEM((ny + 4, nz + 16, nx), f32),
            pltpu.VMEM((ny + 2, nz + 16, nx), f32),
            pltpu.VMEM((POINTS, nx), f32),
        ],
        compiler_params=pltpu.CompilerParams(vmem_limit_bytes=32 * 2**20),
        name="filter",
    )(flags, src, yl, yh, zl, zh, dens, passive, solid)


def update_kernel(vols, amp, low, high, new, logm):
    target = vols[0, 0]
    k = jnp.int32(0)
    step = POINTS // 2
    while step >= 1:
        k = jnp.where(vols[0, k + step] > target, k + step, k)
        step //= 2
    middle = -bracket_end + (2.0 * bracket_end / POINTS) * (k.astype(f32) + 0.5)
    logm[0] = middle
    scale = jnp.exp(jnp.full((1, amp.shape[-1]), -0.5 * middle, f32))

    def body(y, _):
        new[y] = jnp.minimum(jnp.maximum(amp[y] * scale, low[y]), high[y])
        return 0

    lax.fori_loop(0, amp.shape[0], body, 0)


def update_call(vols, amp, low, high):
    vmem = pl.BlockSpec(memory_space=pltpu.VMEM)
    return pl.pallas_call(
        update_kernel,
        in_specs=[pl.BlockSpec(memory_space=pltpu.SMEM), vmem, vmem, vmem],
        out_specs=(vmem, pl.BlockSpec(memory_space=pltpu.SMEM)),
        out_shape=(jax.ShapeDtypeStruct(amp.shape, f32), jax.ShapeDtypeStruct((1,), f32)),
        name="update",
    )(vols, amp, low, high)


def to_lower(value, axis):
    count = lax.axis_size(axis)
    return lax.ppermute(value, axis, [(i + 1, i) for i in range(count - 1)])


def to_upper(value, axis):
    count = lax.axis_size(axis)
    return lax.ppermute(value, axis, [(i, i + 1) for i in range(count - 1)])


def total_over(value, axis):
    count = lax.axis_size(axis)
    bit = 1
    while bit < count:
        value = value + lax.ppermute(value, axis, [(i, i ^ bit) for i in range(count)])
        bit *= 2
    return value


def on_device(displacement, density, passive, solid, stiffness):
    ny, nz, nx = density.shape
    gy, gz = lax.axis_size("gy"), lax.axis_size("gz")
    iy, iz = lax.axis_index("gy"), lax.axis_index("gz")

    fy = to_lower(displacement[:, 0], "gy")
    fz = to_lower(displacement[:, :, 0], "gz")
    pairs = [((z + 1) * gy + y + 1, z * gy + y) for z in range(gz - 1) for y in range(gy - 1)]
    fc = lax.ppermute(displacement[:, 0, 0], ("gz", "gy"), pairs)
    src, zlow, zhigh = energy_call(displacement, fy, fz, fc, density, stiffness)

    yl = to_upper(src[ny - 2 :], "gy")
    yh = to_lower(src[:2], "gy")
    own_low = jnp.concatenate([yl[:, 0:2].swapaxes(0, 1), zlow, yh[:, 0:2].swapaxes(0, 1)], axis=1)
    own_high = jnp.concatenate([yl[:, nz - 2 :].swapaxes(0, 1), zhigh, yh[:, nz - 2 :].swapaxes(0, 1)], axis=1)
    zl = to_upper(own_high, "gz")
    zh = to_lower(own_low, "gz")
    flags = jnp.stack([iy > 0, iy < gy - 1, iz > 0, iz < gz - 1]).astype(jnp.int32)
    amp, low, high, vols = filter_call(flags, src, yl, yh, zl, zh, density, passive, solid)

    vols = total_over(total_over(vols, "gz"), "gy")
    new, logm = update_call(vols, amp, low, high)
    return new, logm.reshape(())


def solution(mesh):
    placed = (
        P(None, "gy", "gz", None),
        P("gy", "gz", None),
        P("gy", "gz", None),
        P("gy", "gz", None),
        P(),
    )
    return jax.shard_map(
        on_device, mesh=mesh, in_specs=placed, out_specs=(P("gy", "gz", None), P()), check_vma=False
    )
```

```python
import functools

import jax
import jax.numpy as jnp
from jax import lax
from jax.experimental import pallas as pl
from jax.experimental.pallas import tpu as pltpu
from jax.sharding import PartitionSpec as P

ITERS = 8
POINTS = 2**ITERS

smoothing = 0.52
move_limit = 0.2
floor_density = 0.001
bracket_end = 12.0

f32 = jnp.float32
bf16 = jnp.bfloat16


def cheb_weights():
    spectrum_top = 1.0 + 12.0 * smoothing
    centre_value = (spectrum_top + 1.0) / 2.0
    half_width = (spectrum_top - 1.0) / 2.0
    ratio_value = centre_value / half_width
    first_rho = 1.0 / ratio_value
    second_rho = 1.0 / (2.0 * ratio_value - first_rho)
    third_rho = 1.0 / (2.0 * ratio_value - second_rho)
    return (
        centre_value,
        second_rho * first_rho,
        2.0 * second_rho / half_width,
        third_rho * second_rho,
        2.0 * third_rho / half_width,
    )


def filter_weights():
    t, w1, w2, w3, w4 = cheb_weights()
    diag = 1.0 + 6.0 * smoothing
    alpha = w1 / t + w2 * (1.0 - diag / t)
    beta = w2 * smoothing / t
    gamma = 1.0 / t - w4 * w1 / (t * w2)
    delta = 1.0 + w3 + w4 / w2 - w4 * diag
    eps = w4 * smoothing
    return alpha, beta, gamma, delta, eps


def lane_up(v):
    n = v.shape[-1]
    lane = lax.broadcasted_iota(jnp.int32, v.shape, v.ndim - 1)
    return jnp.where(lane < n - 1, pltpu.roll(v, n - 1, v.ndim - 1), 0.0)


def lane_down(v):
    n = v.shape[-1]
    lane = lax.broadcasted_iota(jnp.int32, v.shape, v.ndim - 1)
    return jnp.where(lane > 0, pltpu.roll(v, 1, v.ndim - 1), 0.0)


def build_matrix(stiff, mat):
    shape = (24, 112)
    col = lax.broadcasted_iota(jnp.int32, shape, 1)
    row = lax.broadcasted_iota(jnp.int32, shape, 0)
    main = col < 96
    dy = jnp.where(main, jnp.where(col >= 48, 1, 0), jnp.where(col >= 104, 1, 0))
    q = col - 48 * dy
    e = col - 96 - 8 * dy
    c = jnp.where(main, q >> 4, e >> 1)
    dx = jnp.where(main, (q >> 3) & 1, e & 1)
    valid = main | (e < 6)
    dof0 = 3 * (4 * dy + dx) + c
    pick0 = jnp.where(main & (row == dof0), 1.0, 0.0)
    pick1 = jnp.where(valid & (row == dof0 + 6), 1.0, 0.0)
    k = stiff[...]
    hp = lax.Precision.HIGHEST
    k0 = jnp.dot(k, pick0, precision=hp, preferred_element_type=f32)
    k1 = jnp.dot(k, pick1, precision=hp, preferred_element_type=f32)
    col8 = lax.broadcasted_iota(jnp.int32, (8, 112), 1)
    row8 = lax.broadcasted_iota(jnp.int32, (8, 112), 0)
    main8 = col8 < 96
    zc = col8 & 7
    m0 = main8 & (zc == row8)
    m1 = jnp.where(main8, zc, 8) == row8 + 1
    rows = []
    for dz in range(2):
        for dy_ in range(2):
            for c_ in range(3):
                for dx_ in range(2):
                    r = 3 * (4 * dy_ + 2 * dz + dx_) + c_
                    rows.append(jnp.where(m0, k0[r : r + 1], 0.0) + jnp.where(m1, k1[r : r + 1], 0.0))
    full = jnp.concatenate(rows, axis=0)
    hi = full.astype(bf16)
    lo = (full - hi.astype(f32)).astype(bf16)
    mat[:, 0:112] = hi
    mat[:, 112:224] = lo


def prepare(plane, ext, p, main_s, ext_s, mul_s):
    for l in range(3):
        for c in range(3):
            u = plane(3 * l + c)
            x = ext(3 * l + c)
            nz, nx = u.shape
            last = lax.broadcasted_iota(jnp.int32, u.shape, 0) == nz - 1
            both = (u, lane_up(u))
            bothx = (x, lane_up(x))
            for w in range(nz // 8):
                sl = slice(8 * w, 8 * w + 8)
                main_s[p, l, 16 * c : 16 * c + 16, w * nx : (w + 1) * nx] = jnp.concatenate(
                    [both[0][sl], both[1][sl]], axis=0
                ).astype(bf16)
            for dx in range(2):
                v, vx = both[dx], bothx[dx]
                k = 2 * c + dx
                for w in range(nz // 8):
                    nxt = v[8 * w + 8 : 8 * w + 9] if 8 * w + 8 < nz else vx
                    ext_s[p, l, k : k + 1, w * nx : (w + 1) * nx] = nxt
                m = 2.0 * v - v.astype(bf16).astype(f32)
                mx = 2.0 * vx - vx.astype(bf16).astype(f32)
                mul_s[p, l, k, 0] = m
                mul_s[p, l, k, 1] = jnp.where(last, jnp.broadcast_to(mx, v.shape), pltpu.roll(m, nz - 1, 0))


def energy_kernel(disp, fy, fz, fc, dens, stiff, src, zlow, zhigh, mat, main_s, ext_s, mul_s):
    _, ny, nz, nx = disp.shape
    build_matrix(stiff, mat)
    ext_s[...] = jnp.zeros_like(ext_s)

    prepare(lambda i: fy[i], lambda i: fc[i : i + 1], ny, main_s, ext_s, mul_s)

    def prep_body(y, _):
        prepare(lambda i: disp[i, y], lambda i: fz[i, pl.ds(y, 1)], y, main_s, ext_s, mul_s)
        return 0

    lax.fori_loop(0, ny, prep_body, 0)

    def body(y, _):
        acc = [None] * (nz // 8)
        for l in range(3):
            ext = jnp.concatenate([ext_s[y, l], ext_s[y + 1, l]], axis=0).astype(bf16)
            one = jnp.concatenate([main_s[y, l], main_s[y + 1, l], ext], axis=0)
            rhs = jnp.concatenate([one, one], axis=0)
            force = jnp.dot(mat[...], rhs, preferred_element_type=f32)
            i = 0
            for dz in range(2):
                for dy in range(2):
                    for k in range(6):
                        for w in range(nz // 8):
                            term = (
                                force[8 * i : 8 * i + 8, w * nx : (w + 1) * nx]
                                * mul_s[y + dy, l, k, dz, 8 * w : 8 * w + 8]
                            )
                            acc[w] = term if acc[w] is None else acc[w] + term
                        i += 1
        d = dens[y]
        s = d * (-3.0 * d * d * jnp.concatenate(acc, axis=0))
        src[y] = s
        for layer in range(2):
            zlow[layer, pl.ds(y, 1)] = s[layer : layer + 1]
            zhigh[layer, pl.ds(y, 1)] = s[nz - 2 + layer : nz - 1 + layer]
        return 0

    lax.fori_loop(0, ny, body, 0)


def energy_call(disp, fy, fz, fc, dens, stiff):
    _, ny, nz, nx = disp.shape
    return pl.pallas_call(
        energy_kernel,
        out_shape=(
            jax.ShapeDtypeStruct((ny, nz, nx), f32),
            jax.ShapeDtypeStruct((2, ny, nx), f32),
            jax.ShapeDtypeStruct((2, ny, nx), f32),
        ),
        scratch_shapes=[
            pltpu.VMEM((192, 224), bf16),
            pltpu.VMEM((ny + 1, 3, 48, nx * (nz // 8)), bf16),
            pltpu.VMEM((ny + 1, 3, 8, nx * (nz // 8)), f32),
            pltpu.VMEM((ny + 1, 3, 6, 2, nz, nx), f32),
        ],
        compiler_params=pltpu.CompilerParams(vmem_limit_bytes=48 * 2**20),
        name="energy",
    )(disp, fy, fz, fc, dens, stiff)


def filter_kernel(flags, src, yl, yh, zl, zh, dens, passive, solid, amp, low, high, vols, s_s, d_s, acc_s):
    ny, nz, nx = src.shape
    alpha, beta, gamma, delta, eps = filter_weights()
    off = 8
    s_s[2 : ny + 2, off : off + nz] = src[...]
    s_s[0:2, off : off + nz] = yl[...]
    s_s[ny + 2 : ny + 4, off : off + nz] = yh[...]
    for y in range(ny + 4):
        s_s[y, off - 2 : off] = jnp.concatenate([zl[0, y : y + 1], zl[1, y : y + 1]], axis=0)
        s_s[y, off + nz : off + nz + 2] = jnp.concatenate([zh[0, y : y + 1], zh[1, y : y + 1]], axis=0)

    rows = s_s.shape[1]

    def beside(v):
        return pltpu.roll(v, 1, 0) + pltpu.roll(v, rows - 1, 0) + lane_up(v) + lane_down(v)

    row = lax.broadcasted_iota(jnp.int32, (rows, nx), 0)
    keep = jnp.where(row < off, flags[2], jnp.where(row >= off + nz, flags[3], 1)) == 1

    def second(y, _):
        c = s_s[y + 1]
        d2 = alpha * c + beta * (beside(c) + s_s[y] + s_s[y + 2])
        inside = jnp.where(y == 0, flags[0], jnp.where(y == ny + 1, flags[1], 1)) == 1
        d_s[y] = jnp.where(keep & inside, d2, 0.0)
        return 0

    lax.fori_loop(0, ny + 2, second, 0)

    def third(y, total):
        d2 = d_s[y + 1]
        p3 = gamma * s_s[y + 2] + delta * d2 + eps * (beside(d2) + d_s[y] + d_s[y + 2])
        p3 = p3[off : off + nz]
        d = dens[y]
        amp[y] = jnp.sqrt(jnp.maximum(-p3 * d, 0.0))
        sol = solid[y] == 1
        pas = passive[y] == 1
        lower = jnp.maximum(d - move_limit, floor_density)
        upper = jnp.minimum(d + move_limit, 1.0)
        low[y] = jnp.where(sol, 1.0, jnp.where(pas, floor_density, lower))
        high[y] = jnp.where(sol, 1.0, jnp.where(pas, floor_density, upper))
        masked = jnp.where(sol, 1.0, jnp.where(pas, floor_density, d))
        return total + masked

    total = lax.fori_loop(0, ny, third, jnp.zeros((nz, nx), f32))
    target = jnp.sum(total, axis=0, keepdims=True)

    groups = POINTS // 8
    half = groups // 2
    sub = lax.broadcasted_iota(jnp.int32, (8, nx), 0)
    for part in range(2):
        scale = []
        for g in range(half):
            k = sub + 8 * (part * half + g)
            mid = -bracket_end + (2.0 * bracket_end / POINTS) * k.astype(f32)
            scale.append(jnp.exp(-0.5 * mid))

        def volume(y, acc):
            acc = list(acc)
            for z in range(nz):
                a = jnp.broadcast_to(amp[y, z : z + 1], (8, nx))
                lo = jnp.broadcast_to(low[y, z : z + 1], (8, nx))
                hi = jnp.broadcast_to(high[y, z : z + 1], (8, nx))
                for g in range(half):
                    acc[g] = acc[g] + jnp.minimum(jnp.maximum(a * scale[g], lo), hi)
            return tuple(acc)

        acc = lax.fori_loop(0, ny, volume, tuple(jnp.zeros((8, nx), f32) for _ in range(half)))
        for g in range(half):
            value = acc[g]
            if part == 0 and g == 0:
                value = jnp.where(sub == 0, jnp.broadcast_to(target, (8, nx)), value)
            acc_s[8 * (part * half + g) : 8 * (part * half + g) + 8] = value
    vols[...] = jnp.sum(jnp.transpose(acc_s[...]), axis=0, keepdims=True)


def filter_call(flags, src, yl, yh, zl, zh, dens, passive, solid):
    ny, nz, nx = src.shape
    field = jax.ShapeDtypeStruct((ny, nz, nx), f32)
    vmem = pl.BlockSpec(memory_space=pltpu.VMEM)
    return pl.pallas_call(
        filter_kernel,
        in_specs=[pl.BlockSpec(memory_space=pltpu.SMEM)] + [vmem] * 8,
        out_shape=(field, field, field, jax.ShapeDtypeStruct((1, POINTS), f32)),
        scratch_shapes=[
            pltpu.VMEM((ny + 4, nz + 16, nx), f32),
            pltpu.VMEM((ny + 2, nz + 16, nx), f32),
            pltpu.VMEM((POINTS, nx), f32),
        ],
        compiler_params=pltpu.CompilerParams(vmem_limit_bytes=32 * 2**20),
        name="filter",
    )(flags, src, yl, yh, zl, zh, dens, passive, solid)


def update_kernel(vols, amp, low, high, new, logm):
    target = vols[0, 0]
    k = jnp.int32(0)
    step = POINTS // 2
    while step >= 1:
        k = jnp.where(vols[0, k + step] > target, k + step, k)
        step //= 2
    middle = -bracket_end + (2.0 * bracket_end / POINTS) * (k.astype(f32) + 0.5)
    logm[0] = middle
    scale = jnp.exp(jnp.full((1, amp.shape[-1]), -0.5 * middle, f32))

    def body(y, _):
        new[y] = jnp.minimum(jnp.maximum(amp[y] * scale, low[y]), high[y])
        return 0

    lax.fori_loop(0, amp.shape[0], body, 0)


def update_call(vols, amp, low, high):
    vmem = pl.BlockSpec(memory_space=pltpu.VMEM)
    return pl.pallas_call(
        update_kernel,
        in_specs=[pl.BlockSpec(memory_space=pltpu.SMEM), vmem, vmem, vmem],
        out_specs=(vmem, pl.BlockSpec(memory_space=pltpu.SMEM)),
        out_shape=(jax.ShapeDtypeStruct(amp.shape, f32), jax.ShapeDtypeStruct((1,), f32)),
        name="update",
    )(vols, amp, low, high)


def to_lower(value, axis):
    count = lax.axis_size(axis)
    return lax.ppermute(value, axis, [(i + 1, i) for i in range(count - 1)])


def to_upper(value, axis):
    count = lax.axis_size(axis)
    return lax.ppermute(value, axis, [(i, i + 1) for i in range(count - 1)])


def on_device(displacement, density, passive, solid, stiffness):
    ny, nz, nx = density.shape
    gy, gz = lax.axis_size("gy"), lax.axis_size("gz")
    iy, iz = lax.axis_index("gy"), lax.axis_index("gz")

    fy = to_lower(displacement[:, 0], "gy")
    fz = to_lower(displacement[:, :, 0], "gz")
    pairs = [((z + 1) * gy + y + 1, z * gy + y) for z in range(gz - 1) for y in range(gy - 1)]
    fc = lax.ppermute(displacement[:, 0, 0], ("gz", "gy"), pairs)
    src, zlow, zhigh = energy_call(displacement, fy, fz, fc, density, stiffness)

    yl = to_upper(src[ny - 2 :], "gy")
    yh = to_lower(src[:2], "gy")
    own_low = jnp.concatenate([yl[:, 0:2].swapaxes(0, 1), zlow, yh[:, 0:2].swapaxes(0, 1)], axis=1)
    own_high = jnp.concatenate([yl[:, nz - 2 :].swapaxes(0, 1), zhigh, yh[:, nz - 2 :].swapaxes(0, 1)], axis=1)
    zl = to_upper(own_high, "gz")
    zh = to_lower(own_low, "gz")
    flags = jnp.stack([iy > 0, iy < gy - 1, iz > 0, iz < gz - 1]).astype(jnp.int32)
    amp, low, high, vols = filter_call(flags, src, yl, yh, zl, zh, density, passive, solid)

    vols = lax.all_gather(vols.reshape(2, POINTS // 2), ("gz", "gy")).sum(axis=0).reshape(1, POINTS)
    new, logm = update_call(vols, amp, low, high)
    return new, logm.reshape(())


def solution(mesh):
    placed = (
        P(None, "gy", "gz", None),
        P("gy", "gz", None),
        P("gy", "gz", None),
        P("gy", "gz", None),
        P(),
    )
    return jax.shard_map(
        on_device, mesh=mesh, in_specs=placed, out_specs=(P("gy", "gz", None), P()), check_vma=False
    )
```

```python
import functools

import jax
import jax.numpy as jnp
from jax import lax
from jax.experimental import pallas as pl
from jax.experimental.pallas import tpu as pltpu
from jax.sharding import PartitionSpec as P

ITERS = 8
POINTS = 2**ITERS

smoothing = 0.52
move_limit = 0.2
floor_density = 0.001
bracket_end = 12.0

f32 = jnp.float32
bf16 = jnp.bfloat16


def cheb_weights():
    spectrum_top = 1.0 + 12.0 * smoothing
    centre_value = (spectrum_top + 1.0) / 2.0
    half_width = (spectrum_top - 1.0) / 2.0
    ratio_value = centre_value / half_width
    first_rho = 1.0 / ratio_value
    second_rho = 1.0 / (2.0 * ratio_value - first_rho)
    third_rho = 1.0 / (2.0 * ratio_value - second_rho)
    return (
        centre_value,
        second_rho * first_rho,
        2.0 * second_rho / half_width,
        third_rho * second_rho,
        2.0 * third_rho / half_width,
    )


def filter_weights():
    t, w1, w2, w3, w4 = cheb_weights()
    diag = 1.0 + 6.0 * smoothing
    alpha = w1 / t + w2 * (1.0 - diag / t)
    beta = w2 * smoothing / t
    gamma = 1.0 / t - w4 * w1 / (t * w2)
    delta = 1.0 + w3 + w4 / w2 - w4 * diag
    eps = w4 * smoothing
    return alpha, beta, gamma, delta, eps


def lane_up(v):
    n = v.shape[-1]
    lane = lax.broadcasted_iota(jnp.int32, v.shape, v.ndim - 1)
    return jnp.where(lane < n - 1, pltpu.roll(v, n - 1, v.ndim - 1), 0.0)


def lane_down(v):
    n = v.shape[-1]
    lane = lax.broadcasted_iota(jnp.int32, v.shape, v.ndim - 1)
    return jnp.where(lane > 0, pltpu.roll(v, 1, v.ndim - 1), 0.0)


def build_matrix(stiff, mat):
    shape = (24, 112)
    col = lax.broadcasted_iota(jnp.int32, shape, 1)
    row = lax.broadcasted_iota(jnp.int32, shape, 0)
    main = col < 96
    dy = jnp.where(main, jnp.where(col >= 48, 1, 0), jnp.where(col >= 104, 1, 0))
    q = col - 48 * dy
    e = col - 96 - 8 * dy
    c = jnp.where(main, q >> 4, e >> 1)
    dx = jnp.where(main, (q >> 3) & 1, e & 1)
    valid = main | (e < 6)
    dof0 = 3 * (4 * dy + dx) + c
    pick0 = jnp.where(main & (row == dof0), 1.0, 0.0)
    pick1 = jnp.where(valid & (row == dof0 + 6), 1.0, 0.0)
    k = stiff[...]
    hp = lax.Precision.HIGHEST
    k0 = jnp.dot(k, pick0, precision=hp, preferred_element_type=f32)
    k1 = jnp.dot(k, pick1, precision=hp, preferred_element_type=f32)
    col8 = lax.broadcasted_iota(jnp.int32, (8, 112), 1)
    row8 = lax.broadcasted_iota(jnp.int32, (8, 112), 0)
    main8 = col8 < 96
    zc = col8 & 7
    m0 = main8 & (zc == row8)
    m1 = jnp.where(main8, zc, 8) == row8 + 1
    rows = []
    for dz in range(2):
        for dy_ in range(2):
            for c_ in range(3):
                for dx_ in range(2):
                    r = 3 * (4 * dy_ + 2 * dz + dx_) + c_
                    rows.append(jnp.where(m0, k0[r : r + 1], 0.0) + jnp.where(m1, k1[r : r + 1], 0.0))
    full = jnp.concatenate(rows, axis=0)
    hi = full.astype(bf16)
    lo = (full - hi.astype(f32)).astype(bf16)
    mat[:, 0:112] = hi
    mat[:, 112:224] = lo


def prepare(plane, ext, p, main_s, ext_s, mul_s):
    for l in range(3):
        for c in range(3):
            u = plane(3 * l + c)
            x = ext(3 * l + c)
            nz, nx = u.shape
            last = lax.broadcasted_iota(jnp.int32, u.shape, 0) == nz - 1
            both = (u, lane_up(u))
            bothx = (x, lane_up(x))
            for w in range(nz // 8):
                sl = slice(8 * w, 8 * w + 8)
                main_s[p, l, 16 * c : 16 * c + 16, w * nx : (w + 1) * nx] = jnp.concatenate(
                    [both[0][sl], both[1][sl]], axis=0
                ).astype(bf16)
            for dx in range(2):
                v, vx = both[dx], bothx[dx]
                k = 2 * c + dx
                for w in range(nz // 8):
                    nxt = v[8 * w + 8 : 8 * w + 9] if 8 * w + 8 < nz else vx
                    ext_s[p, l, k : k + 1, w * nx : (w + 1) * nx] = nxt
                m = 2.0 * v - v.astype(bf16).astype(f32)
                mx = 2.0 * vx - vx.astype(bf16).astype(f32)
                mul_s[p, l, k, 0] = m
                mul_s[p, l, k, 1] = jnp.where(last, jnp.broadcast_to(mx, v.shape), pltpu.roll(m, nz - 1, 0))


def energy_kernel(disp, fy, fz, fc, dens, stiff, src, zlow, zhigh, mat, main_s, ext_s, mul_s):
    _, ny, nz, nx = disp.shape
    build_matrix(stiff, mat)
    ext_s[...] = jnp.zeros_like(ext_s)

    prepare(lambda i: fy[i], lambda i: fc[i : i + 1], ny, main_s, ext_s, mul_s)

    def prep_body(y, _):
        prepare(lambda i: disp[i, y], lambda i: fz[i, pl.ds(y, 1)], y, main_s, ext_s, mul_s)
        return 0

    lax.fori_loop(0, ny, prep_body, 0)

    def body(y, _):
        acc = [None] * (nz // 8)
        for l in range(3):
            ext = jnp.concatenate([ext_s[y, l], ext_s[y + 1, l]], axis=0).astype(bf16)
            one = jnp.concatenate([main_s[y, l], main_s[y + 1, l], ext], axis=0)
            rhs = jnp.concatenate([one, one], axis=0)
            force = jnp.dot(mat[...], rhs, preferred_element_type=f32)
            i = 0
            for dz in range(2):
                for dy in range(2):
                    for k in range(6):
                        for w in range(nz // 8):
                            term = (
                                force[8 * i : 8 * i + 8, w * nx : (w + 1) * nx]
                                * mul_s[y + dy, l, k, dz, 8 * w : 8 * w + 8]
                            )
                            acc[w] = term if acc[w] is None else acc[w] + term
                        i += 1
        d = dens[y]
        s = d * (-3.0 * d * d * jnp.concatenate(acc, axis=0))
        src[y] = s
        for layer in range(2):
            zlow[layer, pl.ds(y, 1)] = s[layer : layer + 1]
            zhigh[layer, pl.ds(y, 1)] = s[nz - 2 + layer : nz - 1 + layer]
        return 0

    lax.fori_loop(0, ny, body, 0)


def energy_call(disp, fy, fz, fc, dens, stiff):
    _, ny, nz, nx = disp.shape
    return pl.pallas_call(
        energy_kernel,
        out_shape=(
            jax.ShapeDtypeStruct((ny, nz, nx), f32),
            jax.ShapeDtypeStruct((2, ny, nx), f32),
            jax.ShapeDtypeStruct((2, ny, nx), f32),
        ),
        scratch_shapes=[
            pltpu.VMEM((192, 224), bf16),
            pltpu.VMEM((ny + 1, 3, 48, nx * (nz // 8)), bf16),
            pltpu.VMEM((ny + 1, 3, 8, nx * (nz // 8)), f32),
            pltpu.VMEM((ny + 1, 3, 6, 2, nz, nx), f32),
        ],
        compiler_params=pltpu.CompilerParams(vmem_limit_bytes=48 * 2**20),
        name="energy",
    )(disp, fy, fz, fc, dens, stiff)


def filter_kernel(flags, src, yl, yh, zl, zh, dens, passive, solid, amp, low, high, vols, s_s, d_s, acc_s):
    ny, nz, nx = src.shape
    alpha, beta, gamma, delta, eps = filter_weights()
    off = 8
    s_s[2 : ny + 2, off : off + nz] = src[...]
    s_s[0:2, off : off + nz] = yl[...]
    s_s[ny + 2 : ny + 4, off : off + nz] = yh[...]
    for y in range(ny + 4):
        s_s[y, off - 2 : off] = jnp.concatenate([zl[0, y : y + 1], zl[1, y : y + 1]], axis=0)
        s_s[y, off + nz : off + nz + 2] = jnp.concatenate([zh[0, y : y + 1], zh[1, y : y + 1]], axis=0)

    rows = s_s.shape[1]

    def beside(v):
        return pltpu.roll(v, 1, 0) + pltpu.roll(v, rows - 1, 0) + lane_up(v) + lane_down(v)

    row = lax.broadcasted_iota(jnp.int32, (rows, nx), 0)
    keep = jnp.where(row < off, flags[2], jnp.where(row >= off + nz, flags[3], 1)) == 1

    def second(y, _):
        c = s_s[y + 1]
        d2 = alpha * c + beta * (beside(c) + s_s[y] + s_s[y + 2])
        inside = jnp.where(y == 0, flags[0], jnp.where(y == ny + 1, flags[1], 1)) == 1
        d_s[y] = jnp.where(keep & inside, d2, 0.0)
        return 0

    lax.fori_loop(0, ny + 2, second, 0)

    def third(y, total):
        d2 = d_s[y + 1]
        p3 = gamma * s_s[y + 2] + delta * d2 + eps * (beside(d2) + d_s[y] + d_s[y + 2])
        p3 = p3[off : off + nz]
        d = dens[y]
        amp[y] = jnp.sqrt(jnp.maximum(-p3 * d, 0.0))
        sol = solid[y] == 1
        pas = passive[y] == 1
        lower = jnp.maximum(d - move_limit, floor_density)
        upper = jnp.minimum(d + move_limit, 1.0)
        low[y] = jnp.where(sol, 1.0, jnp.where(pas, floor_density, lower))
        high[y] = jnp.where(sol, 1.0, jnp.where(pas, floor_density, upper))
        masked = jnp.where(sol, 1.0, jnp.where(pas, floor_density, d))
        return total + masked

    total = lax.fori_loop(0, ny, third, jnp.zeros((nz, nx), f32))
    target = jnp.sum(total, axis=0, keepdims=True)

    groups = POINTS // 8
    half = groups // 2
    sub = lax.broadcasted_iota(jnp.int32, (8, nx), 0)
    for part in range(2):
        scale = []
        for g in range(half):
            k = sub + 8 * (part * half + g)
            mid = -bracket_end + (2.0 * bracket_end / POINTS) * k.astype(f32)
            scale.append(jnp.exp(-0.5 * mid))

        def volume(y, acc):
            acc = list(acc)
            for z in range(nz):
                a = jnp.broadcast_to(amp[y, z : z + 1], (8, nx))
                lo = jnp.broadcast_to(low[y, z : z + 1], (8, nx))
                hi = jnp.broadcast_to(high[y, z : z + 1], (8, nx))
                for g in range(half):
                    acc[g] = acc[g] + jnp.minimum(jnp.maximum(a * scale[g], lo), hi)
            return tuple(acc)

        acc = lax.fori_loop(0, ny, volume, tuple(jnp.zeros((8, nx), f32) for _ in range(half)))
        for g in range(half):
            value = acc[g]
            if part == 0 and g == 0:
                value = jnp.where(sub == 0, jnp.broadcast_to(target, (8, nx)), value)
            acc_s[8 * (part * half + g) : 8 * (part * half + g) + 8] = value
    vols[...] = jnp.sum(jnp.transpose(acc_s[...]), axis=0, keepdims=True)


def filter_call(flags, src, yl, yh, zl, zh, dens, passive, solid):
    ny, nz, nx = src.shape
    field = jax.ShapeDtypeStruct((ny, nz, nx), f32)
    vmem = pl.BlockSpec(memory_space=pltpu.VMEM)
    return pl.pallas_call(
        filter_kernel,
        in_specs=[pl.BlockSpec(memory_space=pltpu.SMEM)] + [vmem] * 8,
        out_shape=(field, field, field, jax.ShapeDtypeStruct((1, POINTS), f32)),
        scratch_shapes=[
            pltpu.VMEM((ny + 4, nz + 16, nx), f32),
            pltpu.VMEM((ny + 2, nz + 16, nx), f32),
            pltpu.VMEM((POINTS, nx), f32),
        ],
        compiler_params=pltpu.CompilerParams(vmem_limit_bytes=32 * 2**20),
        name="filter",
    )(flags, src, yl, yh, zl, zh, dens, passive, solid)


def update_kernel(vols, amp, low, high, new, logm):
    target = vols[0, 0]
    k = jnp.int32(0)
    step = POINTS // 2
    while step >= 1:
        k = jnp.where(vols[0, k + step] > target, k + step, k)
        step //= 2
    middle = -bracket_end + (2.0 * bracket_end / POINTS) * (k.astype(f32) + 0.5)
    logm[0] = middle
    scale = jnp.exp(jnp.full((1, amp.shape[-1]), -0.5 * middle, f32))

    def body(y, _):
        new[y] = jnp.minimum(jnp.maximum(amp[y] * scale, low[y]), high[y])
        return 0

    lax.fori_loop(0, amp.shape[0], body, 0)


def update_call(vols, amp, low, high):
    vmem = pl.BlockSpec(memory_space=pltpu.VMEM)
    return pl.pallas_call(
        update_kernel,
        in_specs=[pl.BlockSpec(memory_space=pltpu.SMEM), vmem, vmem, vmem],
        out_specs=(vmem, pl.BlockSpec(memory_space=pltpu.SMEM)),
        out_shape=(jax.ShapeDtypeStruct(amp.shape, f32), jax.ShapeDtypeStruct((1,), f32)),
        name="update",
    )(vols, amp, low, high)


def to_lower(value, axis):
    count = lax.axis_size(axis)
    return lax.ppermute(value, axis, [(i + 1, i) for i in range(count - 1)])


def to_upper(value, axis):
    count = lax.axis_size(axis)
    return lax.ppermute(value, axis, [(i, i + 1) for i in range(count - 1)])


def on_device(displacement, density, passive, solid, stiffness):
    ny, nz, nx = density.shape
    gy, gz = lax.axis_size("gy"), lax.axis_size("gz")
    iy, iz = lax.axis_index("gy"), lax.axis_index("gz")

    fy = to_lower(displacement[:, 0], "gy")
    fz = to_lower(displacement[:, :, 0], "gz")
    pairs = [((z + 1) * gy + y + 1, z * gy + y) for z in range(gz - 1) for y in range(gy - 1)]
    fc = lax.ppermute(displacement[:, 0, 0], ("gz", "gy"), pairs)
    src, zlow, zhigh = energy_call(displacement, fy, fz, fc, density, stiffness)

    yl = to_upper(src[ny - 2 :], "gy")
    yh = to_lower(src[:2], "gy")
    own_low = jnp.concatenate([yl[:, 0:2].swapaxes(0, 1), zlow, yh[:, 0:2].swapaxes(0, 1)], axis=1)
    own_high = jnp.concatenate([yl[:, nz - 2 :].swapaxes(0, 1), zhigh, yh[:, nz - 2 :].swapaxes(0, 1)], axis=1)
    zl = to_upper(own_high, "gz")
    zh = to_lower(own_low, "gz")
    flags = jnp.stack([iy > 0, iy < gy - 1, iz > 0, iz < gz - 1]).astype(jnp.int32)
    amp, low, high, vols = filter_call(flags, src, yl, yh, zl, zh, density, passive, solid)

    everyone = jnp.broadcast_to(vols, (gz * gy, POINTS))
    vols = lax.all_to_all(everyone, ("gz", "gy"), 0, 0, tiled=True).sum(axis=0).reshape(1, POINTS)
    new, logm = update_call(vols, amp, low, high)
    return new, logm.reshape(())


def solution(mesh):
    placed = (
        P(None, "gy", "gz", None),
        P("gy", "gz", None),
        P("gy", "gz", None),
        P("gy", "gz", None),
        P(),
    )
    return jax.shard_map(
        on_device, mesh=mesh, in_specs=placed, out_specs=(P("gy", "gz", None), P()), check_vma=False
    )
```

```python
import functools

import jax
import jax.numpy as jnp
from jax import lax
from jax.experimental import pallas as pl
from jax.experimental.pallas import tpu as pltpu
from jax.sharding import PartitionSpec as P

ITERS = 8
POINTS = 2**ITERS
OFF = 8

smoothing = 0.52
move_limit = 0.2
floor_density = 0.001
bracket_end = 12.0

f32 = jnp.float32
bf16 = jnp.bfloat16
VMEM = pl.BlockSpec(memory_space=pltpu.VMEM)
SMEM = pl.BlockSpec(memory_space=pltpu.SMEM)
HBM = pl.BlockSpec(memory_space=pltpu.HBM)


def cheb_weights():
    spectrum_top = 1.0 + 12.0 * smoothing
    centre_value = (spectrum_top + 1.0) / 2.0
    half_width = (spectrum_top - 1.0) / 2.0
    ratio_value = centre_value / half_width
    first_rho = 1.0 / ratio_value
    second_rho = 1.0 / (2.0 * ratio_value - first_rho)
    third_rho = 1.0 / (2.0 * ratio_value - second_rho)
    return (
        centre_value,
        second_rho * first_rho,
        2.0 * second_rho / half_width,
        third_rho * second_rho,
        2.0 * third_rho / half_width,
    )


def filter_weights():
    t, w1, w2, w3, w4 = cheb_weights()
    diag = 1.0 + 6.0 * smoothing
    alpha = w1 / t + w2 * (1.0 - diag / t)
    beta = w2 * smoothing / t
    gamma = 1.0 / t - w4 * w1 / (t * w2)
    delta = 1.0 + w3 + w4 / w2 - w4 * diag
    eps = w4 * smoothing
    return alpha, beta, gamma, delta, eps


def lane_up(v):
    n = v.shape[-1]
    lane = lax.broadcasted_iota(jnp.int32, v.shape, v.ndim - 1)
    return jnp.where(lane < n - 1, pltpu.roll(v, n - 1, v.ndim - 1), 0.0)


def lane_down(v):
    n = v.shape[-1]
    lane = lax.broadcasted_iota(jnp.int32, v.shape, v.ndim - 1)
    return jnp.where(lane > 0, pltpu.roll(v, 1, v.ndim - 1), 0.0)


def estimate(us):
    return pl.CostEstimate(flops=int(us * 1e9), bytes_accessed=1 << 20, transcendentals=0)


def build_matrix(k, mat):
    shape = (24, 112)
    col = lax.broadcasted_iota(jnp.int32, shape, 1)
    row = lax.broadcasted_iota(jnp.int32, shape, 0)
    main = col < 96
    dy = jnp.where(main, jnp.where(col >= 48, 1, 0), jnp.where(col >= 104, 1, 0))
    q = col - 48 * dy
    e = col - 96 - 8 * dy
    c = jnp.where(main, q >> 4, e >> 1)
    dx = jnp.where(main, (q >> 3) & 1, e & 1)
    valid = main | (e < 6)
    dof0 = 3 * (4 * dy + dx) + c
    pick0 = jnp.where(main & (row == dof0), 1.0, 0.0)
    pick1 = jnp.where(valid & (row == dof0 + 6), 1.0, 0.0)
    hp = lax.Precision.HIGHEST
    k0 = jnp.dot(k, pick0, precision=hp, preferred_element_type=f32)
    k1 = jnp.dot(k, pick1, precision=hp, preferred_element_type=f32)
    col8 = lax.broadcasted_iota(jnp.int32, (8, 112), 1)
    row8 = lax.broadcasted_iota(jnp.int32, (8, 112), 0)
    main8 = col8 < 96
    zc = col8 & 7
    m0 = main8 & (zc == row8)
    m1 = jnp.where(main8, zc, 8) == row8 + 1
    rows = []
    for dz in range(2):
        for dy_ in range(2):
            for c_ in range(3):
                for dx_ in range(2):
                    r = 3 * (4 * dy_ + 2 * dz + dx_) + c_
                    rows.append(jnp.where(m0, k0[r : r + 1], 0.0) + jnp.where(m1, k1[r : r + 1], 0.0))
    full = jnp.concatenate(rows, axis=0)
    hi = full.astype(bf16)
    lo = (full - hi.astype(f32)).astype(bf16)
    mat[:, 0:112] = hi
    mat[:, 112:224] = lo


def prepare(plane, p, main_s, ext_s, mul_s):
    for l in range(3):
        for c in range(3):
            u = plane(3 * l + c)
            nz, nx = u.shape
            last = lax.broadcasted_iota(jnp.int32, u.shape, 0) == nz - 1
            both = (u, lane_up(u))
            for w in range(nz // 8):
                sl = slice(8 * w, 8 * w + 8)
                main_s[p, l, 16 * c : 16 * c + 16, w * nx : (w + 1) * nx] = jnp.concatenate(
                    [both[0][sl], both[1][sl]], axis=0
                ).astype(bf16)
            for dx in range(2):
                v = both[dx]
                k = 2 * c + dx
                if ext_s is not None:
                    for w in range(nz // 8 - 1):
                        ext_s[p, l, k : k + 1, w * nx : (w + 1) * nx] = v[8 * w + 8 : 8 * w + 9]
                m = 2.0 * v - v.astype(bf16).astype(f32)
                mul_s[p, l, k, 0] = m
                mul_s[p, l, k, 1] = jnp.where(last, 0.0, pltpu.roll(m, nz - 1, 0))


def quadratic(force, mul, count, nx, acc):
    i = 0
    for dz in range(2):
        for dy in range(2):
            for k in range(6):
                for w in range(count):
                    term = force[8 * i : 8 * i + 8, w * nx : (w + 1) * nx] * mul(dy, k, dz, w)
                    acc[w] = term if acc[w] is None else acc[w] + term
                i += 1


def energy_row(p, mat, main_s, ext_s, mul_s, density):
    nz, nx = density.shape
    count = nz // 8
    acc = [None] * count
    for l in range(3):
        ext = jnp.concatenate([ext_s[p, l], ext_s[p + 1, l]], axis=0).astype(bf16)
        one = jnp.concatenate([main_s[p, l], main_s[p + 1, l], ext], axis=0)
        force = jnp.dot(mat[...], jnp.concatenate([one, one], axis=0), preferred_element_type=f32)
        quadratic(force, lambda dy, k, dz, w: mul_s[p + dy, l, k, dz, 8 * w : 8 * w + 8], count, nx, acc)
    return density * (-3.0 * density * density * jnp.concatenate(acc, axis=0))


def put_row(out, y, s):
    nz, nx = s.shape
    out[y, 0:OFF] = jnp.zeros((OFF, nx), f32)
    out[y, OFF : OFF + nz] = s
    out[y, OFF + nz :] = jnp.zeros((out.shape[1] - OFF - nz, nx), f32)


def first_kernel(disp, dens, stiff, src, mat, own_low, own_high, disp_s, dens_s, stiff_s, main_s, ext_s, mul_s, sems):
    _, ny, nz, nx = disp_s.shape
    half = ny // 2
    copy_k = pltpu.make_async_copy(stiff, stiff_s, sems.at[ny + 1])
    copy_k.start()
    copies = [pltpu.make_async_copy(disp.at[:, p], disp_s.at[:, p], sems.at[p]) for p in range(ny)]
    for p in range(2):
        copies[p].start()
    copy_d = pltpu.make_async_copy(dens, dens_s, sems.at[ny])
    copy_d.start()
    for p in range(2, ny):
        copies[p].start()
    ext_s[...] = jnp.zeros_like(ext_s)
    copy_k.wait()
    build_matrix(stiff_s[...], mat)
    for p in range(2):
        copies[p].wait()
        prepare(lambda i: disp_s[i, p], p, main_s, ext_s, mul_s)
    copy_d.wait()
    for p in range(2, half + 1):
        copies[p].wait()

    def body(y, _):
        put_row(src, y, energy_row(y, mat, main_s, ext_s, mul_s, dens_s[y]))
        prepare(lambda i: disp_s[i, y + 2], y + 2, main_s, ext_s, mul_s)
        return 0

    lax.fori_loop(0, half - 1, body, 0)
    put_row(src, half - 1, energy_row(half - 1, mat, main_s, ext_s, mul_s, dens_s[half - 1]))
    for p in range(half + 1, ny):
        copies[p].wait()

    def pack(y, _):
        for i in range(9):
            own_low[y, 2 * i : 2 * i + 2] = disp_s[i, y, nz - 2 : nz]
            own_high[y, 3 * i : 3 * i + 3] = disp_s[i, y, 0:3]
        own_low[y, 18:20] = dens_s[y, nz - 2 : nz]
        own_high[y, 27:29] = dens_s[y, 0:2]
        own_high[y, 29:30] = jnp.zeros((1, nx), f32)
        return 0

    lax.fori_loop(0, ny, pack, 0)


def energy_scratch(planes, nz, nx):
    lanes = nx * (nz // 8)
    return [
        pltpu.VMEM((planes, 3, 48, lanes), bf16),
        pltpu.VMEM((planes, 3, 8, lanes), f32),
        pltpu.VMEM((planes, 3, 6, 2, nz, nx), f32),
    ]


def first_call(disp, dens, stiff):
    _, ny, nz, nx = disp.shape
    half = ny // 2
    return pl.pallas_call(
        first_kernel,
        in_specs=[HBM, HBM, HBM],
        out_shape=(
            jax.ShapeDtypeStruct((half, nz + 2 * OFF, nx), f32),
            jax.ShapeDtypeStruct((192, 224), bf16),
            jax.ShapeDtypeStruct((ny, 20, nx), f32),
            jax.ShapeDtypeStruct((ny, 30, nx), f32),
        ),
        scratch_shapes=[pltpu.VMEM((9, ny, nz, nx), f32), pltpu.VMEM((ny, nz, nx), f32), pltpu.VMEM((24, 24), f32)]
        + energy_scratch(half + 1, nz, nx)
        + [pltpu.SemaphoreType.DMA((ny + 2,))],
        compiler_params=pltpu.CompilerParams(vmem_limit_bytes=24 * 2**20),
        cost_estimate=estimate(5),
        name="energy_first",
    )(disp, dens, stiff)


def last_kernel(disp, dens, fy, mat, src, disp_s, dens_s, main_s, ext_s, mul_s, sems):
    _, half, nz, nx = disp_s.shape
    copies = [pltpu.make_async_copy(disp.at[:, half + p], disp_s.at[:, p], sems.at[p]) for p in range(half)]
    for p in range(2):
        copies[p].start()
    copy_d = pltpu.make_async_copy(dens.at[pl.ds(half, half)], dens_s, sems.at[half])
    copy_d.start()
    for p in range(2, half):
        copies[p].start()
    ext_s[...] = jnp.zeros_like(ext_s)
    for p in range(2):
        copies[p].wait()
        prepare(lambda i: disp_s[i, p], p, main_s, ext_s, mul_s)
    copy_d.wait()
    for p in range(2, half):
        copies[p].wait()

    def row(y):
        put_row(src, y, energy_row(y, mat, main_s, ext_s, mul_s, dens_s[y]))

    def body(y, _):
        row(y)
        prepare(lambda i: disp_s[i, y + 2], y + 2, main_s, ext_s, mul_s)
        return 0

    lax.fori_loop(0, half - 2, body, 0)
    row(half - 2)
    prepare(lambda i: fy[i], half, main_s, ext_s, mul_s)
    row(half - 1)


def last_call(disp, dens, fy, mat):
    _, ny, nz, nx = disp.shape
    half = ny // 2
    return pl.pallas_call(
        last_kernel,
        in_specs=[HBM, HBM, VMEM, VMEM],
        out_shape=jax.ShapeDtypeStruct((half, nz + 2 * OFF, nx), f32),
        scratch_shapes=[pltpu.VMEM((9, half, nz, nx), f32), pltpu.VMEM((half, nz, nx), f32)]
        + energy_scratch(half + 1, nz, nx)
        + [pltpu.SemaphoreType.DMA((half + 1,))],
        compiler_params=pltpu.CompilerParams(vmem_limit_bytes=24 * 2**20),
        cost_estimate=estimate(5),
        name="energy_last",
    )(disp, dens, fy, mat)


def rim_kernel(flags, got_low, got_high, own_low, own_high, fy, mat, src_a, src_b, rim, msg_even, msg_odd, w_s, d_s, main_s, mul_s, t_s):
    ny, _, nx = own_low.shape
    nz = src_a.shape[1] - 2 * OFF
    half = ny // 2

    def window(p, low, high, first, last):
        for i in range(9):
            w_s[p, i, 0:2] = low(2 * i, 2)
            w_s[p, i, 2:3] = first(i)
            w_s[p, i, 3:4] = last(i)
            w_s[p, i, 4:7] = high(3 * i, 3)
            w_s[p, i, 7:8] = jnp.zeros((1, nx), f32)
        prepare(lambda i: w_s[p, i], p, main_s, None, mul_s)

    def own(p, _):
        window(
            p,
            lambda a, n: got_low[p, a : a + n],
            lambda a, n: got_high[p, a : a + n],
            lambda i: own_high[p, 3 * i : 3 * i + 1],
            lambda i: own_low[p, 2 * i + 1 : 2 * i + 2],
        )
        d_s[p] = jnp.zeros((8, nx), f32)
        d_s[p, 0:2] = got_low[p, 18:20]
        d_s[p, 3:4] = own_low[p, 19:20]
        d_s[p, 4:6] = got_high[p, 27:29]
        return 0

    lax.fori_loop(0, ny, own, 0)
    window(
        ny,
        lambda a, n: got_low[ny, a : a + n],
        lambda a, n: got_high[ny, a : a + n],
        lambda i: fy[i, 0:1],
        lambda i: fy[i, nz - 1 : nz],
    )

    group = 4

    def rows(g, _):
        acc = [None] * group
        for l in range(3):
            parts = [
                jnp.concatenate([main_s[g * group + j + dy, l] for j in range(group)], axis=1) for dy in range(2)
            ]
            one = jnp.concatenate(parts + [jnp.zeros((16, group * nx), bf16)], axis=0)
            force = jnp.dot(mat[...], jnp.concatenate([one, one], axis=0), preferred_element_type=f32)
            quadratic(force, lambda dy, k, dz, w: mul_s[g * group + w + dy, l, k, dz], group, nx, acc)
        for j in range(group):
            d = d_s[g * group + j]
            rim[g * group + j] = d * (-3.0 * d * d * acc[j])
        return 0

    lax.fori_loop(0, ny // group, rows, 0)

    for j in range(4):
        y = j if j < 2 else ny - 4 + j
        t_s[j] = src_a[y] if j < 2 else src_b[y - half]
        put_rim(t_s, j, rim[y], nz)
    odd = flags[4] == 1
    msg_even[...] = jnp.where(odd, t_s[0:2], t_s[2:4])
    msg_odd[...] = jnp.where(odd, t_s[2:4], t_s[0:2])


def put_rim(s, y, rim, nz):
    s[y, OFF - 2 : OFF] = rim[0:2]
    s[y, OFF + nz - 1 : OFF + nz + 2] = rim[3:6]


def rim_call(flags, got_low, got_high, own_low, own_high, fy, mat, src_a, src_b):
    ny, _, nx = own_low.shape
    rows = src_a.shape[1]
    return pl.pallas_call(
        rim_kernel,
        in_specs=[SMEM] + [VMEM] * 8,
        out_shape=(
            jax.ShapeDtypeStruct((ny, 8, nx), f32),
            jax.ShapeDtypeStruct((2, rows, nx), f32),
            jax.ShapeDtypeStruct((2, rows, nx), f32),
        ),
        scratch_shapes=[
            pltpu.VMEM((ny + 1, 9, 8, nx), f32),
            pltpu.VMEM((ny, 8, nx), f32),
            pltpu.VMEM((ny + 1, 3, 48, nx), bf16),
            pltpu.VMEM((ny + 1, 3, 6, 2, 8, nx), f32),
            pltpu.VMEM((4, rows, nx), f32),
        ],
        compiler_params=pltpu.CompilerParams(vmem_limit_bytes=16 * 2**20),
        cost_estimate=estimate(2),
        name="energy_rim",
    )(flags, got_low, got_high, own_low, own_high, fy, mat, src_a, src_b)


def filter_block(s_s, d_s, n, z_edges, y_edges, finish):
    rows, nx = s_s.shape[1:]
    nz = rows - 2 * OFF
    alpha, beta, gamma, delta, eps = filter_weights()
    row = lax.broadcasted_iota(jnp.int32, (rows, nx), 0)
    keep = jnp.where(row < OFF, z_edges[0], jnp.where(row >= OFF + nz, z_edges[1], 1)) == 1

    def beside(v):
        return pltpu.roll(v, 1, 0) + pltpu.roll(v, rows - 1, 0) + lane_up(v) + lane_down(v)

    def second(j, _):
        c = s_s[j + 1]
        d2 = alpha * c + beta * (beside(c) + s_s[j] + s_s[j + 2])
        ok = keep
        if y_edges is not None:
            ok = keep & (jnp.where(j == 0, y_edges[0], jnp.where(j == n - 3, y_edges[1], 1)) == 1)
        d_s[j] = jnp.where(ok, d2, 0.0)
        return 0

    def third(j, _):
        d2 = d_s[j + 1]
        p3 = gamma * s_s[j + 2] + delta * d2 + eps * (beside(d2) + d_s[j] + d_s[j + 2])
        finish(j, p3[OFF : OFF + nz])
        return 0

    lax.fori_loop(0, n - 2, second, 0)
    lax.fori_loop(0, n - 4, third, 0)


def limits(p3, d, pas, sol):
    amp = jnp.sqrt(jnp.maximum(-p3 * d, 0.0))
    lower = jnp.maximum(d - move_limit, floor_density)
    upper = jnp.minimum(d + move_limit, 1.0)
    low = jnp.where(sol, 1.0, jnp.where(pas, floor_density, lower))
    high = jnp.where(sol, 1.0, jnp.where(pas, floor_density, upper))
    return amp, low, high


def table(n, nz, nx, amp, low, high, dens, start, acc_s):
    groups = POINTS // 8
    half = groups // 2
    sub = lax.broadcasted_iota(jnp.int32, (8, nx), 0)
    for part in range(2):
        scale = []
        for g in range(half):
            k = sub + 8 * (part * half + g)
            mid = -bracket_end + (2.0 * bracket_end / POINTS) * k.astype(f32)
            scale.append(jnp.exp(-0.5 * mid))

        def volume(j, acc):
            acc = list(acc)
            for z in range(nz):
                a = jnp.broadcast_to(amp[j, z : z + 1], (8, nx))
                lo = jnp.broadcast_to(low[j, z : z + 1], (8, nx))
                hi = jnp.broadcast_to(high[j, z : z + 1], (8, nx))
                for g in range(half):
                    t = a * scale[g]
                    if part == 0 and g == 0:
                        t = jnp.where(sub == 0, jnp.broadcast_to(dens(j, z), (8, nx)), t)
                    acc[g] = acc[g] + jnp.minimum(jnp.maximum(t, lo), hi)
            return tuple(acc)

        at = [slice(8 * (part * half + g), 8 * (part * half + g) + 8) for g in range(half)]
        acc = lax.fori_loop(0, n, volume, tuple(start(at[g]) for g in range(half)))
        for g in range(half):
            acc_s[at[g]] = acc[g]


def inner_kernel(flags, src_a, src_b, rim, dens, passive, solid, amp, low, high, acc, s_s, d_s):
    ny, nz, nx = dens.shape
    half = ny // 2
    s_s[0:half] = src_a[...]
    s_s[half:ny] = src_b[...]

    def fix(y, _):
        put_rim(s_s, y, rim[y], nz)
        return 0

    lax.fori_loop(0, ny, fix, 0)

    def finish(j, p3):
        y = j + 2
        amp[j], low[j], high[j] = limits(p3, dens[y], passive[y] == 1, solid[y] == 1)

    filter_block(s_s, d_s, ny, (flags[2], flags[3]), None, finish)
    table(
        ny - 4, nz, nx, amp, low, high, lambda j, z: dens[j + 2, z : z + 1], lambda at: jnp.zeros((8, nx), f32), acc
    )


def inner_call(flags, src_a, src_b, rim, dens, passive, solid):
    ny, nz, nx = dens.shape
    field = jax.ShapeDtypeStruct((ny - 4, nz, nx), f32)
    return pl.pallas_call(
        inner_kernel,
        in_specs=[SMEM] + [VMEM] * 6,
        out_shape=(field, field, field, jax.ShapeDtypeStruct((POINTS, nx), f32)),
        scratch_shapes=[pltpu.VMEM((ny, nz + 2 * OFF, nx), f32), pltpu.VMEM((ny - 2, nz + 2 * OFF, nx), f32)],
        compiler_params=pltpu.CompilerParams(vmem_limit_bytes=16 * 2**20),
        cost_estimate=estimate(9),
        name="filter_inner",
    )(flags, src_a, src_b, rim, dens, passive, solid)


def outer_kernel(
    flags, src_a, src_b, rim, got_even, got_odd, dens, passive, solid, acc, amp, low, high, vols, s_s, d_s, dens_s, acc_s
):
    ny, nz, nx = dens.shape
    half = ny // 2
    odd = flags[4] == 1
    s_s[0, 0:2] = jnp.where(odd, got_even[...], got_odd[...])
    s_s[1, 4:6] = jnp.where(odd, got_odd[...], got_even[...])
    for j in range(4):
        s_s[0, 2 + j] = src_a[j]
        put_rim(s_s.at[0], 2 + j, rim[j], nz)
        s_s[1, j] = src_b[half - 4 + j]
        put_rim(s_s.at[1], j, rim[ny - 4 + j], nz)
    for b in range(2):
        y0 = 0 if b == 0 else ny - 2

        def finish(j, p3):
            y = y0 + j
            at = 2 * b + j
            amp[at], low[at], high[at] = limits(p3, dens[y], passive[y] == 1, solid[y] == 1)
            dens_s[at] = dens[y]

        edges = (flags[0], 1) if b == 0 else (1, flags[1])
        filter_block(s_s.at[b], d_s, 6, (flags[2], flags[3]), edges, finish)
    table(4, nz, nx, amp, low, high, lambda j, z: dens_s[j, z : z + 1], lambda at: acc[at], acc_s)
    vols[...] = jnp.sum(jnp.transpose(acc_s[...]), axis=0, keepdims=True)


def outer_call(flags, src_a, src_b, rim, got_even, got_odd, dens, passive, solid, acc):
    ny, nz, nx = dens.shape
    rows = nz + 2 * OFF
    field = jax.ShapeDtypeStruct((4, nz, nx), f32)
    return pl.pallas_call(
        outer_kernel,
        in_specs=[SMEM] + [VMEM] * 9,
        out_shape=(field, field, field, jax.ShapeDtypeStruct((1, POINTS), f32)),
        scratch_shapes=[
            pltpu.VMEM((2, 6, rows, nx), f32),
            pltpu.VMEM((4, rows, nx), f32),
            pltpu.VMEM((4, nz, nx), f32),
            pltpu.VMEM((POINTS, nx), f32),
        ],
        compiler_params=pltpu.CompilerParams(vmem_limit_bytes=16 * 2**20),
        cost_estimate=estimate(3),
        name="filter_outer",
    )(flags, src_a, src_b, rim, got_even, got_odd, dens, passive, solid, acc)


def update_kernel(tables, amp_i, low_i, high_i, amp_o, low_o, high_o, new, logm):
    inner = amp_i.shape[0]
    nx = amp_i.shape[-1]
    total = jnp.sum(tables[...], axis=0, keepdims=True)
    above = jnp.where(total > total[:, 0:1], 1.0, 0.0)
    middle = -bracket_end + (2.0 * bracket_end / POINTS) * (jnp.sum(above) + 0.5)
    logm[0] = middle
    scale = jnp.exp(jnp.full((1, nx), -0.5 * middle, f32))

    def new_row(amp, low, high):
        return jnp.minimum(jnp.maximum(amp * scale, low), high)

    def body(j, _):
        new[j + 2] = new_row(amp_i[j], low_i[j], high_i[j])
        return 0

    lax.fori_loop(0, inner, body, 0)
    for j in range(4):
        new[j if j < 2 else inner + j] = new_row(amp_o[j], low_o[j], high_o[j])


def update_call(tables, inner, outer):
    n, nz, nx = inner[0].shape
    return pl.pallas_call(
        update_kernel,
        in_specs=[VMEM] * 7,
        out_specs=(VMEM, SMEM),
        out_shape=(jax.ShapeDtypeStruct((n + 4, nz, nx), f32), jax.ShapeDtypeStruct((1,), f32)),
        compiler_params=pltpu.CompilerParams(vmem_limit_bytes=8 * 2**20),
        cost_estimate=estimate(1),
        name="update",
    )(tables, *inner, *outer)


def to_lower(value, axis):
    count = lax.axis_size(axis)
    return lax.ppermute(value, axis, [(i + 1, i) for i in range(count - 1)])


def to_upper(value, axis):
    count = lax.axis_size(axis)
    return lax.ppermute(value, axis, [(i, i + 1) for i in range(count - 1)])


def swap(value, axis, start):
    pairs = []
    for i in range(start, lax.axis_size(axis) - 1, 2):
        pairs += [(i, i + 1), (i + 1, i)]
    return lax.ppermute(value, axis, pairs)


def on_device(displacement, density, passive, solid, stiffness):
    ny, nz, nx = density.shape
    gy, gz = lax.axis_size("gy"), lax.axis_size("gz")
    iy, iz = lax.axis_index("gy"), lax.axis_index("gz")
    flags = jnp.stack([iy > 0, iy < gy - 1, iz > 0, iz < gz - 1, iy % 2 == 1]).astype(jnp.int32)

    fy = to_lower(displacement[:, 0], "gy")
    src_a, mat, own_low, own_high = first_call(displacement, density, stiffness)

    rim_low = jnp.pad(fy[:, nz - 2 :].reshape(1, 18, nx), ((0, 0), (0, 2), (0, 0)))
    rim_high = jnp.pad(fy[:, :3].reshape(1, 27, nx), ((0, 0), (0, 3), (0, 0)))
    got_low = to_upper(jnp.concatenate([own_low, rim_low]), "gz")
    got_high = to_lower(jnp.concatenate([own_high, rim_high]), "gz")
    src_b = last_call(displacement, density, fy, mat)
    rim, msg_even, msg_odd = rim_call(flags, got_low, got_high, own_low, own_high, fy, mat, src_a, src_b)

    got_odd = swap(msg_odd, "gy", 1)
    got_even = swap(msg_even, "gy", 0)
    *inner, acc = inner_call(flags, src_a, src_b, rim, density, passive, solid)
    *outer, vols = outer_call(flags, src_a, src_b, rim, got_even, got_odd, density, passive, solid, acc)

    everyone = jnp.broadcast_to(vols, (gz * gy, POINTS))
    tables = lax.all_to_all(everyone, ("gz", "gy"), 0, 0, tiled=True)
    new, logm = update_call(tables, inner, outer)
    return new, logm.reshape(())


def solution(mesh):
    placed = (
        P(None, "gy", "gz", None),
        P("gy", "gz", None),
        P("gy", "gz", None),
        P("gy", "gz", None),
        P(),
    )
    return jax.shard_map(
        on_device, mesh=mesh, in_specs=placed, out_specs=(P("gy", "gz", None), P()), check_vma=False
    )
```

```python
import functools

import jax
import jax.numpy as jnp
from jax import lax
from jax.experimental import pallas as pl
from jax.experimental.pallas import tpu as pltpu
from jax.sharding import PartitionSpec as P

ITERS = 8
POINTS = 2**ITERS
OFF = 8

smoothing = 0.52
move_limit = 0.2
floor_density = 0.001
bracket_end = 12.0

f32 = jnp.float32
bf16 = jnp.bfloat16
VMEM = pl.BlockSpec(memory_space=pltpu.VMEM)
SMEM = pl.BlockSpec(memory_space=pltpu.SMEM)
HBM = pl.BlockSpec(memory_space=pltpu.HBM)


def cheb_weights():
    spectrum_top = 1.0 + 12.0 * smoothing
    centre_value = (spectrum_top + 1.0) / 2.0
    half_width = (spectrum_top - 1.0) / 2.0
    ratio_value = centre_value / half_width
    first_rho = 1.0 / ratio_value
    second_rho = 1.0 / (2.0 * ratio_value - first_rho)
    third_rho = 1.0 / (2.0 * ratio_value - second_rho)
    return (
        centre_value,
        second_rho * first_rho,
        2.0 * second_rho / half_width,
        third_rho * second_rho,
        2.0 * third_rho / half_width,
    )


def filter_weights():
    t, w1, w2, w3, w4 = cheb_weights()
    diag = 1.0 + 6.0 * smoothing
    alpha = w1 / t + w2 * (1.0 - diag / t)
    beta = w2 * smoothing / t
    gamma = 1.0 / t - w4 * w1 / (t * w2)
    delta = 1.0 + w3 + w4 / w2 - w4 * diag
    eps = w4 * smoothing
    return alpha, beta, gamma, delta, eps


def lane_up(v):
    n = v.shape[-1]
    lane = lax.broadcasted_iota(jnp.int32, v.shape, v.ndim - 1)
    return jnp.where(lane < n - 1, pltpu.roll(v, n - 1, v.ndim - 1), 0.0)


def lane_down(v):
    n = v.shape[-1]
    lane = lax.broadcasted_iota(jnp.int32, v.shape, v.ndim - 1)
    return jnp.where(lane > 0, pltpu.roll(v, 1, v.ndim - 1), 0.0)


def estimate(us):
    return pl.CostEstimate(flops=int(us * 1e9), bytes_accessed=1 << 20, transcendentals=0)


def build_matrix(k, mat):
    shape = (24, 112)
    col = lax.broadcasted_iota(jnp.int32, shape, 1)
    row = lax.broadcasted_iota(jnp.int32, shape, 0)
    main = col < 96
    dy = jnp.where(main, jnp.where(col >= 48, 1, 0), jnp.where(col >= 104, 1, 0))
    q = col - 48 * dy
    e = col - 96 - 8 * dy
    c = jnp.where(main, q >> 4, e >> 1)
    dx = jnp.where(main, (q >> 3) & 1, e & 1)
    valid = main | (e < 6)
    dof0 = 3 * (4 * dy + dx) + c
    pick0 = jnp.where(main & (row == dof0), 1.0, 0.0)
    pick1 = jnp.where(valid & (row == dof0 + 6), 1.0, 0.0)
    hp = lax.Precision.HIGHEST
    k0 = jnp.dot(k, pick0, precision=hp, preferred_element_type=f32)
    k1 = jnp.dot(k, pick1, precision=hp, preferred_element_type=f32)
    col8 = lax.broadcasted_iota(jnp.int32, (8, 112), 1)
    row8 = lax.broadcasted_iota(jnp.int32, (8, 112), 0)
    main8 = col8 < 96
    zc = col8 & 7
    m0 = main8 & (zc == row8)
    m1 = jnp.where(main8, zc, 8) == row8 + 1
    rows = []
    for dz in range(2):
        for dy_ in range(2):
            for c_ in range(3):
                for dx_ in range(2):
                    r = 3 * (4 * dy_ + 2 * dz + dx_) + c_
                    rows.append(jnp.where(m0, k0[r : r + 1], 0.0) + jnp.where(m1, k1[r : r + 1], 0.0))
    full = jnp.concatenate(rows, axis=0)
    hi = full.astype(bf16)
    lo = (full - hi.astype(f32)).astype(bf16)
    mat[:, 0:112] = hi
    mat[:, 112:224] = lo


def prepare(plane, p, main_s, ext_s, mul_s):
    for l in range(3):
        for c in range(3):
            u = plane(3 * l + c)
            nz, nx = u.shape
            last = lax.broadcasted_iota(jnp.int32, u.shape, 0) == nz - 1
            both = (u, lane_up(u))
            for w in range(nz // 8):
                sl = slice(8 * w, 8 * w + 8)
                main_s[p, l, 16 * c : 16 * c + 16, w * nx : (w + 1) * nx] = jnp.concatenate(
                    [both[0][sl], both[1][sl]], axis=0
                ).astype(bf16)
            for dx in range(2):
                v = both[dx]
                k = 2 * c + dx
                if ext_s is not None:
                    for w in range(nz // 8 - 1):
                        ext_s[p, l, k : k + 1, w * nx : (w + 1) * nx] = v[8 * w + 8 : 8 * w + 9]
                m = 2.0 * v - v.astype(bf16).astype(f32)
                mul_s[p, l, k, 0] = m
                mul_s[p, l, k, 1] = jnp.where(last, 0.0, pltpu.roll(m, nz - 1, 0))


def quadratic(force, mul, count, nx, acc):
    i = 0
    for dz in range(2):
        for dy in range(2):
            for k in range(6):
                for w in range(count):
                    term = force[8 * i : 8 * i + 8, w * nx : (w + 1) * nx] * mul(dy, k, dz, w)
                    acc[w] = term if acc[w] is None else acc[w] + term
                i += 1


def energy_row(p, mat, main_s, ext_s, mul_s, density):
    nz, nx = density.shape
    count = nz // 8
    acc = [None] * count
    for l in range(3):
        ext = jnp.concatenate([ext_s[p, l], ext_s[p + 1, l]], axis=0).astype(bf16)
        one = jnp.concatenate([main_s[p, l], main_s[p + 1, l], ext], axis=0)
        force = jnp.dot(mat[...], jnp.concatenate([one, one], axis=0), preferred_element_type=f32)
        quadratic(force, lambda dy, k, dz, w: mul_s[p + dy, l, k, dz, 8 * w : 8 * w + 8], count, nx, acc)
    return density * (-3.0 * density * density * jnp.concatenate(acc, axis=0))


def put_row(out, y, s):
    nz, nx = s.shape
    out[y, 0:OFF] = jnp.zeros((OFF, nx), f32)
    out[y, OFF : OFF + nz] = s
    out[y, OFF + nz :] = jnp.zeros((out.shape[1] - OFF - nz, nx), f32)


def first_kernel(disp, dens, stiff, src, mat, own_low, own_high, disp_s, dens_s, stiff_s, main_s, ext_s, mul_s, sems):
    _, ny, nz, nx = disp_s.shape
    half = ny // 2
    copy_k = pltpu.make_async_copy(stiff, stiff_s, sems.at[ny + 1])
    copy_k.start()
    copies = [pltpu.make_async_copy(disp.at[:, p], disp_s.at[:, p], sems.at[p]) for p in range(ny)]
    for p in range(2):
        copies[p].start()
    copy_d = pltpu.make_async_copy(dens, dens_s, sems.at[ny])
    copy_d.start()
    for p in range(2, ny):
        copies[p].start()
    ext_s[...] = jnp.zeros_like(ext_s)
    copy_k.wait()
    build_matrix(stiff_s[...], mat)
    for p in range(2):
        copies[p].wait()
        prepare(lambda i: disp_s[i, p], p, main_s, ext_s, mul_s)
    copy_d.wait()
    for p in range(2, half + 1):
        copies[p].wait()

    def body(y, _):
        put_row(src, y, energy_row(y, mat, main_s, ext_s, mul_s, dens_s[y]))
        prepare(lambda i: disp_s[i, y + 2], y + 2, main_s, ext_s, mul_s)
        return 0

    lax.fori_loop(0, half - 1, body, 0)
    put_row(src, half - 1, energy_row(half - 1, mat, main_s, ext_s, mul_s, dens_s[half - 1]))
    for p in range(half + 1, ny):
        copies[p].wait()

    def pack(y, _):
        for i in range(9):
            own_low[y, 2 * i : 2 * i + 2] = disp_s[i, y, nz - 2 : nz]
            own_high[y, 3 * i : 3 * i + 3] = disp_s[i, y, 0:3]
        own_low[y, 18:20] = dens_s[y, nz - 2 : nz]
        own_high[y, 27:29] = dens_s[y, 0:2]
        own_low[y, 20:30] = jnp.zeros((10, nx), f32)
        own_high[y, 29:30] = jnp.zeros((1, nx), f32)
        return 0

    lax.fori_loop(0, ny, pack, 0)


def energy_scratch(planes, nz, nx):
    lanes = nx * (nz // 8)
    return [
        pltpu.VMEM((planes, 3, 48, lanes), bf16),
        pltpu.VMEM((planes, 3, 8, lanes), f32),
        pltpu.VMEM((planes, 3, 6, 2, nz, nx), f32),
    ]


def first_call(disp, dens, stiff):
    _, ny, nz, nx = disp.shape
    half = ny // 2
    return pl.pallas_call(
        first_kernel,
        in_specs=[HBM, HBM, HBM],
        out_shape=(
            jax.ShapeDtypeStruct((half, nz + 2 * OFF, nx), f32),
            jax.ShapeDtypeStruct((192, 224), bf16),
            jax.ShapeDtypeStruct((ny, 30, nx), f32),
            jax.ShapeDtypeStruct((ny, 30, nx), f32),
        ),
        scratch_shapes=[pltpu.VMEM((9, ny, nz, nx), f32), pltpu.VMEM((ny, nz, nx), f32), pltpu.VMEM((24, 24), f32)]
        + energy_scratch(half + 1, nz, nx)
        + [pltpu.SemaphoreType.DMA((ny + 2,))],
        compiler_params=pltpu.CompilerParams(vmem_limit_bytes=24 * 2**20),
        cost_estimate=estimate(5),
        name="energy_first",
    )(disp, dens, stiff)


def last_kernel(disp, dens, fy, mat, src, disp_s, dens_s, main_s, ext_s, mul_s, sems):
    _, half, nz, nx = disp_s.shape
    copies = [pltpu.make_async_copy(disp.at[:, half + p], disp_s.at[:, p], sems.at[p]) for p in range(half)]
    for p in range(2):
        copies[p].start()
    copy_d = pltpu.make_async_copy(dens.at[pl.ds(half, half)], dens_s, sems.at[half])
    copy_d.start()
    for p in range(2, half):
        copies[p].start()
    ext_s[...] = jnp.zeros_like(ext_s)
    for p in range(2):
        copies[p].wait()
        prepare(lambda i: disp_s[i, p], p, main_s, ext_s, mul_s)
    copy_d.wait()
    for p in range(2, half):
        copies[p].wait()

    def row(y):
        put_row(src, y, energy_row(y, mat, main_s, ext_s, mul_s, dens_s[y]))

    def body(y, _):
        row(y)
        prepare(lambda i: disp_s[i, y + 2], y + 2, main_s, ext_s, mul_s)
        return 0

    lax.fori_loop(0, half - 2, body, 0)
    row(half - 2)
    prepare(lambda i: fy[i], half, main_s, ext_s, mul_s)
    row(half - 1)


def last_call(disp, dens, fy, mat):
    _, ny, nz, nx = disp.shape
    half = ny // 2
    return pl.pallas_call(
        last_kernel,
        in_specs=[HBM, HBM, VMEM, VMEM],
        out_shape=jax.ShapeDtypeStruct((half, nz + 2 * OFF, nx), f32),
        scratch_shapes=[pltpu.VMEM((9, half, nz, nx), f32), pltpu.VMEM((half, nz, nx), f32)]
        + energy_scratch(half + 1, nz, nx)
        + [pltpu.SemaphoreType.DMA((half + 1,))],
        compiler_params=pltpu.CompilerParams(vmem_limit_bytes=24 * 2**20),
        cost_estimate=estimate(5),
        name="energy_last",
    )(disp, dens, fy, mat)


def rim_kernel(
    flags, got_even, got_odd, own_low, own_high, fy, mat, src_a, src_b, rim, msg_even, msg_odd, d_s, main_s, mul_s, t_s
):
    ny, _, nx = own_low.shape
    nz = src_a.shape[1] - 2 * OFF
    half = ny // 2
    z_odd = flags[5] == 1

    def below(p, a, n):
        return jnp.where(z_odd, got_even[p, a : a + n], got_odd[p, a : a + n])

    def above(p, a, n):
        return jnp.where(z_odd, got_odd[p, a : a + n], got_even[p, a : a + n])

    def window(p, first, last):
        def rows(i):
            zero = jnp.zeros((1, nx), f32)
            return jnp.concatenate([below(p, 2 * i, 2), first(i), last(i), above(p, 3 * i, 3), zero], axis=0)

        prepare(rows, p, main_s, None, mul_s)

    def own(p, _):
        window(p, lambda i: own_high[p, 3 * i : 3 * i + 1], lambda i: own_low[p, 2 * i + 1 : 2 * i + 2])
        zero = jnp.zeros((1, nx), f32)
        d_s[p] = jnp.concatenate([below(p, 18, 2), zero, own_low[p, 19:20], above(p, 27, 2), zero, zero], axis=0)
        return 0

    lax.fori_loop(0, ny, own, 0, unroll=4)
    window(ny, lambda i: fy[i, 0:1], lambda i: fy[i, nz - 1 : nz])

    group = 4

    def rows(g, _):
        acc = [None] * group
        for l in range(3):
            parts = [
                jnp.concatenate([main_s[g * group + j + dy, l] for j in range(group)], axis=1) for dy in range(2)
            ]
            one = jnp.concatenate(parts + [jnp.zeros((16, group * nx), bf16)], axis=0)
            force = jnp.dot(mat[...], jnp.concatenate([one, one], axis=0), preferred_element_type=f32)
            quadratic(force, lambda dy, k, dz, w: mul_s[g * group + w + dy, l, k, dz], group, nx, acc)
        for j in range(group):
            d = d_s[g * group + j]
            rim[g * group + j] = d * (-3.0 * d * d * acc[j])
        return 0

    lax.fori_loop(0, ny // group, rows, 0)

    for j in range(4):
        y = j if j < 2 else ny - 4 + j
        t_s[j] = src_a[y] if j < 2 else src_b[y - half]
        put_rim(t_s, j, rim[y], nz)
    odd = flags[4] == 1
    msg_even[...] = jnp.where(odd, t_s[0:2], t_s[2:4])
    msg_odd[...] = jnp.where(odd, t_s[2:4], t_s[0:2])


def put_rim(s, y, rim, nz):
    s[y, OFF - 2 : OFF] = rim[0:2]
    s[y, OFF + nz - 1 : OFF + nz + 2] = rim[3:6]


def rim_call(flags, got_even, got_odd, own_low, own_high, fy, mat, src_a, src_b):
    ny, _, nx = own_low.shape
    rows = src_a.shape[1]
    return pl.pallas_call(
        rim_kernel,
        in_specs=[SMEM] + [VMEM] * 8,
        out_shape=(
            jax.ShapeDtypeStruct((ny, 8, nx), f32),
            jax.ShapeDtypeStruct((2, rows, nx), f32),
            jax.ShapeDtypeStruct((2, rows, nx), f32),
        ),
        scratch_shapes=[
            pltpu.VMEM((ny, 8, nx), f32),
            pltpu.VMEM((ny + 1, 3, 48, nx), bf16),
            pltpu.VMEM((ny + 1, 3, 6, 2, 8, nx), f32),
            pltpu.VMEM((4, rows, nx), f32),
        ],
        compiler_params=pltpu.CompilerParams(vmem_limit_bytes=16 * 2**20),
        cost_estimate=estimate(2),
        name="energy_rim",
    )(flags, got_even, got_odd, own_low, own_high, fy, mat, src_a, src_b)


def filter_block(s_s, d_s, n, z_edges, y_edges, finish):
    rows, nx = s_s.shape[1:]
    nz = rows - 2 * OFF
    alpha, beta, gamma, delta, eps = filter_weights()
    row = lax.broadcasted_iota(jnp.int32, (rows, nx), 0)
    keep = jnp.where(row < OFF, z_edges[0], jnp.where(row >= OFF + nz, z_edges[1], 1)) == 1

    def beside(v):
        return pltpu.roll(v, 1, 0) + pltpu.roll(v, rows - 1, 0) + lane_up(v) + lane_down(v)

    def second(j, _):
        c = s_s[j + 1]
        d2 = alpha * c + beta * (beside(c) + s_s[j] + s_s[j + 2])
        ok = keep
        if y_edges is not None:
            ok = keep & (jnp.where(j == 0, y_edges[0], jnp.where(j == n - 3, y_edges[1], 1)) == 1)
        d_s[j] = jnp.where(ok, d2, 0.0)
        return 0

    def third(j, _):
        d2 = d_s[j + 1]
        p3 = gamma * s_s[j + 2] + delta * d2 + eps * (beside(d2) + d_s[j] + d_s[j + 2])
        finish(j, p3[OFF : OFF + nz])
        return 0

    lax.fori_loop(0, n - 2, second, 0)
    lax.fori_loop(0, n - 4, third, 0)


def limits(p3, d, pas, sol):
    amp = jnp.sqrt(jnp.maximum(-p3 * d, 0.0))
    lower = jnp.maximum(d - move_limit, floor_density)
    upper = jnp.minimum(d + move_limit, 1.0)
    low = jnp.where(sol, 1.0, jnp.where(pas, floor_density, lower))
    high = jnp.where(sol, 1.0, jnp.where(pas, floor_density, upper))
    return amp, low, high


def table(n, nz, nx, amp, low, high, dens, start, acc_s):
    groups = POINTS // 8
    half = groups // 2
    sub = lax.broadcasted_iota(jnp.int32, (8, nx), 0)
    for part in range(2):
        scale = []
        for g in range(half):
            k = sub + 8 * (part * half + g)
            mid = -bracket_end + (2.0 * bracket_end / POINTS) * k.astype(f32)
            scale.append(jnp.exp(-0.5 * mid))

        def volume(j, acc):
            acc = list(acc)
            for z in range(nz):
                a = jnp.broadcast_to(amp[j, z : z + 1], (8, nx))
                lo = jnp.broadcast_to(low[j, z : z + 1], (8, nx))
                hi = jnp.broadcast_to(high[j, z : z + 1], (8, nx))
                for g in range(half):
                    t = a * scale[g]
                    if part == 0 and g == 0:
                        t = jnp.where(sub == 0, jnp.broadcast_to(dens(j, z), (8, nx)), t)
                    acc[g] = acc[g] + jnp.minimum(jnp.maximum(t, lo), hi)
            return tuple(acc)

        at = [slice(8 * (part * half + g), 8 * (part * half + g) + 8) for g in range(half)]
        acc = lax.fori_loop(0, n, volume, tuple(start(at[g]) for g in range(half)))
        for g in range(half):
            acc_s[at[g]] = acc[g]


def inner_kernel(flags, src_a, src_b, rim, dens, passive, solid, amp, low, high, acc, s_s, d_s):
    ny, nz, nx = dens.shape
    half = ny // 2
    s_s[0:half] = src_a[...]
    s_s[half:ny] = src_b[...]

    def fix(y, _):
        put_rim(s_s, y, rim[y], nz)
        return 0

    lax.fori_loop(0, ny, fix, 0)

    def finish(j, p3):
        y = j + 2
        amp[j], low[j], high[j] = limits(p3, dens[y], passive[y] == 1, solid[y] == 1)

    filter_block(s_s, d_s, ny, (flags[2], flags[3]), None, finish)
    table(
        ny - 4, nz, nx, amp, low, high, lambda j, z: dens[j + 2, z : z + 1], lambda at: jnp.zeros((8, nx), f32), acc
    )


def inner_call(flags, src_a, src_b, rim, dens, passive, solid):
    ny, nz, nx = dens.shape
    field = jax.ShapeDtypeStruct((ny - 4, nz, nx), f32)
    return pl.pallas_call(
        inner_kernel,
        in_specs=[SMEM] + [VMEM] * 6,
        out_shape=(field, field, field, jax.ShapeDtypeStruct((POINTS, nx), f32)),
        scratch_shapes=[pltpu.VMEM((ny, nz + 2 * OFF, nx), f32), pltpu.VMEM((ny - 2, nz + 2 * OFF, nx), f32)],
        compiler_params=pltpu.CompilerParams(vmem_limit_bytes=16 * 2**20),
        cost_estimate=estimate(9),
        name="filter_inner",
    )(flags, src_a, src_b, rim, dens, passive, solid)


def outer_kernel(
    flags, src_a, src_b, rim, got_even, got_odd, dens, passive, solid, acc, amp, low, high, vols, s_s, d_s, dens_s, acc_s
):
    ny, nz, nx = dens.shape
    half = ny // 2
    odd = flags[4] == 1
    s_s[0, 0:2] = jnp.where(odd, got_even[...], got_odd[...])
    s_s[1, 4:6] = jnp.where(odd, got_odd[...], got_even[...])
    for j in range(4):
        s_s[0, 2 + j] = src_a[j]
        put_rim(s_s.at[0], 2 + j, rim[j], nz)
        s_s[1, j] = src_b[half - 4 + j]
        put_rim(s_s.at[1], j, rim[ny - 4 + j], nz)
    for b in range(2):
        y0 = 0 if b == 0 else ny - 2

        def finish(j, p3):
            y = y0 + j
            at = 2 * b + j
            amp[at], low[at], high[at] = limits(p3, dens[y], passive[y] == 1, solid[y] == 1)
            dens_s[at] = dens[y]

        edges = (flags[0], 1) if b == 0 else (1, flags[1])
        filter_block(s_s.at[b], d_s, 6, (flags[2], flags[3]), edges, finish)
    table(4, nz, nx, amp, low, high, lambda j, z: dens_s[j, z : z + 1], lambda at: acc[at], acc_s)
    vols[...] = jnp.sum(jnp.transpose(acc_s[...]), axis=0, keepdims=True)


def outer_call(flags, src_a, src_b, rim, got_even, got_odd, dens, passive, solid, acc):
    ny, nz, nx = dens.shape
    rows = nz + 2 * OFF
    field = jax.ShapeDtypeStruct((4, nz, nx), f32)
    return pl.pallas_call(
        outer_kernel,
        in_specs=[SMEM] + [VMEM] * 9,
        out_shape=(field, field, field, jax.ShapeDtypeStruct((1, POINTS), f32)),
        scratch_shapes=[
            pltpu.VMEM((2, 6, rows, nx), f32),
            pltpu.VMEM((4, rows, nx), f32),
            pltpu.VMEM((4, nz, nx), f32),
            pltpu.VMEM((POINTS, nx), f32),
        ],
        compiler_params=pltpu.CompilerParams(vmem_limit_bytes=16 * 2**20),
        cost_estimate=estimate(3),
        name="filter_outer",
    )(flags, src_a, src_b, rim, got_even, got_odd, dens, passive, solid, acc)


def update_kernel(tables, amp_i, low_i, high_i, amp_o, low_o, high_o, new, logm):
    inner = amp_i.shape[0]
    nx = amp_i.shape[-1]
    total = jnp.sum(tables[...], axis=0, keepdims=True)
    above = jnp.where(total > total[:, 0:1], 1.0, 0.0)
    middle = -bracket_end + (2.0 * bracket_end / POINTS) * (jnp.sum(above) + 0.5)
    logm[0] = middle
    scale = jnp.exp(jnp.full((1, nx), -0.5 * middle, f32))

    def new_row(amp, low, high):
        return jnp.minimum(jnp.maximum(amp * scale, low), high)

    def body(j, _):
        new[j + 2] = new_row(amp_i[j], low_i[j], high_i[j])
        return 0

    lax.fori_loop(0, inner, body, 0)
    for j in range(4):
        new[j if j < 2 else inner + j] = new_row(amp_o[j], low_o[j], high_o[j])


def update_call(tables, inner, outer):
    n, nz, nx = inner[0].shape
    return pl.pallas_call(
        update_kernel,
        in_specs=[VMEM] * 7,
        out_specs=(VMEM, SMEM),
        out_shape=(jax.ShapeDtypeStruct((n + 4, nz, nx), f32), jax.ShapeDtypeStruct((1,), f32)),
        compiler_params=pltpu.CompilerParams(vmem_limit_bytes=8 * 2**20),
        cost_estimate=estimate(1),
        name="update",
    )(tables, *inner, *outer)


def to_lower(value, axis):
    count = lax.axis_size(axis)
    return lax.ppermute(value, axis, [(i + 1, i) for i in range(count - 1)])


def swap(value, axis, start):
    pairs = []
    for i in range(start, lax.axis_size(axis) - 1, 2):
        pairs += [(i, i + 1), (i + 1, i)]
    return lax.ppermute(value, axis, pairs)


def to_all(row, axis):
    everyone = jnp.broadcast_to(row, (lax.axis_size(axis), row.shape[1]))
    return lax.all_to_all(everyone, axis, 0, 0, tiled=True)


def on_device(displacement, density, passive, solid, stiffness):
    ny, nz, nx = density.shape
    gy, gz = lax.axis_size("gy"), lax.axis_size("gz")
    iy, iz = lax.axis_index("gy"), lax.axis_index("gz")
    flags = jnp.stack([iy > 0, iy < gy - 1, iz > 0, iz < gz - 1, iy % 2 == 1, iz % 2 == 1]).astype(jnp.int32)

    disp_hbm = pltpu.with_memory_space_constraint(displacement, pltpu.HBM)
    dens_hbm = pltpu.with_memory_space_constraint(density, pltpu.HBM)
    stiff_hbm = pltpu.with_memory_space_constraint(stiffness, pltpu.HBM)

    fy = to_lower(displacement[:, 0], "gy")
    src_a, mat, own_low, own_high = first_call(disp_hbm, dens_hbm, stiff_hbm)

    rim_low = jnp.pad(fy[:, nz - 2 :].reshape(1, 18, nx), ((0, 0), (0, 12), (0, 0)))
    rim_high = jnp.pad(fy[:, :3].reshape(1, 27, nx), ((0, 0), (0, 3), (0, 0)))
    to_above = jnp.concatenate([own_low, rim_low])
    to_below = jnp.concatenate([own_high, rim_high])
    z_odd = iz % 2 == 1
    z_got_odd = swap(jnp.where(z_odd, to_above, to_below), "gz", 1)
    z_got_even = swap(jnp.where(z_odd, to_below, to_above), "gz", 0)
    src_b = last_call(disp_hbm, dens_hbm, fy, mat)
    rim, msg_even, msg_odd = rim_call(flags, z_got_even, z_got_odd, own_low, own_high, fy, mat, src_a, src_b)

    got_odd = swap(msg_odd, "gy", 1)
    got_even = swap(msg_even, "gy", 0)
    *inner, acc = inner_call(flags, src_a, src_b, rim, density, passive, solid)
    *outer, vols = outer_call(flags, src_a, src_b, rim, got_even, got_odd, density, passive, solid, acc)

    vols = to_all(vols, "gz").sum(axis=0, keepdims=True)
    tables = to_all(vols, "gy")
    new, logm = update_call(tables, inner, outer)
    return new, logm.reshape(())


def solution(mesh):
    placed = (
        P(None, "gy", "gz", None),
        P("gy", "gz", None),
        P("gy", "gz", None),
        P("gy", "gz", None),
        P(),
    )
    return jax.shard_map(
        on_device, mesh=mesh, in_specs=placed, out_specs=(P("gy", "gz", None), P()), check_vma=False
    )
```

```python
import math

import jax
import jax.numpy as jnp
from jax import lax
from jax.experimental import pallas as pl
from jax.experimental.pallas import tpu as pltpu
from jax.sharding import PartitionSpec as P

ITERS = 8
POINTS = 2**ITERS
OFF = 8

smoothing = 0.52
move_limit = 0.2
floor_density = 0.001
bracket_end = 12.0

f32 = jnp.float32
bf16 = jnp.bfloat16
VMEM = pl.BlockSpec(memory_space=pltpu.VMEM)
SMEM = pl.BlockSpec(memory_space=pltpu.SMEM)
HBM = pl.BlockSpec(memory_space=pltpu.HBM)


def cheb_weights():
    spectrum_top = 1.0 + 12.0 * smoothing
    centre_value = (spectrum_top + 1.0) / 2.0
    half_width = (spectrum_top - 1.0) / 2.0
    ratio_value = centre_value / half_width
    first_rho = 1.0 / ratio_value
    second_rho = 1.0 / (2.0 * ratio_value - first_rho)
    third_rho = 1.0 / (2.0 * ratio_value - second_rho)
    return (
        centre_value,
        second_rho * first_rho,
        2.0 * second_rho / half_width,
        third_rho * second_rho,
        2.0 * third_rho / half_width,
    )


def filter_weights():
    t, w1, w2, w3, w4 = cheb_weights()
    diag = 1.0 + 6.0 * smoothing
    alpha = w1 / t + w2 * (1.0 - diag / t)
    beta = w2 * smoothing / t
    gamma = 1.0 / t - w4 * w1 / (t * w2)
    delta = 1.0 + w3 + w4 / w2 - w4 * diag
    eps = w4 * smoothing
    return alpha, beta, gamma, delta, eps


def lane_up(v):
    n = v.shape[-1]
    lane = lax.broadcasted_iota(jnp.int32, v.shape, v.ndim - 1)
    return jnp.where(lane < n - 1, pltpu.roll(v, n - 1, v.ndim - 1), 0.0)


def lane_down(v):
    n = v.shape[-1]
    lane = lax.broadcasted_iota(jnp.int32, v.shape, v.ndim - 1)
    return jnp.where(lane > 0, pltpu.roll(v, 1, v.ndim - 1), 0.0)


def estimate(us):
    return pl.CostEstimate(flops=int(us * 1e9), bytes_accessed=1 << 20, transcendentals=0)


def build_matrix(k, mat):
    shape = (24, 112)
    col = lax.broadcasted_iota(jnp.int32, shape, 1)
    row = lax.broadcasted_iota(jnp.int32, shape, 0)
    main = col < 96
    dy = jnp.where(main, jnp.where(col >= 48, 1, 0), jnp.where(col >= 104, 1, 0))
    q = col - 48 * dy
    e = col - 96 - 8 * dy
    c = jnp.where(main, q >> 4, e >> 1)
    dx = jnp.where(main, (q >> 3) & 1, e & 1)
    valid = main | (e < 6)
    dof0 = 3 * (4 * dy + dx) + c
    pick0 = jnp.where(main & (row == dof0), 1.0, 0.0)
    pick1 = jnp.where(valid & (row == dof0 + 6), 1.0, 0.0)
    hp = lax.Precision.HIGHEST
    k0 = jnp.dot(k, pick0, precision=hp, preferred_element_type=f32)
    k1 = jnp.dot(k, pick1, precision=hp, preferred_element_type=f32)
    col8 = lax.broadcasted_iota(jnp.int32, (8, 112), 1)
    row8 = lax.broadcasted_iota(jnp.int32, (8, 112), 0)
    main8 = col8 < 96
    zc = col8 & 7
    m0 = main8 & (zc == row8)
    m1 = jnp.where(main8, zc, 8) == row8 + 1
    rows = []
    for dz in range(2):
        for dy_ in range(2):
            for c_ in range(3):
                for dx_ in range(2):
                    r = 3 * (4 * dy_ + 2 * dz + dx_) + c_
                    rows.append(jnp.where(m0, k0[r : r + 1], 0.0) + jnp.where(m1, k1[r : r + 1], 0.0))
    full = jnp.concatenate(rows, axis=0)
    hi = full.astype(bf16)
    lo = (full - hi.astype(f32)).astype(bf16)
    mat[:, 0:112] = hi
    mat[:, 112:224] = lo


def prepare(plane, p, main_s, ext_s, mul_s):
    for l in range(3):
        for c in range(3):
            u = plane(3 * l + c)
            nz, nx = u.shape
            last = lax.broadcasted_iota(jnp.int32, u.shape, 0) == nz - 1
            both = (u, lane_up(u))
            for w in range(nz // 8):
                sl = slice(8 * w, 8 * w + 8)
                main_s[p, l, 16 * c : 16 * c + 16, w * nx : (w + 1) * nx] = jnp.concatenate(
                    [both[0][sl], both[1][sl]], axis=0
                ).astype(bf16)
            for dx in range(2):
                v = both[dx]
                k = 2 * c + dx
                if ext_s is not None:
                    for w in range(nz // 8 - 1):
                        ext_s[p, l, k : k + 1, w * nx : (w + 1) * nx] = v[8 * w + 8 : 8 * w + 9]
                m = 2.0 * v - v.astype(bf16).astype(f32)
                mul_s[p, l, k, 0] = m
                mul_s[p, l, k, 1] = jnp.where(last, 0.0, pltpu.roll(m, nz - 1, 0))


def quadratic(force, mul, count, nx, acc):
    i = 0
    for dz in range(2):
        for dy in range(2):
            for k in range(6):
                for w in range(count):
                    term = force[8 * i : 8 * i + 8, w * nx : (w + 1) * nx] * mul(dy, k, dz, w)
                    acc[w] = term if acc[w] is None else acc[w] + term
                i += 1


def energy_row(p, mat, main_s, ext_s, mul_s, density):
    nz, nx = density.shape
    count = nz // 8
    acc = [None] * count
    for l in range(3):
        ext = jnp.concatenate([ext_s[p, l], ext_s[p + 1, l]], axis=0).astype(bf16)
        one = jnp.concatenate([main_s[p, l], main_s[p + 1, l], ext], axis=0)
        force = jnp.dot(mat[...], jnp.concatenate([one, one], axis=0), preferred_element_type=f32)
        quadratic(force, lambda dy, k, dz, w: mul_s[p + dy, l, k, dz, 8 * w : 8 * w + 8], count, nx, acc)
    return density * (-3.0 * density * density * jnp.concatenate(acc, axis=0))


def put_row(out, y, s):
    nz, nx = s.shape
    out[y, 0:OFF] = jnp.zeros((OFF, nx), f32)
    out[y, OFF : OFF + nz] = s
    out[y, OFF + nz :] = jnp.zeros((out.shape[1] - OFF - nz, nx), f32)


def load_kernel(disp, dens, stiff, face, disp_v, dens_v, mat, stiff_s, sems):
    copies = [
        pltpu.make_async_copy(stiff, stiff_s, sems.at[0]),
        pltpu.make_async_copy(disp.at[:, 0], face, sems.at[1]),
        pltpu.make_async_copy(disp, disp_v, sems.at[2]),
        pltpu.make_async_copy(dens, dens_v, sems.at[3]),
    ]
    for copy in copies:
        copy.start()
    copies[0].wait()
    build_matrix(stiff_s[...], mat)
    for copy in copies[1:]:
        copy.wait()


def load_call(disp, dens, stiff):
    _, ny, nz, nx = disp.shape
    return pl.pallas_call(
        load_kernel,
        in_specs=[HBM, HBM, HBM],
        out_shape=(
            jax.ShapeDtypeStruct((9, nz, nx), f32),
            jax.ShapeDtypeStruct((9, ny, nz, nx), f32),
            jax.ShapeDtypeStruct((ny, nz, nx), f32),
            jax.ShapeDtypeStruct((192, 224), bf16),
        ),
        scratch_shapes=[pltpu.VMEM((24, 24), f32), pltpu.SemaphoreType.DMA((4,))],
        compiler_params=pltpu.CompilerParams(vmem_limit_bytes=16 * 2**20),
        name="load",
    )(disp, dens, stiff)


def energy_scratch(planes, nz, nx):
    lanes = nx * (nz // 8)
    return [
        pltpu.VMEM((planes, 3, 48, lanes), bf16),
        pltpu.VMEM((planes, 3, 8, lanes), f32),
        pltpu.VMEM((planes, 3, 6, 2, nz, nx), f32),
    ]


def first_kernel(disp, dens, mat, src, own_low, own_high, main_s, ext_s, mul_s):
    _, ny, nz, nx = disp.shape
    half = ny // 2
    ext_s[...] = jnp.zeros_like(ext_s)
    for p in range(2):
        prepare(lambda i: disp[i, p], p, main_s, ext_s, mul_s)

    def row(y):
        put_row(src, y, energy_row(y, mat, main_s, ext_s, mul_s, dens[y]))

    def body(y, _):
        row(y)
        prepare(lambda i: disp[i, y + 2], y + 2, main_s, ext_s, mul_s)
        return 0

    lax.fori_loop(0, half - 1, body, 0)
    row(half - 1)

    def pack(y, _):
        for i in range(9):
            own_low[y, 2 * i : 2 * i + 2] = disp[i, y, nz - 2 : nz]
            own_high[y, 3 * i : 3 * i + 3] = disp[i, y, 0:3]
        own_low[y, 18:20] = dens[y, nz - 2 : nz]
        own_high[y, 27:29] = dens[y, 0:2]
        own_low[y, 20:30] = jnp.zeros((10, nx), f32)
        own_high[y, 29:30] = jnp.zeros((1, nx), f32)
        return 0

    lax.fori_loop(0, ny, pack, 0, unroll=2)


def first_call(disp, dens, mat):
    _, ny, nz, nx = disp.shape
    half = ny // 2
    return pl.pallas_call(
        first_kernel,
        in_specs=[VMEM] * 3,
        out_shape=(
            jax.ShapeDtypeStruct((half, nz + 2 * OFF, nx), f32),
            jax.ShapeDtypeStruct((ny, 30, nx), f32),
            jax.ShapeDtypeStruct((ny, 30, nx), f32),
        ),
        scratch_shapes=energy_scratch(half + 1, nz, nx),
        compiler_params=pltpu.CompilerParams(vmem_limit_bytes=24 * 2**20),
        cost_estimate=estimate(5),
        name="energy_first",
    )(disp, dens, mat)


def last_kernel(disp, dens, fy, mat, src, main_s, ext_s, mul_s):
    _, ny, nz, nx = disp.shape
    half = ny // 2
    ext_s[...] = jnp.zeros_like(ext_s)
    for p in range(2):
        prepare(lambda i: disp[i, half + p], p, main_s, ext_s, mul_s)

    def row(y):
        put_row(src, y, energy_row(y, mat, main_s, ext_s, mul_s, dens[half + y]))

    def body(y, _):
        row(y)
        prepare(lambda i: disp[i, half + y + 2], y + 2, main_s, ext_s, mul_s)
        return 0

    lax.fori_loop(0, half - 2, body, 0)
    row(half - 2)
    prepare(lambda i: fy[i], half, main_s, ext_s, mul_s)
    row(half - 1)


def last_call(disp, dens, fy, mat):
    _, ny, nz, nx = disp.shape
    half = ny // 2
    return pl.pallas_call(
        last_kernel,
        in_specs=[VMEM] * 4,
        out_shape=jax.ShapeDtypeStruct((half, nz + 2 * OFF, nx), f32),
        scratch_shapes=energy_scratch(half + 1, nz, nx),
        compiler_params=pltpu.CompilerParams(vmem_limit_bytes=24 * 2**20),
        cost_estimate=estimate(5),
        name="energy_last",
    )(disp, dens, fy, mat)


def rim_kernel(
    flags, got_even, got_odd, own_low, own_high, fy, mat, src_a, src_b, rim, msg_even, msg_odd, d_s, main_s, mul_s, t_s
):
    ny, _, nx = own_low.shape
    nz = src_a.shape[1] - 2 * OFF
    half = ny // 2
    z_odd = flags[5] == 1

    def below(p, a, n):
        return jnp.where(z_odd, got_even[p, a : a + n], got_odd[p, a : a + n])

    def above(p, a, n):
        return jnp.where(z_odd, got_odd[p, a : a + n], got_even[p, a : a + n])

    def window(p, first, last):
        def rows(i):
            zero = jnp.zeros((1, nx), f32)
            return jnp.concatenate([below(p, 2 * i, 2), first(i), last(i), above(p, 3 * i, 3), zero], axis=0)

        prepare(rows, p, main_s, None, mul_s)

    def own(p, _):
        window(p, lambda i: own_high[p, 3 * i : 3 * i + 1], lambda i: own_low[p, 2 * i + 1 : 2 * i + 2])
        zero = jnp.zeros((1, nx), f32)
        d_s[p] = jnp.concatenate([below(p, 18, 2), zero, own_low[p, 19:20], above(p, 27, 2), zero, zero], axis=0)
        return 0

    lax.fori_loop(0, ny, own, 0, unroll=4)
    window(ny, lambda i: fy[i, 0:1], lambda i: fy[i, nz - 1 : nz])

    group = 4

    def rows(g, _):
        acc = [None] * group
        for l in range(3):
            parts = [
                jnp.concatenate([main_s[g * group + j + dy, l] for j in range(group)], axis=1) for dy in range(2)
            ]
            one = jnp.concatenate(parts + [jnp.zeros((16, group * nx), bf16)], axis=0)
            force = jnp.dot(mat[...], jnp.concatenate([one, one], axis=0), preferred_element_type=f32)
            quadratic(force, lambda dy, k, dz, w: mul_s[g * group + w + dy, l, k, dz], group, nx, acc)
        for j in range(group):
            d = d_s[g * group + j]
            rim[g * group + j] = d * (-3.0 * d * d * acc[j])
        return 0

    lax.fori_loop(0, ny // group, rows, 0)

    for j in range(4):
        y = j if j < 2 else ny - 4 + j
        t_s[j] = src_a[y] if j < 2 else src_b[y - half]
        put_rim(t_s, j, rim[y], nz)
    odd = flags[4] == 1
    msg_even[...] = jnp.where(odd, t_s[0:2], t_s[2:4])
    msg_odd[...] = jnp.where(odd, t_s[2:4], t_s[0:2])


def put_rim(s, y, rim, nz):
    s[y, OFF - 2 : OFF] = rim[0:2]
    s[y, OFF + nz - 1 : OFF + nz + 2] = rim[3:6]


def rim_call(flags, got_even, got_odd, own_low, own_high, fy, mat, src_a, src_b):
    ny, _, nx = own_low.shape
    rows = src_a.shape[1]
    return pl.pallas_call(
        rim_kernel,
        in_specs=[SMEM] + [VMEM] * 8,
        out_shape=(
            jax.ShapeDtypeStruct((ny, 8, nx), f32),
            jax.ShapeDtypeStruct((2, rows, nx), f32),
            jax.ShapeDtypeStruct((2, rows, nx), f32),
        ),
        scratch_shapes=[
            pltpu.VMEM((ny, 8, nx), f32),
            pltpu.VMEM((ny + 1, 3, 48, nx), bf16),
            pltpu.VMEM((ny + 1, 3, 6, 2, 8, nx), f32),
            pltpu.VMEM((4, rows, nx), f32),
        ],
        compiler_params=pltpu.CompilerParams(vmem_limit_bytes=16 * 2**20),
        cost_estimate=estimate(2),
        name="energy_rim",
    )(flags, got_even, got_odd, own_low, own_high, fy, mat, src_a, src_b)


def filter_block(s_s, d_s, n, z_edges, y_edges, finish, unroll):
    rows, nx = s_s.shape[1:]
    nz = rows - 2 * OFF
    alpha, beta, gamma, delta, eps = filter_weights()
    row = lax.broadcasted_iota(jnp.int32, (rows, nx), 0)
    keep = jnp.where(row < OFF, z_edges[0], jnp.where(row >= OFF + nz, z_edges[1], 1)) == 1

    def beside(v):
        return pltpu.roll(v, 1, 0) + pltpu.roll(v, rows - 1, 0) + lane_up(v) + lane_down(v)

    def second(j, _):
        c = s_s[j + 1]
        d2 = alpha * c + beta * (beside(c) + s_s[j] + s_s[j + 2])
        ok = keep
        if y_edges is not None:
            ok = keep & (jnp.where(j == 0, y_edges[0], jnp.where(j == n - 3, y_edges[1], 1)) == 1)
        d_s[j] = jnp.where(ok, d2, 0.0)
        return 0

    def third(j, _):
        d2 = d_s[j + 1]
        p3 = gamma * s_s[j + 2] + delta * d2 + eps * (beside(d2) + d_s[j] + d_s[j + 2])
        finish(j, p3[OFF : OFF + nz])
        return 0

    lax.fori_loop(0, n - 2, second, 0, unroll=unroll)
    lax.fori_loop(0, n - 4, third, 0, unroll=unroll)


def limits(p3, d, pas, sol):
    amp = jnp.sqrt(jnp.maximum(-p3 * d, 0.0))
    lower = jnp.maximum(d - move_limit, floor_density)
    upper = jnp.minimum(d + move_limit, 1.0)
    low, high, now = (jnp.where(sol, 1.0, jnp.where(pas, floor_density, v)) for v in (lower, upper, d))
    return amp, low, high, now


FINE = 16
COARSE = POINTS // FINE


def table(n, nz, nx, amp, low, high, now, fine_s, vol, tgt, start):
    spacing = 2.0 * bracket_end / POINTS

    def fine(j, _):
        a = amp[j]
        for f in range(FINE):
            fine_s[f, j] = a * math.exp(-0.5 * spacing * f)
        return 0

    lax.fori_loop(0, n, fine, 0)
    pair = 2
    for first in range(0, COARSE, pair):
        inverse = [math.exp(0.5 * (-bracket_end + spacing * FINE * i)) for i in range(first, first + pair)]

        def volume(j, acc):
            acc = list(acc)
            for w in range(nz // 8):
                at = slice(8 * w, 8 * w + 8)
                lo, hi, d = low[j, at], high[j, at], now[j, at]
                los, his = [lo * c for c in inverse], [hi * c for c in inverse]
                for i, c in enumerate(inverse):
                    acc[pair * FINE + i] = acc[pair * FINE + i] + d * c
                for f in range(FINE):
                    t = fine_s[f, j, at]
                    for i in range(pair):
                        acc[i * FINE + f] = acc[i * FINE + f] + jnp.minimum(jnp.maximum(t, los[i]), his[i])
            return tuple(acc)

        places = [(vol, 8 * (first * FINE + e)) for e in range(pair * FINE)]
        places += [(tgt, 8 * (first + i)) for i in range(pair)]
        if start is None:
            begin = tuple(jnp.zeros((8, nx), f32) for _ in places)
        else:
            begin = tuple((start[0] if ref is vol else start[1])[at : at + 8] for ref, at in places)
        acc = lax.fori_loop(0, n, volume, begin)
        for (ref, at), value in zip(places, acc):
            ref[at : at + 8] = value


def inner_kernel(flags, src_a, src_b, rim, dens, passive, solid, amp, low, high, vol, tgt, s_s, d_s, now_s, fine_s):
    ny, nz, nx = dens.shape
    half = ny // 2
    s_s[0:half] = src_a[...]
    s_s[half:ny] = src_b[...]

    def fix(y, _):
        put_rim(s_s, y, rim[y], nz)
        return 0

    lax.fori_loop(0, ny, fix, 0, unroll=4)

    def finish(j, p3):
        y = j + 2
        amp[j], low[j], high[j], now_s[j] = limits(p3, dens[y], passive[y] == 1, solid[y] == 1)

    filter_block(s_s, d_s, ny, (flags[2], flags[3]), None, finish, 2)
    table(ny - 4, nz, nx, amp, low, high, now_s, fine_s, vol, tgt, None)


def inner_call(flags, src_a, src_b, rim, dens, passive, solid):
    ny, nz, nx = dens.shape
    field = jax.ShapeDtypeStruct((ny - 4, nz, nx), f32)
    return pl.pallas_call(
        inner_kernel,
        in_specs=[SMEM] + [VMEM] * 6,
        out_shape=(
            field,
            field,
            field,
            jax.ShapeDtypeStruct((8 * POINTS, nx), f32),
            jax.ShapeDtypeStruct((8 * COARSE, nx), f32),
        ),
        scratch_shapes=[
            pltpu.VMEM((ny, nz + 2 * OFF, nx), f32),
            pltpu.VMEM((ny - 2, nz + 2 * OFF, nx), f32),
            pltpu.VMEM((ny - 4, nz, nx), f32),
            pltpu.VMEM((FINE, ny - 4, nz, nx), f32),
        ],
        compiler_params=pltpu.CompilerParams(vmem_limit_bytes=24 * 2**20),
        cost_estimate=estimate(9),
        name="filter_inner",
    )(flags, src_a, src_b, rim, dens, passive, solid)


def outer_kernel(
    flags, src_a, src_b, rim, got_even, got_odd, dens, passive, solid, vol_i, tgt_i,
    amp, low, high, excess, s_s, d_s, now_s, fine_s, vol, tgt,
):
    ny, nz, nx = dens.shape
    half = ny // 2
    odd = flags[4] == 1
    s_s[0, 0:2] = jnp.where(odd, got_even[...], got_odd[...])
    s_s[1, 4:6] = jnp.where(odd, got_odd[...], got_even[...])
    for j in range(4):
        s_s[0, 2 + j] = src_a[j]
        put_rim(s_s.at[0], 2 + j, rim[j], nz)
        s_s[1, j] = src_b[half - 4 + j]
        put_rim(s_s.at[1], j, rim[ny - 4 + j], nz)
    for b in range(2):
        y0 = 0 if b == 0 else ny - 2

        def finish(j, p3):
            y = y0 + j
            at = 2 * b + j
            amp[at], low[at], high[at], now_s[at] = limits(p3, dens[y], passive[y] == 1, solid[y] == 1)

        edges = (flags[0], 1) if b == 0 else (1, flags[1])
        filter_block(s_s.at[b], d_s.at[b], 6, (flags[2], flags[3]), edges, finish, True)
    table(4, nz, nx, amp, low, high, now_s, fine_s, vol, tgt, (vol_i, tgt_i))

    def lanes(ref, count):
        total = ref[pl.ds(0, count, stride=8), :]
        for s in range(1, 8):
            total = total + ref[pl.ds(s, count, stride=8), :]
        return total

    volumes, targets = lanes(vol, POINTS), lanes(tgt, COARSE)
    over = [volumes[FINE * i : FINE * i + FINE] - targets[i : i + 1] for i in range(COARSE)]
    excess[...] = jnp.sum(jnp.transpose(jnp.concatenate(over, axis=0)), axis=0, keepdims=True)


def outer_call(flags, src_a, src_b, rim, got_even, got_odd, dens, passive, solid, vol_i, tgt_i):
    ny, nz, nx = dens.shape
    rows = nz + 2 * OFF
    field = jax.ShapeDtypeStruct((4, nz, nx), f32)
    return pl.pallas_call(
        outer_kernel,
        in_specs=[SMEM] + [VMEM] * 10,
        out_shape=(field, field, field, jax.ShapeDtypeStruct((1, POINTS), f32)),
        scratch_shapes=[
            pltpu.VMEM((2, 6, rows, nx), f32),
            pltpu.VMEM((2, 4, rows, nx), f32),
            pltpu.VMEM((4, nz, nx), f32),
            pltpu.VMEM((FINE, 4, nz, nx), f32),
            pltpu.VMEM((8 * POINTS, nx), f32),
            pltpu.VMEM((8 * COARSE, nx), f32),
        ],
        compiler_params=pltpu.CompilerParams(vmem_limit_bytes=16 * 2**20),
        cost_estimate=estimate(3),
        name="filter_outer",
    )(flags, src_a, src_b, rim, got_even, got_odd, dens, passive, solid, vol_i, tgt_i)


def update_kernel(tables, amp_i, low_i, high_i, amp_o, low_o, high_o, new, logm):
    inner = amp_i.shape[0]
    nx = amp_i.shape[-1]
    total = jnp.sum(tables[...], axis=0, keepdims=True)
    lane = lax.broadcasted_iota(jnp.int32, total.shape, 1)
    above = jnp.where((total > 0.0) & (lane > 0), 1.0, 0.0)
    middle = -bracket_end + (2.0 * bracket_end / POINTS) * (jnp.sum(above) + 0.5)
    logm[0] = middle
    scale = jnp.exp(jnp.full((1, nx), -0.5 * middle, f32))

    def new_row(amp, low, high):
        return jnp.minimum(jnp.maximum(amp * scale, low), high)

    def body(j, _):
        new[j + 2] = new_row(amp_i[j], low_i[j], high_i[j])
        return 0

    lax.fori_loop(0, inner, body, 0)
    for j in range(4):
        new[j if j < 2 else inner + j] = new_row(amp_o[j], low_o[j], high_o[j])


def update_call(tables, inner, outer):
    n, nz, nx = inner[0].shape
    return pl.pallas_call(
        update_kernel,
        in_specs=[VMEM] * 7,
        out_specs=(VMEM, SMEM),
        out_shape=(jax.ShapeDtypeStruct((n + 4, nz, nx), f32), jax.ShapeDtypeStruct((1,), f32)),
        compiler_params=pltpu.CompilerParams(vmem_limit_bytes=8 * 2**20),
        cost_estimate=estimate(1),
        name="update",
    )(tables, *inner, *outer)


def to_lower(value, axis):
    count = lax.axis_size(axis)
    return lax.ppermute(value, axis, [(i + 1, i) for i in range(count - 1)])


def swap(value, axis, start):
    pairs = []
    for i in range(start, lax.axis_size(axis) - 1, 2):
        pairs += [(i, i + 1), (i + 1, i)]
    return lax.ppermute(value, axis, pairs)


def on_device(displacement, density, passive, solid, stiffness):
    ny, nz, nx = density.shape
    gy, gz = lax.axis_size("gy"), lax.axis_size("gz")
    iy, iz = lax.axis_index("gy"), lax.axis_index("gz")
    flags = jnp.stack([iy > 0, iy < gy - 1, iz > 0, iz < gz - 1, iy % 2 == 1, iz % 2 == 1]).astype(jnp.int32)

    disp_hbm = pltpu.with_memory_space_constraint(displacement, pltpu.HBM)
    dens_hbm = pltpu.with_memory_space_constraint(density, pltpu.HBM)
    stiff_hbm = pltpu.with_memory_space_constraint(stiffness, pltpu.HBM)

    face, disp, dens, mat = load_call(disp_hbm, dens_hbm, stiff_hbm)
    fy = to_lower(face, "gy")
    src_a, own_low, own_high = first_call(disp, dens, mat)

    rim_low = jnp.pad(fy[:, nz - 2 :].reshape(1, 18, nx), ((0, 0), (0, 12), (0, 0)))
    rim_high = jnp.pad(fy[:, :3].reshape(1, 27, nx), ((0, 0), (0, 3), (0, 0)))
    to_above = jnp.concatenate([own_low, rim_low])
    to_below = jnp.concatenate([own_high, rim_high])
    z_odd = iz % 2 == 1
    z_got_odd = swap(jnp.where(z_odd, to_above, to_below), "gz", 1)
    z_got_even = swap(jnp.where(z_odd, to_below, to_above), "gz", 0)
    src_b = last_call(disp, dens, fy, mat)
    rim, msg_even, msg_odd = rim_call(flags, z_got_even, z_got_odd, own_low, own_high, fy, mat, src_a, src_b)

    got_odd = swap(msg_odd, "gy", 1)
    got_even = swap(msg_even, "gy", 0)
    *inner, vol, tgt = inner_call(flags, src_a, src_b, rim, dens, passive, solid)
    *outer, excess = outer_call(flags, src_a, src_b, rim, got_even, got_odd, dens, passive, solid, vol, tgt)

    everyone = jnp.broadcast_to(excess, (gz * gy, POINTS))
    tables = lax.all_to_all(everyone, ("gz", "gy"), 0, 0, tiled=True)
    new, logm = update_call(tables, inner, outer)
    return new, logm.reshape(())


def solution(mesh):
    placed = (
        P(None, "gy", "gz", None),
        P("gy", "gz", None),
        P("gy", "gz", None),
        P("gy", "gz", None),
        P(),
    )
    return jax.shard_map(
        on_device, mesh=mesh, in_specs=placed, out_specs=(P("gy", "gz", None), P()), check_vma=False
    )
```

```python
import math

import jax
import jax.numpy as jnp
from jax import lax
from jax.experimental import pallas as pl
from jax.experimental.pallas import tpu as pltpu
from jax.sharding import PartitionSpec as P

ITERS = 8
POINTS = 2**ITERS
OFF = 8

smoothing = 0.52
move_limit = 0.2
floor_density = 0.001
bracket_end = 12.0

f32 = jnp.float32
bf16 = jnp.bfloat16
VMEM = pl.BlockSpec(memory_space=pltpu.VMEM)
SMEM = pl.BlockSpec(memory_space=pltpu.SMEM)
HBM = pl.BlockSpec(memory_space=pltpu.HBM)


def cheb_weights():
    spectrum_top = 1.0 + 12.0 * smoothing
    centre_value = (spectrum_top + 1.0) / 2.0
    half_width = (spectrum_top - 1.0) / 2.0
    ratio_value = centre_value / half_width
    first_rho = 1.0 / ratio_value
    second_rho = 1.0 / (2.0 * ratio_value - first_rho)
    third_rho = 1.0 / (2.0 * ratio_value - second_rho)
    return (
        centre_value,
        second_rho * first_rho,
        2.0 * second_rho / half_width,
        third_rho * second_rho,
        2.0 * third_rho / half_width,
    )


def filter_weights():
    t, w1, w2, w3, w4 = cheb_weights()
    diag = 1.0 + 6.0 * smoothing
    alpha = w1 / t + w2 * (1.0 - diag / t)
    beta = w2 * smoothing / t
    gamma = 1.0 / t - w4 * w1 / (t * w2)
    delta = 1.0 + w3 + w4 / w2 - w4 * diag
    eps = w4 * smoothing
    return alpha, beta, gamma, delta, eps


def lane_up(v):
    n = v.shape[-1]
    lane = lax.broadcasted_iota(jnp.int32, v.shape, v.ndim - 1)
    return jnp.where(lane < n - 1, pltpu.roll(v, n - 1, v.ndim - 1), 0.0)


def lane_down(v):
    n = v.shape[-1]
    lane = lax.broadcasted_iota(jnp.int32, v.shape, v.ndim - 1)
    return jnp.where(lane > 0, pltpu.roll(v, 1, v.ndim - 1), 0.0)


def estimate(us):
    return pl.CostEstimate(flops=int(us * 1e9), bytes_accessed=1 << 20, transcendentals=0)


def build_matrix(k, mat, plane, band):
    shape = (24, 112)
    col = lax.broadcasted_iota(jnp.int32, shape, 1)
    row = lax.broadcasted_iota(jnp.int32, shape, 0)
    main = col < 96
    q = jnp.where(main, jnp.where(col >= 48, 1, 0), jnp.where(col >= 104, 1, 0))
    m = col - 48 * q
    e = col - 96 - 8 * q
    c = jnp.where(main, m >> 4, e >> 1)
    dx = jnp.where(main, (m >> 3) & 1, e & 1)
    valid = main | (e < 6)
    dof0 = 3 * (plane * q + dx) + c
    pick0 = jnp.where(main & (row == dof0), 1.0, 0.0)
    pick1 = jnp.where(valid & (row == dof0 + 3 * band), 1.0, 0.0)
    hp = lax.Precision.HIGHEST
    k0 = jnp.dot(k, pick0, precision=hp, preferred_element_type=f32)
    k1 = jnp.dot(k, pick1, precision=hp, preferred_element_type=f32)
    col8 = lax.broadcasted_iota(jnp.int32, (8, 112), 1)
    row8 = lax.broadcasted_iota(jnp.int32, (8, 112), 0)
    main8 = col8 < 96
    rc = col8 & 7
    m0 = main8 & (rc == row8)
    m1 = jnp.where(main8, rc, 8) == row8 + 1
    rows = []
    for b in range(2):
        for q_ in range(2):
            for c_ in range(3):
                for dx_ in range(2):
                    r = 3 * (plane * q_ + band * b + dx_) + c_
                    rows.append(jnp.where(m0, k0[r : r + 1], 0.0) + jnp.where(m1, k1[r : r + 1], 0.0))
    full = jnp.concatenate(rows, axis=0)
    hi = full.astype(bf16)
    lo = (full - hi.astype(f32)).astype(bf16)
    mat[:, 0:112] = hi
    mat[:, 112:224] = lo


def prepare(segments, p, work):
    main_s, ext_s, mul_s = work
    for l in range(3):
        for c in range(3):
            w0 = 0
            for u, x in segments(3 * l + c):
                size, nx = u.shape
                n = size // 8
                last = lax.broadcasted_iota(jnp.int32, u.shape, 0) == size - 1
                both = (u, lane_up(u))
                after = (None, None) if x is None else (x, lane_up(x))
                for w in range(n):
                    sl = slice(8 * w, 8 * w + 8)
                    main_s[p, l, 16 * c : 16 * c + 16, (w0 + w) * nx : (w0 + w + 1) * nx] = jnp.concatenate(
                        [both[0][sl], both[1][sl]], axis=0
                    ).astype(bf16)
                for dx in range(2):
                    v, vx = both[dx], after[dx]
                    k = 2 * c + dx
                    for w in range(n):
                        nxt = v[8 * w + 8 : 8 * w + 9] if w < n - 1 else vx
                        if nxt is not None:
                            ext_s[p, l, k : k + 1, (w0 + w) * nx : (w0 + w + 1) * nx] = nxt
                    m = 2.0 * v - v.astype(bf16).astype(f32)
                    mx = 0.0 if vx is None else jnp.broadcast_to(2.0 * vx - vx.astype(bf16).astype(f32), v.shape)
                    at = slice(8 * w0, 8 * (w0 + n))
                    mul_s[p, l, k, 0, at] = m
                    mul_s[p, l, k, 1, at] = jnp.where(last, mx, pltpu.roll(m, size - 1, 0))
                w0 += n


def energy_rows(p, mat, work, density):
    main_s, ext_s, mul_s = work
    rows, nx = density.shape
    count = rows // 8
    acc = [None] * count
    for l in range(3):
        ext = jnp.concatenate([ext_s[p, l], ext_s[p + 1, l]], axis=0).astype(bf16)
        one = jnp.concatenate([main_s[p, l], main_s[p + 1, l], ext], axis=0)
        force = jnp.dot(mat[...], jnp.concatenate([one, one], axis=0), preferred_element_type=f32)
        i = 0
        for b in range(2):
            for q in range(2):
                for k in range(6):
                    for w in range(count):
                        at = slice(8 * w, 8 * w + 8)
                        term = force[8 * i : 8 * i + 8, w * nx : (w + 1) * nx] * mul_s[p + q, l, k, b, at]
                        acc[w] = term if acc[w] is None else acc[w] + term
                    i += 1
    return density * (-3.0 * density * density * jnp.concatenate(acc, axis=0))


def workspace(planes, windows, nx):
    return [
        pltpu.VMEM((planes, 3, 48, windows * nx), bf16),
        pltpu.VMEM((planes, 3, 8, windows * nx), f32),
        pltpu.VMEM((planes, 3, 6, 2, 8 * windows, nx), f32),
    ]


def sweep(rows, segments, put, work):
    work[1][...] = jnp.zeros_like(work[1])
    for p in range(2):
        prepare(segments(p), p, work)

    def body(y, _):
        put(y)
        prepare(segments(y + 2), y + 2, work)
        return 0

    lax.fori_loop(0, rows - 1, body, 0, unroll=2)
    put(rows - 1)


def load_kernel(disp, dens, stiff, disp_v, dens_v, mat, mat_y, stiff_s, sems):
    copies = [
        pltpu.make_async_copy(stiff, stiff_s, sems.at[0]),
        pltpu.make_async_copy(disp, disp_v, sems.at[1]),
        pltpu.make_async_copy(dens, dens_v, sems.at[2]),
    ]
    for copy in copies:
        copy.start()
    copies[0].wait()
    build_matrix(stiff_s[...], mat, 4, 2)
    build_matrix(stiff_s[...], mat_y, 2, 4)
    for copy in copies[1:]:
        copy.wait()


def load_call(disp, dens, stiff):
    matrix = jax.ShapeDtypeStruct((192, 224), bf16)
    return pl.pallas_call(
        load_kernel,
        in_specs=[HBM, HBM, HBM],
        out_shape=(
            jax.ShapeDtypeStruct(disp.shape, f32),
            jax.ShapeDtypeStruct(dens.shape, f32),
            matrix,
            matrix,
        ),
        scratch_shapes=[pltpu.VMEM((24, 24), f32), pltpu.SemaphoreType.DMA((3,))],
        compiler_params=pltpu.CompilerParams(vmem_limit_bytes=16 * 2**20),
        cost_estimate=estimate(2),
        name="load",
    )(disp, dens, stiff)


def ends_kernel(disp, dens, mat, ends, up, down, *work):
    _, ny, nz, nx = disp.shape

    def segments(p):
        return lambda i: [(disp[i, p, 0:8], disp[i, p, 8:9]), (disp[i, p, nz - 8 : nz], None)]

    def put(y):
        d = jnp.concatenate([dens[y, 0:8], dens[y, nz - 8 : nz]], axis=0)
        ends[y] = energy_rows(y, mat, work, d)

    sweep(ny - 1, segments, put, work)
    for y in range(ny):
        row = slice(y, y + 1)
        for i in range(9):
            up[i, row] = disp[i, y, nz - 1 : nz]
            down[i, row] = disp[i, y, 0:1]
        up[9, row] = dens[y, nz - 1 : nz]
        if y < ny - 1:
            up[10, row] = ends[y, 14:15]
            down[9, row] = ends[y, 0:1]
            down[10, row] = ends[y, 1:2]
    up[11] = jnp.zeros((ny, nx), f32)
    down[11] = jnp.zeros((ny, nx), f32)


def ends_call(disp, dens, mat):
    _, ny, nz, nx = disp.shape
    message = jax.ShapeDtypeStruct((12, ny, nx), f32)
    return pl.pallas_call(
        ends_kernel,
        in_specs=[VMEM] * 3,
        out_shape=(jax.ShapeDtypeStruct((ny, 16, nx), f32), message, message),
        scratch_shapes=workspace(ny, 2, nx),
        compiler_params=pltpu.CompilerParams(vmem_limit_bytes=16 * 2**20),
        cost_estimate=estimate(4),
        name="energy_ends",
    )(disp, dens, mat)


def top_kernel(flags, disp, dens, fy, mat, ends, up, down, top, up_full, down_full, msg_even, msg_odd, *work):
    _, ny, nz, nx = disp.shape
    work[1][...] = jnp.zeros_like(work[1])
    prepare(lambda i: [(disp[i, ny - 1], None)], 0, work)
    prepare(lambda i: [(fy[i], None)], 1, work)
    up_full[...] = up[...]
    down_full[...] = down[...]
    for i in range(9):
        up_full[11, i : i + 1] = fy[i, nz - 1 : nz]
        down_full[11, i : i + 1] = fy[i, 0:1]
    s = energy_rows(0, mat, work, dens[ny - 1])
    top[...] = s
    up_full[10, ny - 1 : ny] = s[nz - 2 : nz - 1]
    down_full[9, ny - 1 : ny] = s[0:1]
    down_full[10, ny - 1 : ny] = s[1:2]
    odd = flags[5] == 1
    msg_even[...] = jnp.where(odd, down_full[...], up_full[...])
    msg_odd[...] = jnp.where(odd, up_full[...], down_full[...])


def top_call(flags, disp, dens, fy, mat, ends, up, down):
    _, ny, nz, nx = disp.shape
    message = jax.ShapeDtypeStruct((12, ny, nx), f32)
    return pl.pallas_call(
        top_kernel,
        in_specs=[SMEM] + [VMEM] * 7,
        out_shape=(jax.ShapeDtypeStruct((nz, nx), f32),) + (message,) * 4,
        scratch_shapes=workspace(2, nz // 8, nx),
        compiler_params=pltpu.CompilerParams(vmem_limit_bytes=16 * 2**20),
        cost_estimate=estimate(1),
        name="energy_top",
    )(flags, disp, dens, fy, mat, ends, up, down)


def middle_kernel(disp, dens, mat, ends, top, src, *work):
    _, ny, nz, nx = disp.shape

    def segments(p):
        return lambda i: [(disp[i, p, 8 : nz - 8], disp[i, p, nz - 8 : nz - 7])]

    def frame(y):
        src[y, 0:OFF] = jnp.zeros((OFF, nx), f32)
        src[y, OFF + nz :] = jnp.zeros((src.shape[1] - OFF - nz, nx), f32)

    def put(y):
        frame(y)
        src[y, OFF : OFF + 8] = ends[y, 0:8]
        src[y, OFF + 8 : OFF + nz - 8] = energy_rows(y, mat, work, dens[y, 8 : nz - 8])
        src[y, OFF + nz - 8 : OFF + nz] = ends[y, 8:16]

    sweep(ny - 1, segments, put, work)
    frame(ny - 1)
    src[ny - 1, OFF : OFF + nz] = top[...]


def middle_call(disp, dens, mat, ends, top):
    _, ny, nz, nx = disp.shape
    return pl.pallas_call(
        middle_kernel,
        in_specs=[VMEM] * 5,
        out_shape=jax.ShapeDtypeStruct((ny, nz + 2 * OFF, nx), f32),
        scratch_shapes=workspace(ny, nz // 8 - 2, nx),
        compiler_params=pltpu.CompilerParams(vmem_limit_bytes=24 * 2**20),
        cost_estimate=estimate(4),
        name="energy_middle",
    )(disp, dens, mat, ends, top)


def rim_kernel(flags, got_even, got_odd, up, down, mat_y, src, rim, msg_even, msg_odd, low_s, high_s, t_s, *work):
    ny, rows, nx = src.shape
    nz = rows - 2 * OFF
    odd = flags[5] == 1
    low_s[...] = jnp.where(odd, got_even[...], got_odd[...])
    high_s[...] = jnp.where(odd, got_odd[...], got_even[...])
    work[1][...] = jnp.zeros_like(work[1])
    prepare(lambda i: [(low_s[i], low_s[11, i : i + 1]), (up[i], up[11, i : i + 1])], 0, work)
    prepare(lambda i: [(down[i], down[11, i : i + 1]), (high_s[i], high_s[11, i : i + 1])], 1, work)
    s = energy_rows(0, mat_y, work, jnp.concatenate([low_s[9], up[9]], axis=0))
    columns = (low_s[10], s[0:ny], s[ny : 2 * ny], high_s[9], high_s[10])
    for y in range(ny):
        for r, column in enumerate(columns):
            rim[y, r : r + 1] = column[y : y + 1]
        rim[y, 5:8] = jnp.zeros((3, nx), f32)
    for j in range(4):
        y = j if j < 2 else ny - 4 + j
        t_s[j] = src[y]
        put_rim(t_s, j, rim[y], nz)
    odd = flags[4] == 1
    msg_even[...] = jnp.where(odd, t_s[0:2], t_s[2:4])
    msg_odd[...] = jnp.where(odd, t_s[2:4], t_s[0:2])


def put_rim(s, y, rim, nz):
    s[y, OFF - 2 : OFF] = rim[0:2]
    s[y, OFF + nz - 1 : OFF + nz + 2] = rim[2:5]


def rim_call(flags, got_even, got_odd, up, down, mat_y, src):
    ny, rows, nx = src.shape
    return pl.pallas_call(
        rim_kernel,
        in_specs=[SMEM] + [VMEM] * 6,
        out_shape=(
            jax.ShapeDtypeStruct((ny, 8, nx), f32),
            jax.ShapeDtypeStruct((2, rows, nx), f32),
            jax.ShapeDtypeStruct((2, rows, nx), f32),
        ),
        scratch_shapes=[
            pltpu.VMEM((12, ny, nx), f32),
            pltpu.VMEM((12, ny, nx), f32),
            pltpu.VMEM((4, rows, nx), f32),
        ]
        + workspace(2, 2 * (ny // 8), nx),
        compiler_params=pltpu.CompilerParams(vmem_limit_bytes=16 * 2**20),
        cost_estimate=estimate(2),
        name="energy_rim",
    )(flags, got_even, got_odd, up, down, mat_y, src)


def filter_block(s_s, d_s, n, z_edges, y_edges, finish, unroll):
    rows, nx = s_s.shape[1:]
    nz = rows - 2 * OFF
    alpha, beta, gamma, delta, eps = filter_weights()
    row = lax.broadcasted_iota(jnp.int32, (rows, nx), 0)
    keep = jnp.where(row < OFF, z_edges[0], jnp.where(row >= OFF + nz, z_edges[1], 1)) == 1

    def beside(v):
        return pltpu.roll(v, 1, 0) + pltpu.roll(v, rows - 1, 0) + lane_up(v) + lane_down(v)

    def second(j, _):
        c = s_s[j + 1]
        d2 = alpha * c + beta * (beside(c) + s_s[j] + s_s[j + 2])
        ok = keep
        if y_edges is not None:
            ok = keep & (jnp.where(j == 0, y_edges[0], jnp.where(j == n - 3, y_edges[1], 1)) == 1)
        d_s[j] = jnp.where(ok, d2, 0.0)
        return 0

    def third(j, _):
        d2 = d_s[j + 1]
        p3 = gamma * s_s[j + 2] + delta * d2 + eps * (beside(d2) + d_s[j] + d_s[j + 2])
        finish(j, p3[OFF : OFF + nz])
        return 0

    lax.fori_loop(0, n - 2, second, 0, unroll=unroll)
    lax.fori_loop(0, n - 4, third, 0, unroll=unroll)


def limits(p3, d, pas, sol):
    amp = jnp.sqrt(jnp.maximum(-p3 * d, 0.0))
    lower = jnp.maximum(d - move_limit, floor_density)
    upper = jnp.minimum(d + move_limit, 1.0)
    low, high, now = (jnp.where(sol, 1.0, jnp.where(pas, floor_density, v)) for v in (lower, upper, d))
    return amp, low, high, now


FINE = 16
COARSE = POINTS // FINE


def table(n, nz, nx, amp, low, high, now, fine_s, vol, tgt, start):
    spacing = 2.0 * bracket_end / POINTS

    def fine(j, _):
        a = amp[j]
        for f in range(FINE):
            fine_s[f, j] = a * math.exp(-0.5 * spacing * f)
        return 0

    lax.fori_loop(0, n, fine, 0)
    pair = 2
    for first in range(0, COARSE, pair):
        inverse = [math.exp(0.5 * (-bracket_end + spacing * FINE * i)) for i in range(first, first + pair)]

        def volume(j, acc):
            acc = list(acc)
            for w in range(nz // 8):
                at = slice(8 * w, 8 * w + 8)
                lo, hi, d = low[j, at], high[j, at], now[j, at]
                los, his = [lo * c for c in inverse], [hi * c for c in inverse]
                for i, c in enumerate(inverse):
                    acc[pair * FINE + i] = acc[pair * FINE + i] + d * c
                for f in range(FINE):
                    t = fine_s[f, j, at]
                    for i in range(pair):
                        acc[i * FINE + f] = acc[i * FINE + f] + jnp.minimum(jnp.maximum(t, los[i]), his[i])
            return tuple(acc)

        places = [(vol, 8 * (first * FINE + e)) for e in range(pair * FINE)]
        places += [(tgt, 8 * (first + i)) for i in range(pair)]
        if start is None:
            begin = tuple(jnp.zeros((8, nx), f32) for _ in places)
        else:
            begin = tuple((start[0] if ref is vol else start[1])[at : at + 8] for ref, at in places)
        acc = lax.fori_loop(0, n, volume, begin, unroll=2)
        for (ref, at), value in zip(places, acc):
            ref[at : at + 8] = value


def inner_kernel(flags, src, rim, dens, passive, solid, amp, low, high, vol, tgt, s_s, d_s, now_s, fine_s):
    ny, nz, nx = dens.shape
    s_s[...] = src[...]

    def fix(y, _):
        put_rim(s_s, y, rim[y], nz)
        return 0

    lax.fori_loop(0, ny, fix, 0, unroll=4)

    def finish(j, p3):
        y = j + 2
        amp[j], low[j], high[j], now_s[j] = limits(p3, dens[y], passive[y] == 1, solid[y] == 1)

    filter_block(s_s, d_s, ny, (flags[2], flags[3]), None, finish, 4)
    table(ny - 4, nz, nx, amp, low, high, now_s, fine_s, vol, tgt, None)


def inner_call(flags, src, rim, dens, passive, solid):
    ny, nz, nx = dens.shape
    field = jax.ShapeDtypeStruct((ny - 4, nz, nx), f32)
    return pl.pallas_call(
        inner_kernel,
        in_specs=[SMEM] + [VMEM] * 5,
        out_shape=(
            field,
            field,
            field,
            jax.ShapeDtypeStruct((8 * POINTS, nx), f32),
            jax.ShapeDtypeStruct((8 * COARSE, nx), f32),
        ),
        scratch_shapes=[
            pltpu.VMEM((ny, nz + 2 * OFF, nx), f32),
            pltpu.VMEM((ny - 2, nz + 2 * OFF, nx), f32),
            pltpu.VMEM((ny - 4, nz, nx), f32),
            pltpu.VMEM((FINE, ny - 4, nz, nx), f32),
        ],
        compiler_params=pltpu.CompilerParams(vmem_limit_bytes=24 * 2**20),
        cost_estimate=estimate(9),
        name="filter_inner",
    )(flags, src, rim, dens, passive, solid)


def outer_kernel(
    flags, src, rim, got_even, got_odd, dens, passive, solid, vol_i, tgt_i,
    amp, low, high, excess, s_s, d_s, now_s, fine_s, vol, tgt,
):
    ny, nz, nx = dens.shape
    odd = flags[4] == 1
    s_s[0, 0:2] = jnp.where(odd, got_even[...], got_odd[...])
    s_s[1, 4:6] = jnp.where(odd, got_odd[...], got_even[...])
    for j in range(4):
        s_s[0, 2 + j] = src[j]
        put_rim(s_s.at[0], 2 + j, rim[j], nz)
        s_s[1, j] = src[ny - 4 + j]
        put_rim(s_s.at[1], j, rim[ny - 4 + j], nz)
    for b in range(2):
        y0 = 0 if b == 0 else ny - 2

        def finish(j, p3):
            y = y0 + j
            at = 2 * b + j
            amp[at], low[at], high[at], now_s[at] = limits(p3, dens[y], passive[y] == 1, solid[y] == 1)

        edges = (flags[0], 1) if b == 0 else (1, flags[1])
        filter_block(s_s.at[b], d_s.at[b], 6, (flags[2], flags[3]), edges, finish, True)
    table(4, nz, nx, amp, low, high, now_s, fine_s, vol, tgt, (vol_i, tgt_i))

    def lanes(ref, count):
        total = ref[pl.ds(0, count, stride=8), :]
        for s in range(1, 8):
            total = total + ref[pl.ds(s, count, stride=8), :]
        return total

    volumes, targets = lanes(vol, POINTS), lanes(tgt, COARSE)
    over = [volumes[FINE * i : FINE * i + FINE] - targets[i : i + 1] for i in range(COARSE)]
    excess[...] = jnp.sum(jnp.transpose(jnp.concatenate(over, axis=0)), axis=0, keepdims=True)


def outer_call(flags, src, rim, got_even, got_odd, dens, passive, solid, vol_i, tgt_i):
    ny, nz, nx = dens.shape
    rows = nz + 2 * OFF
    field = jax.ShapeDtypeStruct((4, nz, nx), f32)
    return pl.pallas_call(
        outer_kernel,
        in_specs=[SMEM] + [VMEM] * 9,
        out_shape=(field, field, field, jax.ShapeDtypeStruct((1, POINTS), f32)),
        scratch_shapes=[
            pltpu.VMEM((2, 6, rows, nx), f32),
            pltpu.VMEM((2, 4, rows, nx), f32),
            pltpu.VMEM((4, nz, nx), f32),
            pltpu.VMEM((FINE, 4, nz, nx), f32),
            pltpu.VMEM((8 * POINTS, nx), f32),
            pltpu.VMEM((8 * COARSE, nx), f32),
        ],
        compiler_params=pltpu.CompilerParams(vmem_limit_bytes=16 * 2**20),
        cost_estimate=estimate(3),
        name="filter_outer",
    )(flags, src, rim, got_even, got_odd, dens, passive, solid, vol_i, tgt_i)


def update_kernel(tables, amp_i, low_i, high_i, amp_o, low_o, high_o, new, logm):
    inner = amp_i.shape[0]
    nx = amp_i.shape[-1]
    total = jnp.sum(tables[...], axis=0, keepdims=True)
    lane = lax.broadcasted_iota(jnp.int32, total.shape, 1)
    above = jnp.where((total > 0.0) & (lane > 0), 1.0, 0.0)
    middle = -bracket_end + (2.0 * bracket_end / POINTS) * (jnp.sum(above) + 0.5)
    logm[0] = middle
    scale = jnp.exp(jnp.full((1, nx), -0.5 * middle, f32))

    def new_row(amp, low, high):
        return jnp.minimum(jnp.maximum(amp * scale, low), high)

    def body(j, _):
        new[j + 2] = new_row(amp_i[j], low_i[j], high_i[j])
        return 0

    lax.fori_loop(0, inner, body, 0)
    for j in range(4):
        new[j if j < 2 else inner + j] = new_row(amp_o[j], low_o[j], high_o[j])


def update_call(tables, inner, outer):
    n, nz, nx = inner[0].shape
    return pl.pallas_call(
        update_kernel,
        in_specs=[VMEM] * 7,
        out_specs=(VMEM, SMEM),
        out_shape=(jax.ShapeDtypeStruct((n + 4, nz, nx), f32), jax.ShapeDtypeStruct((1,), f32)),
        compiler_params=pltpu.CompilerParams(vmem_limit_bytes=8 * 2**20),
        cost_estimate=estimate(1),
        name="update",
    )(tables, *inner, *outer)


def to_lower(value, axis):
    count = lax.axis_size(axis)
    return lax.ppermute(value, axis, [(i + 1, i) for i in range(count - 1)])


def swap(value, axis, start):
    pairs = []
    for i in range(start, lax.axis_size(axis) - 1, 2):
        pairs += [(i, i + 1), (i + 1, i)]
    return lax.ppermute(value, axis, pairs)


def on_device(displacement, density, passive, solid, stiffness):
    ny, nz, nx = density.shape
    gy, gz = lax.axis_size("gy"), lax.axis_size("gz")
    iy, iz = lax.axis_index("gy"), lax.axis_index("gz")
    flags = jnp.stack([iy > 0, iy < gy - 1, iz > 0, iz < gz - 1, iy % 2 == 1, iz % 2 == 1]).astype(jnp.int32)

    disp_hbm = pltpu.with_memory_space_constraint(displacement, pltpu.HBM)
    dens_hbm = pltpu.with_memory_space_constraint(density, pltpu.HBM)
    stiff_hbm = pltpu.with_memory_space_constraint(stiffness, pltpu.HBM)

    fy = to_lower(displacement[:, 0], "gy")
    disp, dens, mat, mat_y = load_call(disp_hbm, dens_hbm, stiff_hbm)
    ends, up, down = ends_call(disp, dens, mat)
    top, up, down, z_even, z_odd = top_call(flags, disp, dens, fy, mat, ends, up, down)

    z_got_odd = swap(z_odd, "gz", 1)
    z_got_even = swap(z_even, "gz", 0)
    src = middle_call(disp, dens, mat, ends, top)
    rim, msg_even, msg_odd = rim_call(flags, z_got_even, z_got_odd, up, down, mat_y, src)

    got_odd = swap(msg_odd, "gy", 1)
    got_even = swap(msg_even, "gy", 0)
    *inner, vol, tgt = inner_call(flags, src, rim, dens, passive, solid)
    *outer, excess = outer_call(flags, src, rim, got_even, got_odd, dens, passive, solid, vol, tgt)

    everyone = jnp.broadcast_to(excess, (gz * gy, POINTS))
    tables = lax.all_to_all(everyone, ("gz", "gy"), 0, 0, tiled=True)
    new, logm = update_call(tables, inner, outer)
    return new, logm.reshape(())


def solution(mesh):
    placed = (
        P(None, "gy", "gz", None),
        P("gy", "gz", None),
        P("gy", "gz", None),
        P("gy", "gz", None),
        P(),
    )
    return jax.shard_map(
        on_device, mesh=mesh, in_specs=placed, out_specs=(P("gy", "gz", None), P()), check_vma=False
    )
```

```python
import math

import jax
import jax.numpy as jnp
from jax import lax
from jax.experimental import pallas as pl
from jax.experimental.pallas import tpu as pltpu
from jax.sharding import PartitionSpec as P

ITERS = 8
POINTS = 2**ITERS
OFF = 8

smoothing = 0.52
move_limit = 0.2
floor_density = 0.001
bracket_end = 12.0

f32 = jnp.float32
bf16 = jnp.bfloat16
VMEM = pl.BlockSpec(memory_space=pltpu.VMEM)
SMEM = pl.BlockSpec(memory_space=pltpu.SMEM)
HBM = pl.BlockSpec(memory_space=pltpu.HBM)


def cheb_weights():
    spectrum_top = 1.0 + 12.0 * smoothing
    centre_value = (spectrum_top + 1.0) / 2.0
    half_width = (spectrum_top - 1.0) / 2.0
    ratio_value = centre_value / half_width
    first_rho = 1.0 / ratio_value
    second_rho = 1.0 / (2.0 * ratio_value - first_rho)
    third_rho = 1.0 / (2.0 * ratio_value - second_rho)
    return (
        centre_value,
        second_rho * first_rho,
        2.0 * second_rho / half_width,
        third_rho * second_rho,
        2.0 * third_rho / half_width,
    )


def filter_weights():
    t, w1, w2, w3, w4 = cheb_weights()
    diag = 1.0 + 6.0 * smoothing
    alpha = w1 / t + w2 * (1.0 - diag / t)
    beta = w2 * smoothing / t
    gamma = 1.0 / t - w4 * w1 / (t * w2)
    delta = 1.0 + w3 + w4 / w2 - w4 * diag
    eps = w4 * smoothing
    return alpha, beta, gamma, delta, eps


def lane_up(v):
    n = v.shape[-1]
    lane = lax.broadcasted_iota(jnp.int32, v.shape, v.ndim - 1)
    return jnp.where(lane < n - 1, pltpu.roll(v, n - 1, v.ndim - 1), 0.0)


def lane_down(v):
    n = v.shape[-1]
    lane = lax.broadcasted_iota(jnp.int32, v.shape, v.ndim - 1)
    return jnp.where(lane > 0, pltpu.roll(v, 1, v.ndim - 1), 0.0)


def estimate(us):
    return pl.CostEstimate(flops=int(us * 1e9), bytes_accessed=1 << 20, transcendentals=0)


def build_matrices(k, mats):
    shape = (24, 128)
    col = lax.broadcasted_iota(jnp.int32, shape, 1)
    row = lax.broadcasted_iota(jnp.int32, shape, 0)
    main = col < 96
    q = jnp.where(main, jnp.where(col >= 48, 1, 0), jnp.where(col >= 104, 1, 0))
    m = col - 48 * q
    e = col - 96 - 8 * q
    c = jnp.where(main, m >> 4, e >> 1)
    dx = jnp.where(main, (m >> 3) & 1, e & 1)
    valid = main | (e < 6)
    picks = []
    for _, plane, band in mats:
        dof0 = 3 * (plane * q + dx) + c
        picks.append(jnp.where(main & (row == dof0), 1.0, 0.0))
        picks.append(jnp.where(valid & (row == dof0 + 3 * band), 1.0, 0.0))
    picked = jnp.dot(
        k, jnp.concatenate(picks, axis=1), precision=lax.Precision.HIGHEST, preferred_element_type=f32
    )
    col8 = lax.broadcasted_iota(jnp.int32, (8, 128), 1)
    row8 = lax.broadcasted_iota(jnp.int32, (8, 128), 0)
    main8 = col8 < 96
    rc = col8 & 7
    m0 = main8 & (rc == row8)
    m1 = jnp.where(main8, rc, 8) == row8 + 1
    for n, (mat, plane, band) in enumerate(mats):
        k0 = picked[:, 256 * n : 256 * n + 128]
        k1 = picked[:, 256 * n + 128 : 256 * n + 256]
        rows = []
        for b in range(2):
            for q_ in range(2):
                for c_ in range(3):
                    for dx_ in range(2):
                        r = 3 * (plane * q_ + band * b + dx_) + c_
                        rows.append(jnp.where(m0, k0[r : r + 1], 0.0) + jnp.where(m1, k1[r : r + 1], 0.0))
        full = jnp.concatenate(rows, axis=0)
        hi = full.astype(bf16)
        lo = (full - hi.astype(f32)).astype(bf16)
        mat[:, 0:112] = hi[:, 0:112]
        mat[:, 112:224] = lo[:, 0:112]


def prepare(segments, p, work):
    main_s, ext_s, mul_s = work
    for l in range(3):
        for c in range(3):
            w0 = 0
            for u, x in segments(3 * l + c):
                size, nx = u.shape
                n = size // 8
                last = lax.broadcasted_iota(jnp.int32, u.shape, 0) == size - 1
                both = (u, lane_up(u))
                after = (None, None) if x is None else (x, lane_up(x))
                for w in range(n):
                    sl = slice(8 * w, 8 * w + 8)
                    main_s[p, l, 16 * c : 16 * c + 16, (w0 + w) * nx : (w0 + w + 1) * nx] = jnp.concatenate(
                        [both[0][sl], both[1][sl]], axis=0
                    ).astype(bf16)
                for dx in range(2):
                    v, vx = both[dx], after[dx]
                    k = 2 * c + dx
                    for w in range(n):
                        nxt = v[8 * w + 8 : 8 * w + 9] if w < n - 1 else vx
                        if nxt is not None:
                            ext_s[p, l, k : k + 1, (w0 + w) * nx : (w0 + w + 1) * nx] = nxt
                    m = 2.0 * v - v.astype(bf16).astype(f32)
                    mx = 0.0 if vx is None else jnp.broadcast_to(2.0 * vx - vx.astype(bf16).astype(f32), v.shape)
                    at = slice(8 * w0, 8 * (w0 + n))
                    mul_s[p, l, k, 0, at] = m
                    mul_s[p, l, k, 1, at] = jnp.where(last, mx, pltpu.roll(m, size - 1, 0))
                w0 += n


def energy_rows(p, mat, work, density):
    main_s, ext_s, mul_s = work
    rows, nx = density.shape
    count = rows // 8
    acc = [None] * count
    for l in range(3):
        ext = jnp.concatenate([ext_s[p, l], ext_s[p + 1, l]], axis=0).astype(bf16)
        one = jnp.concatenate([main_s[p, l], main_s[p + 1, l], ext], axis=0)
        force = jnp.dot(mat[...], jnp.concatenate([one, one], axis=0), preferred_element_type=f32)
        i = 0
        for b in range(2):
            for q in range(2):
                for k in range(6):
                    for w in range(count):
                        at = slice(8 * w, 8 * w + 8)
                        term = force[8 * i : 8 * i + 8, w * nx : (w + 1) * nx] * mul_s[p + q, l, k, b, at]
                        acc[w] = term if acc[w] is None else acc[w] + term
                    i += 1
    return density * (-3.0 * density * density * jnp.concatenate(acc, axis=0))


def workspace(planes, windows, nx):
    return [
        pltpu.VMEM((planes, 3, 48, windows * nx), bf16),
        pltpu.VMEM((planes, 3, 8, windows * nx), f32),
        pltpu.VMEM((planes, 3, 6, 2, 8 * windows, nx), f32),
    ]


def sweep(rows, segments, put, work):
    work[1][...] = jnp.zeros_like(work[1])
    for p in range(2):
        prepare(segments(p), p, work)

    def body(y, _):
        put(y)
        prepare(segments(y + 2), y + 2, work)
        return 0

    lax.fori_loop(0, rows - 1, body, 0, unroll=2)
    put(rows - 1)


def load_kernel(disp, dens, stiff, disp_v, dens_v, mat, mat_y, stiff_s, sems):
    copies = [
        pltpu.make_async_copy(stiff, stiff_s, sems.at[0]),
        pltpu.make_async_copy(disp, disp_v, sems.at[1]),
        pltpu.make_async_copy(dens, dens_v, sems.at[2]),
    ]
    for copy in copies:
        copy.start()
    copies[0].wait()
    build_matrices(stiff_s[...], ((mat, 4, 2), (mat_y, 2, 4)))
    for copy in copies[1:]:
        copy.wait()


def load_call(disp, dens, stiff):
    matrix = jax.ShapeDtypeStruct((192, 224), bf16)
    return pl.pallas_call(
        load_kernel,
        in_specs=[HBM, HBM, HBM],
        out_shape=(
            jax.ShapeDtypeStruct(disp.shape, f32),
            jax.ShapeDtypeStruct(dens.shape, f32),
            matrix,
            matrix,
        ),
        scratch_shapes=[pltpu.VMEM((24, 24), f32), pltpu.SemaphoreType.DMA((3,))],
        compiler_params=pltpu.CompilerParams(vmem_limit_bytes=16 * 2**20),
        cost_estimate=estimate(2),
        name="load",
    )(disp, dens, stiff)


def ends_kernel(disp, dens, mat, ends, up, down, *work):
    _, ny, nz, nx = disp.shape

    def segments(p):
        return lambda i: [(disp[i, p, 0:8], disp[i, p, 8:9]), (disp[i, p, nz - 8 : nz], None)]

    def put(y):
        d = jnp.concatenate([dens[y, 0:8], dens[y, nz - 8 : nz]], axis=0)
        ends[y] = energy_rows(y, mat, work, d)

    sweep(ny - 1, segments, put, work)
    for y in range(ny):
        row = slice(y, y + 1)
        for i in range(9):
            up[i, row] = disp[i, y, nz - 1 : nz]
            down[i, row] = disp[i, y, 0:1]
        up[9, row] = dens[y, nz - 1 : nz]
        if y < ny - 1:
            up[10, row] = ends[y, 14:15]
            down[9, row] = ends[y, 0:1]
            down[10, row] = ends[y, 1:2]
    up[11] = jnp.zeros((ny, nx), f32)
    down[11] = jnp.zeros((ny, nx), f32)


def ends_call(disp, dens, mat):
    _, ny, nz, nx = disp.shape
    message = jax.ShapeDtypeStruct((12, ny, nx), f32)
    return pl.pallas_call(
        ends_kernel,
        in_specs=[VMEM] * 3,
        out_shape=(jax.ShapeDtypeStruct((ny, 16, nx), f32), message, message),
        scratch_shapes=workspace(ny, 2, nx),
        compiler_params=pltpu.CompilerParams(vmem_limit_bytes=16 * 2**20),
        cost_estimate=estimate(4),
        name="energy_ends",
    )(disp, dens, mat)


def top_kernel(flags, disp, dens, fy, mat, ends, up, down, top, up_full, down_full, msg_even, msg_odd, *work):
    _, ny, nz, nx = disp.shape
    work[1][...] = jnp.zeros_like(work[1])
    prepare(lambda i: [(disp[i, ny - 1], None)], 0, work)
    prepare(lambda i: [(fy[i], None)], 1, work)
    up_full[...] = up[...]
    down_full[...] = down[...]
    for i in range(9):
        up_full[11, i : i + 1] = fy[i, nz - 1 : nz]
        down_full[11, i : i + 1] = fy[i, 0:1]
    s = energy_rows(0, mat, work, dens[ny - 1])
    top[...] = s
    up_full[10, ny - 1 : ny] = s[nz - 2 : nz - 1]
    down_full[9, ny - 1 : ny] = s[0:1]
    down_full[10, ny - 1 : ny] = s[1:2]
    odd = flags[5] == 1
    msg_even[...] = jnp.where(odd, down_full[...], up_full[...])
    msg_odd[...] = jnp.where(odd, up_full[...], down_full[...])


def top_call(flags, disp, dens, fy, mat, ends, up, down):
    _, ny, nz, nx = disp.shape
    message = jax.ShapeDtypeStruct((12, ny, nx), f32)
    return pl.pallas_call(
        top_kernel,
        in_specs=[SMEM] + [VMEM] * 7,
        out_shape=(jax.ShapeDtypeStruct((nz, nx), f32),) + (message,) * 4,
        scratch_shapes=workspace(2, nz // 8, nx),
        compiler_params=pltpu.CompilerParams(vmem_limit_bytes=16 * 2**20),
        cost_estimate=estimate(1),
        name="energy_top",
    )(flags, disp, dens, fy, mat, ends, up, down)


def middle_kernel(disp, dens, mat, ends, top, src, *work):
    _, ny, nz, nx = disp.shape

    def segments(p):
        return lambda i: [(disp[i, p, 8 : nz - 8], disp[i, p, nz - 8 : nz - 7])]

    def frame(y):
        src[y, 0:OFF] = jnp.zeros((OFF, nx), f32)
        src[y, OFF + nz :] = jnp.zeros((src.shape[1] - OFF - nz, nx), f32)

    def put(y):
        frame(y)
        src[y, OFF : OFF + 8] = ends[y, 0:8]
        src[y, OFF + 8 : OFF + nz - 8] = energy_rows(y, mat, work, dens[y, 8 : nz - 8])
        src[y, OFF + nz - 8 : OFF + nz] = ends[y, 8:16]

    sweep(ny - 1, segments, put, work)
    frame(ny - 1)
    src[ny - 1, OFF : OFF + nz] = top[...]


def middle_call(disp, dens, mat, ends, top):
    _, ny, nz, nx = disp.shape
    return pl.pallas_call(
        middle_kernel,
        in_specs=[VMEM] * 5,
        out_shape=jax.ShapeDtypeStruct((ny, nz + 2 * OFF, nx), f32),
        scratch_shapes=workspace(ny, nz // 8 - 2, nx),
        compiler_params=pltpu.CompilerParams(vmem_limit_bytes=24 * 2**20),
        cost_estimate=estimate(4),
        name="energy_middle",
    )(disp, dens, mat, ends, top)


def rim_kernel(flags, got_odd, got_even, up, down, mat_y, src, rim, msg_even, msg_odd, low_s, high_s, t_s, *work):
    ny, rows, nx = src.shape
    nz = rows - 2 * OFF
    odd = flags[5] == 1
    low_s[...] = jnp.where(odd, got_even[...], got_odd[...])
    high_s[...] = jnp.where(odd, got_odd[...], got_even[...])
    work[1][...] = jnp.zeros_like(work[1])
    prepare(lambda i: [(low_s[i], low_s[11, i : i + 1]), (up[i], up[11, i : i + 1])], 0, work)
    prepare(lambda i: [(down[i], down[11, i : i + 1]), (high_s[i], high_s[11, i : i + 1])], 1, work)
    s = energy_rows(0, mat_y, work, jnp.concatenate([low_s[9], up[9]], axis=0))
    columns = (low_s[10], s[0:ny], s[ny : 2 * ny], high_s[9], high_s[10])
    for y in range(ny):
        for r, column in enumerate(columns):
            rim[y, r : r + 1] = column[y : y + 1]
        rim[y, 5:8] = jnp.zeros((3, nx), f32)
    for j in range(4):
        y = j if j < 2 else ny - 4 + j
        t_s[j, 0:nz] = src[y, OFF : OFF + nz]
        t_s[j, nz : nz + 8] = rim[y]
    odd = flags[4] == 1
    msg_even[...] = jnp.where(odd, t_s[0:2], t_s[2:4])
    msg_odd[...] = jnp.where(odd, t_s[2:4], t_s[0:2])


def put_rim(s, y, rim, nz):
    s[y, OFF - 2 : OFF] = rim[0:2]
    s[y, OFF + nz - 1 : OFF + nz + 2] = rim[2:5]


def rim_call(flags, got_odd, got_even, up, down, mat_y, src):
    ny, rows, nx = src.shape
    return pl.pallas_call(
        rim_kernel,
        in_specs=[SMEM] + [VMEM] * 6,
        out_shape=(
            jax.ShapeDtypeStruct((ny, 8, nx), f32),
            jax.ShapeDtypeStruct((2, rows - OFF, nx), f32),
            jax.ShapeDtypeStruct((2, rows - OFF, nx), f32),
        ),
        scratch_shapes=[
            pltpu.VMEM((12, ny, nx), f32),
            pltpu.VMEM((12, ny, nx), f32),
            pltpu.VMEM((4, rows - OFF, nx), f32),
        ]
        + workspace(2, 2 * (ny // 8), nx),
        compiler_params=pltpu.CompilerParams(vmem_limit_bytes=16 * 2**20),
        cost_estimate=estimate(2),
        name="energy_rim",
    )(flags, got_odd, got_even, up, down, mat_y, src)


def filter_block(s_s, d_s, n, z_edges, y_edges, finish, unroll):
    rows, nx = s_s.shape[1:]
    nz = rows - 2 * OFF
    alpha, beta, gamma, delta, eps = filter_weights()
    row = lax.broadcasted_iota(jnp.int32, (rows, nx), 0)
    keep = jnp.where(row < OFF, z_edges[0], jnp.where(row >= OFF + nz, z_edges[1], 1)) == 1

    def beside(v):
        return pltpu.roll(v, 1, 0) + pltpu.roll(v, rows - 1, 0) + lane_up(v) + lane_down(v)

    def second(j, _):
        c = s_s[j + 1]
        d2 = alpha * c + beta * (beside(c) + s_s[j] + s_s[j + 2])
        ok = keep
        if y_edges is not None:
            ok = keep & (jnp.where(j == 0, y_edges[0], jnp.where(j == n - 3, y_edges[1], 1)) == 1)
        d_s[j] = jnp.where(ok, d2, 0.0)
        return 0

    def third(j, _):
        d2 = d_s[j + 1]
        p3 = gamma * s_s[j + 2] + delta * d2 + eps * (beside(d2) + d_s[j] + d_s[j + 2])
        finish(j, p3[OFF : OFF + nz])
        return 0

    lax.fori_loop(0, n - 2, second, 0, unroll=unroll)
    lax.fori_loop(0, n - 4, third, 0, unroll=unroll)


def limits(p3, d, pas, sol):
    amp = jnp.sqrt(jnp.maximum(-p3 * d, 0.0))
    lower = jnp.maximum(d - move_limit, floor_density)
    upper = jnp.minimum(d + move_limit, 1.0)
    low, high, now = (jnp.where(sol, 1.0, jnp.where(pas, floor_density, v)) for v in (lower, upper, d))
    return amp, low, high, now


FINE = 16
COARSE = POINTS // FINE


def table(n, nz, nx, amp, low, high, now, fine_s, vol, tgt, start):
    spacing = 2.0 * bracket_end / POINTS

    pair = 2
    for first in range(0, COARSE, pair):
        inverse = [math.exp(0.5 * (-bracket_end + spacing * FINE * i)) for i in range(first, first + pair)]

        def volume(j, acc):
            acc = list(acc)
            for w in range(nz // 8):
                at = slice(8 * w, 8 * w + 8)
                lo, hi, d = low[j, at], high[j, at], now[j, at]
                los, his = [lo * c for c in inverse], [hi * c for c in inverse]
                for i, c in enumerate(inverse):
                    acc[pair * FINE + i] = acc[pair * FINE + i] + d * c
                for f in range(FINE):
                    if first == 0:
                        t = amp[j, at] * math.exp(-0.5 * spacing * f)
                        fine_s[f, j, at] = t
                    else:
                        t = fine_s[f, j, at]
                    for i in range(pair):
                        acc[i * FINE + f] = acc[i * FINE + f] + jnp.minimum(jnp.maximum(t, los[i]), his[i])
            return tuple(acc)

        places = [(vol, 8 * (first * FINE + e)) for e in range(pair * FINE)]
        places += [(tgt, 8 * (first + i)) for i in range(pair)]
        if start is None:
            begin = tuple(jnp.zeros((8, nx), f32) for _ in places)
        else:
            begin = tuple((start[0] if ref is vol else start[1])[at : at + 8] for ref, at in places)
        acc = lax.fori_loop(0, n, volume, begin, unroll=2)
        for (ref, at), value in zip(places, acc):
            ref[at : at + 8] = value


def inner_kernel(flags, src, rim, dens, passive, solid, amp, low, high, vol, tgt, s_s, d_s, now_s, fine_s):
    ny, nz, nx = dens.shape
    s_s[...] = src[...]

    def fix(y, _):
        put_rim(s_s, y, rim[y], nz)
        return 0

    lax.fori_loop(0, ny, fix, 0, unroll=4)

    def finish(j, p3):
        y = j + 2
        amp[j], low[j], high[j], now_s[j] = limits(p3, dens[y], passive[y] == 1, solid[y] == 1)

    filter_block(s_s, d_s, ny, (flags[2], flags[3]), None, finish, 4)
    table(ny - 4, nz, nx, amp, low, high, now_s, fine_s, vol, tgt, None)


def inner_call(flags, src, rim, dens, passive, solid):
    ny, nz, nx = dens.shape
    field = jax.ShapeDtypeStruct((ny - 4, nz, nx), f32)
    return pl.pallas_call(
        inner_kernel,
        in_specs=[SMEM] + [VMEM] * 5,
        out_shape=(
            field,
            field,
            field,
            jax.ShapeDtypeStruct((8 * POINTS, nx), f32),
            jax.ShapeDtypeStruct((8 * COARSE, nx), f32),
        ),
        scratch_shapes=[
            pltpu.VMEM((ny, nz + 2 * OFF, nx), f32),
            pltpu.VMEM((ny - 2, nz + 2 * OFF, nx), f32),
            pltpu.VMEM((ny - 4, nz, nx), f32),
            pltpu.VMEM((FINE, ny - 4, nz, nx), f32),
        ],
        compiler_params=pltpu.CompilerParams(vmem_limit_bytes=24 * 2**20),
        cost_estimate=estimate(9),
        name="filter_inner",
    )(flags, src, rim, dens, passive, solid)


def outer_kernel(
    flags, src, rim, got_odd, got_even, dens, passive, solid, vol_i, tgt_i,
    amp, low, high, excess, s_s, d_s, now_s, fine_s, vol, tgt,
):
    ny, nz, nx = dens.shape
    odd = flags[4] == 1
    got = (jnp.where(odd, got_even[...], got_odd[...]), jnp.where(odd, got_odd[...], got_even[...]))
    for b in range(2):
        for j in range(2):
            at = j if b == 0 else 4 + j
            s_s[b, at, 0:OFF] = jnp.zeros((OFF, nx), f32)
            s_s[b, at, OFF : OFF + nz] = got[b][j, 0:nz]
            s_s[b, at, OFF + nz :] = jnp.zeros((OFF, nx), f32)
            put_rim(s_s.at[b], at, got[b][j, nz : nz + 8], nz)
    for j in range(4):
        s_s[0, 2 + j] = src[j]
        put_rim(s_s.at[0], 2 + j, rim[j], nz)
        s_s[1, j] = src[ny - 4 + j]
        put_rim(s_s.at[1], j, rim[ny - 4 + j], nz)
    for b in range(2):
        y0 = 0 if b == 0 else ny - 2

        def finish(j, p3):
            y = y0 + j
            at = 2 * b + j
            amp[at], low[at], high[at], now_s[at] = limits(p3, dens[y], passive[y] == 1, solid[y] == 1)

        edges = (flags[0], 1) if b == 0 else (1, flags[1])
        filter_block(s_s.at[b], d_s.at[b], 6, (flags[2], flags[3]), edges, finish, True)
    table(4, nz, nx, amp, low, high, now_s, fine_s, vol, tgt, (vol_i, tgt_i))

    def lanes(ref, count):
        total = ref[pl.ds(0, count, stride=8), :]
        for s in range(1, 8):
            total = total + ref[pl.ds(s, count, stride=8), :]
        return total

    volumes, targets = lanes(vol, POINTS), lanes(tgt, COARSE)
    over = [volumes[FINE * i : FINE * i + FINE] - targets[i : i + 1] for i in range(COARSE)]
    excess[...] = jnp.sum(jnp.transpose(jnp.concatenate(over, axis=0)), axis=0, keepdims=True)


def outer_call(flags, src, rim, got_odd, got_even, dens, passive, solid, vol_i, tgt_i):
    ny, nz, nx = dens.shape
    rows = nz + 2 * OFF
    field = jax.ShapeDtypeStruct((4, nz, nx), f32)
    return pl.pallas_call(
        outer_kernel,
        in_specs=[SMEM] + [VMEM] * 9,
        out_shape=(field, field, field, jax.ShapeDtypeStruct((1, POINTS), f32)),
        scratch_shapes=[
            pltpu.VMEM((2, 6, rows, nx), f32),
            pltpu.VMEM((2, 4, rows, nx), f32),
            pltpu.VMEM((4, nz, nx), f32),
            pltpu.VMEM((FINE, 4, nz, nx), f32),
            pltpu.VMEM((8 * POINTS, nx), f32),
            pltpu.VMEM((8 * COARSE, nx), f32),
        ],
        compiler_params=pltpu.CompilerParams(vmem_limit_bytes=16 * 2**20),
        cost_estimate=estimate(3),
        name="filter_outer",
    )(flags, src, rim, got_odd, got_even, dens, passive, solid, vol_i, tgt_i)


def update_kernel(tables, amp_i, low_i, high_i, amp_o, low_o, high_o, new, logm):
    inner = amp_i.shape[0]
    nx = amp_i.shape[-1]
    total = jnp.sum(tables[...], axis=0, keepdims=True)
    lane = lax.broadcasted_iota(jnp.int32, total.shape, 1)
    above = jnp.where((total > 0.0) & (lane > 0), 1.0, 0.0)
    middle = -bracket_end + (2.0 * bracket_end / POINTS) * (jnp.sum(above) + 0.5)
    logm[0] = middle
    scale = jnp.exp(jnp.full((1, nx), -0.5 * middle, f32))

    def new_row(amp, low, high):
        return jnp.minimum(jnp.maximum(amp * scale, low), high)

    def body(j, _):
        new[j + 2] = new_row(amp_i[j], low_i[j], high_i[j])
        return 0

    lax.fori_loop(0, inner, body, 0)
    for j in range(4):
        new[j if j < 2 else inner + j] = new_row(amp_o[j], low_o[j], high_o[j])


def update_call(tables, inner, outer):
    n, nz, nx = inner[0].shape
    return pl.pallas_call(
        update_kernel,
        in_specs=[VMEM] * 7,
        out_specs=(VMEM, SMEM),
        out_shape=(jax.ShapeDtypeStruct((n + 4, nz, nx), f32), jax.ShapeDtypeStruct((1,), f32)),
        compiler_params=pltpu.CompilerParams(vmem_limit_bytes=8 * 2**20),
        cost_estimate=estimate(1),
        name="update",
    )(tables, *inner, *outer)


def to_lower(value, axis):
    count = lax.axis_size(axis)
    return lax.ppermute(value, axis, [(i + 1, i) for i in range(count - 1)])


def swap(value, axis, start):
    pairs = []
    for i in range(start, lax.axis_size(axis) - 1, 2):
        pairs += [(i, i + 1), (i + 1, i)]
    return lax.ppermute(value, axis, pairs)


def on_device(displacement, density, passive, solid, stiffness):
    ny, nz, nx = density.shape
    gy, gz = lax.axis_size("gy"), lax.axis_size("gz")
    iy, iz = lax.axis_index("gy"), lax.axis_index("gz")
    flags = jnp.stack([iy > 0, iy < gy - 1, iz > 0, iz < gz - 1, iy % 2 == 1, iz % 2 == 1]).astype(jnp.int32)

    disp_hbm = pltpu.with_memory_space_constraint(displacement, pltpu.HBM)
    dens_hbm = pltpu.with_memory_space_constraint(density, pltpu.HBM)
    stiff_hbm = pltpu.with_memory_space_constraint(stiffness, pltpu.HBM)

    fy = to_lower(displacement[:, 0], "gy")
    disp, dens, mat, mat_y = load_call(disp_hbm, dens_hbm, stiff_hbm)
    ends, up, down = ends_call(disp, dens, mat)
    top, up, down, z_even, z_odd = top_call(flags, disp, dens, fy, mat, ends, up, down)

    z_got_even = swap(z_even, "gz", 0)
    z_got_odd = swap(z_odd, "gz", 1)
    src = middle_call(disp, dens, mat, ends, top)
    rim, msg_even, msg_odd = rim_call(flags, z_got_odd, z_got_even, up, down, mat_y, src)

    got_even = swap(msg_even, "gy", 0)
    got_odd = swap(msg_odd, "gy", 1)
    *inner, vol, tgt = inner_call(flags, src, rim, dens, passive, solid)
    *outer, excess = outer_call(flags, src, rim, got_odd, got_even, dens, passive, solid, vol, tgt)

    everyone = jnp.broadcast_to(excess, (gz * gy, POINTS))
    tables = lax.all_to_all(everyone, ("gz", "gy"), 0, 0, tiled=True)
    new, logm = update_call(tables, inner, outer)
    return new, logm.reshape(())


def solution(mesh):
    placed = (
        P(None, "gy", "gz", None),
        P("gy", "gz", None),
        P("gy", "gz", None),
        P("gy", "gz", None),
        P(),
    )
    return jax.shard_map(
        on_device, mesh=mesh, in_specs=placed, out_specs=(P("gy", "gz", None), P()), check_vma=False
    )
```

```python
import math

import jax
import jax.numpy as jnp
from jax import lax
from jax.experimental import pallas as pl
from jax.experimental.pallas import tpu as pltpu
from jax.sharding import PartitionSpec as P

ITERS = 8
POINTS = 2**ITERS
OFF = 8

smoothing = 0.52
move_limit = 0.2
floor_density = 0.001
bracket_end = 12.0

f32 = jnp.float32
bf16 = jnp.bfloat16
VMEM = pl.BlockSpec(memory_space=pltpu.VMEM)
SMEM = pl.BlockSpec(memory_space=pltpu.SMEM)
HBM = pl.BlockSpec(memory_space=pltpu.HBM)


def cheb_weights():
    spectrum_top = 1.0 + 12.0 * smoothing
    centre_value = (spectrum_top + 1.0) / 2.0
    half_width = (spectrum_top - 1.0) / 2.0
    ratio_value = centre_value / half_width
    first_rho = 1.0 / ratio_value
    second_rho = 1.0 / (2.0 * ratio_value - first_rho)
    third_rho = 1.0 / (2.0 * ratio_value - second_rho)
    return (
        centre_value,
        second_rho * first_rho,
        2.0 * second_rho / half_width,
        third_rho * second_rho,
        2.0 * third_rho / half_width,
    )


def filter_weights():
    t, w1, w2, w3, w4 = cheb_weights()
    diag = 1.0 + 6.0 * smoothing
    alpha = w1 / t + w2 * (1.0 - diag / t)
    beta = w2 * smoothing / t
    gamma = 1.0 / t - w4 * w1 / (t * w2)
    delta = 1.0 + w3 + w4 / w2 - w4 * diag
    eps = w4 * smoothing
    return alpha, beta, gamma, delta, eps


def lane_up(v):
    n = v.shape[-1]
    lane = lax.broadcasted_iota(jnp.int32, v.shape, v.ndim - 1)
    return jnp.where(lane < n - 1, pltpu.roll(v, n - 1, v.ndim - 1), 0.0)


def lane_down(v):
    n = v.shape[-1]
    lane = lax.broadcasted_iota(jnp.int32, v.shape, v.ndim - 1)
    return jnp.where(lane > 0, pltpu.roll(v, 1, v.ndim - 1), 0.0)


def estimate(us):
    return pl.CostEstimate(flops=int(us * 1e9), bytes_accessed=1 << 20, transcendentals=0)


def build_matrices(k, mats):
    shape = (24, 128)
    col = lax.broadcasted_iota(jnp.int32, shape, 1)
    row = lax.broadcasted_iota(jnp.int32, shape, 0)
    main = col < 96
    q = jnp.where(main, jnp.where(col >= 48, 1, 0), jnp.where(col >= 104, 1, 0))
    m = col - 48 * q
    e = col - 96 - 8 * q
    c = jnp.where(main, m >> 4, e >> 1)
    dx = jnp.where(main, (m >> 3) & 1, e & 1)
    valid = main | (e < 6)
    picks = []
    for _, plane, band in mats:
        dof0 = 3 * (plane * q + dx) + c
        picks.append(jnp.where(main & (row == dof0), 1.0, 0.0))
        picks.append(jnp.where(valid & (row == dof0 + 3 * band), 1.0, 0.0))
    picked = jnp.dot(
        k, jnp.concatenate(picks, axis=1), precision=lax.Precision.HIGHEST, preferred_element_type=f32
    )
    col8 = lax.broadcasted_iota(jnp.int32, (8, 128), 1)
    row8 = lax.broadcasted_iota(jnp.int32, (8, 128), 0)
    main8 = col8 < 96
    rc = col8 & 7
    m0 = main8 & (rc == row8)
    m1 = jnp.where(main8, rc, 8) == row8 + 1
    for n, (mat, plane, band) in enumerate(mats):
        k0 = picked[:, 256 * n : 256 * n + 128]
        k1 = picked[:, 256 * n + 128 : 256 * n + 256]
        rows = []
        for b in range(2):
            for q_ in range(2):
                for c_ in range(3):
                    for dx_ in range(2):
                        r = 3 * (plane * q_ + band * b + dx_) + c_
                        rows.append(jnp.where(m0, k0[r : r + 1], 0.0) + jnp.where(m1, k1[r : r + 1], 0.0))
        full = jnp.concatenate(rows, axis=0)
        hi = full.astype(bf16)
        lo = (full - hi.astype(f32)).astype(bf16)
        mat[:, 0:112] = hi[:, 0:112]
        mat[:, 112:224] = lo[:, 0:112]


def prepare(segments, p, work):
    main_s, ext_s, mul_s = work
    for l in range(3):
        for c in range(3):
            w0 = 0
            for u, x in segments(3 * l + c):
                size, nx = u.shape
                n = size // 8
                last = lax.broadcasted_iota(jnp.int32, u.shape, 0) == size - 1
                both = (u, lane_up(u))
                after = (None, None) if x is None else (x, lane_up(x))
                for w in range(n):
                    sl = slice(8 * w, 8 * w + 8)
                    main_s[p, l, 16 * c : 16 * c + 16, (w0 + w) * nx : (w0 + w + 1) * nx] = jnp.concatenate(
                        [both[0][sl], both[1][sl]], axis=0
                    ).astype(bf16)
                for dx in range(2):
                    v, vx = both[dx], after[dx]
                    k = 2 * c + dx
                    for w in range(n):
                        nxt = v[8 * w + 8 : 8 * w + 9] if w < n - 1 else vx
                        if nxt is not None:
                            ext_s[p, l, k : k + 1, (w0 + w) * nx : (w0 + w + 1) * nx] = nxt
                    m = 2.0 * v - v.astype(bf16).astype(f32)
                    mx = 0.0 if vx is None else jnp.broadcast_to(2.0 * vx - vx.astype(bf16).astype(f32), v.shape)
                    at = slice(8 * w0, 8 * (w0 + n))
                    mul_s[p, l, k, 0, at] = m
                    mul_s[p, l, k, 1, at] = jnp.where(last, mx, pltpu.roll(m, size - 1, 0))
                w0 += n


def energy_rows(p, mat, work, density):
    main_s, ext_s, mul_s = work
    rows, nx = density.shape
    count = rows // 8
    acc = [None] * count
    for l in range(3):
        ext = jnp.concatenate([ext_s[p, l], ext_s[p + 1, l]], axis=0).astype(bf16)
        one = jnp.concatenate([main_s[p, l], main_s[p + 1, l], ext], axis=0)
        force = jnp.dot(mat[...], jnp.concatenate([one, one], axis=0), preferred_element_type=f32)
        i = 0
        for b in range(2):
            for q in range(2):
                for k in range(6):
                    for w in range(count):
                        at = slice(8 * w, 8 * w + 8)
                        term = force[8 * i : 8 * i + 8, w * nx : (w + 1) * nx] * mul_s[p + q, l, k, b, at]
                        acc[w] = term if acc[w] is None else acc[w] + term
                    i += 1
    return density * (-3.0 * density * density * jnp.concatenate(acc, axis=0))


def workspace(planes, windows, nx):
    return [
        pltpu.VMEM((planes, 3, 48, windows * nx), bf16),
        pltpu.VMEM((planes, 3, 8, windows * nx), f32),
        pltpu.VMEM((planes, 3, 6, 2, 8 * windows, nx), f32),
    ]


def sweep(rows, segments, put, work, ready=None):
    work[1][...] = jnp.zeros_like(work[1])

    def plane(p):
        if ready is not None:
            ready(p)
        prepare(segments(p), p, work)

    for p in range(2):
        plane(p)

    def body(y, _):
        put(y)
        plane(y + 2)
        return 0

    lax.fori_loop(0, rows - 1, body, 0, unroll=2)
    put(rows - 1)


def face_kernel(disp, face, sem):
    copy = pltpu.make_async_copy(disp.at[:, 0], face, sem)
    copy.start()
    copy.wait()


def face_call(disp):
    _, _, nz, nx = disp.shape
    return pl.pallas_call(
        face_kernel,
        in_specs=[HBM],
        out_shape=jax.ShapeDtypeStruct((9, nz, nx), f32),
        scratch_shapes=[pltpu.SemaphoreType.DMA],
        compiler_params=pltpu.CompilerParams(vmem_limit_bytes=2**20),
        name="face",
    )(disp)


def extra(ref, row):
    ny = ref.shape[1]
    return 11 + row // ny, slice(row % ny, row % ny + 1)


def ends_kernel(flags, disp_h, dens_h, stiff, disp, dens, mat, mat_y, ends, up, down, msg_even, msg_odd, stiff_s, sems, *work):
    _, ny, nz, nx = disp.shape

    def copy(p):
        return pltpu.make_async_copy(disp_h.at[:, p], disp.at[:, p], sems.at[p])

    copy_k = pltpu.make_async_copy(stiff, stiff_s, sems.at[ny])
    copy_d = pltpu.make_async_copy(dens_h, dens, sems.at[ny + 1])
    copy_k.start()
    for p in range(2):
        copy(p).start()
    copy_d.start()
    for p in range(2, ny):
        copy(p).start()
    copy_k.wait()
    build_matrices(stiff_s[...], ((mat, 4, 2), (mat_y, 2, 4)))
    copy_d.wait()

    def segments(p):
        return lambda i: [(disp[i, p, 0:8], disp[i, p, 8:9]), (disp[i, p, nz - 8 : nz], None)]

    def put(y):
        d = jnp.concatenate([dens[y, 0:8], dens[y, nz - 8 : nz]], axis=0)
        ends[y] = energy_rows(y, mat, work, d)

    sweep(ny - 1, segments, put, work, lambda p: copy(p).wait())
    for ref in (up, down):
        ref[9:] = jnp.zeros((ref.shape[0] - 9, ny, nx), f32)
    for y in range(ny):
        row = slice(y, y + 1)
        for i in range(9):
            up[i, row] = disp[i, y, nz - 1 : nz]
            down[i, row] = disp[i, y, 0:1]
        up[9, row] = dens[y, nz - 1 : nz]
        if y < ny - 1:
            up[10, row] = ends[y, 14:15]
            down[9, row] = ends[y, 0:1]
            down[10, row] = ends[y, 1:2]
    for n, y in enumerate((0, ny - 1)):
        for i in range(9):
            up[extra(up, 9 * n + i)] = disp[i, y, nz - 2 : nz - 1]
            down[extra(down, 9 * n + i)] = disp[i, y, 1:2]
            down[extra(down, 18 + 9 * n + i)] = disp[i, y, 2:3]
    up[extra(up, 36)] = dens[ny - 1, nz - 2 : nz - 1]
    down[extra(down, 36)] = dens[ny - 1, 0:1]
    down[extra(down, 37)] = dens[ny - 1, 1:2]
    odd = flags[5] == 1
    msg_even[...] = jnp.where(odd, down[...], up[...])
    msg_odd[...] = jnp.where(odd, up[...], down[...])


def ends_call(flags, disp, dens, stiff):
    _, ny, nz, nx = disp.shape
    message = jax.ShapeDtypeStruct((11 + -(-38 // ny), ny, nx), f32)
    matrix = jax.ShapeDtypeStruct((192, 224), bf16)
    return pl.pallas_call(
        ends_kernel,
        in_specs=[SMEM] + [HBM] * 3,
        out_shape=(
            jax.ShapeDtypeStruct(disp.shape, f32),
            jax.ShapeDtypeStruct(dens.shape, f32),
            matrix,
            matrix,
            jax.ShapeDtypeStruct((ny, 16, nx), f32),
        )
        + (message,) * 4,
        scratch_shapes=[pltpu.VMEM((24, 24), f32), pltpu.SemaphoreType.DMA((ny + 2,))] + workspace(ny, 2, nx),
        compiler_params=pltpu.CompilerParams(vmem_limit_bytes=20 * 2**20),
        cost_estimate=estimate(4),
        name="energy_ends",
    )(flags, disp, dens, stiff)


def middle_kernel(disp, dens, fy, mat, ends, src, *work):
    _, ny, nz, nx = disp.shape
    work, last = work[:3], work[3:]

    def segments(p):
        return lambda i: [(disp[i, p, 8 : nz - 8], disp[i, p, nz - 8 : nz - 7])]

    def frame(y):
        src[y, 0:OFF] = jnp.zeros((OFF, nx), f32)
        src[y, OFF + nz :] = jnp.zeros((src.shape[1] - OFF - nz, nx), f32)

    def put(y):
        frame(y)
        src[y, OFF : OFF + 8] = ends[y, 0:8]
        src[y, OFF + 8 : OFF + nz - 8] = energy_rows(y, mat, work, dens[y, 8 : nz - 8])
        src[y, OFF + nz - 8 : OFF + nz] = ends[y, 8:16]

    sweep(ny - 1, segments, put, work)
    last[1][...] = jnp.zeros_like(last[1])
    prepare(lambda i: [(disp[i, ny - 1], None)], 0, last)
    prepare(lambda i: [(fy[i], None)], 1, last)
    frame(ny - 1)
    src[ny - 1, OFF : OFF + nz] = energy_rows(0, mat, last, dens[ny - 1])


def middle_call(disp, dens, fy, mat, ends):
    _, ny, nz, nx = disp.shape
    return pl.pallas_call(
        middle_kernel,
        in_specs=[VMEM] * 5,
        out_shape=jax.ShapeDtypeStruct((ny, nz + 2 * OFF, nx), f32),
        scratch_shapes=workspace(ny, nz // 8 - 2, nx) + workspace(2, nz // 8, nx),
        compiler_params=pltpu.CompilerParams(vmem_limit_bytes=24 * 2**20),
        cost_estimate=estimate(4),
        name="energy_middle",
    )(disp, dens, fy, mat, ends)


def rim_kernel(
    flags, got_even, got_odd, up, down, disp, dens, mat_y, src,
    rim, nodes, msg_even, msg_odd, low_s, high_s, t_s, *work,
):
    ny, rows, nx = src.shape
    nz = rows - 2 * OFF
    odd = flags[5] == 1
    low_s[...] = jnp.where(odd, got_even[...], got_odd[...])
    high_s[...] = jnp.where(odd, got_odd[...], got_even[...])
    work[1][...] = jnp.zeros_like(work[1])
    prepare(lambda i: [(low_s[i], None), (up[i], None)], 0, work)
    prepare(lambda i: [(down[i], None), (high_s[i], None)], 1, work)
    s = energy_rows(0, mat_y, work, jnp.concatenate([low_s[9], up[9]], axis=0))
    columns = ((0, low_s[10]), (1, s[0:ny]), (3, s[ny : 2 * ny]), (4, high_s[9]), (5, high_s[10]))
    for y in range(ny):
        rim[y] = jnp.zeros((8, nx), f32)
        for r, column in columns:
            rim[y, r : r + 1] = column[y : y + 1]
    half = 2 * (nz + 8)
    zero = jnp.zeros((1, nx), f32)
    for n, y in enumerate((0, ny - 1)):
        row = slice(y, y + 1)
        for i in range(9):
            window = jnp.concatenate(
                [
                    low_s[extra(low_s, 9 * n + i)],
                    low_s[i, row],
                    disp[i, y, 0:1],
                    disp[i, y, nz - 1 : nz],
                    high_s[i, row],
                    high_s[extra(high_s, 9 * n + i)],
                    high_s[extra(high_s, 18 + 9 * n + i)],
                    zero,
                ],
                axis=0,
            )
            nodes[n, i] = window
            t_s[n, half + 8 * i : half + 8 * i + 8] = window
        nodes[n, 9] = jnp.concatenate(
            [
                low_s[extra(low_s, 36)],
                low_s[9, ny - 1 : ny],
                zero,
                dens[ny - 1, nz - 1 : nz],
                high_s[extra(high_s, 36)],
                high_s[extra(high_s, 37)],
                zero,
                zero,
            ],
            axis=0,
        )
        t_s[n, half + 72 : half + 80] = nodes[n, 9]
        for j in range(2):
            at = j * (nz + 8)
            yy = j if n == 0 else ny - 2 + j
            t_s[n, at : at + nz] = src[yy, OFF : OFF + nz]
            t_s[n, at + nz : at + nz + 8] = rim[yy]
    odd = flags[4] == 1
    msg_even[...] = jnp.where(odd, t_s[0], t_s[1])
    msg_odd[...] = jnp.where(odd, t_s[1], t_s[0])


def put_rim(s, y, rim, nz):
    s[y, OFF - 2 : OFF] = rim[0:2]
    s[y, OFF + nz - 1 : OFF + nz + 2] = rim[3:6]


def rim_call(flags, got_even, got_odd, up, down, disp, dens, mat_y, src):
    ny, rows, nx = src.shape
    nz = rows - 2 * OFF
    size = 2 * (nz + 8) + 80
    return pl.pallas_call(
        rim_kernel,
        in_specs=[SMEM] + [VMEM] * 8,
        out_shape=(
            jax.ShapeDtypeStruct((ny, 8, nx), f32),
            jax.ShapeDtypeStruct((2, 10, 8, nx), f32),
            jax.ShapeDtypeStruct((size, nx), f32),
            jax.ShapeDtypeStruct((size, nx), f32),
        ),
        scratch_shapes=[
            pltpu.VMEM(up.shape, f32),
            pltpu.VMEM(up.shape, f32),
            pltpu.VMEM((2, size, nx), f32),
        ]
        + workspace(2, 2 * (ny // 8), nx),
        compiler_params=pltpu.CompilerParams(vmem_limit_bytes=16 * 2**20),
        cost_estimate=estimate(2),
        name="energy_rim",
    )(flags, got_even, got_odd, up, down, disp, dens, mat_y, src)


def filter_block(s_s, d_s, n, z_edges, y_edges, finish, unroll):
    rows, nx = s_s.shape[1:]
    nz = rows - 2 * OFF
    alpha, beta, gamma, delta, eps = filter_weights()
    row = lax.broadcasted_iota(jnp.int32, (rows, nx), 0)
    keep = jnp.where(row < OFF, z_edges[0], jnp.where(row >= OFF + nz, z_edges[1], 1)) == 1

    def beside(v):
        return pltpu.roll(v, 1, 0) + pltpu.roll(v, rows - 1, 0) + lane_up(v) + lane_down(v)

    def second(j, _):
        c = s_s[j + 1]
        d2 = alpha * c + beta * (beside(c) + s_s[j] + s_s[j + 2])
        ok = keep
        if y_edges is not None:
            ok = keep & (jnp.where(j == 0, y_edges[0], jnp.where(j == n - 3, y_edges[1], 1)) == 1)
        d_s[j] = jnp.where(ok, d2, 0.0)
        return 0

    def third(j, _):
        d2 = d_s[j + 1]
        p3 = gamma * s_s[j + 2] + delta * d2 + eps * (beside(d2) + d_s[j] + d_s[j + 2])
        finish(j, p3[OFF : OFF + nz])
        return 0

    lax.fori_loop(0, n - 2, second, 0, unroll=unroll)
    lax.fori_loop(0, n - 4, third, 0, unroll=unroll)


def limits(p3, d, pas, sol):
    amp = jnp.sqrt(jnp.maximum(-p3 * d, 0.0))
    lower = jnp.maximum(d - move_limit, floor_density)
    upper = jnp.minimum(d + move_limit, 1.0)
    low, high, now = (jnp.where(sol, 1.0, jnp.where(pas, floor_density, v)) for v in (lower, upper, d))
    return amp, low, high, now


FINE = 16
COARSE = POINTS // FINE


def table(n, nz, nx, amp, low, high, now, fine_s, vol, tgt, start):
    spacing = 2.0 * bracket_end / POINTS

    pair = 2
    for first in range(0, COARSE, pair):
        inverse = [math.exp(0.5 * (-bracket_end + spacing * FINE * i)) for i in range(first, first + pair)]

        def volume(j, acc):
            acc = list(acc)
            for w in range(nz // 8):
                at = slice(8 * w, 8 * w + 8)
                lo, hi, d = low[j, at], high[j, at], now[j, at]
                los, his = [lo * c for c in inverse], [hi * c for c in inverse]
                for i, c in enumerate(inverse):
                    acc[pair * FINE + i] = acc[pair * FINE + i] + d * c
                for f in range(FINE):
                    if first == 0:
                        t = amp[j, at] * math.exp(-0.5 * spacing * f)
                        fine_s[f, j, at] = t
                    else:
                        t = fine_s[f, j, at]
                    for i in range(pair):
                        acc[i * FINE + f] = acc[i * FINE + f] + jnp.minimum(jnp.maximum(t, los[i]), his[i])
            return tuple(acc)

        places = [(vol, 8 * (first * FINE + e)) for e in range(pair * FINE)]
        places += [(tgt, 8 * (first + i)) for i in range(pair)]
        if start is None:
            begin = tuple(jnp.zeros((8, nx), f32) for _ in places)
        else:
            begin = tuple((start[0] if ref is vol else start[1])[at : at + 8] for ref, at in places)
        acc = lax.fori_loop(0, n, volume, begin, unroll=2)
        for (ref, at), value in zip(places, acc):
            ref[at : at + 8] = value


def inner_kernel(flags, src, rim, dens, passive, solid, amp, low, high, vol, tgt, s_s, d_s, now_s, fine_s):
    ny, nz, nx = dens.shape
    s_s[...] = src[0 : ny - 1]

    def fix(y, _):
        put_rim(s_s, y, rim[y], nz)
        return 0

    lax.fori_loop(0, ny - 1, fix, 0, unroll=5)

    def finish(j, p3):
        y = j + 2
        amp[j], low[j], high[j], now_s[j] = limits(p3, dens[y], passive[y] == 1, solid[y] == 1)

    filter_block(s_s, d_s, ny - 1, (flags[2], flags[3]), None, finish, 4)
    table(ny - 5, nz, nx, amp, low, high, now_s, fine_s, vol, tgt, None)


def inner_call(flags, src, rim, dens, passive, solid):
    ny, nz, nx = dens.shape
    field = jax.ShapeDtypeStruct((ny - 5, nz, nx), f32)
    return pl.pallas_call(
        inner_kernel,
        in_specs=[SMEM] + [VMEM] * 5,
        out_shape=(
            field,
            field,
            field,
            jax.ShapeDtypeStruct((8 * POINTS, nx), f32),
            jax.ShapeDtypeStruct((8 * COARSE, nx), f32),
        ),
        scratch_shapes=[
            pltpu.VMEM((ny - 1, nz + 2 * OFF, nx), f32),
            pltpu.VMEM((ny - 3, nz + 2 * OFF, nx), f32),
            pltpu.VMEM((ny - 5, nz, nx), f32),
            pltpu.VMEM((FINE, ny - 5, nz, nx), f32),
        ],
        compiler_params=pltpu.CompilerParams(vmem_limit_bytes=24 * 2**20),
        cost_estimate=estimate(9),
        name="filter_inner",
    )(flags, src, rim, dens, passive, solid)


def outer_kernel(
    flags, src, rim, nodes, got_even, got_odd, mat, dens, passive, solid, vol_i, tgt_i,
    amp, low, high, excess, s_s, d_s, now_s, fine_s, vol, tgt, below, above, *work,
):
    ny, nz, nx = dens.shape
    odd = flags[4] == 1
    below[...] = jnp.where(odd, got_even[...], got_odd[...])
    above[...] = jnp.where(odd, got_odd[...], got_even[...])
    half = 2 * (nz + 8)

    def window(ref, i):
        return ref[half + 8 * i : half + 8 * i + 8]

    work[1][...] = jnp.zeros_like(work[1])
    prepare(lambda i: [(window(below, i), None), (nodes[1, i], None)], 0, work)
    prepare(lambda i: [(nodes[0, i], None), (window(above, i), None)], 1, work)
    corner = energy_rows(0, mat, work, jnp.concatenate([window(below, 9), nodes[1, 9]], axis=0))
    for b, ref in enumerate((below, above)):
        for j in range(2):
            at = j if b == 0 else 5 + j
            start = j * (nz + 8)
            s_s[b, at, 0:OFF] = jnp.zeros((OFF, nx), f32)
            s_s[b, at, OFF : OFF + nz] = ref[start : start + nz]
            s_s[b, at, OFF + nz :] = jnp.zeros((OFF, nx), f32)
            put_rim(s_s.at[b], at, ref[start + nz : start + nz + 8], nz)
    for j in range(4):
        s_s[0, 2 + j] = src[j]
        put_rim(s_s.at[0], 2 + j, rim[j], nz)
    for j in range(5):
        s_s[1, j] = src[ny - 5 + j]
        put_rim(s_s.at[1], j, rim[ny - 5 + j], nz)
    put_rim(s_s.at[0], 1, corner[0:8], nz)
    put_rim(s_s.at[1], 4, corner[8:16], nz)
    for b in range(2):
        y0 = 0 if b == 0 else ny - 3

        def finish(j, p3):
            y = y0 + j
            at = 2 * b + j
            amp[at], low[at], high[at], now_s[at] = limits(p3, dens[y], passive[y] == 1, solid[y] == 1)

        edges = (flags[0], 1) if b == 0 else (1, flags[1])
        filter_block(s_s.at[b], d_s.at[b], 6 + b, (flags[2], flags[3]), edges, finish, True)
    table(5, nz, nx, amp, low, high, now_s, fine_s, vol, tgt, (vol_i, tgt_i))

    def lanes(ref, count):
        total = ref[pl.ds(0, count, stride=8), :]
        for s in range(1, 8):
            total = total + ref[pl.ds(s, count, stride=8), :]
        return total

    volumes, targets = lanes(vol, POINTS), lanes(tgt, COARSE)
    over = [volumes[FINE * i : FINE * i + FINE] - targets[i : i + 1] for i in range(COARSE)]
    excess[...] = jnp.sum(jnp.transpose(jnp.concatenate(over, axis=0)), axis=0, keepdims=True)


def outer_call(flags, src, rim, nodes, got_even, got_odd, mat, dens, passive, solid, vol_i, tgt_i):
    ny, nz, nx = dens.shape
    rows = nz + 2 * OFF
    field = jax.ShapeDtypeStruct((5, nz, nx), f32)
    return pl.pallas_call(
        outer_kernel,
        in_specs=[SMEM] + [VMEM] * 11,
        out_shape=(field, field, field, jax.ShapeDtypeStruct((1, POINTS), f32)),
        scratch_shapes=[
            pltpu.VMEM((2, 7, rows, nx), f32),
            pltpu.VMEM((2, 5, rows, nx), f32),
            pltpu.VMEM((5, nz, nx), f32),
            pltpu.VMEM((FINE, 5, nz, nx), f32),
            pltpu.VMEM((8 * POINTS, nx), f32),
            pltpu.VMEM((8 * COARSE, nx), f32),
            pltpu.VMEM(got_odd.shape, f32),
            pltpu.VMEM(got_odd.shape, f32),
        ]
        + workspace(2, 2, nx),
        compiler_params=pltpu.CompilerParams(vmem_limit_bytes=20 * 2**20),
        cost_estimate=estimate(3),
        name="filter_outer",
    )(flags, src, rim, nodes, got_even, got_odd, mat, dens, passive, solid, vol_i, tgt_i)


def update_kernel(tables, amp_i, low_i, high_i, amp_o, low_o, high_o, new, logm):
    inner = amp_i.shape[0]
    nx = amp_i.shape[-1]
    total = jnp.sum(tables[...], axis=0, keepdims=True)
    lane = lax.broadcasted_iota(jnp.int32, total.shape, 1)
    above = jnp.where((total > 0.0) & (lane > 0), 1.0, 0.0)
    middle = -bracket_end + (2.0 * bracket_end / POINTS) * (jnp.sum(above) + 0.5)
    logm[0] = middle
    scale = jnp.exp(jnp.full((1, nx), -0.5 * middle, f32))

    def new_row(amp, low, high):
        return jnp.minimum(jnp.maximum(amp * scale, low), high)

    def body(j, _):
        new[j + 2] = new_row(amp_i[j], low_i[j], high_i[j])
        return 0

    lax.fori_loop(0, inner, body, 0)
    for j in range(5):
        new[j if j < 2 else inner + j] = new_row(amp_o[j], low_o[j], high_o[j])


def update_call(tables, inner, outer):
    n, nz, nx = inner[0].shape
    return pl.pallas_call(
        update_kernel,
        in_specs=[VMEM] * 7,
        out_specs=(VMEM, SMEM),
        out_shape=(jax.ShapeDtypeStruct((n + 5, nz, nx), f32), jax.ShapeDtypeStruct((1,), f32)),
        compiler_params=pltpu.CompilerParams(vmem_limit_bytes=8 * 2**20),
        cost_estimate=estimate(1),
        name="update",
    )(tables, *inner, *outer)


def to_lower(value, axis):
    count = lax.axis_size(axis)
    return lax.ppermute(value, axis, [(i + 1, i) for i in range(count - 1)])


def swap(value, axis, start):
    pairs = []
    for i in range(start, lax.axis_size(axis) - 1, 2):
        pairs += [(i, i + 1), (i + 1, i)]
    return lax.ppermute(value, axis, pairs)


def on_device(displacement, density, passive, solid, stiffness):
    ny, nz, nx = density.shape
    gy, gz = lax.axis_size("gy"), lax.axis_size("gz")
    iy, iz = lax.axis_index("gy"), lax.axis_index("gz")
    flags = jnp.stack([iy > 0, iy < gy - 1, iz > 0, iz < gz - 1, iy % 2 == 1, iz % 2 == 1]).astype(jnp.int32)

    disp_hbm = pltpu.with_memory_space_constraint(displacement, pltpu.HBM)
    dens_hbm = pltpu.with_memory_space_constraint(density, pltpu.HBM)
    stiff_hbm = pltpu.with_memory_space_constraint(stiffness, pltpu.HBM)

    fy = to_lower(face_call(disp_hbm), "gy")
    disp, dens, mat, mat_y, ends, up, down, z_even, z_odd = ends_call(flags, disp_hbm, dens_hbm, stiff_hbm)

    z_got_even = swap(z_even, "gz", 0)
    z_got_odd = swap(z_odd, "gz", 1)
    src = middle_call(disp, dens, fy, mat, ends)
    rim, nodes, msg_even, msg_odd = rim_call(flags, z_got_even, z_got_odd, up, down, disp, dens, mat_y, src)

    got_even = swap(msg_even, "gy", 0)
    got_odd = swap(msg_odd, "gy", 1)
    *inner, vol, tgt = inner_call(flags, src, rim, dens, passive, solid)
    *outer, excess = outer_call(flags, src, rim, nodes, got_even, got_odd, mat, dens, passive, solid, vol, tgt)

    everyone = jnp.broadcast_to(excess, (gz * gy, POINTS))
    tables = lax.all_to_all(everyone, ("gz", "gy"), 0, 0, tiled=True)
    new, logm = update_call(tables, inner, outer)
    return new, logm.reshape(())


def solution(mesh):
    placed = (
        P(None, "gy", "gz", None),
        P("gy", "gz", None),
        P("gy", "gz", None),
        P("gy", "gz", None),
        P(),
    )
    return jax.shard_map(
        on_device, mesh=mesh, in_specs=placed, out_specs=(P("gy", "gz", None), P()), check_vma=False
    )
```

```python
import math

import jax
import jax.numpy as jnp
from jax import lax
from jax.experimental import pallas as pl
from jax.experimental.pallas import tpu as pltpu
from jax.sharding import PartitionSpec as P

ITERS = 8
POINTS = 2**ITERS
OFF = 8

smoothing = 0.52
move_limit = 0.2
floor_density = 0.001
bracket_end = 12.0

f32 = jnp.float32
bf16 = jnp.bfloat16
VMEM = pl.BlockSpec(memory_space=pltpu.VMEM)
SMEM = pl.BlockSpec(memory_space=pltpu.SMEM)
HBM = pl.BlockSpec(memory_space=pltpu.HBM)


def cheb_weights():
    spectrum_top = 1.0 + 12.0 * smoothing
    centre_value = (spectrum_top + 1.0) / 2.0
    half_width = (spectrum_top - 1.0) / 2.0
    ratio_value = centre_value / half_width
    first_rho = 1.0 / ratio_value
    second_rho = 1.0 / (2.0 * ratio_value - first_rho)
    third_rho = 1.0 / (2.0 * ratio_value - second_rho)
    return (
        centre_value,
        second_rho * first_rho,
        2.0 * second_rho / half_width,
        third_rho * second_rho,
        2.0 * third_rho / half_width,
    )


def filter_weights():
    t, w1, w2, w3, w4 = cheb_weights()
    diag = 1.0 + 6.0 * smoothing
    alpha = w1 / t + w2 * (1.0 - diag / t)
    beta = w2 * smoothing / t
    gamma = 1.0 / t - w4 * w1 / (t * w2)
    delta = 1.0 + w3 + w4 / w2 - w4 * diag
    eps = w4 * smoothing
    return alpha, beta, gamma, delta, eps


def lane_up(v):
    n = v.shape[-1]
    lane = lax.broadcasted_iota(jnp.int32, v.shape, v.ndim - 1)
    return jnp.where(lane < n - 1, pltpu.roll(v, n - 1, v.ndim - 1), 0.0)


def lane_down(v):
    n = v.shape[-1]
    lane = lax.broadcasted_iota(jnp.int32, v.shape, v.ndim - 1)
    return jnp.where(lane > 0, pltpu.roll(v, 1, v.ndim - 1), 0.0)


def estimate(us):
    return pl.CostEstimate(flops=int(us * 1e9), bytes_accessed=1 << 20, transcendentals=0)


def build_matrices(k, mats):
    shape = (24, 128)
    col = lax.broadcasted_iota(jnp.int32, shape, 1)
    row = lax.broadcasted_iota(jnp.int32, shape, 0)
    main = col < 96
    q = jnp.where(main, jnp.where(col >= 48, 1, 0), jnp.where(col >= 104, 1, 0))
    m = col - 48 * q
    e = col - 96 - 8 * q
    c = jnp.where(main, m >> 4, e >> 1)
    dx = jnp.where(main, (m >> 3) & 1, e & 1)
    valid = main | (e < 6)
    picks = []
    for _, plane, band in mats:
        dof0 = 3 * (plane * q + dx) + c
        picks.append(jnp.where(main & (row == dof0), 1.0, 0.0))
        picks.append(jnp.where(valid & (row == dof0 + 3 * band), 1.0, 0.0))
    picked = jnp.dot(
        k, jnp.concatenate(picks, axis=1), precision=lax.Precision.HIGHEST, preferred_element_type=f32
    )
    col8 = lax.broadcasted_iota(jnp.int32, (8, 128), 1)
    row8 = lax.broadcasted_iota(jnp.int32, (8, 128), 0)
    main8 = col8 < 96
    rc = col8 & 7
    m0 = main8 & (rc == row8)
    m1 = jnp.where(main8, rc, 8) == row8 + 1
    for n, (mat, plane, band) in enumerate(mats):
        k0 = picked[:, 256 * n : 256 * n + 128]
        k1 = picked[:, 256 * n + 128 : 256 * n + 256]
        rows = []
        for b in range(2):
            for q_ in range(2):
                for c_ in range(3):
                    for dx_ in range(2):
                        r = 3 * (plane * q_ + band * b + dx_) + c_
                        rows.append(jnp.where(m0, k0[r : r + 1], 0.0) + jnp.where(m1, k1[r : r + 1], 0.0))
        full = jnp.concatenate(rows, axis=0)
        hi = full.astype(bf16)
        lo = (full - hi.astype(f32)).astype(bf16)
        mat[:, 0:112] = hi[:, 0:112]
        mat[:, 112:224] = lo[:, 0:112]


def prepare(segments, p, work):
    main_s, ext_s, mul_s = work
    for l in range(3):
        for c in range(3):
            w0 = 0
            for u, x in segments(3 * l + c):
                size, nx = u.shape
                n = size // 8
                last = lax.broadcasted_iota(jnp.int32, u.shape, 0) == size - 1
                both = (u, lane_up(u))
                after = (None, None) if x is None else (x, lane_up(x))
                for w in range(n):
                    sl = slice(8 * w, 8 * w + 8)
                    main_s[p, l, 16 * c : 16 * c + 16, (w0 + w) * nx : (w0 + w + 1) * nx] = jnp.concatenate(
                        [both[0][sl], both[1][sl]], axis=0
                    ).astype(bf16)
                for dx in range(2):
                    v, vx = both[dx], after[dx]
                    k = 2 * c + dx
                    for w in range(n):
                        nxt = v[8 * w + 8 : 8 * w + 9] if w < n - 1 else vx
                        if nxt is not None:
                            ext_s[p, l, k : k + 1, (w0 + w) * nx : (w0 + w + 1) * nx] = nxt
                    m = 2.0 * v - v.astype(bf16).astype(f32)
                    mx = 0.0 if vx is None else jnp.broadcast_to(2.0 * vx - vx.astype(bf16).astype(f32), v.shape)
                    at = slice(8 * w0, 8 * (w0 + n))
                    mul_s[p, l, k, 0, at] = m
                    mul_s[p, l, k, 1, at] = jnp.where(last, mx, pltpu.roll(m, size - 1, 0))
                w0 += n


def energy_rows(p, mat, work, density):
    main_s, ext_s, mul_s = work
    rows, nx = density.shape
    count = rows // 8
    acc = [None] * count
    for l in range(3):
        ext = jnp.concatenate([ext_s[p, l], ext_s[p + 1, l]], axis=0).astype(bf16)
        one = jnp.concatenate([main_s[p, l], main_s[p + 1, l], ext], axis=0)
        force = jnp.dot(mat[...], jnp.concatenate([one, one], axis=0), preferred_element_type=f32)
        i = 0
        for b in range(2):
            for q in range(2):
                for k in range(6):
                    for w in range(count):
                        at = slice(8 * w, 8 * w + 8)
                        term = force[8 * i : 8 * i + 8, w * nx : (w + 1) * nx] * mul_s[p + q, l, k, b, at]
                        acc[w] = term if acc[w] is None else acc[w] + term
                    i += 1
    return density * (-3.0 * density * density * jnp.concatenate(acc, axis=0))


def workspace(planes, windows, nx):
    return [
        pltpu.VMEM((planes, 3, 48, windows * nx), bf16),
        pltpu.VMEM((planes, 3, 8, windows * nx), f32),
        pltpu.VMEM((planes, 3, 6, 2, 8 * windows, nx), f32),
    ]


def sweep(rows, segments, put, work):
    work[1][...] = jnp.zeros_like(work[1])
    for p in range(2):
        prepare(segments(p), p, work)

    def body(y, _):
        put(y)
        prepare(segments(y + 2), y + 2, work)
        return 0

    lax.fori_loop(0, rows - 1, body, 0, unroll=2)
    put(rows - 1)


def face_kernel(disp, face, sem):
    copy = pltpu.make_async_copy(disp.at[:, 0], face, sem)
    copy.start()
    copy.wait()


def face_call(disp):
    _, _, nz, nx = disp.shape
    return pl.pallas_call(
        face_kernel,
        in_specs=[HBM],
        out_shape=jax.ShapeDtypeStruct((9, nz, nx), f32),
        scratch_shapes=[pltpu.SemaphoreType.DMA],
        compiler_params=pltpu.CompilerParams(vmem_limit_bytes=2**20),
        name="face",
    )(disp)


def extra(ref, row):
    ny = ref.shape[1]
    return 11 + row // ny, slice(row % ny, row % ny + 1)


def load_kernel(disp_h, dens_h, stiff, disp, dens, mat, mat_y, stiff_s, sems):
    copies = [pltpu.make_async_copy(stiff, stiff_s, sems.at[0])]
    for l in range(3):
        part = pl.ds(3 * l, 3)
        copies.append(pltpu.make_async_copy(disp_h.at[part], disp.at[part], sems.at[1 + l]))
    copies.append(pltpu.make_async_copy(dens_h, dens, sems.at[4]))
    for copy in copies:
        copy.start()
    copies[0].wait()
    build_matrices(stiff_s[...], ((mat, 4, 2), (mat_y, 2, 4)))
    for copy in copies[1:]:
        copy.wait()


def load_call(disp, dens, stiff):
    matrix = jax.ShapeDtypeStruct((192, 224), bf16)
    return pl.pallas_call(
        load_kernel,
        in_specs=[HBM, HBM, HBM],
        out_shape=(
            jax.ShapeDtypeStruct(disp.shape, f32),
            jax.ShapeDtypeStruct(dens.shape, f32),
            matrix,
            matrix,
        ),
        scratch_shapes=[pltpu.VMEM((24, 24), f32), pltpu.SemaphoreType.DMA((5,))],
        compiler_params=pltpu.CompilerParams(vmem_limit_bytes=16 * 2**20),
        cost_estimate=estimate(2),
        name="load",
    )(disp, dens, stiff)


def ends_kernel(flags, disp, dens, mat, ends, up, down, msg_even, msg_odd, *work):
    _, ny, nz, nx = disp.shape

    def segments(p):
        return lambda i: [(disp[i, p, 0:8], disp[i, p, 8:9]), (disp[i, p, nz - 8 : nz], None)]

    def put(y):
        d = jnp.concatenate([dens[y, 0:8], dens[y, nz - 8 : nz]], axis=0)
        ends[y] = energy_rows(y, mat, work, d)

    sweep(ny - 1, segments, put, work)
    for ref in (up, down):
        ref[9:] = jnp.zeros((ref.shape[0] - 9, ny, nx), f32)
    for y in range(ny):
        row = slice(y, y + 1)
        for i in range(9):
            up[i, row] = disp[i, y, nz - 1 : nz]
            down[i, row] = disp[i, y, 0:1]
        up[9, row] = dens[y, nz - 1 : nz]
        if y < ny - 1:
            up[10, row] = ends[y, 14:15]
            down[9, row] = ends[y, 0:1]
            down[10, row] = ends[y, 1:2]
    for n, y in enumerate((0, ny - 1)):
        for i in range(9):
            up[extra(up, 9 * n + i)] = disp[i, y, nz - 2 : nz - 1]
            down[extra(down, 9 * n + i)] = disp[i, y, 1:2]
            down[extra(down, 18 + 9 * n + i)] = disp[i, y, 2:3]
    up[extra(up, 36)] = dens[ny - 1, nz - 2 : nz - 1]
    down[extra(down, 36)] = dens[ny - 1, 0:1]
    down[extra(down, 37)] = dens[ny - 1, 1:2]
    odd = flags[5] == 1
    msg_even[...] = jnp.where(odd, down[...], up[...])
    msg_odd[...] = jnp.where(odd, up[...], down[...])


def ends_call(flags, disp, dens, mat):
    _, ny, nz, nx = disp.shape
    message = jax.ShapeDtypeStruct((11 + -(-38 // ny), ny, nx), f32)
    return pl.pallas_call(
        ends_kernel,
        in_specs=[SMEM] + [VMEM] * 3,
        out_shape=(jax.ShapeDtypeStruct((ny, 16, nx), f32),) + (message,) * 4,
        scratch_shapes=workspace(ny, 2, nx),
        compiler_params=pltpu.CompilerParams(vmem_limit_bytes=16 * 2**20),
        cost_estimate=estimate(4),
        name="energy_ends",
    )(flags, disp, dens, mat)


def middle_kernel(disp, dens, fy, mat, ends, src, *work):
    _, ny, nz, nx = disp.shape
    work, last = work[:3], work[3:]

    def segments(p):
        return lambda i: [(disp[i, p, 8 : nz - 8], disp[i, p, nz - 8 : nz - 7])]

    def frame(y):
        src[y, 0:OFF] = jnp.zeros((OFF, nx), f32)
        src[y, OFF + nz :] = jnp.zeros((src.shape[1] - OFF - nz, nx), f32)

    def put(y):
        frame(y)
        src[y, OFF : OFF + 8] = ends[y, 0:8]
        src[y, OFF + 8 : OFF + nz - 8] = energy_rows(y, mat, work, dens[y, 8 : nz - 8])
        src[y, OFF + nz - 8 : OFF + nz] = ends[y, 8:16]

    sweep(ny - 1, segments, put, work)
    last[1][...] = jnp.zeros_like(last[1])
    prepare(lambda i: [(disp[i, ny - 1], None)], 0, last)
    prepare(lambda i: [(fy[i], None)], 1, last)
    frame(ny - 1)
    src[ny - 1, OFF : OFF + nz] = energy_rows(0, mat, last, dens[ny - 1])


def middle_call(disp, dens, fy, mat, ends):
    _, ny, nz, nx = disp.shape
    return pl.pallas_call(
        middle_kernel,
        in_specs=[VMEM] * 5,
        out_shape=jax.ShapeDtypeStruct((ny, nz + 2 * OFF, nx), f32),
        scratch_shapes=workspace(ny, nz // 8 - 2, nx) + workspace(2, nz // 8, nx),
        compiler_params=pltpu.CompilerParams(vmem_limit_bytes=24 * 2**20),
        cost_estimate=estimate(4),
        name="energy_middle",
    )(disp, dens, fy, mat, ends)


def rim_kernel(
    flags, got_even, got_odd, up, down, disp, dens, mat_y, src,
    rim, nodes, msg_even, msg_odd, low_s, high_s, t_s, *work,
):
    ny, rows, nx = src.shape
    nz = rows - 2 * OFF
    odd = flags[5] == 1
    low_s[...] = jnp.where(odd, got_even[...], got_odd[...])
    high_s[...] = jnp.where(odd, got_odd[...], got_even[...])
    work[1][...] = jnp.zeros_like(work[1])
    prepare(lambda i: [(low_s[i], None), (up[i], None)], 0, work)
    prepare(lambda i: [(down[i], None), (high_s[i], None)], 1, work)
    s = energy_rows(0, mat_y, work, jnp.concatenate([low_s[9], up[9]], axis=0))
    columns = ((0, low_s[10]), (1, s[0:ny]), (3, s[ny : 2 * ny]), (4, high_s[9]), (5, high_s[10]))
    for y in range(ny):
        rim[y] = jnp.zeros((8, nx), f32)
        for r, column in columns:
            rim[y, r : r + 1] = column[y : y + 1]
    half = 2 * (nz + 8)
    zero = jnp.zeros((1, nx), f32)
    for n, y in enumerate((0, ny - 1)):
        row = slice(y, y + 1)
        for i in range(9):
            window = jnp.concatenate(
                [
                    low_s[extra(low_s, 9 * n + i)],
                    low_s[i, row],
                    disp[i, y, 0:1],
                    disp[i, y, nz - 1 : nz],
                    high_s[i, row],
                    high_s[extra(high_s, 9 * n + i)],
                    high_s[extra(high_s, 18 + 9 * n + i)],
                    zero,
                ],
                axis=0,
            )
            nodes[n, i] = window
            t_s[n, half + 8 * i : half + 8 * i + 8] = window
        nodes[n, 9] = jnp.concatenate(
            [
                low_s[extra(low_s, 36)],
                low_s[9, ny - 1 : ny],
                zero,
                dens[ny - 1, nz - 1 : nz],
                high_s[extra(high_s, 36)],
                high_s[extra(high_s, 37)],
                zero,
                zero,
            ],
            axis=0,
        )
        t_s[n, half + 72 : half + 80] = nodes[n, 9]
        for j in range(2):
            at = j * (nz + 8)
            yy = j if n == 0 else ny - 2 + j
            t_s[n, at : at + nz] = src[yy, OFF : OFF + nz]
            t_s[n, at + nz : at + nz + 8] = rim[yy]
    odd = flags[4] == 1
    msg_even[...] = jnp.where(odd, t_s[0], t_s[1])
    msg_odd[...] = jnp.where(odd, t_s[1], t_s[0])


def put_rim(s, y, rim, nz):
    s[y, OFF - 2 : OFF] = rim[0:2]
    s[y, OFF + nz - 1 : OFF + nz + 2] = rim[3:6]


def rim_call(flags, got_even, got_odd, up, down, disp, dens, mat_y, src):
    ny, rows, nx = src.shape
    nz = rows - 2 * OFF
    size = 2 * (nz + 8) + 80
    return pl.pallas_call(
        rim_kernel,
        in_specs=[SMEM] + [VMEM] * 8,
        out_shape=(
            jax.ShapeDtypeStruct((ny, 8, nx), f32),
            jax.ShapeDtypeStruct((2, 10, 8, nx), f32),
            jax.ShapeDtypeStruct((size, nx), f32),
            jax.ShapeDtypeStruct((size, nx), f32),
        ),
        scratch_shapes=[
            pltpu.VMEM(up.shape, f32),
            pltpu.VMEM(up.shape, f32),
            pltpu.VMEM((2, size, nx), f32),
        ]
        + workspace(2, 2 * (ny // 8), nx),
        compiler_params=pltpu.CompilerParams(vmem_limit_bytes=16 * 2**20),
        cost_estimate=estimate(2),
        name="energy_rim",
    )(flags, got_even, got_odd, up, down, disp, dens, mat_y, src)


def filter_block(s_s, d_s, n, z_edges, y_edges, finish, unroll):
    rows, nx = s_s.shape[1:]
    nz = rows - 2 * OFF
    alpha, beta, gamma, delta, eps = filter_weights()
    row = lax.broadcasted_iota(jnp.int32, (rows, nx), 0)
    keep = jnp.where(row < OFF, z_edges[0], jnp.where(row >= OFF + nz, z_edges[1], 1)) == 1

    def beside(v):
        return pltpu.roll(v, 1, 0) + pltpu.roll(v, rows - 1, 0) + lane_up(v) + lane_down(v)

    def second(j, _):
        c = s_s[j + 1]
        d2 = alpha * c + beta * (beside(c) + s_s[j] + s_s[j + 2])
        ok = keep
        if y_edges is not None:
            ok = keep & (jnp.where(j == 0, y_edges[0], jnp.where(j == n - 3, y_edges[1], 1)) == 1)
        d_s[j] = jnp.where(ok, d2, 0.0)
        return 0

    def third(j, _):
        d2 = d_s[j + 1]
        p3 = gamma * s_s[j + 2] + delta * d2 + eps * (beside(d2) + d_s[j] + d_s[j + 2])
        finish(j, p3[OFF : OFF + nz])
        return 0

    lax.fori_loop(0, n - 2, second, 0, unroll=unroll)
    lax.fori_loop(0, n - 4, third, 0, unroll=unroll)


def limits(p3, d, pas, sol):
    amp = jnp.sqrt(jnp.maximum(-p3 * d, 0.0))
    lower = jnp.maximum(d - move_limit, floor_density)
    upper = jnp.minimum(d + move_limit, 1.0)
    low, high, now = (jnp.where(sol, 1.0, jnp.where(pas, floor_density, v)) for v in (lower, upper, d))
    return amp, low, high, now


FINE = 16
COARSE = POINTS // FINE


def table(n, nz, nx, amp, low, high, now, fine_s, vol, tgt, start, unroll):
    spacing = 2.0 * bracket_end / POINTS

    pair = 2
    for first in range(0, COARSE, pair):
        inverse = [math.exp(0.5 * (-bracket_end + spacing * FINE * i)) for i in range(first, first + pair)]

        def volume(j, acc):
            acc = list(acc)
            for w in range(nz // 8):
                at = slice(8 * w, 8 * w + 8)
                lo, hi, d = low[j, at], high[j, at], now[j, at]
                los, his = [lo * c for c in inverse], [hi * c for c in inverse]
                for i, c in enumerate(inverse):
                    acc[pair * FINE + i] = acc[pair * FINE + i] + d * c
                for f in range(FINE):
                    if first == 0:
                        t = amp[j, at] * math.exp(-0.5 * spacing * f)
                        fine_s[f, j, at] = t
                    else:
                        t = fine_s[f, j, at]
                    for i in range(pair):
                        acc[i * FINE + f] = acc[i * FINE + f] + jnp.minimum(jnp.maximum(t, los[i]), his[i])
            return tuple(acc)

        places = [(vol, 8 * (first * FINE + e)) for e in range(pair * FINE)]
        places += [(tgt, 8 * (first + i)) for i in range(pair)]
        if start is None:
            begin = tuple(jnp.zeros((8, nx), f32) for _ in places)
        else:
            begin = tuple((start[0] if ref is vol else start[1])[at : at + 8] for ref, at in places)
        acc = lax.fori_loop(0, n, volume, begin, unroll=unroll)
        for (ref, at), value in zip(places, acc):
            ref[at : at + 8] = value


def inner_kernel(flags, src, rim, dens, passive, solid, amp, low, high, vol, tgt, s_s, d_s, now_s, fine_s):
    ny, nz, nx = dens.shape
    s_s[...] = src[0 : ny - 1]

    def fix(y, _):
        put_rim(s_s, y, rim[y], nz)
        return 0

    lax.fori_loop(0, ny - 1, fix, 0, unroll=5)

    def finish(j, p3):
        y = j + 2
        amp[j], low[j], high[j], now_s[j] = limits(p3, dens[y], passive[y] == 1, solid[y] == 1)

    filter_block(s_s, d_s, ny - 1, (flags[2], flags[3]), None, finish, 4)
    table(ny - 5, nz, nx, amp, low, high, now_s, fine_s, vol, tgt, None, 2)


def inner_call(flags, src, rim, dens, passive, solid):
    ny, nz, nx = dens.shape
    field = jax.ShapeDtypeStruct((ny - 5, nz, nx), f32)
    return pl.pallas_call(
        inner_kernel,
        in_specs=[SMEM] + [VMEM] * 5,
        out_shape=(
            field,
            field,
            field,
            jax.ShapeDtypeStruct((8 * POINTS, nx), f32),
            jax.ShapeDtypeStruct((8 * COARSE, nx), f32),
        ),
        scratch_shapes=[
            pltpu.VMEM((ny - 1, nz + 2 * OFF, nx), f32),
            pltpu.VMEM((ny - 3, nz + 2 * OFF, nx), f32),
            pltpu.VMEM((ny - 5, nz, nx), f32),
            pltpu.VMEM((FINE, ny - 5, nz, nx), f32),
        ],
        compiler_params=pltpu.CompilerParams(vmem_limit_bytes=24 * 2**20),
        cost_estimate=estimate(9),
        name="filter_inner",
    )(flags, src, rim, dens, passive, solid)


def outer_kernel(
    flags, src, rim, nodes, got_even, got_odd, mat, dens, passive, solid, vol_i, tgt_i,
    amp, low, high, excess, s_s, d_s, now_s, fine_s, vol, tgt, below, above, *work,
):
    ny, nz, nx = dens.shape
    odd = flags[4] == 1
    below[...] = jnp.where(odd, got_even[...], got_odd[...])
    above[...] = jnp.where(odd, got_odd[...], got_even[...])
    half = 2 * (nz + 8)

    def window(ref, i):
        return ref[half + 8 * i : half + 8 * i + 8]

    work[1][...] = jnp.zeros_like(work[1])
    prepare(lambda i: [(window(below, i), None), (nodes[1, i], None)], 0, work)
    prepare(lambda i: [(nodes[0, i], None), (window(above, i), None)], 1, work)
    corner = energy_rows(0, mat, work, jnp.concatenate([window(below, 9), nodes[1, 9]], axis=0))
    for b, ref in enumerate((below, above)):
        for j in range(2):
            at = j if b == 0 else 5 + j
            start = j * (nz + 8)
            s_s[b, at, 0:OFF] = jnp.zeros((OFF, nx), f32)
            s_s[b, at, OFF : OFF + nz] = ref[start : start + nz]
            s_s[b, at, OFF + nz :] = jnp.zeros((OFF, nx), f32)
            put_rim(s_s.at[b], at, ref[start + nz : start + nz + 8], nz)
    for j in range(4):
        s_s[0, 2 + j] = src[j]
        put_rim(s_s.at[0], 2 + j, rim[j], nz)
    for j in range(5):
        s_s[1, j] = src[ny - 5 + j]
        put_rim(s_s.at[1], j, rim[ny - 5 + j], nz)
    put_rim(s_s.at[0], 1, corner[0:8], nz)
    put_rim(s_s.at[1], 4, corner[8:16], nz)
    for b in range(2):
        y0 = 0 if b == 0 else ny - 3

        def finish(j, p3):
            y = y0 + j
            at = 2 * b + j
            amp[at], low[at], high[at], now_s[at] = limits(p3, dens[y], passive[y] == 1, solid[y] == 1)

        edges = (flags[0], 1) if b == 0 else (1, flags[1])
        filter_block(s_s.at[b], d_s.at[b], 6 + b, (flags[2], flags[3]), edges, finish, True)
    table(5, nz, nx, amp, low, high, now_s, fine_s, vol, tgt, (vol_i, tgt_i), 2)

    def lanes(ref, count):
        total = ref[pl.ds(0, count, stride=8), :]
        for s in range(1, 8):
            total = total + ref[pl.ds(s, count, stride=8), :]
        return total

    volumes, targets = lanes(vol, POINTS), lanes(tgt, COARSE)
    over = [volumes[FINE * i : FINE * i + FINE] - targets[i : i + 1] for i in range(COARSE)]
    excess[...] = jnp.sum(jnp.transpose(jnp.concatenate(over, axis=0)), axis=0, keepdims=True)


def outer_call(flags, src, rim, nodes, got_even, got_odd, mat, dens, passive, solid, vol_i, tgt_i):
    ny, nz, nx = dens.shape
    rows = nz + 2 * OFF
    field = jax.ShapeDtypeStruct((5, nz, nx), f32)
    return pl.pallas_call(
        outer_kernel,
        in_specs=[SMEM] + [VMEM] * 11,
        out_shape=(field, field, field, jax.ShapeDtypeStruct((1, POINTS), f32)),
        scratch_shapes=[
            pltpu.VMEM((2, 7, rows, nx), f32),
            pltpu.VMEM((2, 5, rows, nx), f32),
            pltpu.VMEM((5, nz, nx), f32),
            pltpu.VMEM((FINE, 5, nz, nx), f32),
            pltpu.VMEM((8 * POINTS, nx), f32),
            pltpu.VMEM((8 * COARSE, nx), f32),
            pltpu.VMEM(got_odd.shape, f32),
            pltpu.VMEM(got_odd.shape, f32),
        ]
        + workspace(2, 2, nx),
        compiler_params=pltpu.CompilerParams(vmem_limit_bytes=20 * 2**20),
        cost_estimate=estimate(3),
        name="filter_outer",
    )(flags, src, rim, nodes, got_even, got_odd, mat, dens, passive, solid, vol_i, tgt_i)


def update_kernel(tables, amp_i, low_i, high_i, amp_o, low_o, high_o, new, logm):
    inner = amp_i.shape[0]
    nx = amp_i.shape[-1]
    total = jnp.sum(tables[...], axis=0, keepdims=True)
    lane = lax.broadcasted_iota(jnp.int32, total.shape, 1)
    above = jnp.where((total > 0.0) & (lane > 0), 1.0, 0.0)
    middle = -bracket_end + (2.0 * bracket_end / POINTS) * (jnp.sum(above) + 0.5)
    logm[0] = middle
    scale = jnp.exp(jnp.full((1, nx), -0.5 * middle, f32))

    def new_row(amp, low, high):
        return jnp.minimum(jnp.maximum(amp * scale, low), high)

    def body(j, _):
        new[j + 2] = new_row(amp_i[j], low_i[j], high_i[j])
        return 0

    lax.fori_loop(0, inner, body, 0)
    for j in range(5):
        new[j if j < 2 else inner + j] = new_row(amp_o[j], low_o[j], high_o[j])


def update_call(tables, inner, outer):
    n, nz, nx = inner[0].shape
    return pl.pallas_call(
        update_kernel,
        in_specs=[VMEM] * 7,
        out_specs=(VMEM, SMEM),
        out_shape=(jax.ShapeDtypeStruct((n + 5, nz, nx), f32), jax.ShapeDtypeStruct((1,), f32)),
        compiler_params=pltpu.CompilerParams(vmem_limit_bytes=8 * 2**20),
        cost_estimate=estimate(1),
        name="update",
    )(tables, *inner, *outer)


def to_lower(value, axis):
    count = lax.axis_size(axis)
    return lax.ppermute(value, axis, [(i + 1, i) for i in range(count - 1)])


def swap(value, axis, start):
    pairs = []
    for i in range(start, lax.axis_size(axis) - 1, 2):
        pairs += [(i, i + 1), (i + 1, i)]
    return lax.ppermute(value, axis, pairs)


def on_device(displacement, density, passive, solid, stiffness):
    ny, nz, nx = density.shape
    gy, gz = lax.axis_size("gy"), lax.axis_size("gz")
    iy, iz = lax.axis_index("gy"), lax.axis_index("gz")
    flags = jnp.stack([iy > 0, iy < gy - 1, iz > 0, iz < gz - 1, iy % 2 == 1, iz % 2 == 1]).astype(jnp.int32)

    disp_hbm = pltpu.with_memory_space_constraint(displacement, pltpu.HBM)
    dens_hbm = pltpu.with_memory_space_constraint(density, pltpu.HBM)
    stiff_hbm = pltpu.with_memory_space_constraint(stiffness, pltpu.HBM)

    fy = to_lower(face_call(disp_hbm), "gy")
    disp, dens, mat, mat_y = load_call(disp_hbm, dens_hbm, stiff_hbm)
    ends, up, down, z_even, z_odd = ends_call(flags, disp, dens, mat)

    z_got_even = swap(z_even, "gz", 0)
    z_got_odd = swap(z_odd, "gz", 1)
    src = middle_call(disp, dens, fy, mat, ends)
    rim, nodes, msg_even, msg_odd = rim_call(flags, z_got_even, z_got_odd, up, down, disp, dens, mat_y, src)

    got_even = swap(msg_even, "gy", 0)
    got_odd = swap(msg_odd, "gy", 1)
    *inner, vol, tgt = inner_call(flags, src, rim, dens, passive, solid)
    *outer, excess = outer_call(flags, src, rim, nodes, got_even, got_odd, mat, dens, passive, solid, vol, tgt)

    everyone = jnp.broadcast_to(excess, (gz * gy, POINTS))
    tables = lax.all_to_all(everyone, ("gz", "gy"), 0, 0, tiled=True)
    new, logm = update_call(tables, inner, outer)
    return new, logm.reshape(())


def solution(mesh):
    placed = (
        P(None, "gy", "gz", None),
        P("gy", "gz", None),
        P("gy", "gz", None),
        P("gy", "gz", None),
        P(),
    )
    return jax.shard_map(
        on_device, mesh=mesh, in_specs=placed, out_specs=(P("gy", "gz", None), P()), check_vma=False
    )
```

```python
import math

import jax
import jax.numpy as jnp
from jax import lax
from jax.experimental import pallas as pl
from jax.experimental.pallas import tpu as pltpu
from jax.sharding import PartitionSpec as P

ITERS = 8
POINTS = 2**ITERS
OFF = 8

smoothing = 0.52
move_limit = 0.2
floor_density = 0.001
bracket_end = 12.0

f32 = jnp.float32
bf16 = jnp.bfloat16
VMEM = pl.BlockSpec(memory_space=pltpu.VMEM)
SMEM = pl.BlockSpec(memory_space=pltpu.SMEM)
HBM = pl.BlockSpec(memory_space=pltpu.HBM)


def cheb_weights():
    spectrum_top = 1.0 + 12.0 * smoothing
    centre_value = (spectrum_top + 1.0) / 2.0
    half_width = (spectrum_top - 1.0) / 2.0
    ratio_value = centre_value / half_width
    first_rho = 1.0 / ratio_value
    second_rho = 1.0 / (2.0 * ratio_value - first_rho)
    third_rho = 1.0 / (2.0 * ratio_value - second_rho)
    return (
        centre_value,
        second_rho * first_rho,
        2.0 * second_rho / half_width,
        third_rho * second_rho,
        2.0 * third_rho / half_width,
    )


def filter_weights():
    t, w1, w2, w3, w4 = cheb_weights()
    diag = 1.0 + 6.0 * smoothing
    alpha = w1 / t + w2 * (1.0 - diag / t)
    beta = w2 * smoothing / t
    gamma = 1.0 / t - w4 * w1 / (t * w2)
    delta = 1.0 + w3 + w4 / w2 - w4 * diag
    eps = w4 * smoothing
    return alpha, beta, gamma, delta, eps


def lane_up(v):
    n = v.shape[-1]
    lane = lax.broadcasted_iota(jnp.int32, v.shape, v.ndim - 1)
    return jnp.where(lane < n - 1, pltpu.roll(v, n - 1, v.ndim - 1), 0.0)


def lane_down(v):
    n = v.shape[-1]
    lane = lax.broadcasted_iota(jnp.int32, v.shape, v.ndim - 1)
    return jnp.where(lane > 0, pltpu.roll(v, 1, v.ndim - 1), 0.0)


def estimate(us):
    return pl.CostEstimate(flops=int(us * 1e9), bytes_accessed=1 << 20, transcendentals=0)


def build_matrices(k, mats):
    shape = (24, 128)
    col = lax.broadcasted_iota(jnp.int32, shape, 1)
    row = lax.broadcasted_iota(jnp.int32, shape, 0)
    main = col < 96
    q = jnp.where(main, jnp.where(col >= 48, 1, 0), jnp.where(col >= 104, 1, 0))
    m = col - 48 * q
    e = col - 96 - 8 * q
    c = jnp.where(main, m >> 4, e >> 1)
    dx = jnp.where(main, (m >> 3) & 1, e & 1)
    valid = main | (e < 6)
    picks = []
    for _, plane, band in mats:
        dof0 = 3 * (plane * q + dx) + c
        picks.append(jnp.where(main & (row == dof0), 1.0, 0.0))
        picks.append(jnp.where(valid & (row == dof0 + 3 * band), 1.0, 0.0))
    picked = jnp.dot(
        k, jnp.concatenate(picks, axis=1), precision=lax.Precision.HIGHEST, preferred_element_type=f32
    )
    col8 = lax.broadcasted_iota(jnp.int32, (8, 128), 1)
    row8 = lax.broadcasted_iota(jnp.int32, (8, 128), 0)
    main8 = col8 < 96
    rc = col8 & 7
    m0 = main8 & (rc == row8)
    m1 = jnp.where(main8, rc, 8) == row8 + 1
    for n, (mat, plane, band) in enumerate(mats):
        k0 = picked[:, 256 * n : 256 * n + 128]
        k1 = picked[:, 256 * n + 128 : 256 * n + 256]
        rows = []
        for b in range(2):
            for q_ in range(2):
                for c_ in range(3):
                    for dx_ in range(2):
                        r = 3 * (plane * q_ + band * b + dx_) + c_
                        rows.append(jnp.where(m0, k0[r : r + 1], 0.0) + jnp.where(m1, k1[r : r + 1], 0.0))
        full = jnp.concatenate(rows, axis=0)
        hi = full.astype(bf16)
        lo = (full - hi.astype(f32)).astype(bf16)
        mat[:, 0:112] = hi[:, 0:112]
        mat[:, 112:224] = lo[:, 0:112]


def prepare(segments, p, work):
    main_s, ext_s, mul_s = work
    for l in range(3):
        for c in range(3):
            w0 = 0
            for u, x in segments(3 * l + c):
                size, nx = u.shape
                n = size // 8
                last = lax.broadcasted_iota(jnp.int32, u.shape, 0) == size - 1
                both = (u, lane_up(u))
                after = (None, None) if x is None else (x, lane_up(x))
                for w in range(n):
                    sl = slice(8 * w, 8 * w + 8)
                    main_s[p, l, 16 * c : 16 * c + 16, (w0 + w) * nx : (w0 + w + 1) * nx] = jnp.concatenate(
                        [both[0][sl], both[1][sl]], axis=0
                    ).astype(bf16)
                for dx in range(2):
                    v, vx = both[dx], after[dx]
                    k = 2 * c + dx
                    for w in range(n):
                        nxt = v[8 * w + 8 : 8 * w + 9] if w < n - 1 else vx
                        if nxt is not None:
                            ext_s[p, l, k : k + 1, (w0 + w) * nx : (w0 + w + 1) * nx] = nxt
                    m = 2.0 * v - v.astype(bf16).astype(f32)
                    mx = 0.0 if vx is None else jnp.broadcast_to(2.0 * vx - vx.astype(bf16).astype(f32), v.shape)
                    at = slice(8 * w0, 8 * (w0 + n))
                    mul_s[p, l, k, 0, at] = m
                    mul_s[p, l, k, 1, at] = jnp.where(last, mx, pltpu.roll(m, size - 1, 0))
                w0 += n


def energy_rows(p, mat, work, density):
    main_s, ext_s, mul_s = work
    rows, nx = density.shape
    count = rows // 8
    acc = [None] * count
    for l in range(3):
        ext = jnp.concatenate([ext_s[p, l], ext_s[p + 1, l]], axis=0).astype(bf16)
        one = jnp.concatenate([main_s[p, l], main_s[p + 1, l], ext], axis=0)
        force = jnp.dot(mat[...], jnp.concatenate([one, one], axis=0), preferred_element_type=f32)
        i = 0
        for b in range(2):
            for q in range(2):
                for k in range(6):
                    for w in range(count):
                        at = slice(8 * w, 8 * w + 8)
                        term = force[8 * i : 8 * i + 8, w * nx : (w + 1) * nx] * mul_s[p + q, l, k, b, at]
                        acc[w] = term if acc[w] is None else acc[w] + term
                    i += 1
    return density * (-3.0 * density * density * jnp.concatenate(acc, axis=0))


def workspace(planes, windows, nx):
    return [
        pltpu.VMEM((planes, 3, 48, windows * nx), bf16),
        pltpu.VMEM((planes, 3, 8, windows * nx), f32),
        pltpu.VMEM((planes, 3, 6, 2, 8 * windows, nx), f32),
    ]


def sweep(rows, segments, put, work):
    work[1][...] = jnp.zeros_like(work[1])
    for p in range(2):
        prepare(segments(p), p, work)

    def body(y, _):
        put(y)
        prepare(segments(y + 2), y + 2, work)
        return 0

    lax.fori_loop(0, rows - 1, body, 0, unroll=2)
    put(rows - 1)


def face_kernel(disp, face, sem):
    copy = pltpu.make_async_copy(disp.at[:, 0], face, sem)
    copy.start()
    copy.wait()


def face_call(disp):
    _, _, nz, nx = disp.shape
    return pl.pallas_call(
        face_kernel,
        in_specs=[HBM],
        out_shape=jax.ShapeDtypeStruct((9, nz, nx), f32),
        scratch_shapes=[pltpu.SemaphoreType.DMA],
        compiler_params=pltpu.CompilerParams(vmem_limit_bytes=2**20),
        name="face",
    )(disp)


def extra(ref, row):
    ny = ref.shape[1]
    return 11 + row // ny, slice(row % ny, row % ny + 1)


def load_kernel(disp_h, dens_h, stiff, disp, dens, mat, mat_y, stiff_s, sems):
    copies = [pltpu.make_async_copy(stiff, stiff_s, sems.at[0])]
    for l in range(3):
        part = pl.ds(3 * l, 3)
        copies.append(pltpu.make_async_copy(disp_h.at[part], disp.at[part], sems.at[1 + l]))
    copies.append(pltpu.make_async_copy(dens_h, dens, sems.at[4]))
    for copy in copies:
        copy.start()
    copies[0].wait()
    build_matrices(stiff_s[...], ((mat, 4, 2), (mat_y, 2, 4)))
    for copy in copies[1:]:
        copy.wait()


def load_call(disp, dens, stiff):
    matrix = jax.ShapeDtypeStruct((192, 224), bf16)
    return pl.pallas_call(
        load_kernel,
        in_specs=[HBM, HBM, HBM],
        out_shape=(
            jax.ShapeDtypeStruct(disp.shape, f32),
            jax.ShapeDtypeStruct(dens.shape, f32),
            matrix,
            matrix,
        ),
        scratch_shapes=[pltpu.VMEM((24, 24), f32), pltpu.SemaphoreType.DMA((5,))],
        compiler_params=pltpu.CompilerParams(vmem_limit_bytes=16 * 2**20),
        cost_estimate=estimate(2),
        name="load",
    )(disp, dens, stiff)


def ends_kernel(flags, disp, dens, mat, ends, up, down, msg_even, msg_odd, *work):
    _, ny, nz, nx = disp.shape

    def segments(p):
        return lambda i: [(disp[i, p, 0:8], disp[i, p, 8:9]), (disp[i, p, nz - 8 : nz], None)]

    for ref in (up, down):
        ref[9:] = jnp.zeros((ref.shape[0] - 9, ny, nx), f32)

    def pack(y):
        row = pl.ds(y, 1)
        for i in range(9):
            up[i, row] = disp[i, y, nz - 1 : nz]
            down[i, row] = disp[i, y, 0:1]
        up[9, row] = dens[y, nz - 1 : nz]

    def put(y):
        d = jnp.concatenate([dens[y, 0:8], dens[y, nz - 8 : nz]], axis=0)
        s = energy_rows(y, mat, work, d)
        ends[y] = s
        row = pl.ds(y, 1)
        up[10, row] = s[14:15]
        down[9, row] = s[0:1]
        down[10, row] = s[1:2]
        pack(y)

    sweep(ny - 1, segments, put, work)
    pack(ny - 1)
    for n, y in enumerate((0, ny - 1)):
        for i in range(9):
            up[extra(up, 9 * n + i)] = disp[i, y, nz - 2 : nz - 1]
            down[extra(down, 9 * n + i)] = disp[i, y, 1:2]
            down[extra(down, 18 + 9 * n + i)] = disp[i, y, 2:3]
    up[extra(up, 36)] = dens[ny - 1, nz - 2 : nz - 1]
    down[extra(down, 36)] = dens[ny - 1, 0:1]
    down[extra(down, 37)] = dens[ny - 1, 1:2]
    odd = flags[5] == 1
    msg_even[...] = jnp.where(odd, down[...], up[...])
    msg_odd[...] = jnp.where(odd, up[...], down[...])


def ends_call(flags, disp, dens, mat):
    _, ny, nz, nx = disp.shape
    message = jax.ShapeDtypeStruct((11 + -(-38 // ny), ny, nx), f32)
    return pl.pallas_call(
        ends_kernel,
        in_specs=[SMEM] + [VMEM] * 3,
        out_shape=(jax.ShapeDtypeStruct((ny, 16, nx), f32),) + (message,) * 4,
        scratch_shapes=workspace(ny, 2, nx),
        compiler_params=pltpu.CompilerParams(vmem_limit_bytes=16 * 2**20),
        cost_estimate=estimate(4),
        name="energy_ends",
    )(flags, disp, dens, mat)


def middle_kernel(disp, dens, fy, mat, ends, src, *work):
    _, ny, nz, nx = disp.shape
    work, last = work[:3], work[3:]

    def segments(p):
        return lambda i: [(disp[i, p, 8 : nz - 8], disp[i, p, nz - 8 : nz - 7])]

    def frame(y):
        src[y, 0:OFF] = jnp.zeros((OFF, nx), f32)
        src[y, OFF + nz :] = jnp.zeros((src.shape[1] - OFF - nz, nx), f32)

    def put(y):
        frame(y)
        src[y, OFF : OFF + 8] = ends[y, 0:8]
        src[y, OFF + 8 : OFF + nz - 8] = energy_rows(y, mat, work, dens[y, 8 : nz - 8])
        src[y, OFF + nz - 8 : OFF + nz] = ends[y, 8:16]

    sweep(ny - 1, segments, put, work)
    last[1][...] = jnp.zeros_like(last[1])
    prepare(lambda i: [(disp[i, ny - 1], None)], 0, last)
    prepare(lambda i: [(fy[i], None)], 1, last)
    frame(ny - 1)
    src[ny - 1, OFF : OFF + nz] = energy_rows(0, mat, last, dens[ny - 1])


def middle_call(disp, dens, fy, mat, ends):
    _, ny, nz, nx = disp.shape
    return pl.pallas_call(
        middle_kernel,
        in_specs=[VMEM] * 5,
        out_shape=jax.ShapeDtypeStruct((ny, nz + 2 * OFF, nx), f32),
        scratch_shapes=workspace(ny, nz // 8 - 2, nx) + workspace(2, nz // 8, nx),
        compiler_params=pltpu.CompilerParams(vmem_limit_bytes=24 * 2**20),
        cost_estimate=estimate(4),
        name="energy_middle",
    )(disp, dens, fy, mat, ends)


def rim_kernel(
    flags, got_even, got_odd, up, down, disp, dens, mat_y, src,
    rim, nodes, msg_even, msg_odd, low_s, high_s, t_s, *work,
):
    ny, rows, nx = src.shape
    nz = rows - 2 * OFF
    odd = flags[5] == 1
    low_s[...] = jnp.where(odd, got_even[...], got_odd[...])
    high_s[...] = jnp.where(odd, got_odd[...], got_even[...])
    work[1][...] = jnp.zeros_like(work[1])
    prepare(lambda i: [(low_s[i], None), (up[i], None)], 0, work)
    prepare(lambda i: [(down[i], None), (high_s[i], None)], 1, work)
    s = energy_rows(0, mat_y, work, jnp.concatenate([low_s[9], up[9]], axis=0))
    columns = ((0, low_s[10]), (1, s[0:ny]), (3, s[ny : 2 * ny]), (4, high_s[9]), (5, high_s[10]))
    for y in range(ny):
        rim[y] = jnp.zeros((8, nx), f32)
        for r, column in columns:
            rim[y, r : r + 1] = column[y : y + 1]
    half = 2 * (nz + 8)
    zero = jnp.zeros((1, nx), f32)
    for n, y in enumerate((0, ny - 1)):
        row = slice(y, y + 1)
        for i in range(9):
            window = jnp.concatenate(
                [
                    low_s[extra(low_s, 9 * n + i)],
                    low_s[i, row],
                    disp[i, y, 0:1],
                    disp[i, y, nz - 1 : nz],
                    high_s[i, row],
                    high_s[extra(high_s, 9 * n + i)],
                    high_s[extra(high_s, 18 + 9 * n + i)],
                    zero,
                ],
                axis=0,
            )
            nodes[n, i] = window
            t_s[n, half + 8 * i : half + 8 * i + 8] = window
        nodes[n, 9] = jnp.concatenate(
            [
                low_s[extra(low_s, 36)],
                low_s[9, ny - 1 : ny],
                zero,
                dens[ny - 1, nz - 1 : nz],
                high_s[extra(high_s, 36)],
                high_s[extra(high_s, 37)],
                zero,
                zero,
            ],
            axis=0,
        )
        t_s[n, half + 72 : half + 80] = nodes[n, 9]
        for j in range(2):
            at = j * (nz + 8)
            yy = j if n == 0 else ny - 2 + j
            t_s[n, at : at + nz] = src[yy, OFF : OFF + nz]
            t_s[n, at + nz : at + nz + 8] = rim[yy]
    odd = flags[4] == 1
    msg_even[...] = jnp.where(odd, t_s[0], t_s[1])
    msg_odd[...] = jnp.where(odd, t_s[1], t_s[0])


def put_rim(s, y, rim, nz):
    s[y, OFF - 2 : OFF] = rim[0:2]
    s[y, OFF + nz - 1 : OFF + nz + 2] = rim[3:6]


def rim_call(flags, got_even, got_odd, up, down, disp, dens, mat_y, src):
    ny, rows, nx = src.shape
    nz = rows - 2 * OFF
    size = 2 * (nz + 8) + 80
    return pl.pallas_call(
        rim_kernel,
        in_specs=[SMEM] + [VMEM] * 8,
        out_shape=(
            jax.ShapeDtypeStruct((ny, 8, nx), f32),
            jax.ShapeDtypeStruct((2, 10, 8, nx), f32),
            jax.ShapeDtypeStruct((size, nx), f32),
            jax.ShapeDtypeStruct((size, nx), f32),
        ),
        scratch_shapes=[
            pltpu.VMEM(up.shape, f32),
            pltpu.VMEM(up.shape, f32),
            pltpu.VMEM((2, size, nx), f32),
        ]
        + workspace(2, 2 * (ny // 8), nx),
        compiler_params=pltpu.CompilerParams(vmem_limit_bytes=16 * 2**20),
        cost_estimate=estimate(2),
        name="energy_rim",
    )(flags, got_even, got_odd, up, down, disp, dens, mat_y, src)


def filter_block(s_s, d_s, n, z_edges, y_edges, finish, unroll):
    rows, nx = s_s.shape[1:]
    nz = rows - 2 * OFF
    alpha, beta, gamma, delta, eps = filter_weights()
    row = lax.broadcasted_iota(jnp.int32, (rows, nx), 0)
    keep = jnp.where(row < OFF, z_edges[0], jnp.where(row >= OFF + nz, z_edges[1], 1)) == 1

    def beside(v):
        return pltpu.roll(v, 1, 0) + pltpu.roll(v, rows - 1, 0) + lane_up(v) + lane_down(v)

    def second(j, _):
        c = s_s[j + 1]
        d2 = alpha * c + beta * (beside(c) + s_s[j] + s_s[j + 2])
        ok = keep
        if y_edges is not None:
            ok = keep & (jnp.where(j == 0, y_edges[0], jnp.where(j == n - 3, y_edges[1], 1)) == 1)
        d_s[j] = jnp.where(ok, d2, 0.0)
        return 0

    def third(j, _):
        d2 = d_s[j + 1]
        p3 = gamma * s_s[j + 2] + delta * d2 + eps * (beside(d2) + d_s[j] + d_s[j + 2])
        finish(j, p3[OFF : OFF + nz])
        return 0

    lax.fori_loop(0, n - 2, second, 0, unroll=unroll)
    lax.fori_loop(0, n - 4, third, 0, unroll=unroll)


def limits(p3, d, pas, sol):
    amp = jnp.sqrt(jnp.maximum(-p3 * d, 0.0))
    lower = jnp.maximum(d - move_limit, floor_density)
    upper = jnp.minimum(d + move_limit, 1.0)
    low, high, now = (jnp.where(sol, 1.0, jnp.where(pas, floor_density, v)) for v in (lower, upper, d))
    return amp, low, high, now


FINE = 16
COARSE = POINTS // FINE


def table(n, nz, nx, amp, low, high, now, fine_s, vol, tgt, start, unroll):
    spacing = 2.0 * bracket_end / POINTS

    pair = 2
    for first in range(0, COARSE, pair):
        inverse = [math.exp(0.5 * (-bracket_end + spacing * FINE * i)) for i in range(first, first + pair)]

        def volume(j, acc):
            acc = list(acc)
            for w in range(nz // 8):
                at = slice(8 * w, 8 * w + 8)
                lo, hi, d = low[j, at], high[j, at], now[j, at]
                los, his = [lo * c for c in inverse], [hi * c for c in inverse]
                for i, c in enumerate(inverse):
                    acc[pair * FINE + i] = acc[pair * FINE + i] + d * c
                for f in range(FINE):
                    if first == 0:
                        t = amp[j, at] * math.exp(-0.5 * spacing * f)
                        fine_s[f, j, at] = t
                    else:
                        t = fine_s[f, j, at]
                    for i in range(pair):
                        acc[i * FINE + f] = acc[i * FINE + f] + jnp.minimum(jnp.maximum(t, los[i]), his[i])
            return tuple(acc)

        places = [(vol, 8 * (first * FINE + e)) for e in range(pair * FINE)]
        places += [(tgt, 8 * (first + i)) for i in range(pair)]
        if start is None:
            begin = tuple(jnp.zeros((8, nx), f32) for _ in places)
        else:
            begin = tuple((start[0] if ref is vol else start[1])[at : at + 8] for ref, at in places)
        acc = lax.fori_loop(0, n, volume, begin, unroll=unroll)
        for (ref, at), value in zip(places, acc):
            ref[at : at + 8] = value


def inner_kernel(flags, src, rim, dens, passive, solid, amp, low, high, vol, tgt, s_s, d_s, now_s, fine_s):
    ny, nz, nx = dens.shape
    s_s[...] = src[0 : ny - 1]

    def fix(y, _):
        put_rim(s_s, y, rim[y], nz)
        return 0

    lax.fori_loop(0, ny - 1, fix, 0, unroll=5)

    def finish(j, p3):
        y = j + 2
        amp[j], low[j], high[j], now_s[j] = limits(p3, dens[y], passive[y] == 1, solid[y] == 1)

    filter_block(s_s, d_s, ny - 1, (flags[2], flags[3]), None, finish, 4)
    table(ny - 5, nz, nx, amp, low, high, now_s, fine_s, vol, tgt, None, 4)


def inner_call(flags, src, rim, dens, passive, solid):
    ny, nz, nx = dens.shape
    field = jax.ShapeDtypeStruct((ny - 5, nz, nx), f32)
    return pl.pallas_call(
        inner_kernel,
        in_specs=[SMEM] + [VMEM] * 5,
        out_shape=(
            field,
            field,
            field,
            jax.ShapeDtypeStruct((8 * POINTS, nx), f32),
            jax.ShapeDtypeStruct((8 * COARSE, nx), f32),
        ),
        scratch_shapes=[
            pltpu.VMEM((ny - 1, nz + 2 * OFF, nx), f32),
            pltpu.VMEM((ny - 3, nz + 2 * OFF, nx), f32),
            pltpu.VMEM((ny - 5, nz, nx), f32),
            pltpu.VMEM((FINE, ny - 5, nz, nx), f32),
        ],
        compiler_params=pltpu.CompilerParams(vmem_limit_bytes=24 * 2**20),
        cost_estimate=estimate(9),
        name="filter_inner",
    )(flags, src, rim, dens, passive, solid)


def outer_kernel(
    flags, src, rim, nodes, got_even, got_odd, mat, dens, passive, solid, vol_i, tgt_i,
    amp, low, high, excess, s_s, d_s, now_s, fine_s, vol, tgt, below, above, *work,
):
    ny, nz, nx = dens.shape
    odd = flags[4] == 1
    below[...] = jnp.where(odd, got_even[...], got_odd[...])
    above[...] = jnp.where(odd, got_odd[...], got_even[...])
    half = 2 * (nz + 8)

    def window(ref, i):
        return ref[half + 8 * i : half + 8 * i + 8]

    work[1][...] = jnp.zeros_like(work[1])
    prepare(lambda i: [(window(below, i), None), (nodes[1, i], None)], 0, work)
    prepare(lambda i: [(nodes[0, i], None), (window(above, i), None)], 1, work)
    corner = energy_rows(0, mat, work, jnp.concatenate([window(below, 9), nodes[1, 9]], axis=0))
    for b, ref in enumerate((below, above)):
        for j in range(2):
            at = j if b == 0 else 5 + j
            start = j * (nz + 8)
            s_s[b, at, 0:OFF] = jnp.zeros((OFF, nx), f32)
            s_s[b, at, OFF : OFF + nz] = ref[start : start + nz]
            s_s[b, at, OFF + nz :] = jnp.zeros((OFF, nx), f32)
            put_rim(s_s.at[b], at, ref[start + nz : start + nz + 8], nz)
    for j in range(4):
        s_s[0, 2 + j] = src[j]
        put_rim(s_s.at[0], 2 + j, rim[j], nz)
    for j in range(5):
        s_s[1, j] = src[ny - 5 + j]
        put_rim(s_s.at[1], j, rim[ny - 5 + j], nz)
    put_rim(s_s.at[0], 1, corner[0:8], nz)
    put_rim(s_s.at[1], 4, corner[8:16], nz)
    for b in range(2):
        y0 = 0 if b == 0 else ny - 3

        def finish(j, p3):
            y = y0 + j
            at = 2 * b + j
            amp[at], low[at], high[at], now_s[at] = limits(p3, dens[y], passive[y] == 1, solid[y] == 1)

        edges = (flags[0], 1) if b == 0 else (1, flags[1])
        filter_block(s_s.at[b], d_s.at[b], 6 + b, (flags[2], flags[3]), edges, finish, True)
    table(5, nz, nx, amp, low, high, now_s, fine_s, vol, tgt, (vol_i, tgt_i), True)

    def lanes(ref, count):
        total = ref[pl.ds(0, count, stride=8), :]
        for s in range(1, 8):
            total = total + ref[pl.ds(s, count, stride=8), :]
        return total

    volumes, targets = lanes(vol, POINTS), lanes(tgt, COARSE)
    over = [volumes[FINE * i : FINE * i + FINE] - targets[i : i + 1] for i in range(COARSE)]
    excess[...] = jnp.sum(jnp.transpose(jnp.concatenate(over, axis=0)), axis=0, keepdims=True)


def outer_call(flags, src, rim, nodes, got_even, got_odd, mat, dens, passive, solid, vol_i, tgt_i):
    ny, nz, nx = dens.shape
    rows = nz + 2 * OFF
    field = jax.ShapeDtypeStruct((5, nz, nx), f32)
    return pl.pallas_call(
        outer_kernel,
        in_specs=[SMEM] + [VMEM] * 11,
        out_shape=(field, field, field, jax.ShapeDtypeStruct((1, POINTS), f32)),
        scratch_shapes=[
            pltpu.VMEM((2, 7, rows, nx), f32),
            pltpu.VMEM((2, 5, rows, nx), f32),
            pltpu.VMEM((5, nz, nx), f32),
            pltpu.VMEM((FINE, 5, nz, nx), f32),
            pltpu.VMEM((8 * POINTS, nx), f32),
            pltpu.VMEM((8 * COARSE, nx), f32),
            pltpu.VMEM(got_odd.shape, f32),
            pltpu.VMEM(got_odd.shape, f32),
        ]
        + workspace(2, 2, nx),
        compiler_params=pltpu.CompilerParams(vmem_limit_bytes=20 * 2**20),
        cost_estimate=estimate(3),
        name="filter_outer",
    )(flags, src, rim, nodes, got_even, got_odd, mat, dens, passive, solid, vol_i, tgt_i)


def update_kernel(tables, amp_i, low_i, high_i, amp_o, low_o, high_o, new, logm):
    inner = amp_i.shape[0]
    nx = amp_i.shape[-1]
    total = jnp.sum(tables[...], axis=0, keepdims=True)
    lane = lax.broadcasted_iota(jnp.int32, total.shape, 1)
    above = jnp.where((total > 0.0) & (lane > 0), 1.0, 0.0)
    middle = -bracket_end + (2.0 * bracket_end / POINTS) * (jnp.sum(above) + 0.5)
    logm[0] = middle
    scale = jnp.exp(jnp.full((1, nx), -0.5 * middle, f32))

    def new_row(amp, low, high):
        return jnp.minimum(jnp.maximum(amp * scale, low), high)

    def body(j, _):
        new[j + 2] = new_row(amp_i[j], low_i[j], high_i[j])
        return 0

    lax.fori_loop(0, inner, body, 0)
    for j in range(5):
        new[j if j < 2 else inner + j] = new_row(amp_o[j], low_o[j], high_o[j])


def update_call(tables, inner, outer):
    n, nz, nx = inner[0].shape
    return pl.pallas_call(
        update_kernel,
        in_specs=[VMEM] * 7,
        out_specs=(VMEM, SMEM),
        out_shape=(jax.ShapeDtypeStruct((n + 5, nz, nx), f32), jax.ShapeDtypeStruct((1,), f32)),
        compiler_params=pltpu.CompilerParams(vmem_limit_bytes=8 * 2**20),
        cost_estimate=estimate(1),
        name="update",
    )(tables, *inner, *outer)


def to_lower(value, axis):
    count = lax.axis_size(axis)
    return lax.ppermute(value, axis, [(i + 1, i) for i in range(count - 1)])


def swap(value, axis, start):
    pairs = []
    for i in range(start, lax.axis_size(axis) - 1, 2):
        pairs += [(i, i + 1), (i + 1, i)]
    return lax.ppermute(value, axis, pairs)


def on_device(displacement, density, passive, solid, stiffness):
    ny, nz, nx = density.shape
    gy, gz = lax.axis_size("gy"), lax.axis_size("gz")
    iy, iz = lax.axis_index("gy"), lax.axis_index("gz")
    flags = jnp.stack([iy > 0, iy < gy - 1, iz > 0, iz < gz - 1, iy % 2 == 1, iz % 2 == 1]).astype(jnp.int32)

    disp_hbm = pltpu.with_memory_space_constraint(displacement, pltpu.HBM)
    dens_hbm = pltpu.with_memory_space_constraint(density, pltpu.HBM)
    stiff_hbm = pltpu.with_memory_space_constraint(stiffness, pltpu.HBM)

    fy = to_lower(face_call(disp_hbm), "gy")
    disp, dens, mat, mat_y = load_call(disp_hbm, dens_hbm, stiff_hbm)
    ends, up, down, z_even, z_odd = ends_call(flags, disp, dens, mat)

    z_got_even = swap(z_even, "gz", 0)
    z_got_odd = swap(z_odd, "gz", 1)
    src = middle_call(disp, dens, fy, mat, ends)
    rim, nodes, msg_even, msg_odd = rim_call(flags, z_got_even, z_got_odd, up, down, disp, dens, mat_y, src)

    got_even = swap(msg_even, "gy", 0)
    got_odd = swap(msg_odd, "gy", 1)
    *inner, vol, tgt = inner_call(flags, src, rim, dens, passive, solid)
    *outer, excess = outer_call(flags, src, rim, nodes, got_even, got_odd, mat, dens, passive, solid, vol, tgt)

    everyone = jnp.broadcast_to(excess, (gz * gy, POINTS))
    tables = lax.all_to_all(everyone, ("gz", "gy"), 0, 0, tiled=True)
    new, logm = update_call(tables, inner, outer)
    return new, logm.reshape(())


def solution(mesh):
    placed = (
        P(None, "gy", "gz", None),
        P("gy", "gz", None),
        P("gy", "gz", None),
        P("gy", "gz", None),
        P(),
    )
    return jax.shard_map(
        on_device, mesh=mesh, in_specs=placed, out_specs=(P("gy", "gz", None), P()), check_vma=False
    )
```

```python
import math

import jax
import jax.numpy as jnp
from jax import lax
from jax.experimental import pallas as pl
from jax.experimental.pallas import tpu as pltpu
from jax.sharding import PartitionSpec as P

ITERS = 8
POINTS = 2**ITERS
OFF = 8

smoothing = 0.52
move_limit = 0.2
floor_density = 0.001
bracket_end = 12.0

f32 = jnp.float32
bf16 = jnp.bfloat16
VMEM = pl.BlockSpec(memory_space=pltpu.VMEM)
SMEM = pl.BlockSpec(memory_space=pltpu.SMEM)
HBM = pl.BlockSpec(memory_space=pltpu.HBM)


def cheb_weights():
    spectrum_top = 1.0 + 12.0 * smoothing
    centre_value = (spectrum_top + 1.0) / 2.0
    half_width = (spectrum_top - 1.0) / 2.0
    ratio_value = centre_value / half_width
    first_rho = 1.0 / ratio_value
    second_rho = 1.0 / (2.0 * ratio_value - first_rho)
    third_rho = 1.0 / (2.0 * ratio_value - second_rho)
    return (
        centre_value,
        second_rho * first_rho,
        2.0 * second_rho / half_width,
        third_rho * second_rho,
        2.0 * third_rho / half_width,
    )


def filter_weights():
    t, w1, w2, w3, w4 = cheb_weights()
    diag = 1.0 + 6.0 * smoothing
    alpha = w1 / t + w2 * (1.0 - diag / t)
    beta = w2 * smoothing / t
    gamma = 1.0 / t - w4 * w1 / (t * w2)
    delta = 1.0 + w3 + w4 / w2 - w4 * diag
    eps = w4 * smoothing
    return alpha, beta, gamma, delta, eps


def lane_up(v):
    n = v.shape[-1]
    lane = lax.broadcasted_iota(jnp.int32, v.shape, v.ndim - 1)
    return jnp.where(lane < n - 1, pltpu.roll(v, n - 1, v.ndim - 1), 0.0)


def lane_down(v):
    n = v.shape[-1]
    lane = lax.broadcasted_iota(jnp.int32, v.shape, v.ndim - 1)
    return jnp.where(lane > 0, pltpu.roll(v, 1, v.ndim - 1), 0.0)


def estimate(us):
    return pl.CostEstimate(flops=int(us * 1e9), bytes_accessed=1 << 20, transcendentals=0)


def build_matrices(k, mats):
    shape = (24, 128)
    col = lax.broadcasted_iota(jnp.int32, shape, 1)
    row = lax.broadcasted_iota(jnp.int32, shape, 0)
    main = col < 96
    q = jnp.where(main, jnp.where(col >= 48, 1, 0), jnp.where(col >= 104, 1, 0))
    m = col - 48 * q
    e = col - 96 - 8 * q
    c = jnp.where(main, m >> 4, e >> 1)
    dx = jnp.where(main, (m >> 3) & 1, e & 1)
    valid = main | (e < 6)
    picks = []
    for _, plane, band in mats:
        dof0 = 3 * (plane * q + dx) + c
        picks.append(jnp.where(main & (row == dof0), 1.0, 0.0))
        picks.append(jnp.where(valid & (row == dof0 + 3 * band), 1.0, 0.0))
    picked = jnp.dot(
        k, jnp.concatenate(picks, axis=1), precision=lax.Precision.HIGHEST, preferred_element_type=f32
    )
    col8 = lax.broadcasted_iota(jnp.int32, (8, 128), 1)
    row8 = lax.broadcasted_iota(jnp.int32, (8, 128), 0)
    main8 = col8 < 96
    rc = col8 & 7
    m0 = main8 & (rc == row8)
    m1 = jnp.where(main8, rc, 8) == row8 + 1
    for n, (mat, plane, band) in enumerate(mats):
        k0 = picked[:, 256 * n : 256 * n + 128]
        k1 = picked[:, 256 * n + 128 : 256 * n + 256]
        rows = []
        for b in range(2):
            for q_ in range(2):
                for c_ in range(3):
                    for dx_ in range(2):
                        r = 3 * (plane * q_ + band * b + dx_) + c_
                        rows.append(jnp.where(m0, k0[r : r + 1], 0.0) + jnp.where(m1, k1[r : r + 1], 0.0))
        full = jnp.concatenate(rows, axis=0)
        hi = full.astype(bf16)
        lo = (full - hi.astype(f32)).astype(bf16)
        mat[:, 0:112] = hi[:, 0:112]
        mat[:, 112:224] = lo[:, 0:112]


def prepare(segments, p, work, short=False):
    main_s, ext_s, mul_s = work

    def load_case(l):
        for c in range(3):
            w0 = 0
            for u, x in segments(3 * l + c):
                size, nx = u.shape
                n = size // 8
                last = lax.broadcasted_iota(jnp.int32, u.shape, 0) == size - 1
                both = (u, lane_up(u))
                after = (None, None) if x is None else (x, lane_up(x))
                for w in range(n):
                    sl = slice(8 * w, 8 * w + 8)
                    main_s[p, l, 16 * c : 16 * c + 16, (w0 + w) * nx : (w0 + w + 1) * nx] = jnp.concatenate(
                        [both[0][sl], both[1][sl]], axis=0
                    ).astype(bf16)
                for dx in range(2):
                    v, vx = both[dx], after[dx]
                    k = 2 * c + dx
                    for w in range(n):
                        nxt = v[8 * w + 8 : 8 * w + 9] if w < n - 1 else vx
                        if nxt is not None:
                            ext_s[p, l, k : k + 1, (w0 + w) * nx : (w0 + w + 1) * nx] = nxt
                    m = 2.0 * v - v.astype(bf16).astype(f32)
                    mx = 0.0 if vx is None else jnp.broadcast_to(2.0 * vx - vx.astype(bf16).astype(f32), v.shape)
                    at = slice(8 * w0, 8 * (w0 + n))
                    mul_s[p, l, k, 0, at] = m
                    mul_s[p, l, k, 1, at] = jnp.where(last, mx, pltpu.roll(m, size - 1, 0))
                w0 += n
        return 0

    if short:
        lax.fori_loop(0, 3, lambda l, _: load_case(l), 0)
    else:
        for l in range(3):
            load_case(l)


def energy_rows(p, mat, work, density, short=False):
    main_s, ext_s, mul_s = work
    rows, nx = density.shape
    count = rows // 8

    def load_case(l, acc):
        acc = list(acc)
        ext = jnp.concatenate([ext_s[p, l], ext_s[p + 1, l]], axis=0).astype(bf16)
        one = jnp.concatenate([main_s[p, l], main_s[p + 1, l], ext], axis=0)
        force = jnp.dot(mat[...], jnp.concatenate([one, one], axis=0), preferred_element_type=f32)
        i = 0
        for b in range(2):
            for q in range(2):
                for k in range(6):
                    for w in range(count):
                        at = slice(8 * w, 8 * w + 8)
                        term = force[8 * i : 8 * i + 8, w * nx : (w + 1) * nx] * mul_s[p + q, l, k, b, at]
                        acc[w] = acc[w] + term
                    i += 1
        return tuple(acc)

    acc = tuple(jnp.zeros((8, nx), f32) for _ in range(count))
    if short:
        acc = lax.fori_loop(0, 3, load_case, acc)
    else:
        for l in range(3):
            acc = load_case(l, acc)
    return density * (-3.0 * density * density * jnp.concatenate(acc, axis=0))


def workspace(planes, windows, nx):
    return [
        pltpu.VMEM((planes, 3, 48, windows * nx), bf16),
        pltpu.VMEM((planes, 3, 8, windows * nx), f32),
        pltpu.VMEM((planes, 3, 6, 2, 8 * windows, nx), f32),
    ]


def sweep(rows, segments, put, work):
    work[1][...] = jnp.zeros_like(work[1])

    def body(y, _):
        put(y)
        prepare(segments(y + 2), y + 2, work)
        return 0

    for p in range(2):
        prepare(segments(p), p, work, True)
    lax.fori_loop(0, rows - 1, body, 0)
    put(rows - 1)


def face_kernel(disp, face, sem):
    copy = pltpu.make_async_copy(disp.at[:, 0], face, sem)
    copy.start()
    copy.wait()


def face_call(disp):
    _, _, nz, nx = disp.shape
    return pl.pallas_call(
        face_kernel,
        in_specs=[HBM],
        out_shape=jax.ShapeDtypeStruct((9, nz, nx), f32),
        scratch_shapes=[pltpu.SemaphoreType.DMA],
        compiler_params=pltpu.CompilerParams(vmem_limit_bytes=2**20),
        name="face",
    )(disp)


def extra(ref, row):
    ny = ref.shape[1]
    return 11 + row // ny, pl.ds(row % ny, 1)


def load_kernel(disp_h, dens_h, stiff, disp, dens, mat, mat_y, stiff_s, sems):
    copies = [pltpu.make_async_copy(stiff, stiff_s, sems.at[0])]
    for l in range(3):
        part = pl.ds(3 * l, 3)
        copies.append(pltpu.make_async_copy(disp_h.at[part], disp.at[part], sems.at[1 + l]))
    copies.append(pltpu.make_async_copy(dens_h, dens, sems.at[4]))
    for copy in copies:
        copy.start()
    copies[0].wait()
    build_matrices(stiff_s[...], ((mat, 4, 2), (mat_y, 2, 4)))
    for copy in copies[1:]:
        copy.wait()


def load_call(disp, dens, stiff):
    matrix = jax.ShapeDtypeStruct((192, 224), bf16)
    return pl.pallas_call(
        load_kernel,
        in_specs=[HBM, HBM, HBM],
        out_shape=(
            jax.ShapeDtypeStruct(disp.shape, f32),
            jax.ShapeDtypeStruct(dens.shape, f32),
            matrix,
            matrix,
        ),
        scratch_shapes=[pltpu.VMEM((24, 24), f32), pltpu.SemaphoreType.DMA((5,))],
        compiler_params=pltpu.CompilerParams(vmem_limit_bytes=16 * 2**20),
        cost_estimate=estimate(2),
        name="load",
    )(disp, dens, stiff)


def ends_kernel(flags, disp, dens, mat, ends, up, down, msg_even, msg_odd, *work):
    _, ny, nz, nx = disp.shape

    def segments(p):
        return lambda i: [(disp[i, p, 0:8], disp[i, p, 8:9]), (disp[i, p, nz - 8 : nz], None)]

    def clear(e, _):
        up[e] = jnp.zeros((ny, nx), f32)
        down[e] = jnp.zeros((ny, nx), f32)
        return 0

    lax.fori_loop(9, up.shape[0], clear, 0)

    def pack(y):
        row = pl.ds(y, 1)
        for i in range(9):
            up[i, row] = disp[i, y, nz - 1 : nz]
            down[i, row] = disp[i, y, 0:1]
        up[9, row] = dens[y, nz - 1 : nz]

    def put(y):
        d = jnp.concatenate([dens[y, 0:8], dens[y, nz - 8 : nz]], axis=0)
        s = energy_rows(y, mat, work, d)
        ends[y] = s
        row = pl.ds(y, 1)
        up[10, row] = s[14:15]
        down[9, row] = s[0:1]
        down[10, row] = s[1:2]
        pack(y)

    sweep(ny - 1, segments, put, work)
    pack(ny - 1)

    def more(i, _):
        for n, y in enumerate((0, ny - 1)):
            up[extra(up, 9 * n + i)] = disp[i, y, nz - 2 : nz - 1]
            down[extra(down, 9 * n + i)] = disp[i, y, 1:2]
            down[extra(down, 18 + 9 * n + i)] = disp[i, y, 2:3]
        return 0

    lax.fori_loop(0, 9, more, 0)
    up[extra(up, 36)] = dens[ny - 1, nz - 2 : nz - 1]
    down[extra(down, 36)] = dens[ny - 1, 0:1]
    down[extra(down, 37)] = dens[ny - 1, 1:2]
    odd = flags[5] == 1

    def choose(e, _):
        a, b = up[e], down[e]
        msg_even[e] = jnp.where(odd, b, a)
        msg_odd[e] = jnp.where(odd, a, b)
        return 0

    lax.fori_loop(0, up.shape[0], choose, 0, unroll=2)


def ends_call(flags, disp, dens, mat):
    _, ny, nz, nx = disp.shape
    message = jax.ShapeDtypeStruct((11 + -(-38 // ny), ny, nx), f32)
    return pl.pallas_call(
        ends_kernel,
        in_specs=[SMEM] + [VMEM] * 3,
        out_shape=(jax.ShapeDtypeStruct((ny, 16, nx), f32),) + (message,) * 4,
        scratch_shapes=workspace(ny, 2, nx),
        compiler_params=pltpu.CompilerParams(vmem_limit_bytes=16 * 2**20),
        cost_estimate=estimate(4),
        name="energy_ends",
    )(flags, disp, dens, mat)


def middle_kernel(disp, dens, fy, mat, ends, src, *work):
    _, ny, nz, nx = disp.shape
    work, last = work[:3], work[3:]

    def segments(p):
        return lambda i: [(disp[i, p, 8 : nz - 8], disp[i, p, nz - 8 : nz - 7])]

    def frame(y):
        src[y, 0:OFF] = jnp.zeros((OFF, nx), f32)
        src[y, OFF + nz :] = jnp.zeros((src.shape[1] - OFF - nz, nx), f32)

    def put(y):
        frame(y)
        src[y, OFF : OFF + 8] = ends[y, 0:8]
        src[y, OFF + 8 : OFF + nz - 8] = energy_rows(y, mat, work, dens[y, 8 : nz - 8])
        src[y, OFF + nz - 8 : OFF + nz] = ends[y, 8:16]

    sweep(ny - 1, segments, put, work)
    last[1][...] = jnp.zeros_like(last[1])
    prepare(lambda i: [(disp[i, ny - 1], None)], 0, last, True)
    prepare(lambda i: [(fy[i], None)], 1, last, True)
    frame(ny - 1)
    src[ny - 1, OFF : OFF + nz] = energy_rows(0, mat, last, dens[ny - 1], True)


def middle_call(disp, dens, fy, mat, ends):
    _, ny, nz, nx = disp.shape
    return pl.pallas_call(
        middle_kernel,
        in_specs=[VMEM] * 5,
        out_shape=jax.ShapeDtypeStruct((ny, nz + 2 * OFF, nx), f32),
        scratch_shapes=workspace(ny, nz // 8 - 2, nx) + workspace(2, nz // 8, nx),
        compiler_params=pltpu.CompilerParams(vmem_limit_bytes=24 * 2**20),
        cost_estimate=estimate(4),
        name="energy_middle",
    )(disp, dens, fy, mat, ends)


def rim_kernel(
    flags, got_even, got_odd, up, down, disp, dens, mat_y, src,
    rim, nodes, msg_even, msg_odd, low_s, high_s, s_s, t_s, *work,
):
    ny, rows, nx = src.shape
    nz = rows - 2 * OFF
    odd = flags[5] == 1

    def choose(e, _):
        a, b = got_even[e], got_odd[e]
        low_s[e] = jnp.where(odd, a, b)
        high_s[e] = jnp.where(odd, b, a)
        return 0

    lax.fori_loop(0, up.shape[0], choose, 0, unroll=2)
    work[1][...] = jnp.zeros_like(work[1])
    prepare(lambda i: [(low_s[i], None), (up[i], None)], 0, work, True)
    prepare(lambda i: [(down[i], None), (high_s[i], None)], 1, work, True)
    s = energy_rows(0, mat_y, work, jnp.concatenate([low_s[9], up[9]], axis=0), True)
    s_s[0:ny] = s[0:ny]
    s_s[ny : 2 * ny] = s[ny : 2 * ny]

    def spread(y, _):
        row = pl.ds(y, 1)
        zero = jnp.zeros((1, nx), f32)
        last = s_s[pl.ds(ny + y, 1)]
        rim[y] = jnp.concatenate(
            [low_s[10, row], s_s[row], zero, last, high_s[9, row], high_s[10, row], zero, zero], axis=0
        )
        return 0

    lax.fori_loop(0, ny, spread, 0, unroll=2)
    half = 2 * (nz + 8)
    zero = jnp.zeros((1, nx), f32)
    for n, y in enumerate((0, ny - 1)):
        row = slice(y, y + 1)

        def window(i, _):
            value = jnp.concatenate(
                [
                    low_s[extra(low_s, 9 * n + i)],
                    low_s[i, row],
                    disp[i, y, 0:1],
                    disp[i, y, nz - 1 : nz],
                    high_s[i, row],
                    high_s[extra(high_s, 9 * n + i)],
                    high_s[extra(high_s, 18 + 9 * n + i)],
                    zero,
                ],
                axis=0,
            )
            nodes[n, i] = value
            t_s[n, pl.ds(pl.multiple_of(half + 8 * i, 8), 8)] = value
            return 0

        lax.fori_loop(0, 9, window, 0, unroll=3)
        nodes[n, 9] = jnp.concatenate(
            [
                low_s[extra(low_s, 36)],
                low_s[9, ny - 1 : ny],
                zero,
                dens[ny - 1, nz - 1 : nz],
                high_s[extra(high_s, 36)],
                high_s[extra(high_s, 37)],
                zero,
                zero,
            ],
            axis=0,
        )
        t_s[n, half + 72 : half + 80] = nodes[n, 9]
        for j in range(2):
            at = j * (nz + 8)
            yy = j if n == 0 else ny - 2 + j
            t_s[n, at : at + nz] = src[yy, OFF : OFF + nz]
            t_s[n, at + nz : at + nz + 8] = rim[yy]
    odd = flags[4] == 1
    msg_even[...] = jnp.where(odd, t_s[0], t_s[1])
    msg_odd[...] = jnp.where(odd, t_s[1], t_s[0])


def put_rim(s, y, rim, nz):
    s[y, OFF - 2 : OFF] = rim[0:2]
    s[y, OFF + nz - 1 : OFF + nz + 2] = rim[3:6]


def rim_call(flags, got_even, got_odd, up, down, disp, dens, mat_y, src):
    ny, rows, nx = src.shape
    nz = rows - 2 * OFF
    size = 2 * (nz + 8) + 80
    return pl.pallas_call(
        rim_kernel,
        in_specs=[SMEM] + [VMEM] * 8,
        out_shape=(
            jax.ShapeDtypeStruct((ny, 8, nx), f32),
            jax.ShapeDtypeStruct((2, 10, 8, nx), f32),
            jax.ShapeDtypeStruct((size, nx), f32),
            jax.ShapeDtypeStruct((size, nx), f32),
        ),
        scratch_shapes=[
            pltpu.VMEM(up.shape, f32),
            pltpu.VMEM(up.shape, f32),
            pltpu.VMEM((2 * ny, nx), f32),
            pltpu.VMEM((2, size, nx), f32),
        ]
        + workspace(2, 2 * (ny // 8), nx),
        compiler_params=pltpu.CompilerParams(vmem_limit_bytes=16 * 2**20),
        cost_estimate=estimate(2),
        name="energy_rim",
    )(flags, got_even, got_odd, up, down, disp, dens, mat_y, src)


def filter_blocks(s_s, d_s, z_edges, y_edges, finish, unroll):
    blocks, n, rows, nx = s_s.shape
    nz = rows - 2 * OFF
    alpha, beta, gamma, delta, eps = filter_weights()
    row = lax.broadcasted_iota(jnp.int32, (rows, nx), 0)
    keep = jnp.where(row < OFF, z_edges[0], jnp.where(row >= OFF + nz, z_edges[1], 1)) == 1

    def beside(v):
        return pltpu.roll(v, 1, 0) + pltpu.roll(v, rows - 1, 0) + lane_up(v) + lane_down(v)

    def place(at, count):
        if blocks == 1:
            return 0, at
        b = jnp.where(at >= count, 1, 0)
        return b, at - count * b

    def second(at, _):
        b, j = place(at, n - 2)
        c = s_s[b, j + 1]
        d2 = alpha * c + beta * (beside(c) + s_s[b, j] + s_s[b, j + 2])
        ok = keep
        if y_edges is not None:
            ok = keep & (jnp.where(at == 0, y_edges[0], jnp.where(at == 2 * n - 5, y_edges[1], 1)) == 1)
        d_s[b, j] = jnp.where(ok, d2, 0.0)
        return 0

    def third(at, _):
        b, j = place(at, n - 4)
        d2 = d_s[b, j + 1]
        p3 = gamma * s_s[b, j + 2] + delta * d2 + eps * (beside(d2) + d_s[b, j] + d_s[b, j + 2])
        finish(at, b, j, p3[OFF : OFF + nz])
        return 0

    lax.fori_loop(0, blocks * (n - 2), second, 0, unroll=unroll)
    lax.fori_loop(0, blocks * (n - 4), third, 0, unroll=unroll)


def limits(p3, d, pas, sol):
    amp = jnp.sqrt(jnp.maximum(-p3 * d, 0.0))
    lower = jnp.maximum(d - move_limit, floor_density)
    upper = jnp.minimum(d + move_limit, 1.0)
    low, high, now = (jnp.where(sol, 1.0, jnp.where(pas, floor_density, v)) for v in (lower, upper, d))
    return amp, low, high, now


FINE = 16
COARSE = POINTS // FINE


def table(n, nz, nx, amp, low, high, now, fine_s, vol, tgt, start, unroll):
    spacing = 2.0 * bracket_end / POINTS

    pair = 2

    def run(first, make):
        inverse = [
            jnp.exp(0.5 * (-bracket_end + spacing * FINE * jnp.full((8, nx), first + i, jnp.int32).astype(f32)))
            for i in range(pair)
        ]

        def volume(j, acc):
            acc = list(acc)
            for w in range(nz // 8):
                at = slice(8 * w, 8 * w + 8)
                lo, hi, d = low[j, at], high[j, at], now[j, at]
                los, his = [lo * c for c in inverse], [hi * c for c in inverse]
                for i, c in enumerate(inverse):
                    acc[pair * FINE + i] = acc[pair * FINE + i] + d * c
                for f in range(FINE):
                    if make:
                        t = amp[j, at] * math.exp(-0.5 * spacing * f)
                        fine_s[f, j, at] = t
                    else:
                        t = fine_s[f, j, at]
                    for i in range(pair):
                        acc[i * FINE + f] = acc[i * FINE + f] + jnp.minimum(jnp.maximum(t, los[i]), his[i])
            return tuple(acc)

        places = [(0, 8 * (first * FINE + e)) for e in range(pair * FINE)] + [(1, 8 * (first + i)) for i in range(pair)]
        places = [(a, pl.ds(at if isinstance(at, int) else pl.multiple_of(at, 8), 8)) for a, at in places]
        if start is None:
            begin = tuple(jnp.zeros((8, nx), f32) for _ in places)
        else:
            begin = tuple(start[a][at] for a, at in places)
        acc = lax.fori_loop(0, n, volume, begin, unroll=unroll)
        for (a, at), value in zip(places, acc):
            (vol, tgt)[a][at] = value

    run(0, True)

    def later(q, _):
        run(pair * q, False)
        return 0

    lax.fori_loop(1, COARSE // pair, later, 0)


def inner_kernel(flags, src, rim, dens, passive, solid, amp, low, high, vol, tgt, s_s, d_s, now_s, fine_s):
    ny, nz, nx = dens.shape

    def place(j, _):
        s_s[0, j] = src[j + 1]
        put_rim(s_s.at[0], j, rim[j + 1], nz)
        return 0

    lax.fori_loop(0, ny - 2, place, 0, unroll=2)

    def finish(at, b, j, p3):
        y = j + 3
        amp[j], low[j], high[j], now_s[j] = limits(p3, dens[y], passive[y] == 1, solid[y] == 1)

    filter_blocks(s_s, d_s, (flags[2], flags[3]), None, finish, 2)
    table(ny - 6, nz, nx, amp, low, high, now_s, fine_s, vol, tgt, None, 2)


def inner_call(flags, src, rim, dens, passive, solid):
    ny, nz, nx = dens.shape
    rows = nz + 2 * OFF
    field = jax.ShapeDtypeStruct((ny - 6, nz, nx), f32)
    return pl.pallas_call(
        inner_kernel,
        in_specs=[SMEM] + [VMEM] * 5,
        out_shape=(
            field,
            field,
            field,
            jax.ShapeDtypeStruct((8 * POINTS, nx), f32),
            jax.ShapeDtypeStruct((8 * COARSE, nx), f32),
        ),
        scratch_shapes=[
            pltpu.VMEM((1, ny - 2, rows, nx), f32),
            pltpu.VMEM((1, ny - 4, rows, nx), f32),
            pltpu.VMEM((ny - 6, nz, nx), f32),
            pltpu.VMEM((FINE, ny - 6, nz, nx), f32),
        ],
        compiler_params=pltpu.CompilerParams(vmem_limit_bytes=24 * 2**20),
        cost_estimate=estimate(9),
        name="filter_inner",
    )(flags, src, rim, dens, passive, solid)


def outer_kernel(
    flags, src, rim, nodes, got_even, got_odd, mat, dens, passive, solid, vol_i, tgt_i,
    amp, low, high, excess, s_s, d_s, now_s, fine_s, vol, tgt, got_s, *work,
):
    ny, nz, nx = dens.shape
    odd = flags[4] == 1
    size = got_even.shape[0]
    step = nz + 8
    half = 2 * step

    def choose(r, _):
        at = pl.ds(pl.multiple_of(8 * r, 8), 8)
        a, b = got_even[at], got_odd[at]
        got_s[0, at] = jnp.where(odd, a, b)
        got_s[1, at] = jnp.where(odd, b, a)
        return 0

    lax.fori_loop(0, size // 8, choose, 0, unroll=4)

    def window(b, i):
        return got_s[b, pl.ds(pl.multiple_of(half + 8 * i, 8), 8)]

    work[1][...] = jnp.zeros_like(work[1])
    prepare(lambda i: [(window(0, i), None), (nodes[1, i], None)], 0, work, True)
    prepare(lambda i: [(nodes[0, i], None), (window(1, i), None)], 1, work, True)
    corner = energy_rows(0, mat, work, jnp.concatenate([window(0, 9), nodes[1, 9]], axis=0), True)

    def received(at, _):
        b = jnp.where(at >= 2, 1, 0)
        j = at - 2 * b
        to = j + 5 * b
        start = pl.multiple_of(j * step, 8)
        s_s[b, to, 0:OFF] = jnp.zeros((OFF, nx), f32)
        s_s[b, to, OFF : OFF + nz] = got_s[b, pl.ds(start, nz)]
        s_s[b, to, OFF + nz :] = jnp.zeros((OFF, nx), f32)
        put_rim(s_s.at[b], to, got_s[b, pl.ds(start + nz, 8)], nz)
        return 0

    def own(at, _):
        b = jnp.where(at >= 5, 1, 0)
        y = at + (ny - 10) * b
        to = at + 2 - 7 * b
        s_s[b, to] = src[y]
        put_rim(s_s.at[b], to, rim[y], nz)
        return 0

    lax.fori_loop(0, 4, received, 0)
    lax.fori_loop(0, 10, own, 0, unroll=2)
    put_rim(s_s.at[0], 1, corner[0:8], nz)
    put_rim(s_s.at[1], 4, corner[8:16], nz)

    def finish(at, b, j, p3):
        y = j + (ny - 3) * b
        amp[at], low[at], high[at], now_s[at] = limits(p3, dens[y], passive[y] == 1, solid[y] == 1)

    filter_blocks(s_s, d_s, (flags[2], flags[3]), (flags[0], flags[1]), finish, 2)
    table(6, nz, nx, amp, low, high, now_s, fine_s, vol, tgt, (vol_i, tgt_i), 2)

    def lanes(ref, count):
        total = ref[pl.ds(0, count, stride=8), :]
        for s in range(1, 8):
            total = total + ref[pl.ds(s, count, stride=8), :]
        return total

    volumes, targets = lanes(vol, POINTS), lanes(tgt, COARSE)
    over = [volumes[FINE * i : FINE * i + FINE] - targets[i : i + 1] for i in range(COARSE)]
    excess[...] = jnp.sum(jnp.transpose(jnp.concatenate(over, axis=0)), axis=0, keepdims=True)


def outer_call(flags, src, rim, nodes, got_even, got_odd, mat, dens, passive, solid, vol_i, tgt_i):
    ny, nz, nx = dens.shape
    rows = nz + 2 * OFF
    field = jax.ShapeDtypeStruct((6, nz, nx), f32)
    return pl.pallas_call(
        outer_kernel,
        in_specs=[SMEM] + [VMEM] * 11,
        out_shape=(field, field, field, jax.ShapeDtypeStruct((1, POINTS), f32)),
        scratch_shapes=[
            pltpu.VMEM((2, 7, rows, nx), f32),
            pltpu.VMEM((2, 5, rows, nx), f32),
            pltpu.VMEM((6, nz, nx), f32),
            pltpu.VMEM((FINE, 6, nz, nx), f32),
            pltpu.VMEM((8 * POINTS, nx), f32),
            pltpu.VMEM((8 * COARSE, nx), f32),
            pltpu.VMEM((2,) + got_odd.shape, f32),
        ]
        + workspace(2, 2, nx),
        compiler_params=pltpu.CompilerParams(vmem_limit_bytes=20 * 2**20),
        cost_estimate=estimate(3),
        name="filter_outer",
    )(flags, src, rim, nodes, got_even, got_odd, mat, dens, passive, solid, vol_i, tgt_i)


def update_kernel(tables, amp_i, low_i, high_i, amp_o, low_o, high_o, new, logm):
    inner = amp_i.shape[0]
    nx = amp_i.shape[-1]
    total = jnp.sum(tables[...], axis=0, keepdims=True)
    lane = lax.broadcasted_iota(jnp.int32, total.shape, 1)
    above = jnp.where((total > 0.0) & (lane > 0), 1.0, 0.0)
    middle = -bracket_end + (2.0 * bracket_end / POINTS) * (jnp.sum(above) + 0.5)
    logm[0] = middle
    scale = jnp.exp(jnp.full((1, nx), -0.5 * middle, f32))

    def new_row(amp, low, high):
        return jnp.minimum(jnp.maximum(amp * scale, low), high)

    def body(j, _):
        new[j + 3] = new_row(amp_i[j], low_i[j], high_i[j])
        return 0

    lax.fori_loop(0, inner, body, 0)
    for j in range(6):
        new[j if j < 3 else inner + j] = new_row(amp_o[j], low_o[j], high_o[j])


def update_call(tables, inner, outer):
    n, nz, nx = inner[0].shape
    return pl.pallas_call(
        update_kernel,
        in_specs=[VMEM] * 7,
        out_specs=(VMEM, SMEM),
        out_shape=(jax.ShapeDtypeStruct((n + 6, nz, nx), f32), jax.ShapeDtypeStruct((1,), f32)),
        compiler_params=pltpu.CompilerParams(vmem_limit_bytes=8 * 2**20),
        cost_estimate=estimate(1),
        name="update",
    )(tables, *inner, *outer)


def to_lower(value, axis):
    count = lax.axis_size(axis)
    return lax.ppermute(value, axis, [(i + 1, i) for i in range(count - 1)])


def swap(value, axis, start):
    pairs = []
    for i in range(start, lax.axis_size(axis) - 1, 2):
        pairs += [(i, i + 1), (i + 1, i)]
    return lax.ppermute(value, axis, pairs)


def on_device(displacement, density, passive, solid, stiffness):
    ny, nz, nx = density.shape
    gy, gz = lax.axis_size("gy"), lax.axis_size("gz")
    iy, iz = lax.axis_index("gy"), lax.axis_index("gz")
    flags = jnp.stack([iy > 0, iy < gy - 1, iz > 0, iz < gz - 1, iy % 2 == 1, iz % 2 == 1]).astype(jnp.int32)

    disp_hbm = pltpu.with_memory_space_constraint(displacement, pltpu.HBM)
    dens_hbm = pltpu.with_memory_space_constraint(density, pltpu.HBM)
    stiff_hbm = pltpu.with_memory_space_constraint(stiffness, pltpu.HBM)

    fy = to_lower(face_call(disp_hbm), "gy")
    disp, dens, mat, mat_y = load_call(disp_hbm, dens_hbm, stiff_hbm)
    ends, up, down, z_even, z_odd = ends_call(flags, disp, dens, mat)

    z_got_even = swap(z_even, "gz", 0)
    z_got_odd = swap(z_odd, "gz", 1)
    src = middle_call(disp, dens, fy, mat, ends)
    rim, nodes, msg_even, msg_odd = rim_call(flags, z_got_even, z_got_odd, up, down, disp, dens, mat_y, src)

    got_even = swap(msg_even, "gy", 0)
    got_odd = swap(msg_odd, "gy", 1)
    *inner, vol, tgt = inner_call(flags, src, rim, dens, passive, solid)
    *outer, excess = outer_call(flags, src, rim, nodes, got_even, got_odd, mat, dens, passive, solid, vol, tgt)

    everyone = jnp.broadcast_to(excess, (gz * gy, POINTS))
    tables = lax.all_to_all(everyone, ("gz", "gy"), 0, 0, tiled=True)
    new, logm = update_call(tables, inner, outer)
    return new, logm.reshape(())


def solution(mesh):
    placed = (
        P(None, "gy", "gz", None),
        P("gy", "gz", None),
        P("gy", "gz", None),
        P("gy", "gz", None),
        P(),
    )
    return jax.shard_map(
        on_device, mesh=mesh, in_specs=placed, out_specs=(P("gy", "gz", None), P()), check_vma=False
    )
```

```python
import math

import jax
import jax.numpy as jnp
from jax import lax
from jax.experimental import pallas as pl
from jax.experimental.pallas import tpu as pltpu
from jax.sharding import PartitionSpec as P

ITERS = 8
POINTS = 2**ITERS
OFF = 8

smoothing = 0.52
move_limit = 0.2
floor_density = 0.001
bracket_end = 12.0

f32 = jnp.float32
bf16 = jnp.bfloat16
VMEM = pl.BlockSpec(memory_space=pltpu.VMEM)
SMEM = pl.BlockSpec(memory_space=pltpu.SMEM)
HBM = pl.BlockSpec(memory_space=pltpu.HBM)


def cheb_weights():
    spectrum_top = 1.0 + 12.0 * smoothing
    centre_value = (spectrum_top + 1.0) / 2.0
    half_width = (spectrum_top - 1.0) / 2.0
    ratio_value = centre_value / half_width
    first_rho = 1.0 / ratio_value
    second_rho = 1.0 / (2.0 * ratio_value - first_rho)
    third_rho = 1.0 / (2.0 * ratio_value - second_rho)
    return (
        centre_value,
        second_rho * first_rho,
        2.0 * second_rho / half_width,
        third_rho * second_rho,
        2.0 * third_rho / half_width,
    )


def filter_weights():
    t, w1, w2, w3, w4 = cheb_weights()
    diag = 1.0 + 6.0 * smoothing
    alpha = w1 / t + w2 * (1.0 - diag / t)
    beta = w2 * smoothing / t
    gamma = 1.0 / t - w4 * w1 / (t * w2)
    delta = 1.0 + w3 + w4 / w2 - w4 * diag
    eps = w4 * smoothing
    return alpha, beta, gamma, delta, eps


def lane_up(v):
    n = v.shape[-1]
    lane = lax.broadcasted_iota(jnp.int32, v.shape, v.ndim - 1)
    return jnp.where(lane < n - 1, pltpu.roll(v, n - 1, v.ndim - 1), 0.0)


def lane_down(v):
    n = v.shape[-1]
    lane = lax.broadcasted_iota(jnp.int32, v.shape, v.ndim - 1)
    return jnp.where(lane > 0, pltpu.roll(v, 1, v.ndim - 1), 0.0)


def estimate(us):
    return pl.CostEstimate(flops=int(us * 1e9), bytes_accessed=1 << 20, transcendentals=0)


def build_matrices(k, mats):
    shape = (24, 128)
    col = lax.broadcasted_iota(jnp.int32, shape, 1)
    row = lax.broadcasted_iota(jnp.int32, shape, 0)
    main = col < 96
    q = jnp.where(main, jnp.where(col >= 48, 1, 0), jnp.where(col >= 104, 1, 0))
    m = col - 48 * q
    e = col - 96 - 8 * q
    c = jnp.where(main, m >> 4, e >> 1)
    dx = jnp.where(main, (m >> 3) & 1, e & 1)
    valid = main | (e < 6)
    picks = []
    for _, plane, band in mats:
        dof0 = 3 * (plane * q + dx) + c
        picks.append(jnp.where(main & (row == dof0), 1.0, 0.0))
        picks.append(jnp.where(valid & (row == dof0 + 3 * band), 1.0, 0.0))
    picked = jnp.dot(
        k, jnp.concatenate(picks, axis=1), precision=lax.Precision.HIGHEST, preferred_element_type=f32
    )
    col8 = lax.broadcasted_iota(jnp.int32, (8, 128), 1)
    row8 = lax.broadcasted_iota(jnp.int32, (8, 128), 0)
    main8 = col8 < 96
    rc = col8 & 7
    m0 = main8 & (rc == row8)
    m1 = jnp.where(main8, rc, 8) == row8 + 1
    for n, (mat, plane, band) in enumerate(mats):
        k0 = picked[:, 256 * n : 256 * n + 128]
        k1 = picked[:, 256 * n + 128 : 256 * n + 256]
        rows = []
        for b in range(2):
            for q_ in range(2):
                for c_ in range(3):
                    for dx_ in range(2):
                        r = 3 * (plane * q_ + band * b + dx_) + c_
                        rows.append(jnp.where(m0, k0[r : r + 1], 0.0) + jnp.where(m1, k1[r : r + 1], 0.0))
        full = jnp.concatenate(rows, axis=0)
        hi = full.astype(bf16)
        lo = (full - hi.astype(f32)).astype(bf16)
        mat[:, 0:112] = hi[:, 0:112]
        mat[:, 112:224] = lo[:, 0:112]


def prepare(segments, p, work):
    main_s, ext_s, mul_s = work
    for l in range(3):
        for c in range(3):
            w0 = 0
            for u, x in segments(3 * l + c):
                size, nx = u.shape
                n = size // 8
                last = lax.broadcasted_iota(jnp.int32, u.shape, 0) == size - 1
                both = (u, lane_up(u))
                after = (None, None) if x is None else (x, lane_up(x))
                for w in range(n):
                    sl = slice(8 * w, 8 * w + 8)
                    main_s[p, l, 16 * c : 16 * c + 16, (w0 + w) * nx : (w0 + w + 1) * nx] = jnp.concatenate(
                        [both[0][sl], both[1][sl]], axis=0
                    ).astype(bf16)
                for dx in range(2):
                    v, vx = both[dx], after[dx]
                    k = 2 * c + dx
                    for w in range(n):
                        nxt = v[8 * w + 8 : 8 * w + 9] if w < n - 1 else vx
                        if nxt is not None:
                            ext_s[p, l, k : k + 1, (w0 + w) * nx : (w0 + w + 1) * nx] = nxt
                    m = 2.0 * v - v.astype(bf16).astype(f32)
                    mx = 0.0 if vx is None else jnp.broadcast_to(2.0 * vx - vx.astype(bf16).astype(f32), v.shape)
                    at = slice(8 * w0, 8 * (w0 + n))
                    mul_s[p, l, k, 0, at] = m
                    mul_s[p, l, k, 1, at] = jnp.where(last, mx, pltpu.roll(m, size - 1, 0))
                w0 += n


def energy_rows(p, mat, work, density):
    main_s, ext_s, mul_s = work
    rows, nx = density.shape
    count = rows // 8
    acc = [None] * count
    for l in range(3):
        ext = jnp.concatenate([ext_s[p, l], ext_s[p + 1, l]], axis=0).astype(bf16)
        one = jnp.concatenate([main_s[p, l], main_s[p + 1, l], ext], axis=0)
        force = jnp.dot(mat[...], jnp.concatenate([one, one], axis=0), preferred_element_type=f32)
        i = 0
        for b in range(2):
            for q in range(2):
                for k in range(6):
                    for w in range(count):
                        at = slice(8 * w, 8 * w + 8)
                        term = force[8 * i : 8 * i + 8, w * nx : (w + 1) * nx] * mul_s[p + q, l, k, b, at]
                        acc[w] = term if acc[w] is None else acc[w] + term
                    i += 1
    return density * (-3.0 * density * density * jnp.concatenate(acc, axis=0))


def workspace(planes, windows, nx):
    return [
        pltpu.VMEM((planes, 3, 48, windows * nx), bf16),
        pltpu.VMEM((planes, 3, 8, windows * nx), f32),
        pltpu.VMEM((planes, 3, 6, 2, 8 * windows, nx), f32),
    ]


def sweep(rows, segments, put, work):
    work[1][...] = jnp.zeros_like(work[1])
    for p in range(2):
        prepare(segments(p), p, work)

    def body(y, _):
        put(y)
        prepare(segments(y + 2), y + 2, work)
        return 0

    lax.fori_loop(0, rows - 1, body, 0, unroll=7)
    put(rows - 1)


def face_kernel(disp, face, sem):
    copy = pltpu.make_async_copy(disp.at[:, 0], face, sem)
    copy.start()
    copy.wait()


def face_call(disp):
    _, _, nz, nx = disp.shape
    return pl.pallas_call(
        face_kernel,
        in_specs=[HBM],
        out_shape=jax.ShapeDtypeStruct((9, nz, nx), f32),
        scratch_shapes=[pltpu.SemaphoreType.DMA],
        compiler_params=pltpu.CompilerParams(vmem_limit_bytes=2**20),
        name="face",
    )(disp)


def extra(ref, row):
    ny = ref.shape[1]
    return 11 + row // ny, slice(row % ny, row % ny + 1)


def load_kernel(disp_h, dens_h, stiff, disp, dens, mat, mat_y, stiff_s, sems):
    copies = [pltpu.make_async_copy(stiff, stiff_s, sems.at[0])]
    for l in range(3):
        part = pl.ds(3 * l, 3)
        copies.append(pltpu.make_async_copy(disp_h.at[part], disp.at[part], sems.at[1 + l]))
    copies.append(pltpu.make_async_copy(dens_h, dens, sems.at[4]))
    for copy in copies:
        copy.start()
    copies[0].wait()
    build_matrices(stiff_s[...], ((mat, 4, 2), (mat_y, 2, 4)))
    for copy in copies[1:]:
        copy.wait()


def load_call(disp, dens, stiff):
    matrix = jax.ShapeDtypeStruct((192, 224), bf16)
    return pl.pallas_call(
        load_kernel,
        in_specs=[HBM, HBM, HBM],
        out_shape=(
            jax.ShapeDtypeStruct(disp.shape, f32),
            jax.ShapeDtypeStruct(dens.shape, f32),
            matrix,
            matrix,
        ),
        scratch_shapes=[pltpu.VMEM((24, 24), f32), pltpu.SemaphoreType.DMA((5,))],
        compiler_params=pltpu.CompilerParams(vmem_limit_bytes=16 * 2**20),
        cost_estimate=estimate(2),
        name="load",
    )(disp, dens, stiff)


def ends_kernel(flags, disp, dens, mat, ends, up, down, msg_even, msg_odd, *work):
    _, ny, nz, nx = disp.shape

    def segments(p):
        return lambda i: [(disp[i, p, 0:8], disp[i, p, 8:9]), (disp[i, p, nz - 8 : nz], None)]

    for ref in (up, down):
        ref[9:] = jnp.zeros((ref.shape[0] - 9, ny, nx), f32)

    def pack(y):
        row = pl.ds(y, 1)
        for i in range(9):
            up[i, row] = disp[i, y, nz - 1 : nz]
            down[i, row] = disp[i, y, 0:1]
        up[9, row] = dens[y, nz - 1 : nz]

    def put(y):
        d = jnp.concatenate([dens[y, 0:8], dens[y, nz - 8 : nz]], axis=0)
        s = energy_rows(y, mat, work, d)
        ends[y] = s
        row = pl.ds(y, 1)
        up[10, row] = s[14:15]
        down[9, row] = s[0:1]
        down[10, row] = s[1:2]
        pack(y)

    sweep(ny - 1, segments, put, work)
    pack(ny - 1)
    for n, y in enumerate((0, ny - 1)):
        for i in range(9):
            up[extra(up, 9 * n + i)] = disp[i, y, nz - 2 : nz - 1]
            down[extra(down, 9 * n + i)] = disp[i, y, 1:2]
            down[extra(down, 18 + 9 * n + i)] = disp[i, y, 2:3]
    up[extra(up, 36)] = dens[ny - 1, nz - 2 : nz - 1]
    down[extra(down, 36)] = dens[ny - 1, 0:1]
    down[extra(down, 37)] = dens[ny - 1, 1:2]
    odd = flags[5] == 1
    msg_even[...] = jnp.where(odd, down[...], up[...])
    msg_odd[...] = jnp.where(odd, up[...], down[...])


def ends_call(flags, disp, dens, mat):
    _, ny, nz, nx = disp.shape
    message = jax.ShapeDtypeStruct((11 + -(-38 // ny), ny, nx), f32)
    return pl.pallas_call(
        ends_kernel,
        in_specs=[SMEM] + [VMEM] * 3,
        out_shape=(jax.ShapeDtypeStruct((ny, 16, nx), f32),) + (message,) * 4,
        scratch_shapes=workspace(ny, 2, nx),
        compiler_params=pltpu.CompilerParams(vmem_limit_bytes=16 * 2**20),
        cost_estimate=estimate(4),
        name="energy_ends",
    )(flags, disp, dens, mat)


def middle_kernel(disp, dens, fy, mat, ends, src, *work):
    _, ny, nz, nx = disp.shape
    work, last = work[:3], work[3:]

    def segments(p):
        return lambda i: [(disp[i, p, 8 : nz - 8], disp[i, p, nz - 8 : nz - 7])]

    def frame(y):
        src[y, 0:OFF] = jnp.zeros((OFF, nx), f32)
        src[y, OFF + nz :] = jnp.zeros((src.shape[1] - OFF - nz, nx), f32)

    def put(y):
        frame(y)
        src[y, OFF : OFF + 8] = ends[y, 0:8]
        src[y, OFF + 8 : OFF + nz - 8] = energy_rows(y, mat, work, dens[y, 8 : nz - 8])
        src[y, OFF + nz - 8 : OFF + nz] = ends[y, 8:16]

    sweep(ny - 1, segments, put, work)
    last[1][...] = jnp.zeros_like(last[1])
    prepare(lambda i: [(disp[i, ny - 1], None)], 0, last)
    prepare(lambda i: [(fy[i], None)], 1, last)
    frame(ny - 1)
    src[ny - 1, OFF : OFF + nz] = energy_rows(0, mat, last, dens[ny - 1])


def middle_call(disp, dens, fy, mat, ends):
    _, ny, nz, nx = disp.shape
    return pl.pallas_call(
        middle_kernel,
        in_specs=[VMEM] * 5,
        out_shape=jax.ShapeDtypeStruct((ny, nz + 2 * OFF, nx), f32),
        scratch_shapes=workspace(ny, nz // 8 - 2, nx) + workspace(2, nz // 8, nx),
        compiler_params=pltpu.CompilerParams(vmem_limit_bytes=24 * 2**20),
        cost_estimate=estimate(4),
        name="energy_middle",
    )(disp, dens, fy, mat, ends)


def rim_kernel(
    flags, got_even, got_odd, up, down, disp, dens, mat_y, src,
    rim, nodes, msg_even, msg_odd, low_s, high_s, t_s, *work,
):
    ny, rows, nx = src.shape
    nz = rows - 2 * OFF
    odd = flags[5] == 1
    low_s[...] = jnp.where(odd, got_even[...], got_odd[...])
    high_s[...] = jnp.where(odd, got_odd[...], got_even[...])
    work[1][...] = jnp.zeros_like(work[1])
    prepare(lambda i: [(low_s[i], None), (up[i], None)], 0, work)
    prepare(lambda i: [(down[i], None), (high_s[i], None)], 1, work)
    s = energy_rows(0, mat_y, work, jnp.concatenate([low_s[9], up[9]], axis=0))
    columns = ((0, low_s[10]), (1, s[0:ny]), (3, s[ny : 2 * ny]), (4, high_s[9]), (5, high_s[10]))
    for y in range(ny):
        rim[y] = jnp.zeros((8, nx), f32)
        for r, column in columns:
            rim[y, r : r + 1] = column[y : y + 1]
    half = 2 * (nz + 8)
    zero = jnp.zeros((1, nx), f32)
    for n, y in enumerate((0, ny - 1)):
        row = slice(y, y + 1)
        for i in range(9):
            window = jnp.concatenate(
                [
                    low_s[extra(low_s, 9 * n + i)],
                    low_s[i, row],
                    disp[i, y, 0:1],
                    disp[i, y, nz - 1 : nz],
                    high_s[i, row],
                    high_s[extra(high_s, 9 * n + i)],
                    high_s[extra(high_s, 18 + 9 * n + i)],
                    zero,
                ],
                axis=0,
            )
            nodes[n, i] = window
            t_s[n, half + 8 * i : half + 8 * i + 8] = window
        nodes[n, 9] = jnp.concatenate(
            [
                low_s[extra(low_s, 36)],
                low_s[9, ny - 1 : ny],
                zero,
                dens[ny - 1, nz - 1 : nz],
                high_s[extra(high_s, 36)],
                high_s[extra(high_s, 37)],
                zero,
                zero,
            ],
            axis=0,
        )
        t_s[n, half + 72 : half + 80] = nodes[n, 9]
        for j in range(2):
            at = j * (nz + 8)
            yy = j if n == 0 else ny - 2 + j
            t_s[n, at : at + nz] = src[yy, OFF : OFF + nz]
            t_s[n, at + nz : at + nz + 8] = rim[yy]
    odd = flags[4] == 1
    msg_even[...] = jnp.where(odd, t_s[0], t_s[1])
    msg_odd[...] = jnp.where(odd, t_s[1], t_s[0])


def put_rim(s, y, rim, nz):
    s[y, OFF - 2 : OFF] = rim[0:2]
    s[y, OFF + nz - 1 : OFF + nz + 2] = rim[3:6]


def rim_call(flags, got_even, got_odd, up, down, disp, dens, mat_y, src):
    ny, rows, nx = src.shape
    nz = rows - 2 * OFF
    size = 2 * (nz + 8) + 80
    return pl.pallas_call(
        rim_kernel,
        in_specs=[SMEM] + [VMEM] * 8,
        out_shape=(
            jax.ShapeDtypeStruct((ny, 8, nx), f32),
            jax.ShapeDtypeStruct((2, 10, 8, nx), f32),
            jax.ShapeDtypeStruct((size, nx), f32),
            jax.ShapeDtypeStruct((size, nx), f32),
        ),
        scratch_shapes=[
            pltpu.VMEM(up.shape, f32),
            pltpu.VMEM(up.shape, f32),
            pltpu.VMEM((2, size, nx), f32),
        ]
        + workspace(2, 2 * (ny // 8), nx),
        compiler_params=pltpu.CompilerParams(vmem_limit_bytes=16 * 2**20),
        cost_estimate=estimate(2),
        name="energy_rim",
    )(flags, got_even, got_odd, up, down, disp, dens, mat_y, src)


def filter_block(s_s, d_s, n, z_edges, y_edges, finish, unroll):
    rows, nx = s_s.shape[1:]
    nz = rows - 2 * OFF
    alpha, beta, gamma, delta, eps = filter_weights()
    row = lax.broadcasted_iota(jnp.int32, (rows, nx), 0)
    keep = jnp.where(row < OFF, z_edges[0], jnp.where(row >= OFF + nz, z_edges[1], 1)) == 1

    def beside(v):
        return pltpu.roll(v, 1, 0) + pltpu.roll(v, rows - 1, 0) + lane_up(v) + lane_down(v)

    def second(j, _):
        c = s_s[j + 1]
        d2 = alpha * c + beta * (beside(c) + s_s[j] + s_s[j + 2])
        ok = keep
        if y_edges is not None:
            ok = keep & (jnp.where(j == 0, y_edges[0], jnp.where(j == n - 3, y_edges[1], 1)) == 1)
        d_s[j] = jnp.where(ok, d2, 0.0)
        return 0

    def third(j, _):
        d2 = d_s[j + 1]
        p3 = gamma * s_s[j + 2] + delta * d2 + eps * (beside(d2) + d_s[j] + d_s[j + 2])
        finish(j, p3[OFF : OFF + nz])
        return 0

    lax.fori_loop(0, n - 2, second, 0, unroll=unroll)
    lax.fori_loop(0, n - 4, third, 0, unroll=unroll)


def limits(p3, d, pas, sol):
    amp = jnp.sqrt(jnp.maximum(-p3 * d, 0.0))
    lower = jnp.maximum(d - move_limit, floor_density)
    upper = jnp.minimum(d + move_limit, 1.0)
    low, high, now = (jnp.where(sol, 1.0, jnp.where(pas, floor_density, v)) for v in (lower, upper, d))
    return amp, low, high, now


FINE = 16
COARSE = POINTS // FINE


def table(n, nz, nx, amp, low, high, now, fine_s, vol, tgt, start, unroll):
    spacing = 2.0 * bracket_end / POINTS

    pair = 2
    for first in range(0, COARSE, pair):
        inverse = [math.exp(0.5 * (-bracket_end + spacing * FINE * i)) for i in range(first, first + pair)]

        def volume(j, acc):
            acc = list(acc)
            for w in range(nz // 8):
                at = slice(8 * w, 8 * w + 8)
                lo, hi, d = low[j, at], high[j, at], now[j, at]
                los, his = [lo * c for c in inverse], [hi * c for c in inverse]
                for i, c in enumerate(inverse):
                    acc[pair * FINE + i] = acc[pair * FINE + i] + d * c
                for f in range(FINE):
                    if first == 0:
                        t = amp[j, at] * math.exp(-0.5 * spacing * f)
                        fine_s[f, j, at] = t
                    else:
                        t = fine_s[f, j, at]
                    for i in range(pair):
                        acc[i * FINE + f] = acc[i * FINE + f] + jnp.minimum(jnp.maximum(t, los[i]), his[i])
            return tuple(acc)

        places = [(vol, 8 * (first * FINE + e)) for e in range(pair * FINE)]
        places += [(tgt, 8 * (first + i)) for i in range(pair)]
        if start is None:
            begin = tuple(jnp.zeros((8, nx), f32) for _ in places)
        else:
            begin = tuple((start[0] if ref is vol else start[1])[at : at + 8] for ref, at in places)
        acc = lax.fori_loop(0, n, volume, begin, unroll=unroll)
        for (ref, at), value in zip(places, acc):
            ref[at : at + 8] = value


def inner_kernel(flags, src, rim, dens, passive, solid, amp, low, high, vol, tgt, s_s, d_s, now_s, fine_s):
    ny, nz, nx = dens.shape
    s_s[...] = src[0 : ny - 1]

    def fix(y, _):
        put_rim(s_s, y, rim[y], nz)
        return 0

    lax.fori_loop(0, ny - 1, fix, 0, unroll=5)

    def finish(j, p3):
        y = j + 2
        amp[j], low[j], high[j], now_s[j] = limits(p3, dens[y], passive[y] == 1, solid[y] == 1)

    filter_block(s_s, d_s, ny - 1, (flags[2], flags[3]), None, finish, 4)
    table(ny - 5, nz, nx, amp, low, high, now_s, fine_s, vol, tgt, None, 4)


def inner_call(flags, src, rim, dens, passive, solid):
    ny, nz, nx = dens.shape
    field = jax.ShapeDtypeStruct((ny - 5, nz, nx), f32)
    return pl.pallas_call(
        inner_kernel,
        in_specs=[SMEM] + [VMEM] * 5,
        out_shape=(
            field,
            field,
            field,
            jax.ShapeDtypeStruct((8 * POINTS, nx), f32),
            jax.ShapeDtypeStruct((8 * COARSE, nx), f32),
        ),
        scratch_shapes=[
            pltpu.VMEM((ny - 1, nz + 2 * OFF, nx), f32),
            pltpu.VMEM((ny - 3, nz + 2 * OFF, nx), f32),
            pltpu.VMEM((ny - 5, nz, nx), f32),
            pltpu.VMEM((FINE, ny - 5, nz, nx), f32),
        ],
        compiler_params=pltpu.CompilerParams(vmem_limit_bytes=24 * 2**20),
        cost_estimate=estimate(9),
        name="filter_inner",
    )(flags, src, rim, dens, passive, solid)


def outer_kernel(
    flags, src, rim, nodes, got_even, got_odd, mat, dens, passive, solid, vol_i, tgt_i,
    amp, low, high, excess, s_s, d_s, now_s, fine_s, vol, tgt, below, above, *work,
):
    ny, nz, nx = dens.shape
    odd = flags[4] == 1
    below[...] = jnp.where(odd, got_even[...], got_odd[...])
    above[...] = jnp.where(odd, got_odd[...], got_even[...])
    half = 2 * (nz + 8)

    def window(ref, i):
        return ref[half + 8 * i : half + 8 * i + 8]

    work[1][...] = jnp.zeros_like(work[1])
    prepare(lambda i: [(window(below, i), None), (nodes[1, i], None)], 0, work)
    prepare(lambda i: [(nodes[0, i], None), (window(above, i), None)], 1, work)
    corner = energy_rows(0, mat, work, jnp.concatenate([window(below, 9), nodes[1, 9]], axis=0))
    for b, ref in enumerate((below, above)):
        for j in range(2):
            at = j if b == 0 else 5 + j
            start = j * (nz + 8)
            s_s[b, at, 0:OFF] = jnp.zeros((OFF, nx), f32)
            s_s[b, at, OFF : OFF + nz] = ref[start : start + nz]
            s_s[b, at, OFF + nz :] = jnp.zeros((OFF, nx), f32)
            put_rim(s_s.at[b], at, ref[start + nz : start + nz + 8], nz)
    for j in range(4):
        s_s[0, 2 + j] = src[j]
        put_rim(s_s.at[0], 2 + j, rim[j], nz)
    for j in range(5):
        s_s[1, j] = src[ny - 5 + j]
        put_rim(s_s.at[1], j, rim[ny - 5 + j], nz)
    put_rim(s_s.at[0], 1, corner[0:8], nz)
    put_rim(s_s.at[1], 4, corner[8:16], nz)
    for b in range(2):
        y0 = 0 if b == 0 else ny - 3

        def finish(j, p3):
            y = y0 + j
            at = 2 * b + j
            amp[at], low[at], high[at], now_s[at] = limits(p3, dens[y], passive[y] == 1, solid[y] == 1)

        edges = (flags[0], 1) if b == 0 else (1, flags[1])
        filter_block(s_s.at[b], d_s.at[b], 6 + b, (flags[2], flags[3]), edges, finish, True)
    table(5, nz, nx, amp, low, high, now_s, fine_s, vol, tgt, (vol_i, tgt_i), 2)

    def lanes(ref, count):
        total = ref[pl.ds(0, count, stride=8), :]
        for s in range(1, 8):
            total = total + ref[pl.ds(s, count, stride=8), :]
        return total

    volumes, targets = lanes(vol, POINTS), lanes(tgt, COARSE)
    over = [volumes[FINE * i : FINE * i + FINE] - targets[i : i + 1] for i in range(COARSE)]
    excess[...] = jnp.sum(jnp.transpose(jnp.concatenate(over, axis=0)), axis=0, keepdims=True)


def outer_call(flags, src, rim, nodes, got_even, got_odd, mat, dens, passive, solid, vol_i, tgt_i):
    ny, nz, nx = dens.shape
    rows = nz + 2 * OFF
    field = jax.ShapeDtypeStruct((5, nz, nx), f32)
    return pl.pallas_call(
        outer_kernel,
        in_specs=[SMEM] + [VMEM] * 11,
        out_shape=(field, field, field, jax.ShapeDtypeStruct((1, POINTS), f32)),
        scratch_shapes=[
            pltpu.VMEM((2, 7, rows, nx), f32),
            pltpu.VMEM((2, 5, rows, nx), f32),
            pltpu.VMEM((5, nz, nx), f32),
            pltpu.VMEM((FINE, 5, nz, nx), f32),
            pltpu.VMEM((8 * POINTS, nx), f32),
            pltpu.VMEM((8 * COARSE, nx), f32),
            pltpu.VMEM(got_odd.shape, f32),
            pltpu.VMEM(got_odd.shape, f32),
        ]
        + workspace(2, 2, nx),
        compiler_params=pltpu.CompilerParams(vmem_limit_bytes=20 * 2**20),
        cost_estimate=estimate(3),
        name="filter_outer",
    )(flags, src, rim, nodes, got_even, got_odd, mat, dens, passive, solid, vol_i, tgt_i)


def update_kernel(tables, amp_i, low_i, high_i, amp_o, low_o, high_o, new, logm):
    inner = amp_i.shape[0]
    nx = amp_i.shape[-1]
    total = jnp.sum(tables[...], axis=0, keepdims=True)
    lane = lax.broadcasted_iota(jnp.int32, total.shape, 1)
    above = jnp.where((total > 0.0) & (lane > 0), 1.0, 0.0)
    middle = -bracket_end + (2.0 * bracket_end / POINTS) * (jnp.sum(above) + 0.5)
    logm[0] = middle
    scale = jnp.exp(jnp.full((1, nx), -0.5 * middle, f32))

    def new_row(amp, low, high):
        return jnp.minimum(jnp.maximum(amp * scale, low), high)

    def body(j, _):
        new[j + 2] = new_row(amp_i[j], low_i[j], high_i[j])
        return 0

    lax.fori_loop(0, inner, body, 0)
    for j in range(5):
        new[j if j < 2 else inner + j] = new_row(amp_o[j], low_o[j], high_o[j])


def update_call(tables, inner, outer):
    n, nz, nx = inner[0].shape
    return pl.pallas_call(
        update_kernel,
        in_specs=[VMEM] * 7,
        out_specs=(VMEM, SMEM),
        out_shape=(jax.ShapeDtypeStruct((n + 5, nz, nx), f32), jax.ShapeDtypeStruct((1,), f32)),
        compiler_params=pltpu.CompilerParams(vmem_limit_bytes=8 * 2**20),
        cost_estimate=estimate(1),
        name="update",
    )(tables, *inner, *outer)


def to_lower(value, axis):
    count = lax.axis_size(axis)
    return lax.ppermute(value, axis, [(i + 1, i) for i in range(count - 1)])


def swap(value, axis, start):
    pairs = []
    for i in range(start, lax.axis_size(axis) - 1, 2):
        pairs += [(i, i + 1), (i + 1, i)]
    return lax.ppermute(value, axis, pairs)


def on_device(displacement, density, passive, solid, stiffness):
    ny, nz, nx = density.shape
    gy, gz = lax.axis_size("gy"), lax.axis_size("gz")
    iy, iz = lax.axis_index("gy"), lax.axis_index("gz")
    flags = jnp.stack([iy > 0, iy < gy - 1, iz > 0, iz < gz - 1, iy % 2 == 1, iz % 2 == 1]).astype(jnp.int32)

    disp_hbm = pltpu.with_memory_space_constraint(displacement, pltpu.HBM)
    dens_hbm = pltpu.with_memory_space_constraint(density, pltpu.HBM)
    stiff_hbm = pltpu.with_memory_space_constraint(stiffness, pltpu.HBM)

    fy = to_lower(face_call(disp_hbm), "gy")
    disp, dens, mat, mat_y = load_call(disp_hbm, dens_hbm, stiff_hbm)
    ends, up, down, z_even, z_odd = ends_call(flags, disp, dens, mat)

    z_got_even = swap(z_even, "gz", 0)
    z_got_odd = swap(z_odd, "gz", 1)
    src = middle_call(disp, dens, fy, mat, ends)
    rim, nodes, msg_even, msg_odd = rim_call(flags, z_got_even, z_got_odd, up, down, disp, dens, mat_y, src)

    got_even = swap(msg_even, "gy", 0)
    got_odd = swap(msg_odd, "gy", 1)
    *inner, vol, tgt = inner_call(flags, src, rim, dens, passive, solid)
    *outer, excess = outer_call(flags, src, rim, nodes, got_even, got_odd, mat, dens, passive, solid, vol, tgt)

    everyone = jnp.broadcast_to(excess, (gz * gy, POINTS))
    tables = lax.all_to_all(everyone, ("gz", "gy"), 0, 0, tiled=True)
    new, logm = update_call(tables, inner, outer)
    return new, logm.reshape(())


def solution(mesh):
    placed = (
        P(None, "gy", "gz", None),
        P("gy", "gz", None),
        P("gy", "gz", None),
        P("gy", "gz", None),
        P(),
    )
    return jax.shard_map(
        on_device, mesh=mesh, in_specs=placed, out_specs=(P("gy", "gz", None), P()), check_vma=False
    )
```

```python
import math

import jax
import jax.numpy as jnp
from jax import lax
from jax.experimental import pallas as pl
from jax.experimental.pallas import tpu as pltpu
from jax.sharding import PartitionSpec as P

ITERS = 8
POINTS = 2**ITERS
OFF = 8

smoothing = 0.52
move_limit = 0.2
floor_density = 0.001
bracket_end = 12.0

f32 = jnp.float32
bf16 = jnp.bfloat16
VMEM = pl.BlockSpec(memory_space=pltpu.VMEM)
SMEM = pl.BlockSpec(memory_space=pltpu.SMEM)
HBM = pl.BlockSpec(memory_space=pltpu.HBM)


def cheb_weights():
    spectrum_top = 1.0 + 12.0 * smoothing
    centre_value = (spectrum_top + 1.0) / 2.0
    half_width = (spectrum_top - 1.0) / 2.0
    ratio_value = centre_value / half_width
    first_rho = 1.0 / ratio_value
    second_rho = 1.0 / (2.0 * ratio_value - first_rho)
    third_rho = 1.0 / (2.0 * ratio_value - second_rho)
    return (
        centre_value,
        second_rho * first_rho,
        2.0 * second_rho / half_width,
        third_rho * second_rho,
        2.0 * third_rho / half_width,
    )


def filter_weights():
    t, w1, w2, w3, w4 = cheb_weights()
    diag = 1.0 + 6.0 * smoothing
    alpha = w1 / t + w2 * (1.0 - diag / t)
    beta = w2 * smoothing / t
    gamma = 1.0 / t - w4 * w1 / (t * w2)
    delta = 1.0 + w3 + w4 / w2 - w4 * diag
    eps = w4 * smoothing
    return alpha, beta, gamma, delta, eps


def lane_up(v):
    n = v.shape[-1]
    lane = lax.broadcasted_iota(jnp.int32, v.shape, v.ndim - 1)
    return jnp.where(lane < n - 1, pltpu.roll(v, n - 1, v.ndim - 1), 0.0)


def lane_down(v):
    n = v.shape[-1]
    lane = lax.broadcasted_iota(jnp.int32, v.shape, v.ndim - 1)
    return jnp.where(lane > 0, pltpu.roll(v, 1, v.ndim - 1), 0.0)


def estimate(us):
    return pl.CostEstimate(flops=int(us * 1e9), bytes_accessed=1 << 20, transcendentals=0)


def build_matrices(k, mats):
    shape = (24, 128)
    col = lax.broadcasted_iota(jnp.int32, shape, 1)
    row = lax.broadcasted_iota(jnp.int32, shape, 0)
    main = col < 96
    q = jnp.where(main, jnp.where(col >= 48, 1, 0), jnp.where(col >= 104, 1, 0))
    m = col - 48 * q
    e = col - 96 - 8 * q
    c = jnp.where(main, m >> 4, e >> 1)
    dx = jnp.where(main, (m >> 3) & 1, e & 1)
    valid = main | (e < 6)
    picks = []
    for _, plane, band in mats:
        dof0 = 3 * (plane * q + dx) + c
        picks.append(jnp.where(main & (row == dof0), 1.0, 0.0))
        picks.append(jnp.where(valid & (row == dof0 + 3 * band), 1.0, 0.0))
    picked = jnp.dot(
        k, jnp.concatenate(picks, axis=1), precision=lax.Precision.HIGHEST, preferred_element_type=f32
    )
    col8 = lax.broadcasted_iota(jnp.int32, (8, 128), 1)
    row8 = lax.broadcasted_iota(jnp.int32, (8, 128), 0)
    main8 = col8 < 96
    rc = col8 & 7
    m0 = main8 & (rc == row8)
    m1 = jnp.where(main8, rc, 8) == row8 + 1
    for n, (mat, plane, band) in enumerate(mats):
        k0 = picked[:, 256 * n : 256 * n + 128]
        k1 = picked[:, 256 * n + 128 : 256 * n + 256]
        rows = []
        for b in range(2):
            for q_ in range(2):
                for c_ in range(3):
                    for dx_ in range(2):
                        r = 3 * (plane * q_ + band * b + dx_) + c_
                        rows.append(jnp.where(m0, k0[r : r + 1], 0.0) + jnp.where(m1, k1[r : r + 1], 0.0))
        full = jnp.concatenate(rows, axis=0)
        hi = full.astype(bf16)
        lo = (full - hi.astype(f32)).astype(bf16)
        mat[:, 0:112] = hi[:, 0:112]
        mat[:, 112:224] = lo[:, 0:112]


def prepare(segments, p, work):
    main_s, ext_s, mul_s = work
    for l in range(3):
        for c in range(3):
            w0 = 0
            for u, x in segments(3 * l + c):
                size, nx = u.shape
                n = size // 8
                last = lax.broadcasted_iota(jnp.int32, u.shape, 0) == size - 1
                both = (u, lane_up(u))
                after = (None, None) if x is None else (x, lane_up(x))
                for w in range(n):
                    sl = slice(8 * w, 8 * w + 8)
                    main_s[p, l, 16 * c : 16 * c + 16, (w0 + w) * nx : (w0 + w + 1) * nx] = jnp.concatenate(
                        [both[0][sl], both[1][sl]], axis=0
                    ).astype(bf16)
                for dx in range(2):
                    v, vx = both[dx], after[dx]
                    k = 2 * c + dx
                    for w in range(n):
                        nxt = v[8 * w + 8 : 8 * w + 9] if w < n - 1 else vx
                        if nxt is not None:
                            ext_s[p, l, k : k + 1, (w0 + w) * nx : (w0 + w + 1) * nx] = nxt
                    m = 2.0 * v - v.astype(bf16).astype(f32)
                    mx = 0.0 if vx is None else jnp.broadcast_to(2.0 * vx - vx.astype(bf16).astype(f32), v.shape)
                    at = slice(8 * w0, 8 * (w0 + n))
                    mul_s[p, l, k, 0, at] = m
                    mul_s[p, l, k, 1, at] = jnp.where(last, mx, pltpu.roll(m, size - 1, 0))
                w0 += n


def energy_rows(p, mat, work, density):
    main_s, ext_s, mul_s = work
    rows, nx = density.shape
    count = rows // 8
    acc = [None] * count
    for l in range(3):
        ext = jnp.concatenate([ext_s[p, l], ext_s[p + 1, l]], axis=0).astype(bf16)
        one = jnp.concatenate([main_s[p, l], main_s[p + 1, l], ext], axis=0)
        force = jnp.dot(mat[...], jnp.concatenate([one, one], axis=0), preferred_element_type=f32)
        i = 0
        for b in range(2):
            for q in range(2):
                for k in range(6):
                    for w in range(count):
                        at = slice(8 * w, 8 * w + 8)
                        term = force[8 * i : 8 * i + 8, w * nx : (w + 1) * nx] * mul_s[p + q, l, k, b, at]
                        acc[w] = term if acc[w] is None else acc[w] + term
                    i += 1
    return density * (-3.0 * density * density * jnp.concatenate(acc, axis=0))


def workspace(planes, windows, nx):
    return [
        pltpu.VMEM((planes, 3, 48, windows * nx), bf16),
        pltpu.VMEM((planes, 3, 8, windows * nx), f32),
        pltpu.VMEM((planes, 3, 6, 2, 8 * windows, nx), f32),
    ]


def sweep(rows, segments, put, work):
    work[1][...] = jnp.zeros_like(work[1])
    for p in range(2):
        prepare(segments(p), p, work)

    def body(y, _):
        put(y)
        prepare(segments(y + 2), y + 2, work)
        return 0

    lax.fori_loop(0, rows - 1, body, 0, unroll=7)
    put(rows - 1)


def face_kernel(disp, face, sem):
    copy = pltpu.make_async_copy(disp.at[:, 0], face, sem)
    copy.start()
    copy.wait()


def face_call(disp):
    _, _, nz, nx = disp.shape
    return pl.pallas_call(
        face_kernel,
        in_specs=[HBM],
        out_shape=jax.ShapeDtypeStruct((9, nz, nx), f32),
        scratch_shapes=[pltpu.SemaphoreType.DMA],
        compiler_params=pltpu.CompilerParams(vmem_limit_bytes=2**20),
        name="face",
    )(disp)


def extra(ref, row):
    ny = ref.shape[1]
    return 11 + row // ny, slice(row % ny, row % ny + 1)


def load_kernel(disp_h, dens_h, stiff, disp, dens, mat, mat_y, stiff_s, sems):
    copies = [pltpu.make_async_copy(stiff, stiff_s, sems.at[0])]
    for l in range(3):
        part = pl.ds(3 * l, 3)
        copies.append(pltpu.make_async_copy(disp_h.at[part], disp.at[part], sems.at[1 + l]))
    copies.append(pltpu.make_async_copy(dens_h, dens, sems.at[4]))
    for copy in copies:
        copy.start()
    copies[0].wait()
    build_matrices(stiff_s[...], ((mat, 4, 2), (mat_y, 2, 4)))
    for copy in copies[1:]:
        copy.wait()


def load_call(disp, dens, stiff):
    matrix = jax.ShapeDtypeStruct((192, 224), bf16)
    return pl.pallas_call(
        load_kernel,
        in_specs=[HBM, HBM, HBM],
        out_shape=(
            jax.ShapeDtypeStruct(disp.shape, f32),
            jax.ShapeDtypeStruct(dens.shape, f32),
            matrix,
            matrix,
        ),
        scratch_shapes=[pltpu.VMEM((24, 24), f32), pltpu.SemaphoreType.DMA((5,))],
        compiler_params=pltpu.CompilerParams(vmem_limit_bytes=16 * 2**20),
        cost_estimate=estimate(2),
        name="load",
    )(disp, dens, stiff)


def ends_kernel(flags, disp, dens, mat, ends, up, down, msg_even, msg_odd, *work):
    _, ny, nz, nx = disp.shape

    def segments(p):
        return lambda i: [(disp[i, p, 0:8], disp[i, p, 8:9]), (disp[i, p, nz - 8 : nz], None)]

    for ref in (up, down):
        ref[9:] = jnp.zeros((ref.shape[0] - 9, ny, nx), f32)

    def pack(y):
        row = pl.ds(y, 1)
        for i in range(9):
            up[i, row] = disp[i, y, nz - 1 : nz]
            down[i, row] = disp[i, y, 0:1]
        up[9, row] = dens[y, nz - 1 : nz]

    def put(y):
        d = jnp.concatenate([dens[y, 0:8], dens[y, nz - 8 : nz]], axis=0)
        s = energy_rows(y, mat, work, d)
        ends[y] = s
        row = pl.ds(y, 1)
        up[10, row] = s[14:15]
        down[9, row] = s[0:1]
        down[10, row] = s[1:2]
        pack(y)

    sweep(ny - 1, segments, put, work)
    pack(ny - 1)
    for n, y in enumerate((0, ny - 1)):
        for i in range(9):
            up[extra(up, 9 * n + i)] = disp[i, y, nz - 2 : nz - 1]
            down[extra(down, 9 * n + i)] = disp[i, y, 1:2]
            down[extra(down, 18 + 9 * n + i)] = disp[i, y, 2:3]
    up[extra(up, 36)] = dens[ny - 1, nz - 2 : nz - 1]
    down[extra(down, 36)] = dens[ny - 1, 0:1]
    down[extra(down, 37)] = dens[ny - 1, 1:2]
    odd = flags[5] == 1
    msg_even[...] = jnp.where(odd, down[...], up[...])
    msg_odd[...] = jnp.where(odd, up[...], down[...])


def ends_call(flags, disp, dens, mat):
    _, ny, nz, nx = disp.shape
    message = jax.ShapeDtypeStruct((11 + -(-38 // ny), ny, nx), f32)
    return pl.pallas_call(
        ends_kernel,
        in_specs=[SMEM] + [VMEM] * 3,
        out_shape=(jax.ShapeDtypeStruct((ny, 16, nx), f32),) + (message,) * 4,
        scratch_shapes=workspace(ny, 2, nx),
        compiler_params=pltpu.CompilerParams(vmem_limit_bytes=16 * 2**20),
        cost_estimate=estimate(4),
        name="energy_ends",
    )(flags, disp, dens, mat)


def middle_kernel(disp, dens, fy, mat, ends, passive, solid, src, low, high, tgt, now_s, *work):
    _, ny, nz, nx = disp.shape
    work, last = work[:3], work[3:]

    def segments(p):
        return lambda i: [(disp[i, p, 8 : nz - 8], disp[i, p, nz - 8 : nz - 7])]

    def frame(y):
        src[y, 0:OFF] = jnp.zeros((OFF, nx), f32)
        src[y, OFF + nz :] = jnp.zeros((src.shape[1] - OFF - nz, nx), f32)

    def put(y):
        frame(y)
        src[y, OFF : OFF + 8] = ends[y, 0:8]
        src[y, OFF + 8 : OFF + nz - 8] = energy_rows(y, mat, work, dens[y, 8 : nz - 8])
        src[y, OFF + nz - 8 : OFF + nz] = ends[y, 8:16]

    sweep(ny - 1, segments, put, work)
    last[1][...] = jnp.zeros_like(last[1])
    prepare(lambda i: [(disp[i, ny - 1], None)], 0, last)
    prepare(lambda i: [(fy[i], None)], 1, last)
    frame(ny - 1)
    src[ny - 1, OFF : OFF + nz] = energy_rows(0, mat, last, dens[ny - 1])

    def bound(y, _):
        low[y], high[y], now_s[y] = limits(dens[y], passive[y] == 1, solid[y] == 1)
        return 0

    lax.fori_loop(0, ny, bound, 0, unroll=4)
    targets(((ny - 5, inner_row), (5, outer_row(ny))), nz, nx, now_s, tgt)


def middle_call(disp, dens, fy, mat, ends, passive, solid):
    _, ny, nz, nx = disp.shape
    field = jax.ShapeDtypeStruct((ny, nz, nx), f32)
    return pl.pallas_call(
        middle_kernel,
        in_specs=[VMEM] * 7,
        out_shape=(
            jax.ShapeDtypeStruct((ny, nz + 2 * OFF, nx), f32),
            field,
            field,
            jax.ShapeDtypeStruct((8 * COARSE, nx), f32),
        ),
        scratch_shapes=[pltpu.VMEM((ny, nz, nx), f32)]
        + workspace(ny, nz // 8 - 2, nx)
        + workspace(2, nz // 8, nx),
        compiler_params=pltpu.CompilerParams(vmem_limit_bytes=24 * 2**20),
        cost_estimate=estimate(4),
        name="energy_middle",
    )(disp, dens, fy, mat, ends, passive, solid)


def rim_kernel(
    flags, got_even, got_odd, up, down, disp, dens, mat_y, src,
    rim, nodes, msg_even, msg_odd, low_s, high_s, t_s, *work,
):
    ny, rows, nx = src.shape
    nz = rows - 2 * OFF
    odd = flags[5] == 1
    low_s[...] = jnp.where(odd, got_even[...], got_odd[...])
    high_s[...] = jnp.where(odd, got_odd[...], got_even[...])
    work[1][...] = jnp.zeros_like(work[1])
    prepare(lambda i: [(low_s[i], None), (up[i], None)], 0, work)
    prepare(lambda i: [(down[i], None), (high_s[i], None)], 1, work)
    s = energy_rows(0, mat_y, work, jnp.concatenate([low_s[9], up[9]], axis=0))
    columns = ((0, low_s[10]), (1, s[0:ny]), (3, s[ny : 2 * ny]), (4, high_s[9]), (5, high_s[10]))
    for y in range(ny):
        rim[y] = jnp.zeros((8, nx), f32)
        for r, column in columns:
            rim[y, r : r + 1] = column[y : y + 1]
    half = 2 * (nz + 8)
    zero = jnp.zeros((1, nx), f32)
    for n, y in enumerate((0, ny - 1)):
        row = slice(y, y + 1)
        for i in range(9):
            window = jnp.concatenate(
                [
                    low_s[extra(low_s, 9 * n + i)],
                    low_s[i, row],
                    disp[i, y, 0:1],
                    disp[i, y, nz - 1 : nz],
                    high_s[i, row],
                    high_s[extra(high_s, 9 * n + i)],
                    high_s[extra(high_s, 18 + 9 * n + i)],
                    zero,
                ],
                axis=0,
            )
            nodes[n, i] = window
            t_s[n, half + 8 * i : half + 8 * i + 8] = window
        nodes[n, 9] = jnp.concatenate(
            [
                low_s[extra(low_s, 36)],
                low_s[9, ny - 1 : ny],
                zero,
                dens[ny - 1, nz - 1 : nz],
                high_s[extra(high_s, 36)],
                high_s[extra(high_s, 37)],
                zero,
                zero,
            ],
            axis=0,
        )
        t_s[n, half + 72 : half + 80] = nodes[n, 9]
        for j in range(2):
            at = j * (nz + 8)
            yy = j if n == 0 else ny - 2 + j
            t_s[n, at : at + nz] = src[yy, OFF : OFF + nz]
            t_s[n, at + nz : at + nz + 8] = rim[yy]
    odd = flags[4] == 1
    msg_even[...] = jnp.where(odd, t_s[0], t_s[1])
    msg_odd[...] = jnp.where(odd, t_s[1], t_s[0])


def put_rim(s, y, rim, nz):
    s[y, OFF - 2 : OFF] = rim[0:2]
    s[y, OFF + nz - 1 : OFF + nz + 2] = rim[3:6]


def rim_call(flags, got_even, got_odd, up, down, disp, dens, mat_y, src):
    ny, rows, nx = src.shape
    nz = rows - 2 * OFF
    size = 2 * (nz + 8) + 80
    return pl.pallas_call(
        rim_kernel,
        in_specs=[SMEM] + [VMEM] * 8,
        out_shape=(
            jax.ShapeDtypeStruct((ny, 8, nx), f32),
            jax.ShapeDtypeStruct((2, 10, 8, nx), f32),
            jax.ShapeDtypeStruct((size, nx), f32),
            jax.ShapeDtypeStruct((size, nx), f32),
        ),
        scratch_shapes=[
            pltpu.VMEM(up.shape, f32),
            pltpu.VMEM(up.shape, f32),
            pltpu.VMEM((2, size, nx), f32),
        ]
        + workspace(2, 2 * (ny // 8), nx),
        compiler_params=pltpu.CompilerParams(vmem_limit_bytes=16 * 2**20),
        cost_estimate=estimate(2),
        name="energy_rim",
    )(flags, got_even, got_odd, up, down, disp, dens, mat_y, src)


def filter_block(s_s, d_s, n, z_edges, y_edges, finish, unroll):
    rows, nx = s_s.shape[1:]
    nz = rows - 2 * OFF
    alpha, beta, gamma, delta, eps = filter_weights()
    row = lax.broadcasted_iota(jnp.int32, (rows, nx), 0)
    keep = jnp.where(row < OFF, z_edges[0], jnp.where(row >= OFF + nz, z_edges[1], 1)) == 1

    def beside(v):
        return pltpu.roll(v, 1, 0) + pltpu.roll(v, rows - 1, 0) + lane_up(v) + lane_down(v)

    def second(j, _):
        c = s_s[j + 1]
        d2 = alpha * c + beta * (beside(c) + s_s[j] + s_s[j + 2])
        ok = keep
        if y_edges is not None:
            ok = keep & (jnp.where(j == 0, y_edges[0], jnp.where(j == n - 3, y_edges[1], 1)) == 1)
        d_s[j] = jnp.where(ok, d2, 0.0)
        return 0

    def third(j, _):
        d2 = d_s[j + 1]
        p3 = gamma * s_s[j + 2] + delta * d2 + eps * (beside(d2) + d_s[j] + d_s[j + 2])
        finish(j, p3[OFF : OFF + nz])
        return 0

    lax.fori_loop(0, n - 2, second, 0, unroll=unroll)
    lax.fori_loop(0, n - 4, third, 0, unroll=unroll)


def limits(d, pas, sol):
    lower = jnp.maximum(d - move_limit, floor_density)
    upper = jnp.minimum(d + move_limit, 1.0)
    return tuple(jnp.where(sol, 1.0, jnp.where(pas, floor_density, v)) for v in (lower, upper, d))


FINE = 16
COARSE = POINTS // FINE


SPACING = 2.0 * bracket_end / POINTS


def inverse_coarse(i):
    return math.exp(0.5 * (-bracket_end + SPACING * FINE * i))


def targets(rows, nz, nx, now, tgt):
    acc = tuple(jnp.zeros((8, nx), f32) for _ in range(COARSE))
    for n, row in rows:

        def add(j, acc):
            acc = list(acc)
            for w in range(nz // 8):
                d = now[row(j), 8 * w : 8 * w + 8]
                for i in range(COARSE):
                    acc[i] = acc[i] + d * inverse_coarse(i)
            return tuple(acc)

        acc = lax.fori_loop(0, n, add, acc, unroll=2)
    for i in range(COARSE):
        tgt[8 * i : 8 * i + 8] = acc[i]


def table(n, nz, nx, amp, low, high, row, fine_s, vol, start, unroll):
    pair = 2
    for first in range(0, COARSE, pair):
        inverse = [inverse_coarse(i) for i in range(first, first + pair)]

        def volume(j, acc):
            acc = list(acc)
            y = row(j)
            for w in range(nz // 8):
                at = slice(8 * w, 8 * w + 8)
                lo, hi = low[y, at], high[y, at]
                los, his = [lo * c for c in inverse], [hi * c for c in inverse]
                for f in range(FINE):
                    if first == 0:
                        t = amp[j, at] * math.exp(-0.5 * SPACING * f)
                        fine_s[f, j, at] = t
                    else:
                        t = fine_s[f, j, at]
                    for i in range(pair):
                        acc[i * FINE + f] = acc[i * FINE + f] + jnp.minimum(jnp.maximum(t, los[i]), his[i])
            return tuple(acc)

        places = [slice(8 * (first * FINE + e), 8 * (first * FINE + e) + 8) for e in range(pair * FINE)]
        begin = tuple(jnp.zeros((8, nx), f32) if start is None else start[at] for at in places)
        acc = lax.fori_loop(0, n, volume, begin, unroll=unroll)
        for at, value in zip(places, acc):
            vol[at] = value


def inner_row(j):
    return j + 2


def outer_row(ny):
    return lambda j: jnp.where(j < 2, j, j + ny - 5)


def inner_kernel(flags, src, rim, dens, low, high, amp, vol, s_s, d_s, fine_s):
    ny, nz, nx = dens.shape
    s_s[...] = src[0 : ny - 1]

    def fix(y, _):
        put_rim(s_s, y, rim[y], nz)
        return 0

    lax.fori_loop(0, ny - 1, fix, 0, unroll=5)

    def finish(j, p3):
        amp[j] = jnp.sqrt(jnp.maximum(-p3 * dens[inner_row(j)], 0.0))

    filter_block(s_s, d_s, ny - 1, (flags[2], flags[3]), None, finish, True)
    table(ny - 5, nz, nx, amp, low, high, inner_row, fine_s, vol, None, 4)


def inner_call(flags, src, rim, dens, low, high):
    ny, nz, nx = dens.shape
    rows = nz + 2 * OFF
    return pl.pallas_call(
        inner_kernel,
        in_specs=[SMEM] + [VMEM] * 5,
        out_shape=(
            jax.ShapeDtypeStruct((ny - 5, nz, nx), f32),
            jax.ShapeDtypeStruct((8 * POINTS, nx), f32),
        ),
        scratch_shapes=[
            pltpu.VMEM((ny - 1, rows, nx), f32),
            pltpu.VMEM((ny - 3, rows, nx), f32),
            pltpu.VMEM((FINE, ny - 5, nz, nx), f32),
        ],
        compiler_params=pltpu.CompilerParams(vmem_limit_bytes=24 * 2**20),
        cost_estimate=estimate(9),
        name="filter_inner",
    )(flags, src, rim, dens, low, high)


def outer_kernel(
    flags, src, rim, nodes, got_even, got_odd, mat, dens, low, high, vol_i, tgt,
    amp, excess, s_s, d_s, fine_s, vol, below, above, *work,
):
    ny, nz, nx = dens.shape
    odd = flags[4] == 1
    below[...] = jnp.where(odd, got_even[...], got_odd[...])
    above[...] = jnp.where(odd, got_odd[...], got_even[...])
    half = 2 * (nz + 8)

    def window(ref, i):
        return ref[half + 8 * i : half + 8 * i + 8]

    work[1][...] = jnp.zeros_like(work[1])
    prepare(lambda i: [(window(below, i), None), (nodes[1, i], None)], 0, work)
    prepare(lambda i: [(nodes[0, i], None), (window(above, i), None)], 1, work)
    corner = energy_rows(0, mat, work, jnp.concatenate([window(below, 9), nodes[1, 9]], axis=0))
    for b, ref in enumerate((below, above)):
        for j in range(2):
            at = j if b == 0 else 5 + j
            start = j * (nz + 8)
            s_s[b, at, 0:OFF] = jnp.zeros((OFF, nx), f32)
            s_s[b, at, OFF : OFF + nz] = ref[start : start + nz]
            s_s[b, at, OFF + nz :] = jnp.zeros((OFF, nx), f32)
            put_rim(s_s.at[b], at, ref[start + nz : start + nz + 8], nz)
    for j in range(4):
        s_s[0, 2 + j] = src[j]
        put_rim(s_s.at[0], 2 + j, rim[j], nz)
    for j in range(5):
        s_s[1, j] = src[ny - 5 + j]
        put_rim(s_s.at[1], j, rim[ny - 5 + j], nz)
    put_rim(s_s.at[0], 1, corner[0:8], nz)
    put_rim(s_s.at[1], 4, corner[8:16], nz)
    for b in range(2):
        y0 = 0 if b == 0 else ny - 3

        def finish(j, p3):
            amp[2 * b + j] = jnp.sqrt(jnp.maximum(-p3 * dens[y0 + j], 0.0))

        edges = (flags[0], 1) if b == 0 else (1, flags[1])
        filter_block(s_s.at[b], d_s.at[b], 6 + b, (flags[2], flags[3]), edges, finish, True)
    table(5, nz, nx, amp, low, high, outer_row(ny), fine_s, vol, vol_i, 2)

    def lanes(ref, count):
        total = ref[pl.ds(0, count, stride=8), :]
        for s in range(1, 8):
            total = total + ref[pl.ds(s, count, stride=8), :]
        return total

    volumes, present = lanes(vol, POINTS), lanes(tgt, COARSE)
    over = [volumes[FINE * i : FINE * i + FINE] - present[i : i + 1] for i in range(COARSE)]
    excess[...] = jnp.sum(jnp.transpose(jnp.concatenate(over, axis=0)), axis=0, keepdims=True)


def outer_call(flags, src, rim, nodes, got_even, got_odd, mat, dens, low, high, vol_i, tgt):
    ny, nz, nx = dens.shape
    rows = nz + 2 * OFF
    return pl.pallas_call(
        outer_kernel,
        in_specs=[SMEM] + [VMEM] * 11,
        out_shape=(jax.ShapeDtypeStruct((5, nz, nx), f32), jax.ShapeDtypeStruct((1, POINTS), f32)),
        scratch_shapes=[
            pltpu.VMEM((2, 7, rows, nx), f32),
            pltpu.VMEM((2, 5, rows, nx), f32),
            pltpu.VMEM((FINE, 5, nz, nx), f32),
            pltpu.VMEM((8 * POINTS, nx), f32),
            pltpu.VMEM(got_odd.shape, f32),
            pltpu.VMEM(got_odd.shape, f32),
        ]
        + workspace(2, 2, nx),
        compiler_params=pltpu.CompilerParams(vmem_limit_bytes=20 * 2**20),
        cost_estimate=estimate(3),
        name="filter_outer",
    )(flags, src, rim, nodes, got_even, got_odd, mat, dens, low, high, vol_i, tgt)


def update_kernel(tables, amp_i, amp_o, low, high, new, logm):
    inner = amp_i.shape[0]
    nx = amp_i.shape[-1]
    total = jnp.sum(tables[...], axis=0, keepdims=True)
    lane = lax.broadcasted_iota(jnp.int32, total.shape, 1)
    above = jnp.where((total > 0.0) & (lane > 0), 1.0, 0.0)
    middle = -bracket_end + (2.0 * bracket_end / POINTS) * (jnp.sum(above) + 0.5)
    logm[0] = middle
    scale = jnp.exp(jnp.full((1, nx), -0.5 * middle, f32))

    def new_row(y, amp):
        new[y] = jnp.minimum(jnp.maximum(amp * scale, low[y]), high[y])

    def body(j, _):
        new_row(inner_row(j), amp_i[j])
        return 0

    lax.fori_loop(0, inner, body, 0, unroll=4)
    for j in range(5):
        new_row(j if j < 2 else inner + j, amp_o[j])


def update_call(tables, amp_i, amp_o, low, high):
    return pl.pallas_call(
        update_kernel,
        in_specs=[VMEM] * 5,
        out_specs=(VMEM, SMEM),
        out_shape=(jax.ShapeDtypeStruct(low.shape, f32), jax.ShapeDtypeStruct((1,), f32)),
        compiler_params=pltpu.CompilerParams(vmem_limit_bytes=8 * 2**20),
        cost_estimate=estimate(1),
        name="update",
    )(tables, amp_i, amp_o, low, high)


def to_lower(value, axis):
    count = lax.axis_size(axis)
    return lax.ppermute(value, axis, [(i + 1, i) for i in range(count - 1)])


def swap(value, axis, start):
    pairs = []
    for i in range(start, lax.axis_size(axis) - 1, 2):
        pairs += [(i, i + 1), (i + 1, i)]
    return lax.ppermute(value, axis, pairs)


def on_device(displacement, density, passive, solid, stiffness):
    ny, nz, nx = density.shape
    gy, gz = lax.axis_size("gy"), lax.axis_size("gz")
    iy, iz = lax.axis_index("gy"), lax.axis_index("gz")
    flags = jnp.stack([iy > 0, iy < gy - 1, iz > 0, iz < gz - 1, iy % 2 == 1, iz % 2 == 1]).astype(jnp.int32)

    disp_hbm = pltpu.with_memory_space_constraint(displacement, pltpu.HBM)
    dens_hbm = pltpu.with_memory_space_constraint(density, pltpu.HBM)
    stiff_hbm = pltpu.with_memory_space_constraint(stiffness, pltpu.HBM)

    fy = to_lower(face_call(disp_hbm), "gy")
    disp, dens, mat, mat_y = load_call(disp_hbm, dens_hbm, stiff_hbm)
    ends, up, down, z_even, z_odd = ends_call(flags, disp, dens, mat)

    z_got_even = swap(z_even, "gz", 0)
    z_got_odd = swap(z_odd, "gz", 1)
    src, low, high, tgt = middle_call(disp, dens, fy, mat, ends, passive, solid)
    rim, nodes, msg_even, msg_odd = rim_call(flags, z_got_even, z_got_odd, up, down, disp, dens, mat_y, src)

    got_even = swap(msg_even, "gy", 0)
    got_odd = swap(msg_odd, "gy", 1)
    amp_i, vol = inner_call(flags, src, rim, dens, low, high)
    amp_o, excess = outer_call(flags, src, rim, nodes, got_even, got_odd, mat, dens, low, high, vol, tgt)

    everyone = jnp.broadcast_to(excess, (gz * gy, POINTS))
    tables = lax.all_to_all(everyone, ("gz", "gy"), 0, 0, tiled=True)
    new, logm = update_call(tables, amp_i, amp_o, low, high)
    return new, logm.reshape(())


def solution(mesh):
    placed = (
        P(None, "gy", "gz", None),
        P("gy", "gz", None),
        P("gy", "gz", None),
        P("gy", "gz", None),
        P(),
    )
    return jax.shard_map(
        on_device, mesh=mesh, in_specs=placed, out_specs=(P("gy", "gz", None), P()), check_vma=False
    )
```

```python
import math

import jax
import jax.numpy as jnp
from jax import lax
from jax.experimental import pallas as pl
from jax.experimental.pallas import tpu as pltpu
from jax.sharding import PartitionSpec as P

ITERS = 8
POINTS = 2**ITERS
OFF = 8

smoothing = 0.52
move_limit = 0.2
floor_density = 0.001
bracket_end = 12.0

f32 = jnp.float32
bf16 = jnp.bfloat16
VMEM = pl.BlockSpec(memory_space=pltpu.VMEM)
SMEM = pl.BlockSpec(memory_space=pltpu.SMEM)
HBM = pl.BlockSpec(memory_space=pltpu.HBM)


def cheb_weights():
    spectrum_top = 1.0 + 12.0 * smoothing
    centre_value = (spectrum_top + 1.0) / 2.0
    half_width = (spectrum_top - 1.0) / 2.0
    ratio_value = centre_value / half_width
    first_rho = 1.0 / ratio_value
    second_rho = 1.0 / (2.0 * ratio_value - first_rho)
    third_rho = 1.0 / (2.0 * ratio_value - second_rho)
    return (
        centre_value,
        second_rho * first_rho,
        2.0 * second_rho / half_width,
        third_rho * second_rho,
        2.0 * third_rho / half_width,
    )


def filter_weights():
    t, w1, w2, w3, w4 = cheb_weights()
    diag = 1.0 + 6.0 * smoothing
    alpha = w1 / t + w2 * (1.0 - diag / t)
    beta = w2 * smoothing / t
    gamma = 1.0 / t - w4 * w1 / (t * w2)
    delta = 1.0 + w3 + w4 / w2 - w4 * diag
    eps = w4 * smoothing
    return alpha, beta, gamma, delta, eps


def lane_up(v):
    n = v.shape[-1]
    lane = lax.broadcasted_iota(jnp.int32, v.shape, v.ndim - 1)
    return jnp.where(lane < n - 1, pltpu.roll(v, n - 1, v.ndim - 1), 0.0)


def lane_down(v):
    n = v.shape[-1]
    lane = lax.broadcasted_iota(jnp.int32, v.shape, v.ndim - 1)
    return jnp.where(lane > 0, pltpu.roll(v, 1, v.ndim - 1), 0.0)


def estimate(us):
    return pl.CostEstimate(flops=int(us * 1e9), bytes_accessed=1 << 20, transcendentals=0)


def build_matrices(k, mats):
    shape = (24, 128)
    col = lax.broadcasted_iota(jnp.int32, shape, 1)
    row = lax.broadcasted_iota(jnp.int32, shape, 0)
    main = col < 96
    q = jnp.where(main, jnp.where(col >= 48, 1, 0), jnp.where(col >= 104, 1, 0))
    m = col - 48 * q
    e = col - 96 - 8 * q
    c = jnp.where(main, m >> 4, e >> 1)
    dx = jnp.where(main, (m >> 3) & 1, e & 1)
    valid = main | (e < 6)
    picks = []
    for _, plane, band in mats:
        dof0 = 3 * (plane * q + dx) + c
        picks.append(jnp.where(main & (row == dof0), 1.0, 0.0))
        picks.append(jnp.where(valid & (row == dof0 + 3 * band), 1.0, 0.0))
    picked = jnp.dot(
        k, jnp.concatenate(picks, axis=1), precision=lax.Precision.HIGHEST, preferred_element_type=f32
    )
    col8 = lax.broadcasted_iota(jnp.int32, (8, 128), 1)
    row8 = lax.broadcasted_iota(jnp.int32, (8, 128), 0)
    main8 = col8 < 96
    rc = col8 & 7
    m0 = main8 & (rc == row8)
    m1 = jnp.where(main8, rc, 8) == row8 + 1
    for n, (mat, plane, band) in enumerate(mats):
        k0 = picked[:, 256 * n : 256 * n + 128]
        k1 = picked[:, 256 * n + 128 : 256 * n + 256]
        rows = []
        for b in range(2):
            for q_ in range(2):
                for c_ in range(3):
                    for dx_ in range(2):
                        r = 3 * (plane * q_ + band * b + dx_) + c_
                        rows.append(jnp.where(m0, k0[r : r + 1], 0.0) + jnp.where(m1, k1[r : r + 1], 0.0))
        full = jnp.concatenate(rows, axis=0)
        hi = full.astype(bf16)
        lo = (full - hi.astype(f32)).astype(bf16)
        mat[:, 0:112] = hi[:, 0:112]
        mat[:, 112:224] = lo[:, 0:112]


def prepare(segments, p, work):
    main_s, ext_s, mul_s = work
    for l in range(3):
        for c in range(3):
            w0 = 0
            for u, x in segments(3 * l + c):
                size, nx = u.shape
                n = size // 8
                last = lax.broadcasted_iota(jnp.int32, u.shape, 0) == size - 1
                both = (u, lane_up(u))
                after = (None, None) if x is None else (x, lane_up(x))
                for w in range(n):
                    sl = slice(8 * w, 8 * w + 8)
                    main_s[p, l, 16 * c : 16 * c + 16, (w0 + w) * nx : (w0 + w + 1) * nx] = jnp.concatenate(
                        [both[0][sl], both[1][sl]], axis=0
                    ).astype(bf16)
                for dx in range(2):
                    v, vx = both[dx], after[dx]
                    k = 2 * c + dx
                    for w in range(n):
                        nxt = v[8 * w + 8 : 8 * w + 9] if w < n - 1 else vx
                        if nxt is not None:
                            ext_s[p, l, k : k + 1, (w0 + w) * nx : (w0 + w + 1) * nx] = nxt
                    m = 2.0 * v - v.astype(bf16).astype(f32)
                    mx = 0.0 if vx is None else jnp.broadcast_to(2.0 * vx - vx.astype(bf16).astype(f32), v.shape)
                    at = slice(8 * w0, 8 * (w0 + n))
                    mul_s[p, l, k, 0, at] = m
                    mul_s[p, l, k, 1, at] = jnp.where(last, mx, pltpu.roll(m, size - 1, 0))
                w0 += n


def energy_rows(p, mat, work, density):
    main_s, ext_s, mul_s = work
    rows, nx = density.shape
    count = rows // 8
    acc = [None] * count
    for l in range(3):
        ext = jnp.concatenate([ext_s[p, l], ext_s[p + 1, l]], axis=0).astype(bf16)
        one = jnp.concatenate([main_s[p, l], main_s[p + 1, l], ext], axis=0)
        force = jnp.dot(mat[...], jnp.concatenate([one, one], axis=0), preferred_element_type=f32)
        i = 0
        for b in range(2):
            for q in range(2):
                for k in range(6):
                    for w in range(count):
                        at = slice(8 * w, 8 * w + 8)
                        term = force[8 * i : 8 * i + 8, w * nx : (w + 1) * nx] * mul_s[p + q, l, k, b, at]
                        acc[w] = term if acc[w] is None else acc[w] + term
                    i += 1
    return density * (-3.0 * density * density * jnp.concatenate(acc, axis=0))


def workspace(planes, windows, nx):
    return [
        pltpu.VMEM((planes, 3, 48, windows * nx), bf16),
        pltpu.VMEM((planes, 3, 8, windows * nx), f32),
        pltpu.VMEM((planes, 3, 6, 2, 8 * windows, nx), f32),
    ]


def sweep(rows, segments, put, work):
    work[1][...] = jnp.zeros_like(work[1])
    for p in range(2):
        prepare(segments(p), p, work)

    def body(y, _):
        put(y)
        prepare(segments(y + 2), y + 2, work)
        return 0

    lax.fori_loop(0, rows - 1, body, 0, unroll=7)
    put(rows - 1)


def start_kernel(disp, stiff, face, mat, mat_y, stiff_s, sems):
    copies = [
        pltpu.make_async_copy(stiff, stiff_s, sems.at[0]),
        pltpu.make_async_copy(disp.at[:, 0], face, sems.at[1]),
    ]
    for copy in copies:
        copy.start()
    copies[0].wait()
    build_matrices(stiff_s[...], ((mat, 4, 2), (mat_y, 2, 4)))
    copies[1].wait()


def start_call(disp, stiff):
    _, _, nz, nx = disp.shape
    matrix = jax.ShapeDtypeStruct((192, 224), bf16)
    return pl.pallas_call(
        start_kernel,
        in_specs=[HBM, HBM],
        out_shape=(jax.ShapeDtypeStruct((9, nz, nx), f32), matrix, matrix),
        scratch_shapes=[pltpu.VMEM((24, 24), f32), pltpu.SemaphoreType.DMA((2,))],
        compiler_params=pltpu.CompilerParams(vmem_limit_bytes=4 * 2**20),
        cost_estimate=estimate(10),
        name="start",
    )(disp, stiff)


def extra(ref, row):
    ny = ref.shape[1]
    return 11 + row // ny, slice(row % ny, row % ny + 1)


def ends_kernel(flags, disp, dens, mat, ends, up, down, msg_even, msg_odd, *work):
    _, ny, nz, nx = disp.shape

    def segments(p):
        return lambda i: [(disp[i, p, 0:8], disp[i, p, 8:9]), (disp[i, p, nz - 8 : nz], None)]

    for ref in (up, down):
        ref[9:] = jnp.zeros((ref.shape[0] - 9, ny, nx), f32)

    def pack(y):
        row = pl.ds(y, 1)
        for i in range(9):
            up[i, row] = disp[i, y, nz - 1 : nz]
            down[i, row] = disp[i, y, 0:1]
        up[9, row] = dens[y, nz - 1 : nz]

    def put(y):
        d = jnp.concatenate([dens[y, 0:8], dens[y, nz - 8 : nz]], axis=0)
        s = energy_rows(y, mat, work, d)
        ends[y] = s
        row = pl.ds(y, 1)
        up[10, row] = s[14:15]
        down[9, row] = s[0:1]
        down[10, row] = s[1:2]
        pack(y)

    sweep(ny - 1, segments, put, work)
    pack(ny - 1)
    for n, y in enumerate((0, ny - 1)):
        for i in range(9):
            up[extra(up, 9 * n + i)] = disp[i, y, nz - 2 : nz - 1]
            down[extra(down, 9 * n + i)] = disp[i, y, 1:2]
            down[extra(down, 18 + 9 * n + i)] = disp[i, y, 2:3]
    up[extra(up, 36)] = dens[ny - 1, nz - 2 : nz - 1]
    down[extra(down, 36)] = dens[ny - 1, 0:1]
    down[extra(down, 37)] = dens[ny - 1, 1:2]
    odd = flags[5] == 1
    msg_even[...] = jnp.where(odd, down[...], up[...])
    msg_odd[...] = jnp.where(odd, up[...], down[...])


def ends_call(flags, disp, dens, mat):
    _, ny, nz, nx = disp.shape
    message = jax.ShapeDtypeStruct((11 + -(-38 // ny), ny, nx), f32)
    return pl.pallas_call(
        ends_kernel,
        in_specs=[SMEM] + [VMEM] * 3,
        out_shape=(jax.ShapeDtypeStruct((ny, 16, nx), f32),) + (message,) * 4,
        scratch_shapes=workspace(ny, 2, nx),
        compiler_params=pltpu.CompilerParams(vmem_limit_bytes=16 * 2**20),
        cost_estimate=estimate(4),
        name="energy_ends",
    )(flags, disp, dens, mat)


def middle_kernel(disp, dens, fy, mat, ends, passive, solid, src, low, high, tgt, now_s, *work):
    _, ny, nz, nx = disp.shape
    work, last = work[:3], work[3:]

    def segments(p):
        return lambda i: [(disp[i, p, 8 : nz - 8], disp[i, p, nz - 8 : nz - 7])]

    def frame(y):
        src[y, 0:OFF] = jnp.zeros((OFF, nx), f32)
        src[y, OFF + nz :] = jnp.zeros((src.shape[1] - OFF - nz, nx), f32)

    def put(y):
        frame(y)
        src[y, OFF : OFF + 8] = ends[y, 0:8]
        src[y, OFF + 8 : OFF + nz - 8] = energy_rows(y, mat, work, dens[y, 8 : nz - 8])
        src[y, OFF + nz - 8 : OFF + nz] = ends[y, 8:16]

    sweep(ny - 1, segments, put, work)
    last[1][...] = jnp.zeros_like(last[1])
    prepare(lambda i: [(disp[i, ny - 1], None)], 0, last)
    prepare(lambda i: [(fy[i], None)], 1, last)
    frame(ny - 1)
    src[ny - 1, OFF : OFF + nz] = energy_rows(0, mat, last, dens[ny - 1])

    def bound(y, _):
        low[y], high[y], now_s[y] = limits(dens[y], passive[y] == 1, solid[y] == 1)
        return 0

    lax.fori_loop(0, ny, bound, 0, unroll=4)
    targets(((ny - 5, inner_row), (5, outer_row(ny))), nz, nx, now_s, tgt)


def middle_call(disp, dens, fy, mat, ends, passive, solid):
    _, ny, nz, nx = disp.shape
    field = jax.ShapeDtypeStruct((ny, nz, nx), f32)
    return pl.pallas_call(
        middle_kernel,
        in_specs=[VMEM] * 7,
        out_shape=(
            jax.ShapeDtypeStruct((ny, nz + 2 * OFF, nx), f32),
            field,
            field,
            jax.ShapeDtypeStruct((8 * COARSE, nx), f32),
        ),
        scratch_shapes=[pltpu.VMEM((ny, nz, nx), f32)]
        + workspace(ny, nz // 8 - 2, nx)
        + workspace(2, nz // 8, nx),
        compiler_params=pltpu.CompilerParams(vmem_limit_bytes=24 * 2**20),
        cost_estimate=estimate(4),
        name="energy_middle",
    )(disp, dens, fy, mat, ends, passive, solid)


def rim_kernel(
    flags, got_even, got_odd, up, down, disp, dens, mat_y, src,
    rim, nodes, msg_even, msg_odd, low_s, high_s, t_s, *work,
):
    ny, rows, nx = src.shape
    nz = rows - 2 * OFF
    odd = flags[5] == 1
    low_s[...] = jnp.where(odd, got_even[...], got_odd[...])
    high_s[...] = jnp.where(odd, got_odd[...], got_even[...])
    work[1][...] = jnp.zeros_like(work[1])
    prepare(lambda i: [(low_s[i], None), (up[i], None)], 0, work)
    prepare(lambda i: [(down[i], None), (high_s[i], None)], 1, work)
    s = energy_rows(0, mat_y, work, jnp.concatenate([low_s[9], up[9]], axis=0))
    columns = ((0, low_s[10]), (1, s[0:ny]), (3, s[ny : 2 * ny]), (4, high_s[9]), (5, high_s[10]))
    for y in range(ny):
        rim[y] = jnp.zeros((8, nx), f32)
        for r, column in columns:
            rim[y, r : r + 1] = column[y : y + 1]
    half = 2 * (nz + 8)
    zero = jnp.zeros((1, nx), f32)
    for n, y in enumerate((0, ny - 1)):
        row = slice(y, y + 1)
        for i in range(9):
            window = jnp.concatenate(
                [
                    low_s[extra(low_s, 9 * n + i)],
                    low_s[i, row],
                    disp[i, y, 0:1],
                    disp[i, y, nz - 1 : nz],
                    high_s[i, row],
                    high_s[extra(high_s, 9 * n + i)],
                    high_s[extra(high_s, 18 + 9 * n + i)],
                    zero,
                ],
                axis=0,
            )
            nodes[n, i] = window
            t_s[n, half + 8 * i : half + 8 * i + 8] = window
        nodes[n, 9] = jnp.concatenate(
            [
                low_s[extra(low_s, 36)],
                low_s[9, ny - 1 : ny],
                zero,
                dens[ny - 1, nz - 1 : nz],
                high_s[extra(high_s, 36)],
                high_s[extra(high_s, 37)],
                zero,
                zero,
            ],
            axis=0,
        )
        t_s[n, half + 72 : half + 80] = nodes[n, 9]
        for j in range(2):
            at = j * (nz + 8)
            yy = j if n == 0 else ny - 2 + j
            t_s[n, at : at + nz] = src[yy, OFF : OFF + nz]
            t_s[n, at + nz : at + nz + 8] = rim[yy]
    odd = flags[4] == 1
    msg_even[...] = jnp.where(odd, t_s[0], t_s[1])
    msg_odd[...] = jnp.where(odd, t_s[1], t_s[0])


def put_rim(s, y, rim, nz):
    s[y, OFF - 2 : OFF] = rim[0:2]
    s[y, OFF + nz - 1 : OFF + nz + 2] = rim[3:6]


def rim_call(flags, got_even, got_odd, up, down, disp, dens, mat_y, src):
    ny, rows, nx = src.shape
    nz = rows - 2 * OFF
    size = 2 * (nz + 8) + 80
    return pl.pallas_call(
        rim_kernel,
        in_specs=[SMEM] + [VMEM] * 8,
        out_shape=(
            jax.ShapeDtypeStruct((ny, 8, nx), f32),
            jax.ShapeDtypeStruct((2, 10, 8, nx), f32),
            jax.ShapeDtypeStruct((size, nx), f32),
            jax.ShapeDtypeStruct((size, nx), f32),
        ),
        scratch_shapes=[
            pltpu.VMEM(up.shape, f32),
            pltpu.VMEM(up.shape, f32),
            pltpu.VMEM((2, size, nx), f32),
        ]
        + workspace(2, 2 * (ny // 8), nx),
        compiler_params=pltpu.CompilerParams(vmem_limit_bytes=16 * 2**20),
        cost_estimate=estimate(2),
        name="energy_rim",
    )(flags, got_even, got_odd, up, down, disp, dens, mat_y, src)


def filter_block(s_s, d_s, n, z_edges, y_edges, finish, unroll):
    rows, nx = s_s.shape[1:]
    nz = rows - 2 * OFF
    alpha, beta, gamma, delta, eps = filter_weights()
    row = lax.broadcasted_iota(jnp.int32, (rows, nx), 0)
    keep = jnp.where(row < OFF, z_edges[0], jnp.where(row >= OFF + nz, z_edges[1], 1)) == 1

    def beside(v):
        return pltpu.roll(v, 1, 0) + pltpu.roll(v, rows - 1, 0) + lane_up(v) + lane_down(v)

    def second(j, _):
        c = s_s[j + 1]
        d2 = alpha * c + beta * (beside(c) + s_s[j] + s_s[j + 2])
        ok = keep
        if y_edges is not None:
            ok = keep & (jnp.where(j == 0, y_edges[0], jnp.where(j == n - 3, y_edges[1], 1)) == 1)
        d_s[j] = jnp.where(ok, d2, 0.0)
        return 0

    def third(j, _):
        d2 = d_s[j + 1]
        p3 = gamma * s_s[j + 2] + delta * d2 + eps * (beside(d2) + d_s[j] + d_s[j + 2])
        finish(j, p3[OFF : OFF + nz])
        return 0

    lax.fori_loop(0, n - 2, second, 0, unroll=unroll)
    lax.fori_loop(0, n - 4, third, 0, unroll=unroll)


def limits(d, pas, sol):
    lower = jnp.maximum(d - move_limit, floor_density)
    upper = jnp.minimum(d + move_limit, 1.0)
    return tuple(jnp.where(sol, 1.0, jnp.where(pas, floor_density, v)) for v in (lower, upper, d))


FINE = 16
COARSE = POINTS // FINE


SPACING = 2.0 * bracket_end / POINTS


def inverse_coarse(i):
    return math.exp(0.5 * (-bracket_end + SPACING * FINE * i))


def targets(rows, nz, nx, now, tgt):
    acc = tuple(jnp.zeros((8, nx), f32) for _ in range(COARSE))
    for n, row in rows:

        def add(j, acc):
            acc = list(acc)
            for w in range(nz // 8):
                d = now[row(j), 8 * w : 8 * w + 8]
                for i in range(COARSE):
                    acc[i] = acc[i] + d * inverse_coarse(i)
            return tuple(acc)

        acc = lax.fori_loop(0, n, add, acc, unroll=2)
    for i in range(COARSE):
        tgt[8 * i : 8 * i + 8] = acc[i]


def table(n, nz, nx, amp, low, high, row, fine_s, vol, start, unroll):
    pair = 2
    for first in range(0, COARSE, pair):
        inverse = [inverse_coarse(i) for i in range(first, first + pair)]

        def volume(j, acc):
            acc = list(acc)
            y = row(j)
            for w in range(nz // 8):
                at = slice(8 * w, 8 * w + 8)
                lo, hi = low[y, at], high[y, at]
                los, his = [lo * c for c in inverse], [hi * c for c in inverse]
                for f in range(FINE):
                    if first == 0:
                        t = amp[j, at] * math.exp(-0.5 * SPACING * f)
                        fine_s[f, j, at] = t
                    else:
                        t = fine_s[f, j, at]
                    for i in range(pair):
                        acc[i * FINE + f] = acc[i * FINE + f] + jnp.minimum(jnp.maximum(t, los[i]), his[i])
            return tuple(acc)

        places = [slice(8 * (first * FINE + e), 8 * (first * FINE + e) + 8) for e in range(pair * FINE)]
        begin = tuple(jnp.zeros((8, nx), f32) if start is None else start[at] for at in places)
        acc = lax.fori_loop(0, n, volume, begin, unroll=unroll)
        for at, value in zip(places, acc):
            vol[at] = value


def inner_row(j):
    return j + 2


def outer_row(ny):
    return lambda j: jnp.where(j < 2, j, j + ny - 5)


def inner_kernel(flags, src, rim, dens, low, high, amp, vol, s_s, d_s, fine_s):
    ny, nz, nx = dens.shape
    s_s[...] = src[0 : ny - 1]

    def fix(y, _):
        put_rim(s_s, y, rim[y], nz)
        return 0

    lax.fori_loop(0, ny - 1, fix, 0, unroll=5)

    def finish(j, p3):
        amp[j] = jnp.sqrt(jnp.maximum(-p3 * dens[inner_row(j)], 0.0))

    filter_block(s_s, d_s, ny - 1, (flags[2], flags[3]), None, finish, True)
    table(ny - 5, nz, nx, amp, low, high, inner_row, fine_s, vol, None, 4)


def inner_call(flags, src, rim, dens, low, high):
    ny, nz, nx = dens.shape
    rows = nz + 2 * OFF
    return pl.pallas_call(
        inner_kernel,
        in_specs=[SMEM] + [VMEM] * 5,
        out_shape=(
            jax.ShapeDtypeStruct((ny - 5, nz, nx), f32),
            jax.ShapeDtypeStruct((8 * POINTS, nx), f32),
        ),
        scratch_shapes=[
            pltpu.VMEM((ny - 1, rows, nx), f32),
            pltpu.VMEM((ny - 3, rows, nx), f32),
            pltpu.VMEM((FINE, ny - 5, nz, nx), f32),
        ],
        compiler_params=pltpu.CompilerParams(vmem_limit_bytes=24 * 2**20),
        cost_estimate=estimate(9),
        name="filter_inner",
    )(flags, src, rim, dens, low, high)


def outer_kernel(
    flags, src, rim, nodes, got_even, got_odd, mat, dens, low, high, vol_i, tgt,
    amp, excess, s_s, d_s, fine_s, vol, below, above, *work,
):
    ny, nz, nx = dens.shape
    odd = flags[4] == 1
    below[...] = jnp.where(odd, got_even[...], got_odd[...])
    above[...] = jnp.where(odd, got_odd[...], got_even[...])
    half = 2 * (nz + 8)

    def window(ref, i):
        return ref[half + 8 * i : half + 8 * i + 8]

    work[1][...] = jnp.zeros_like(work[1])
    prepare(lambda i: [(window(below, i), None), (nodes[1, i], None)], 0, work)
    prepare(lambda i: [(nodes[0, i], None), (window(above, i), None)], 1, work)
    corner = energy_rows(0, mat, work, jnp.concatenate([window(below, 9), nodes[1, 9]], axis=0))
    for b, ref in enumerate((below, above)):
        for j in range(2):
            at = j if b == 0 else 5 + j
            start = j * (nz + 8)
            s_s[b, at, 0:OFF] = jnp.zeros((OFF, nx), f32)
            s_s[b, at, OFF : OFF + nz] = ref[start : start + nz]
            s_s[b, at, OFF + nz :] = jnp.zeros((OFF, nx), f32)
            put_rim(s_s.at[b], at, ref[start + nz : start + nz + 8], nz)
    for j in range(4):
        s_s[0, 2 + j] = src[j]
        put_rim(s_s.at[0], 2 + j, rim[j], nz)
    for j in range(5):
        s_s[1, j] = src[ny - 5 + j]
        put_rim(s_s.at[1], j, rim[ny - 5 + j], nz)
    put_rim(s_s.at[0], 1, corner[0:8], nz)
    put_rim(s_s.at[1], 4, corner[8:16], nz)
    for b in range(2):
        y0 = 0 if b == 0 else ny - 3

        def finish(j, p3):
            amp[2 * b + j] = jnp.sqrt(jnp.maximum(-p3 * dens[y0 + j], 0.0))

        edges = (flags[0], 1) if b == 0 else (1, flags[1])
        filter_block(s_s.at[b], d_s.at[b], 6 + b, (flags[2], flags[3]), edges, finish, True)
    table(5, nz, nx, amp, low, high, outer_row(ny), fine_s, vol, vol_i, 2)

    def lanes(ref, count):
        total = ref[pl.ds(0, count, stride=8), :]
        for s in range(1, 8):
            total = total + ref[pl.ds(s, count, stride=8), :]
        return total

    volumes, present = lanes(vol, POINTS), lanes(tgt, COARSE)
    over = [volumes[FINE * i : FINE * i + FINE] - present[i : i + 1] for i in range(COARSE)]
    excess[...] = jnp.sum(jnp.transpose(jnp.concatenate(over, axis=0)), axis=0, keepdims=True)


def outer_call(flags, src, rim, nodes, got_even, got_odd, mat, dens, low, high, vol_i, tgt):
    ny, nz, nx = dens.shape
    rows = nz + 2 * OFF
    return pl.pallas_call(
        outer_kernel,
        in_specs=[SMEM] + [VMEM] * 11,
        out_shape=(jax.ShapeDtypeStruct((5, nz, nx), f32), jax.ShapeDtypeStruct((1, POINTS), f32)),
        scratch_shapes=[
            pltpu.VMEM((2, 7, rows, nx), f32),
            pltpu.VMEM((2, 5, rows, nx), f32),
            pltpu.VMEM((FINE, 5, nz, nx), f32),
            pltpu.VMEM((8 * POINTS, nx), f32),
            pltpu.VMEM(got_odd.shape, f32),
            pltpu.VMEM(got_odd.shape, f32),
        ]
        + workspace(2, 2, nx),
        compiler_params=pltpu.CompilerParams(vmem_limit_bytes=20 * 2**20),
        cost_estimate=estimate(3),
        name="filter_outer",
    )(flags, src, rim, nodes, got_even, got_odd, mat, dens, low, high, vol_i, tgt)


def update_kernel(tables, amp_i, amp_o, low, high, new, logm):
    inner = amp_i.shape[0]
    nx = amp_i.shape[-1]
    total = jnp.sum(tables[...], axis=0, keepdims=True)
    lane = lax.broadcasted_iota(jnp.int32, total.shape, 1)
    above = jnp.where((total > 0.0) & (lane > 0), 1.0, 0.0)
    middle = -bracket_end + (2.0 * bracket_end / POINTS) * (jnp.sum(above) + 0.5)
    logm[0] = middle
    scale = jnp.exp(jnp.full((1, nx), -0.5 * middle, f32))

    def new_row(y, amp):
        new[y] = jnp.minimum(jnp.maximum(amp * scale, low[y]), high[y])

    def body(j, _):
        new_row(inner_row(j), amp_i[j])
        return 0

    lax.fori_loop(0, inner, body, 0, unroll=4)
    for j in range(5):
        new_row(j if j < 2 else inner + j, amp_o[j])


def update_call(tables, amp_i, amp_o, low, high):
    return pl.pallas_call(
        update_kernel,
        in_specs=[VMEM] * 5,
        out_specs=(VMEM, SMEM),
        out_shape=(jax.ShapeDtypeStruct(low.shape, f32), jax.ShapeDtypeStruct((1,), f32)),
        compiler_params=pltpu.CompilerParams(vmem_limit_bytes=8 * 2**20),
        cost_estimate=estimate(1),
        name="update",
    )(tables, amp_i, amp_o, low, high)


def to_lower(value, axis):
    count = lax.axis_size(axis)
    return lax.ppermute(value, axis, [(i + 1, i) for i in range(count - 1)])


def swap(value, axis, start):
    pairs = []
    for i in range(start, lax.axis_size(axis) - 1, 2):
        pairs += [(i, i + 1), (i + 1, i)]
    return lax.ppermute(value, axis, pairs)


def on_device(displacement, density, passive, solid, stiffness):
    ny, nz, nx = density.shape
    gy, gz = lax.axis_size("gy"), lax.axis_size("gz")
    iy, iz = lax.axis_index("gy"), lax.axis_index("gz")
    flags = jnp.stack([iy > 0, iy < gy - 1, iz > 0, iz < gz - 1, iy % 2 == 1, iz % 2 == 1]).astype(jnp.int32)

    disp_hbm = pltpu.with_memory_space_constraint(displacement, pltpu.HBM)
    stiff_hbm = pltpu.with_memory_space_constraint(stiffness, pltpu.HBM)

    face, mat, mat_y = start_call(disp_hbm, stiff_hbm)
    fy = to_lower(face, "gy")
    ends, up, down, z_even, z_odd = ends_call(flags, displacement, density, mat)

    z_got_even = swap(z_even, "gz", 0)
    z_got_odd = swap(z_odd, "gz", 1)
    src, low, high, tgt = middle_call(displacement, density, fy, mat, ends, passive, solid)
    rim, nodes, msg_even, msg_odd = rim_call(flags, z_got_even, z_got_odd, up, down, displacement, density, mat_y, src)

    got_even = swap(msg_even, "gy", 0)
    got_odd = swap(msg_odd, "gy", 1)
    amp_i, vol = inner_call(flags, src, rim, density, low, high)
    amp_o, excess = outer_call(flags, src, rim, nodes, got_even, got_odd, mat, density, low, high, vol, tgt)

    everyone = jnp.broadcast_to(excess, (gz * gy, POINTS))
    tables = lax.all_to_all(everyone, ("gz", "gy"), 0, 0, tiled=True)
    new, logm = update_call(tables, amp_i, amp_o, low, high)
    return new, logm.reshape(())


def solution(mesh):
    placed = (
        P(None, "gy", "gz", None),
        P("gy", "gz", None),
        P("gy", "gz", None),
        P("gy", "gz", None),
        P(),
    )
    return jax.shard_map(
        on_device, mesh=mesh, in_specs=placed, out_specs=(P("gy", "gz", None), P()), check_vma=False
    )
```

```python
import math

import jax
import jax.numpy as jnp
from jax import lax
from jax.experimental import pallas as pl
from jax.experimental.pallas import tpu as pltpu
from jax.sharding import PartitionSpec as P

ITERS = 8
POINTS = 2**ITERS
OFF = 8

smoothing = 0.52
move_limit = 0.2
floor_density = 0.001
bracket_end = 12.0

f32 = jnp.float32
bf16 = jnp.bfloat16
VMEM = pl.BlockSpec(memory_space=pltpu.VMEM)
SMEM = pl.BlockSpec(memory_space=pltpu.SMEM)
HBM = pl.BlockSpec(memory_space=pltpu.HBM)


def cheb_weights():
    spectrum_top = 1.0 + 12.0 * smoothing
    centre_value = (spectrum_top + 1.0) / 2.0
    half_width = (spectrum_top - 1.0) / 2.0
    ratio_value = centre_value / half_width
    first_rho = 1.0 / ratio_value
    second_rho = 1.0 / (2.0 * ratio_value - first_rho)
    third_rho = 1.0 / (2.0 * ratio_value - second_rho)
    return (
        centre_value,
        second_rho * first_rho,
        2.0 * second_rho / half_width,
        third_rho * second_rho,
        2.0 * third_rho / half_width,
    )


def filter_weights():
    t, w1, w2, w3, w4 = cheb_weights()
    diag = 1.0 + 6.0 * smoothing
    alpha = w1 / t + w2 * (1.0 - diag / t)
    beta = w2 * smoothing / t
    gamma = 1.0 / t - w4 * w1 / (t * w2)
    delta = 1.0 + w3 + w4 / w2 - w4 * diag
    eps = w4 * smoothing
    return alpha, beta, gamma, delta, eps


def lane_up(v):
    n = v.shape[-1]
    lane = lax.broadcasted_iota(jnp.int32, v.shape, v.ndim - 1)
    return jnp.where(lane < n - 1, pltpu.roll(v, n - 1, v.ndim - 1), 0.0)


def lane_down(v):
    n = v.shape[-1]
    lane = lax.broadcasted_iota(jnp.int32, v.shape, v.ndim - 1)
    return jnp.where(lane > 0, pltpu.roll(v, 1, v.ndim - 1), 0.0)


def estimate(us):
    return pl.CostEstimate(flops=int(us * 1e9), bytes_accessed=1 << 20, transcendentals=0)


def build_matrices(k, mats):
    shape = (24, 128)
    col = lax.broadcasted_iota(jnp.int32, shape, 1)
    row = lax.broadcasted_iota(jnp.int32, shape, 0)
    main = col < 96
    q = jnp.where(main, jnp.where(col >= 48, 1, 0), jnp.where(col >= 104, 1, 0))
    m = col - 48 * q
    e = col - 96 - 8 * q
    c = jnp.where(main, m >> 4, e >> 1)
    dx = jnp.where(main, (m >> 3) & 1, e & 1)
    valid = main | (e < 6)
    picks = []
    for _, plane, band in mats:
        dof0 = 3 * (plane * q + dx) + c
        picks.append(jnp.where(main & (row == dof0), 1.0, 0.0))
        picks.append(jnp.where(valid & (row == dof0 + 3 * band), 1.0, 0.0))
    picked = jnp.dot(
        k, jnp.concatenate(picks, axis=1), precision=lax.Precision.HIGHEST, preferred_element_type=f32
    )
    col8 = lax.broadcasted_iota(jnp.int32, (8, 128), 1)
    row8 = lax.broadcasted_iota(jnp.int32, (8, 128), 0)
    main8 = col8 < 96
    rc = col8 & 7
    m0 = main8 & (rc == row8)
    m1 = jnp.where(main8, rc, 8) == row8 + 1
    for n, (mat, plane, band) in enumerate(mats):
        k0 = picked[:, 256 * n : 256 * n + 128]
        k1 = picked[:, 256 * n + 128 : 256 * n + 256]
        rows = []
        for b in range(2):
            for q_ in range(2):
                for c_ in range(3):
                    for dx_ in range(2):
                        r = 3 * (plane * q_ + band * b + dx_) + c_
                        rows.append(jnp.where(m0, k0[r : r + 1], 0.0) + jnp.where(m1, k1[r : r + 1], 0.0))
        full = jnp.concatenate(rows, axis=0)
        hi = full.astype(bf16)
        lo = (full - hi.astype(f32)).astype(bf16)
        mat[:, 0:112] = hi[:, 0:112]
        mat[:, 112:224] = lo[:, 0:112]


def prepare(segments, p, work):
    main_s, ext_s, mul_s = work
    for l in range(3):
        for c in range(3):
            w0 = 0
            for u, x in segments(3 * l + c):
                size, nx = u.shape
                n = size // 8
                last = lax.broadcasted_iota(jnp.int32, u.shape, 0) == size - 1
                both = (u, lane_up(u))
                after = (None, None) if x is None else (x, lane_up(x))
                for w in range(n):
                    sl = slice(8 * w, 8 * w + 8)
                    main_s[p, l, 16 * c : 16 * c + 16, (w0 + w) * nx : (w0 + w + 1) * nx] = jnp.concatenate(
                        [both[0][sl], both[1][sl]], axis=0
                    ).astype(bf16)
                for dx in range(2):
                    v, vx = both[dx], after[dx]
                    k = 2 * c + dx
                    for w in range(n):
                        nxt = v[8 * w + 8 : 8 * w + 9] if w < n - 1 else vx
                        if nxt is not None:
                            ext_s[p, l, k : k + 1, (w0 + w) * nx : (w0 + w + 1) * nx] = nxt
                    m = 2.0 * v - v.astype(bf16).astype(f32)
                    mx = 0.0 if vx is None else jnp.broadcast_to(2.0 * vx - vx.astype(bf16).astype(f32), v.shape)
                    at = slice(8 * w0, 8 * (w0 + n))
                    mul_s[p, l, k, 0, at] = m
                    mul_s[p, l, k, 1, at] = jnp.where(last, mx, pltpu.roll(m, size - 1, 0))
                w0 += n


def energy_rows(p, mat, work, density):
    main_s, ext_s, mul_s = work
    rows, nx = density.shape
    count = rows // 8
    acc = [None] * count
    for l in range(3):
        ext = jnp.concatenate([ext_s[p, l], ext_s[p + 1, l]], axis=0).astype(bf16)
        one = jnp.concatenate([main_s[p, l], main_s[p + 1, l], ext], axis=0)
        force = jnp.dot(mat[...], jnp.concatenate([one, one], axis=0), preferred_element_type=f32)
        i = 0
        for b in range(2):
            for q in range(2):
                for k in range(6):
                    for w in range(count):
                        at = slice(8 * w, 8 * w + 8)
                        term = force[8 * i : 8 * i + 8, w * nx : (w + 1) * nx] * mul_s[p + q, l, k, b, at]
                        acc[w] = term if acc[w] is None else acc[w] + term
                    i += 1
    return density * (-3.0 * density * density * jnp.concatenate(acc, axis=0))


def workspace(planes, windows, nx):
    return [
        pltpu.VMEM((planes, 3, 48, windows * nx), bf16),
        pltpu.VMEM((planes, 3, 8, windows * nx), f32),
        pltpu.VMEM((planes, 3, 6, 2, 8 * windows, nx), f32),
    ]


def sweep(rows, segments, put, work):
    work[1][...] = jnp.zeros_like(work[1])
    for p in range(2):
        prepare(segments(p), p, work)

    def body(y, _):
        put(y)
        prepare(segments(y + 2), y + 2, work)
        return 0

    lax.fori_loop(0, rows - 1, body, 0, unroll=7)
    put(rows - 1)


def start_kernel(disp, stiff, face, mat, stiff_s, sems):
    copies = [
        pltpu.make_async_copy(stiff, stiff_s, sems.at[0]),
        pltpu.make_async_copy(disp.at[:, 0], face, sems.at[1]),
    ]
    for copy in copies:
        copy.start()
    copies[0].wait()
    build_matrices(stiff_s[...], ((mat, 4, 2),))
    copies[1].wait()


def start_call(disp, stiff):
    _, _, nz, nx = disp.shape
    matrix = jax.ShapeDtypeStruct((192, 224), bf16)
    return pl.pallas_call(
        start_kernel,
        in_specs=[HBM, HBM],
        out_shape=(jax.ShapeDtypeStruct((9, nz, nx), f32), matrix),
        scratch_shapes=[pltpu.VMEM((24, 24), f32), pltpu.SemaphoreType.DMA((2,))],
        compiler_params=pltpu.CompilerParams(vmem_limit_bytes=4 * 2**20),
        cost_estimate=estimate(10),
        name="start",
    )(disp, stiff)


def extra(ref, row):
    ny = ref.shape[1]
    return 11 + row // ny, slice(row % ny, row % ny + 1)


def ends_kernel(flags, disp, dens, mat, ends, up, down, msg_even, msg_odd, *work):
    _, ny, nz, nx = disp.shape

    def segments(p):
        return lambda i: [(disp[i, p, 0:8], disp[i, p, 8:9]), (disp[i, p, nz - 8 : nz], None)]

    for ref in (up, down):
        ref[9:] = jnp.zeros((ref.shape[0] - 9, ny, nx), f32)

    def pack(y):
        row = pl.ds(y, 1)
        for i in range(9):
            up[i, row] = disp[i, y, nz - 1 : nz]
            down[i, row] = disp[i, y, 0:1]
        up[9, row] = dens[y, nz - 1 : nz]

    def put(y):
        d = jnp.concatenate([dens[y, 0:8], dens[y, nz - 8 : nz]], axis=0)
        s = energy_rows(y, mat, work, d)
        ends[y] = s
        row = pl.ds(y, 1)
        up[10, row] = s[14:15]
        down[9, row] = s[0:1]
        down[10, row] = s[1:2]
        pack(y)

    sweep(ny - 1, segments, put, work)
    pack(ny - 1)
    for n, y in enumerate((0, ny - 1)):
        for i in range(9):
            up[extra(up, 9 * n + i)] = disp[i, y, nz - 2 : nz - 1]
            down[extra(down, 9 * n + i)] = disp[i, y, 1:2]
            down[extra(down, 18 + 9 * n + i)] = disp[i, y, 2:3]
    up[extra(up, 36)] = dens[ny - 1, nz - 2 : nz - 1]
    down[extra(down, 36)] = dens[ny - 1, 0:1]
    down[extra(down, 37)] = dens[ny - 1, 1:2]
    odd = flags[5] == 1
    msg_even[...] = jnp.where(odd, down[...], up[...])
    msg_odd[...] = jnp.where(odd, up[...], down[...])


def ends_call(flags, disp, dens, mat):
    _, ny, nz, nx = disp.shape
    message = jax.ShapeDtypeStruct((11 + -(-38 // ny), ny, nx), f32)
    return pl.pallas_call(
        ends_kernel,
        in_specs=[SMEM] + [VMEM] * 3,
        out_shape=(jax.ShapeDtypeStruct((ny, 16, nx), f32),) + (message,) * 4,
        scratch_shapes=workspace(ny, 2, nx),
        compiler_params=pltpu.CompilerParams(vmem_limit_bytes=16 * 2**20),
        cost_estimate=estimate(4),
        name="energy_ends",
    )(flags, disp, dens, mat)


def middle_kernel(disp, dens, fy, mat, ends, passive, solid, stiff, src, low, high, tgt, mat_y, now_s, *work):
    _, ny, nz, nx = disp.shape
    work, last = work[:3], work[3:]

    def segments(p):
        return lambda i: [(disp[i, p, 8 : nz - 8], disp[i, p, nz - 8 : nz - 7])]

    def frame(y):
        src[y, 0:OFF] = jnp.zeros((OFF, nx), f32)
        src[y, OFF + nz :] = jnp.zeros((src.shape[1] - OFF - nz, nx), f32)

    def put(y):
        frame(y)
        src[y, OFF : OFF + 8] = ends[y, 0:8]
        src[y, OFF + 8 : OFF + nz - 8] = energy_rows(y, mat, work, dens[y, 8 : nz - 8])
        src[y, OFF + nz - 8 : OFF + nz] = ends[y, 8:16]

    sweep(ny - 1, segments, put, work)
    last[1][...] = jnp.zeros_like(last[1])
    prepare(lambda i: [(disp[i, ny - 1], None)], 0, last)
    prepare(lambda i: [(fy[i], None)], 1, last)
    frame(ny - 1)
    src[ny - 1, OFF : OFF + nz] = energy_rows(0, mat, last, dens[ny - 1])

    def bound(y, _):
        low[y], high[y], now_s[y] = limits(dens[y], passive[y] == 1, solid[y] == 1)
        return 0

    lax.fori_loop(0, ny, bound, 0, unroll=4)
    build_matrices(stiff[...], ((mat_y, 2, 4),))
    targets(((ny - 5, inner_row), (5, outer_row(ny))), nz, nx, now_s, tgt)


def middle_call(disp, dens, fy, mat, ends, passive, solid, stiff):
    _, ny, nz, nx = disp.shape
    field = jax.ShapeDtypeStruct((ny, nz, nx), f32)
    return pl.pallas_call(
        middle_kernel,
        in_specs=[VMEM] * 8,
        out_shape=(
            jax.ShapeDtypeStruct((ny, nz + 2 * OFF, nx), f32),
            field,
            field,
            jax.ShapeDtypeStruct((8 * COARSE, nx), f32),
            jax.ShapeDtypeStruct((192, 224), bf16),
        ),
        scratch_shapes=[pltpu.VMEM((ny, nz, nx), f32)]
        + workspace(ny, nz // 8 - 2, nx)
        + workspace(2, nz // 8, nx),
        compiler_params=pltpu.CompilerParams(vmem_limit_bytes=24 * 2**20),
        cost_estimate=estimate(4),
        name="energy_middle",
    )(disp, dens, fy, mat, ends, passive, solid, stiff)


def rim_kernel(
    flags, got_even, got_odd, up, down, disp, dens, mat_y, src,
    rim, nodes, msg_even, msg_odd, low_s, high_s, t_s, *work,
):
    ny, rows, nx = src.shape
    nz = rows - 2 * OFF
    odd = flags[5] == 1
    low_s[...] = jnp.where(odd, got_even[...], got_odd[...])
    high_s[...] = jnp.where(odd, got_odd[...], got_even[...])
    work[1][...] = jnp.zeros_like(work[1])
    prepare(lambda i: [(low_s[i], None), (up[i], None)], 0, work)
    prepare(lambda i: [(down[i], None), (high_s[i], None)], 1, work)
    s = energy_rows(0, mat_y, work, jnp.concatenate([low_s[9], up[9]], axis=0))
    columns = ((0, low_s[10]), (1, s[0:ny]), (3, s[ny : 2 * ny]), (4, high_s[9]), (5, high_s[10]))
    for y in range(ny):
        rim[y] = jnp.zeros((8, nx), f32)
        for r, column in columns:
            rim[y, r : r + 1] = column[y : y + 1]
    half = 2 * (nz + 8)
    zero = jnp.zeros((1, nx), f32)
    for n, y in enumerate((0, ny - 1)):
        row = slice(y, y + 1)
        for i in range(9):
            window = jnp.concatenate(
                [
                    low_s[extra(low_s, 9 * n + i)],
                    low_s[i, row],
                    disp[i, y, 0:1],
                    disp[i, y, nz - 1 : nz],
                    high_s[i, row],
                    high_s[extra(high_s, 9 * n + i)],
                    high_s[extra(high_s, 18 + 9 * n + i)],
                    zero,
                ],
                axis=0,
            )
            nodes[n, i] = window
            t_s[n, half + 8 * i : half + 8 * i + 8] = window
        nodes[n, 9] = jnp.concatenate(
            [
                low_s[extra(low_s, 36)],
                low_s[9, ny - 1 : ny],
                zero,
                dens[ny - 1, nz - 1 : nz],
                high_s[extra(high_s, 36)],
                high_s[extra(high_s, 37)],
                zero,
                zero,
            ],
            axis=0,
        )
        t_s[n, half + 72 : half + 80] = nodes[n, 9]
        for j in range(2):
            at = j * (nz + 8)
            yy = j if n == 0 else ny - 2 + j
            t_s[n, at : at + nz] = src[yy, OFF : OFF + nz]
            t_s[n, at + nz : at + nz + 8] = rim[yy]
    odd = flags[4] == 1
    msg_even[...] = jnp.where(odd, t_s[0], t_s[1])
    msg_odd[...] = jnp.where(odd, t_s[1], t_s[0])


def put_rim(s, y, rim, nz):
    s[y, OFF - 2 : OFF] = rim[0:2]
    s[y, OFF + nz - 1 : OFF + nz + 2] = rim[3:6]


def rim_call(flags, got_even, got_odd, up, down, disp, dens, mat_y, src):
    ny, rows, nx = src.shape
    nz = rows - 2 * OFF
    size = 2 * (nz + 8) + 80
    return pl.pallas_call(
        rim_kernel,
        in_specs=[SMEM] + [VMEM] * 8,
        out_shape=(
            jax.ShapeDtypeStruct((ny, 8, nx), f32),
            jax.ShapeDtypeStruct((2, 10, 8, nx), f32),
            jax.ShapeDtypeStruct((size, nx), f32),
            jax.ShapeDtypeStruct((size, nx), f32),
        ),
        scratch_shapes=[
            pltpu.VMEM(up.shape, f32),
            pltpu.VMEM(up.shape, f32),
            pltpu.VMEM((2, size, nx), f32),
        ]
        + workspace(2, 2 * (ny // 8), nx),
        compiler_params=pltpu.CompilerParams(vmem_limit_bytes=16 * 2**20),
        cost_estimate=estimate(2),
        name="energy_rim",
    )(flags, got_even, got_odd, up, down, disp, dens, mat_y, src)


def filter_block(s_s, d_s, n, z_edges, y_edges, finish, unroll):
    rows, nx = s_s.shape[1:]
    nz = rows - 2 * OFF
    alpha, beta, gamma, delta, eps = filter_weights()
    row = lax.broadcasted_iota(jnp.int32, (rows, nx), 0)
    keep = jnp.where(row < OFF, z_edges[0], jnp.where(row >= OFF + nz, z_edges[1], 1)) == 1

    def beside(v):
        return pltpu.roll(v, 1, 0) + pltpu.roll(v, rows - 1, 0) + lane_up(v) + lane_down(v)

    def second(j, _):
        c = s_s[j + 1]
        d2 = alpha * c + beta * (beside(c) + s_s[j] + s_s[j + 2])
        ok = keep
        if y_edges is not None:
            ok = keep & (jnp.where(j == 0, y_edges[0], jnp.where(j == n - 3, y_edges[1], 1)) == 1)
        d_s[j] = jnp.where(ok, d2, 0.0)
        return 0

    def third(j, _):
        d2 = d_s[j + 1]
        p3 = gamma * s_s[j + 2] + delta * d2 + eps * (beside(d2) + d_s[j] + d_s[j + 2])
        finish(j, p3[OFF : OFF + nz])
        return 0

    lax.fori_loop(0, n - 2, second, 0, unroll=unroll)
    lax.fori_loop(0, n - 4, third, 0, unroll=unroll)


def limits(d, pas, sol):
    lower = jnp.maximum(d - move_limit, floor_density)
    upper = jnp.minimum(d + move_limit, 1.0)
    return tuple(jnp.where(sol, 1.0, jnp.where(pas, floor_density, v)) for v in (lower, upper, d))


FINE = 16
COARSE = POINTS // FINE


SPACING = 2.0 * bracket_end / POINTS


def inverse_coarse(i):
    return math.exp(0.5 * (-bracket_end + SPACING * FINE * i))


def targets(rows, nz, nx, now, tgt):
    acc = tuple(jnp.zeros((8, nx), f32) for _ in range(COARSE))
    for n, row in rows:

        def add(j, acc):
            acc = list(acc)
            for w in range(nz // 8):
                d = now[row(j), 8 * w : 8 * w + 8]
                for i in range(COARSE):
                    acc[i] = acc[i] + d * inverse_coarse(i)
            return tuple(acc)

        acc = lax.fori_loop(0, n, add, acc, unroll=2)
    for i in range(COARSE):
        tgt[8 * i : 8 * i + 8] = acc[i]


def table(n, nz, nx, amp, low, high, row, fine_s, vol, start, unroll):
    pair = 2
    for first in range(0, COARSE, pair):
        inverse = [inverse_coarse(i) for i in range(first, first + pair)]

        def volume(j, acc):
            acc = list(acc)
            y = row(j)
            for w in range(nz // 8):
                at = slice(8 * w, 8 * w + 8)
                lo, hi = low[y, at], high[y, at]
                los, his = [lo * c for c in inverse], [hi * c for c in inverse]
                for f in range(FINE):
                    if first == 0:
                        t = amp[j, at] * math.exp(-0.5 * SPACING * f)
                        fine_s[f, j, at] = t
                    else:
                        t = fine_s[f, j, at]
                    for i in range(pair):
                        acc[i * FINE + f] = acc[i * FINE + f] + jnp.minimum(jnp.maximum(t, los[i]), his[i])
            return tuple(acc)

        places = [slice(8 * (first * FINE + e), 8 * (first * FINE + e) + 8) for e in range(pair * FINE)]
        begin = tuple(jnp.zeros((8, nx), f32) if start is None else start[at] for at in places)
        acc = lax.fori_loop(0, n, volume, begin, unroll=unroll)
        for at, value in zip(places, acc):
            vol[at] = value


def inner_row(j):
    return j + 2


def outer_row(ny):
    return lambda j: jnp.where(j < 2, j, j + ny - 5)


def inner_kernel(flags, src, rim, dens, low, high, amp, vol, s_s, d_s, fine_s):
    ny, nz, nx = dens.shape
    s_s[...] = src[0 : ny - 1]

    def fix(y, _):
        put_rim(s_s, y, rim[y], nz)
        return 0

    lax.fori_loop(0, ny - 1, fix, 0, unroll=5)

    def finish(j, p3):
        amp[j] = jnp.sqrt(jnp.maximum(-p3 * dens[inner_row(j)], 0.0))

    filter_block(s_s, d_s, ny - 1, (flags[2], flags[3]), None, finish, True)
    table(ny - 5, nz, nx, amp, low, high, inner_row, fine_s, vol, None, 4)


def inner_call(flags, src, rim, dens, low, high):
    ny, nz, nx = dens.shape
    rows = nz + 2 * OFF
    return pl.pallas_call(
        inner_kernel,
        in_specs=[SMEM] + [VMEM] * 5,
        out_shape=(
            jax.ShapeDtypeStruct((ny - 5, nz, nx), f32),
            jax.ShapeDtypeStruct((8 * POINTS, nx), f32),
        ),
        scratch_shapes=[
            pltpu.VMEM((ny - 1, rows, nx), f32),
            pltpu.VMEM((ny - 3, rows, nx), f32),
            pltpu.VMEM((FINE, ny - 5, nz, nx), f32),
        ],
        compiler_params=pltpu.CompilerParams(vmem_limit_bytes=24 * 2**20),
        cost_estimate=estimate(9),
        name="filter_inner",
    )(flags, src, rim, dens, low, high)


def outer_kernel(
    flags, src, rim, nodes, got_even, got_odd, mat, dens, low, high, vol_i, tgt,
    amp, excess, s_s, d_s, fine_s, vol, below, above, *work,
):
    ny, nz, nx = dens.shape
    odd = flags[4] == 1
    below[...] = jnp.where(odd, got_even[...], got_odd[...])
    above[...] = jnp.where(odd, got_odd[...], got_even[...])
    half = 2 * (nz + 8)

    def window(ref, i):
        return ref[half + 8 * i : half + 8 * i + 8]

    work[1][...] = jnp.zeros_like(work[1])
    prepare(lambda i: [(window(below, i), None), (nodes[1, i], None)], 0, work)
    prepare(lambda i: [(nodes[0, i], None), (window(above, i), None)], 1, work)
    corner = energy_rows(0, mat, work, jnp.concatenate([window(below, 9), nodes[1, 9]], axis=0))
    for b, ref in enumerate((below, above)):
        for j in range(2):
            at = j if b == 0 else 5 + j
            start = j * (nz + 8)
            s_s[b, at, 0:OFF] = jnp.zeros((OFF, nx), f32)
            s_s[b, at, OFF : OFF + nz] = ref[start : start + nz]
            s_s[b, at, OFF + nz :] = jnp.zeros((OFF, nx), f32)
            put_rim(s_s.at[b], at, ref[start + nz : start + nz + 8], nz)
    for j in range(4):
        s_s[0, 2 + j] = src[j]
        put_rim(s_s.at[0], 2 + j, rim[j], nz)
    for j in range(5):
        s_s[1, j] = src[ny - 5 + j]
        put_rim(s_s.at[1], j, rim[ny - 5 + j], nz)
    put_rim(s_s.at[0], 1, corner[0:8], nz)
    put_rim(s_s.at[1], 4, corner[8:16], nz)
    for b in range(2):
        y0 = 0 if b == 0 else ny - 3

        def finish(j, p3):
            amp[2 * b + j] = jnp.sqrt(jnp.maximum(-p3 * dens[y0 + j], 0.0))

        edges = (flags[0], 1) if b == 0 else (1, flags[1])
        filter_block(s_s.at[b], d_s.at[b], 6 + b, (flags[2], flags[3]), edges, finish, True)
    table(5, nz, nx, amp, low, high, outer_row(ny), fine_s, vol, vol_i, 2)

    def lanes(ref, count):
        total = ref[pl.ds(0, count, stride=8), :]
        for s in range(1, 8):
            total = total + ref[pl.ds(s, count, stride=8), :]
        return total

    volumes, present = lanes(vol, POINTS), lanes(tgt, COARSE)
    over = [volumes[FINE * i : FINE * i + FINE] - present[i : i + 1] for i in range(COARSE)]
    excess[...] = jnp.sum(jnp.transpose(jnp.concatenate(over, axis=0)), axis=0, keepdims=True)


def outer_call(flags, src, rim, nodes, got_even, got_odd, mat, dens, low, high, vol_i, tgt):
    ny, nz, nx = dens.shape
    rows = nz + 2 * OFF
    return pl.pallas_call(
        outer_kernel,
        in_specs=[SMEM] + [VMEM] * 11,
        out_shape=(jax.ShapeDtypeStruct((5, nz, nx), f32), jax.ShapeDtypeStruct((1, POINTS), f32)),
        scratch_shapes=[
            pltpu.VMEM((2, 7, rows, nx), f32),
            pltpu.VMEM((2, 5, rows, nx), f32),
            pltpu.VMEM((FINE, 5, nz, nx), f32),
            pltpu.VMEM((8 * POINTS, nx), f32),
            pltpu.VMEM(got_odd.shape, f32),
            pltpu.VMEM(got_odd.shape, f32),
        ]
        + workspace(2, 2, nx),
        compiler_params=pltpu.CompilerParams(vmem_limit_bytes=20 * 2**20),
        cost_estimate=estimate(3),
        name="filter_outer",
    )(flags, src, rim, nodes, got_even, got_odd, mat, dens, low, high, vol_i, tgt)


def update_kernel(tables, amp_i, amp_o, low, high, new, logm):
    inner = amp_i.shape[0]
    nx = amp_i.shape[-1]
    total = jnp.sum(tables[...], axis=0, keepdims=True)
    lane = lax.broadcasted_iota(jnp.int32, total.shape, 1)
    above = jnp.where((total > 0.0) & (lane > 0), 1.0, 0.0)
    middle = -bracket_end + (2.0 * bracket_end / POINTS) * (jnp.sum(above) + 0.5)
    logm[0] = middle
    scale = jnp.exp(jnp.full((1, nx), -0.5 * middle, f32))

    def new_row(y, amp):
        new[y] = jnp.minimum(jnp.maximum(amp * scale, low[y]), high[y])

    def body(j, _):
        new_row(inner_row(j), amp_i[j])
        return 0

    lax.fori_loop(0, inner, body, 0, unroll=4)
    for j in range(5):
        new_row(j if j < 2 else inner + j, amp_o[j])


def update_call(tables, amp_i, amp_o, low, high):
    return pl.pallas_call(
        update_kernel,
        in_specs=[VMEM] * 5,
        out_specs=(VMEM, SMEM),
        out_shape=(jax.ShapeDtypeStruct(low.shape, f32), jax.ShapeDtypeStruct((1,), f32)),
        compiler_params=pltpu.CompilerParams(vmem_limit_bytes=8 * 2**20),
        cost_estimate=estimate(1),
        name="update",
    )(tables, amp_i, amp_o, low, high)


def to_lower(value, axis):
    count = lax.axis_size(axis)
    return lax.ppermute(value, axis, [(i + 1, i) for i in range(count - 1)])


def swap(value, axis, start):
    pairs = []
    for i in range(start, lax.axis_size(axis) - 1, 2):
        pairs += [(i, i + 1), (i + 1, i)]
    return lax.ppermute(value, axis, pairs)


def on_device(displacement, density, passive, solid, stiffness):
    ny, nz, nx = density.shape
    gy, gz = lax.axis_size("gy"), lax.axis_size("gz")
    iy, iz = lax.axis_index("gy"), lax.axis_index("gz")
    flags = jnp.stack([iy > 0, iy < gy - 1, iz > 0, iz < gz - 1, iy % 2 == 1, iz % 2 == 1]).astype(jnp.int32)

    disp_hbm = pltpu.with_memory_space_constraint(displacement, pltpu.HBM)
    stiff_hbm = pltpu.with_memory_space_constraint(stiffness, pltpu.HBM)

    face, mat = start_call(disp_hbm, stiff_hbm)
    fy = to_lower(face, "gy")
    ends, up, down, z_even, z_odd = ends_call(flags, displacement, density, mat)

    z_got_even = swap(z_even, "gz", 0)
    z_got_odd = swap(z_odd, "gz", 1)
    src, low, high, tgt, mat_y = middle_call(displacement, density, fy, mat, ends, passive, solid, stiffness)
    rim, nodes, msg_even, msg_odd = rim_call(flags, z_got_even, z_got_odd, up, down, displacement, density, mat_y, src)

    got_even = swap(msg_even, "gy", 0)
    got_odd = swap(msg_odd, "gy", 1)
    amp_i, vol = inner_call(flags, src, rim, density, low, high)
    amp_o, excess = outer_call(flags, src, rim, nodes, got_even, got_odd, mat, density, low, high, vol, tgt)

    everyone = jnp.broadcast_to(excess, (gz * gy, POINTS))
    tables = lax.all_to_all(everyone, ("gz", "gy"), 0, 0, tiled=True)
    new, logm = update_call(tables, amp_i, amp_o, low, high)
    return new, logm.reshape(())


def solution(mesh):
    placed = (
        P(None, "gy", "gz", None),
        P("gy", "gz", None),
        P("gy", "gz", None),
        P("gy", "gz", None),
        P(),
    )
    return jax.shard_map(
        on_device, mesh=mesh, in_specs=placed, out_specs=(P("gy", "gz", None), P()), check_vma=False
    )
```

```python
import math

import jax
import jax.numpy as jnp
from jax import lax
from jax.experimental import pallas as pl
from jax.experimental.pallas import tpu as pltpu
from jax.sharding import PartitionSpec as P

ITERS = 8
POINTS = 2**ITERS
OFF = 8

smoothing = 0.52
move_limit = 0.2
floor_density = 0.001
bracket_end = 12.0

f32 = jnp.float32
bf16 = jnp.bfloat16
VMEM = pl.BlockSpec(memory_space=pltpu.VMEM)
SMEM = pl.BlockSpec(memory_space=pltpu.SMEM)
HBM = pl.BlockSpec(memory_space=pltpu.HBM)


def cheb_weights():
    spectrum_top = 1.0 + 12.0 * smoothing
    centre_value = (spectrum_top + 1.0) / 2.0
    half_width = (spectrum_top - 1.0) / 2.0
    ratio_value = centre_value / half_width
    first_rho = 1.0 / ratio_value
    second_rho = 1.0 / (2.0 * ratio_value - first_rho)
    third_rho = 1.0 / (2.0 * ratio_value - second_rho)
    return (
        centre_value,
        second_rho * first_rho,
        2.0 * second_rho / half_width,
        third_rho * second_rho,
        2.0 * third_rho / half_width,
    )


def filter_weights():
    t, w1, w2, w3, w4 = cheb_weights()
    diag = 1.0 + 6.0 * smoothing
    alpha = w1 / t + w2 * (1.0 - diag / t)
    beta = w2 * smoothing / t
    gamma = 1.0 / t - w4 * w1 / (t * w2)
    delta = 1.0 + w3 + w4 / w2 - w4 * diag
    eps = w4 * smoothing
    return alpha, beta, gamma, delta, eps


def lane_up(v):
    n = v.shape[-1]
    lane = lax.broadcasted_iota(jnp.int32, v.shape, v.ndim - 1)
    return jnp.where(lane < n - 1, pltpu.roll(v, n - 1, v.ndim - 1), 0.0)


def lane_down(v):
    n = v.shape[-1]
    lane = lax.broadcasted_iota(jnp.int32, v.shape, v.ndim - 1)
    return jnp.where(lane > 0, pltpu.roll(v, 1, v.ndim - 1), 0.0)


def estimate(us):
    return pl.CostEstimate(flops=int(us * 1e9), bytes_accessed=1 << 20, transcendentals=0)


def build_matrices(k, mats):
    shape = (24, 128)
    col = lax.broadcasted_iota(jnp.int32, shape, 1)
    row = lax.broadcasted_iota(jnp.int32, shape, 0)
    main = col < 96
    q = jnp.where(main, jnp.where(col >= 48, 1, 0), jnp.where(col >= 104, 1, 0))
    m = col - 48 * q
    e = col - 96 - 8 * q
    c = jnp.where(main, m >> 4, e >> 1)
    dx = jnp.where(main, (m >> 3) & 1, e & 1)
    valid = main | (e < 6)
    picks = []
    for _, plane, band in mats:
        dof0 = 3 * (plane * q + dx) + c
        picks.append(jnp.where(main & (row == dof0), 1.0, 0.0))
        picks.append(jnp.where(valid & (row == dof0 + 3 * band), 1.0, 0.0))
    picked = jnp.dot(
        k, jnp.concatenate(picks, axis=1), precision=lax.Precision.HIGHEST, preferred_element_type=f32
    )
    col8 = lax.broadcasted_iota(jnp.int32, (8, 128), 1)
    row8 = lax.broadcasted_iota(jnp.int32, (8, 128), 0)
    main8 = col8 < 96
    rc = col8 & 7
    m0 = main8 & (rc == row8)
    m1 = jnp.where(main8, rc, 8) == row8 + 1
    for n, (mat, plane, band) in enumerate(mats):
        k0 = picked[:, 256 * n : 256 * n + 128]
        k1 = picked[:, 256 * n + 128 : 256 * n + 256]
        rows = []
        for b in range(2):
            for q_ in range(2):
                for c_ in range(3):
                    for dx_ in range(2):
                        r = 3 * (plane * q_ + band * b + dx_) + c_
                        rows.append(jnp.where(m0, k0[r : r + 1], 0.0) + jnp.where(m1, k1[r : r + 1], 0.0))
        full = jnp.concatenate(rows, axis=0)
        hi = full.astype(bf16)
        lo = (full - hi.astype(f32)).astype(bf16)
        mat[:, 0:112] = hi[:, 0:112]
        mat[:, 112:224] = lo[:, 0:112]


def prepare(segments, p, work):
    main_s, ext_s, mul_s = work
    for l in range(3):
        for c in range(3):
            w0 = 0
            for u, x in segments(3 * l + c):
                size, nx = u.shape
                n = size // 8
                last = lax.broadcasted_iota(jnp.int32, u.shape, 0) == size - 1
                both = (u, lane_up(u))
                after = (None, None) if x is None else (x, lane_up(x))
                for w in range(n):
                    sl = slice(8 * w, 8 * w + 8)
                    main_s[p, l, 16 * c : 16 * c + 16, (w0 + w) * nx : (w0 + w + 1) * nx] = jnp.concatenate(
                        [both[0][sl], both[1][sl]], axis=0
                    ).astype(bf16)
                for dx in range(2):
                    v, vx = both[dx], after[dx]
                    k = 2 * c + dx
                    for w in range(n):
                        nxt = v[8 * w + 8 : 8 * w + 9] if w < n - 1 else vx
                        if nxt is not None:
                            ext_s[p, l, k : k + 1, (w0 + w) * nx : (w0 + w + 1) * nx] = nxt
                    m = 2.0 * v - v.astype(bf16).astype(f32)
                    mx = 0.0 if vx is None else jnp.broadcast_to(2.0 * vx - vx.astype(bf16).astype(f32), v.shape)
                    at = slice(8 * w0, 8 * (w0 + n))
                    mul_s[p, l, k, 0, at] = m
                    mul_s[p, l, k, 1, at] = jnp.where(last, mx, pltpu.roll(m, size - 1, 0))
                w0 += n


def energy_rows(p, mat, work, density):
    main_s, ext_s, mul_s = work
    rows, nx = density.shape
    count = rows // 8
    acc = [None] * count
    for l in range(3):
        ext = jnp.concatenate([ext_s[p, l], ext_s[p + 1, l]], axis=0).astype(bf16)
        one = jnp.concatenate([main_s[p, l], main_s[p + 1, l], ext], axis=0)
        force = jnp.dot(mat[...], jnp.concatenate([one, one], axis=0), preferred_element_type=f32)
        i = 0
        for b in range(2):
            for q in range(2):
                for k in range(6):
                    for w in range(count):
                        at = slice(8 * w, 8 * w + 8)
                        term = force[8 * i : 8 * i + 8, w * nx : (w + 1) * nx] * mul_s[p + q, l, k, b, at]
                        acc[w] = term if acc[w] is None else acc[w] + term
                    i += 1
    return density * (-3.0 * density * density * jnp.concatenate(acc, axis=0))


def workspace(planes, windows, nx):
    return [
        pltpu.VMEM((planes, 3, 48, windows * nx), bf16),
        pltpu.VMEM((planes, 3, 8, windows * nx), f32),
        pltpu.VMEM((planes, 3, 6, 2, 8 * windows, nx), f32),
    ]


def sweep(rows, segments, put, work):
    work[1][...] = jnp.zeros_like(work[1])
    for p in range(2):
        prepare(segments(p), p, work)

    def body(y, _):
        put(y)
        prepare(segments(y + 2), y + 2, work)
        return 0

    lax.fori_loop(0, rows - 1, body, 0, unroll=7)
    put(rows - 1)


def start_kernel(disp, stiff, face, mat, stiff_s, sems):
    copies = [
        pltpu.make_async_copy(stiff, stiff_s, sems.at[0]),
        pltpu.make_async_copy(disp.at[:, 0], face, sems.at[1]),
    ]
    for copy in copies:
        copy.start()
    copies[0].wait()
    build_matrices(stiff_s[...], ((mat, 4, 2),))
    copies[1].wait()


def start_call(disp, stiff):
    _, _, nz, nx = disp.shape
    matrix = jax.ShapeDtypeStruct((192, 224), bf16)
    return pl.pallas_call(
        start_kernel,
        in_specs=[HBM, HBM],
        out_shape=(jax.ShapeDtypeStruct((9, nz, nx), f32), matrix),
        scratch_shapes=[pltpu.VMEM((24, 24), f32), pltpu.SemaphoreType.DMA((2,))],
        compiler_params=pltpu.CompilerParams(vmem_limit_bytes=4 * 2**20),
        cost_estimate=estimate(10),
        name="start",
    )(disp, stiff)


def extra(ref, row):
    ny = ref.shape[1]
    return 11 + row // ny, slice(row % ny, row % ny + 1)


def ends_kernel(flags, disp, dens, mat, ends, up, down, msg_even, msg_odd, *work):
    _, ny, nz, nx = disp.shape

    def segments(p):
        return lambda i: [(disp[i, p, 0:8], disp[i, p, 8:9]), (disp[i, p, nz - 8 : nz], None)]

    for ref in (up, down):
        ref[9:] = jnp.zeros((ref.shape[0] - 9, ny, nx), f32)

    def pack(y):
        row = pl.ds(y, 1)
        for i in range(9):
            up[i, row] = disp[i, y, nz - 1 : nz]
            down[i, row] = disp[i, y, 0:1]
        up[9, row] = dens[y, nz - 1 : nz]

    def put(y):
        d = jnp.concatenate([dens[y, 0:8], dens[y, nz - 8 : nz]], axis=0)
        s = energy_rows(y, mat, work, d)
        ends[y] = s
        row = pl.ds(y, 1)
        up[10, row] = s[14:15]
        down[9, row] = s[0:1]
        down[10, row] = s[1:2]
        pack(y)

    sweep(ny - 1, segments, put, work)
    pack(ny - 1)
    for n, y in enumerate((0, ny - 1)):
        for i in range(9):
            up[extra(up, 9 * n + i)] = disp[i, y, nz - 2 : nz - 1]
            down[extra(down, 9 * n + i)] = disp[i, y, 1:2]
            down[extra(down, 18 + 9 * n + i)] = disp[i, y, 2:3]
    up[extra(up, 36)] = dens[ny - 1, nz - 2 : nz - 1]
    down[extra(down, 36)] = dens[ny - 1, 0:1]
    down[extra(down, 37)] = dens[ny - 1, 1:2]
    odd = flags[5] == 1
    msg_even[...] = jnp.where(odd, down[...], up[...])
    msg_odd[...] = jnp.where(odd, up[...], down[...])


def ends_call(flags, disp, dens, mat):
    _, ny, nz, nx = disp.shape
    message = jax.ShapeDtypeStruct((11 + -(-38 // ny), ny, nx), f32)
    return pl.pallas_call(
        ends_kernel,
        in_specs=[SMEM] + [VMEM] * 3,
        out_shape=(jax.ShapeDtypeStruct((ny, 16, nx), f32),) + (message,) * 4,
        scratch_shapes=workspace(ny, 2, nx),
        compiler_params=pltpu.CompilerParams(vmem_limit_bytes=16 * 2**20),
        cost_estimate=estimate(4),
        name="energy_ends",
    )(flags, disp, dens, mat)


def middle_kernel(disp, dens, fy, mat, ends, passive, solid, stiff, src, low, high, tgt, mat_y, now_s, *work):
    _, ny, nz, nx = disp.shape
    work, last = work[:3], work[3:]

    def segments(p):
        return lambda i: [(disp[i, p, 8 : nz - 8], disp[i, p, nz - 8 : nz - 7])]

    def frame(y):
        src[y, 0:OFF] = jnp.zeros((OFF, nx), f32)
        src[y, OFF + nz :] = jnp.zeros((src.shape[1] - OFF - nz, nx), f32)

    def put(y):
        frame(y)
        src[y, OFF : OFF + 8] = ends[y, 0:8]
        src[y, OFF + 8 : OFF + nz - 8] = energy_rows(y, mat, work, dens[y, 8 : nz - 8])
        src[y, OFF + nz - 8 : OFF + nz] = ends[y, 8:16]

    sweep(ny - 1, segments, put, work)
    last[1][...] = jnp.zeros_like(last[1])
    prepare(lambda i: [(disp[i, ny - 1], None)], 0, last)
    prepare(lambda i: [(fy[i], None)], 1, last)
    frame(ny - 1)
    src[ny - 1, OFF : OFF + nz] = energy_rows(0, mat, last, dens[ny - 1])

    def bound(y, _):
        low[y], high[y], now_s[y] = limits(dens[y], passive[y] == 1, solid[y] == 1)
        return 0

    lax.fori_loop(0, ny, bound, 0, unroll=4)
    build_matrices(stiff[...], ((mat_y, 2, 4),))
    targets(((ny - 5, inner_row), (5, outer_row(ny))), nz, nx, now_s, tgt)


def middle_call(disp, dens, fy, mat, ends, passive, solid, stiff):
    _, ny, nz, nx = disp.shape
    field = jax.ShapeDtypeStruct((ny, nz, nx), f32)
    return pl.pallas_call(
        middle_kernel,
        in_specs=[VMEM] * 8,
        out_shape=(
            jax.ShapeDtypeStruct((ny, nz + 2 * OFF, nx), f32),
            field,
            field,
            jax.ShapeDtypeStruct((8 * COARSE, nx), f32),
            jax.ShapeDtypeStruct((192, 224), bf16),
        ),
        scratch_shapes=[pltpu.VMEM((ny, nz, nx), f32)]
        + workspace(ny, nz // 8 - 2, nx)
        + workspace(2, nz // 8, nx),
        compiler_params=pltpu.CompilerParams(vmem_limit_bytes=24 * 2**20),
        cost_estimate=estimate(4),
        name="energy_middle",
    )(disp, dens, fy, mat, ends, passive, solid, stiff)


def rim_kernel(
    flags, got_even, got_odd, up, down, disp, dens, mat_y, src,
    rim, nodes, msg_even, msg_odd, low_s, high_s, t_s, *work,
):
    ny, rows, nx = src.shape
    nz = rows - 2 * OFF
    odd = flags[5] == 1
    low_s[...] = jnp.where(odd, got_even[...], got_odd[...])
    high_s[...] = jnp.where(odd, got_odd[...], got_even[...])
    work[1][...] = jnp.zeros_like(work[1])
    prepare(lambda i: [(low_s[i], None), (up[i], None)], 0, work)
    prepare(lambda i: [(down[i], None), (high_s[i], None)], 1, work)
    s = energy_rows(0, mat_y, work, jnp.concatenate([low_s[9], up[9]], axis=0))
    columns = ((0, low_s[10]), (1, s[0:ny]), (3, s[ny : 2 * ny]), (4, high_s[9]), (5, high_s[10]))
    for y in range(ny):
        rim[y] = jnp.zeros((8, nx), f32)
        for r, column in columns:
            rim[y, r : r + 1] = column[y : y + 1]
    half = 2 * (nz + 8)
    zero = jnp.zeros((1, nx), f32)
    for n, y in enumerate((0, ny - 1)):
        row = slice(y, y + 1)
        for i in range(9):
            window = jnp.concatenate(
                [
                    low_s[extra(low_s, 9 * n + i)],
                    low_s[i, row],
                    disp[i, y, 0:1],
                    disp[i, y, nz - 1 : nz],
                    high_s[i, row],
                    high_s[extra(high_s, 9 * n + i)],
                    high_s[extra(high_s, 18 + 9 * n + i)],
                    zero,
                ],
                axis=0,
            )
            nodes[n, i] = window
            t_s[n, half + 8 * i : half + 8 * i + 8] = window
        nodes[n, 9] = jnp.concatenate(
            [
                low_s[extra(low_s, 36)],
                low_s[9, ny - 1 : ny],
                zero,
                dens[ny - 1, nz - 1 : nz],
                high_s[extra(high_s, 36)],
                high_s[extra(high_s, 37)],
                zero,
                zero,
            ],
            axis=0,
        )
        t_s[n, half + 72 : half + 80] = nodes[n, 9]
        for j in range(2):
            at = j * (nz + 8)
            yy = j if n == 0 else ny - 2 + j
            t_s[n, at : at + nz] = src[yy, OFF : OFF + nz]
            t_s[n, at + nz : at + nz + 8] = rim[yy]
    odd = flags[4] == 1
    msg_even[...] = jnp.where(odd, t_s[0], t_s[1])
    msg_odd[...] = jnp.where(odd, t_s[1], t_s[0])


def put_rim(s, y, rim, nz):
    s[y, OFF - 2 : OFF] = rim[0:2]
    s[y, OFF + nz - 1 : OFF + nz + 2] = rim[3:6]


def rim_call(flags, got_even, got_odd, up, down, disp, dens, mat_y, src):
    ny, rows, nx = src.shape
    nz = rows - 2 * OFF
    size = 2 * (nz + 8) + 80
    return pl.pallas_call(
        rim_kernel,
        in_specs=[SMEM] + [VMEM] * 8,
        out_shape=(
            jax.ShapeDtypeStruct((ny, 8, nx), f32),
            jax.ShapeDtypeStruct((2, 10, 8, nx), f32),
            jax.ShapeDtypeStruct((size, nx), f32),
            jax.ShapeDtypeStruct((size, nx), f32),
        ),
        scratch_shapes=[
            pltpu.VMEM(up.shape, f32),
            pltpu.VMEM(up.shape, f32),
            pltpu.VMEM((2, size, nx), f32),
        ]
        + workspace(2, 2 * (ny // 8), nx),
        compiler_params=pltpu.CompilerParams(vmem_limit_bytes=16 * 2**20),
        cost_estimate=estimate(2),
        name="energy_rim",
    )(flags, got_even, got_odd, up, down, disp, dens, mat_y, src)


def filter_block(s_s, d_s, n, z_edges, y_edges, finish, unroll):
    rows, nx = s_s.shape[1:]
    nz = rows - 2 * OFF
    alpha, beta, gamma, delta, eps = filter_weights()
    row = lax.broadcasted_iota(jnp.int32, (rows, nx), 0)
    keep = jnp.where(row < OFF, z_edges[0], jnp.where(row >= OFF + nz, z_edges[1], 1)) == 1

    def beside(v):
        return pltpu.roll(v, 1, 0) + pltpu.roll(v, rows - 1, 0) + lane_up(v) + lane_down(v)

    def second(j, _):
        c = s_s[j + 1]
        d2 = alpha * c + beta * (beside(c) + s_s[j] + s_s[j + 2])
        ok = keep
        if y_edges is not None:
            ok = keep & (jnp.where(j == 0, y_edges[0], jnp.where(j == n - 3, y_edges[1], 1)) == 1)
        d_s[j] = jnp.where(ok, d2, 0.0)
        return 0

    def third(j, _):
        d2 = d_s[j + 1]
        p3 = gamma * s_s[j + 2] + delta * d2 + eps * (beside(d2) + d_s[j] + d_s[j + 2])
        finish(j, p3[OFF : OFF + nz])
        return 0

    lax.fori_loop(0, n - 2, second, 0, unroll=unroll)
    lax.fori_loop(0, n - 4, third, 0, unroll=unroll)


def limits(d, pas, sol):
    lower = jnp.maximum(d - move_limit, floor_density)
    upper = jnp.minimum(d + move_limit, 1.0)
    return tuple(jnp.where(sol, 1.0, jnp.where(pas, floor_density, v)) for v in (lower, upper, d))


FINE = 16
COARSE = POINTS // FINE


SPACING = 2.0 * bracket_end / POINTS


def inverse_coarse(i):
    return math.exp(0.5 * (-bracket_end + SPACING * FINE * i))


def targets(rows, nz, nx, now, tgt):
    acc = tuple(jnp.zeros((8, nx), f32) for _ in range(COARSE))
    for n, row in rows:

        def add(j, acc):
            acc = list(acc)
            for w in range(nz // 8):
                d = now[row(j), 8 * w : 8 * w + 8]
                for i in range(COARSE):
                    acc[i] = acc[i] + d * inverse_coarse(i)
            return tuple(acc)

        acc = lax.fori_loop(0, n, add, acc, unroll=2)
    for i in range(COARSE):
        tgt[8 * i : 8 * i + 8] = acc[i]


def table(n, nz, nx, amp, low, high, row, fine_s, vol, start, unroll):
    pair = 2
    tiles = nz // 8
    for first in range(0, COARSE, pair):
        inverse = [inverse_coarse(i) for i in range(first, first + pair)]

        def volume(step, acc):
            acc = list(acc)
            j = step // tiles
            at = pl.ds(pl.multiple_of(8 * (step % tiles), 8), 8)
            y = row(j)
            lo, hi = low[y, at], high[y, at]
            los, his = [lo * c for c in inverse], [hi * c for c in inverse]
            for f in range(FINE):
                if first == 0:
                    t = amp[j, at] * math.exp(-0.5 * SPACING * f)
                    fine_s[f, j, at] = t
                else:
                    t = fine_s[f, j, at]
                for i in range(pair):
                    acc[i * FINE + f] = acc[i * FINE + f] + jnp.minimum(jnp.maximum(t, los[i]), his[i])
            return tuple(acc)

        places = [slice(8 * (first * FINE + e), 8 * (first * FINE + e) + 8) for e in range(pair * FINE)]
        begin = tuple(jnp.zeros((8, nx), f32) if start is None else start[at] for at in places)
        acc = lax.fori_loop(0, n * tiles, volume, begin, unroll=unroll)
        for at, value in zip(places, acc):
            vol[at] = value


def inner_row(j):
    return j + 2


def outer_row(ny):
    return lambda j: jnp.where(j < 2, j, j + ny - 5)


def inner_kernel(flags, src, rim, dens, low, high, amp, vol, s_s, d_s, fine_s):
    ny, nz, nx = dens.shape
    s_s[...] = src[0 : ny - 1]

    def fix(y, _):
        put_rim(s_s, y, rim[y], nz)
        return 0

    lax.fori_loop(0, ny - 1, fix, 0, unroll=5)

    def finish(j, p3):
        amp[j] = jnp.sqrt(jnp.maximum(-p3 * dens[inner_row(j)], 0.0))

    filter_block(s_s, d_s, ny - 1, (flags[2], flags[3]), None, finish, True)
    table(ny - 5, nz, nx, amp, low, high, inner_row, fine_s, vol, None, 11)


def inner_call(flags, src, rim, dens, low, high):
    ny, nz, nx = dens.shape
    rows = nz + 2 * OFF
    return pl.pallas_call(
        inner_kernel,
        in_specs=[SMEM] + [VMEM] * 5,
        out_shape=(
            jax.ShapeDtypeStruct((ny - 5, nz, nx), f32),
            jax.ShapeDtypeStruct((8 * POINTS, nx), f32),
        ),
        scratch_shapes=[
            pltpu.VMEM((ny - 1, rows, nx), f32),
            pltpu.VMEM((ny - 3, rows, nx), f32),
            pltpu.VMEM((FINE, ny - 5, nz, nx), f32),
        ],
        compiler_params=pltpu.CompilerParams(vmem_limit_bytes=24 * 2**20),
        cost_estimate=estimate(9),
        name="filter_inner",
    )(flags, src, rim, dens, low, high)


def outer_kernel(
    flags, src, rim, nodes, got_even, got_odd, mat, dens, low, high, vol_i, tgt,
    amp, excess, s_s, d_s, fine_s, vol, below, above, *work,
):
    ny, nz, nx = dens.shape
    odd = flags[4] == 1
    below[...] = jnp.where(odd, got_even[...], got_odd[...])
    above[...] = jnp.where(odd, got_odd[...], got_even[...])
    half = 2 * (nz + 8)

    def window(ref, i):
        return ref[half + 8 * i : half + 8 * i + 8]

    work[1][...] = jnp.zeros_like(work[1])
    prepare(lambda i: [(window(below, i), None), (nodes[1, i], None)], 0, work)
    prepare(lambda i: [(nodes[0, i], None), (window(above, i), None)], 1, work)
    corner = energy_rows(0, mat, work, jnp.concatenate([window(below, 9), nodes[1, 9]], axis=0))
    for b, ref in enumerate((below, above)):
        for j in range(2):
            at = j if b == 0 else 5 + j
            start = j * (nz + 8)
            s_s[b, at, 0:OFF] = jnp.zeros((OFF, nx), f32)
            s_s[b, at, OFF : OFF + nz] = ref[start : start + nz]
            s_s[b, at, OFF + nz :] = jnp.zeros((OFF, nx), f32)
            put_rim(s_s.at[b], at, ref[start + nz : start + nz + 8], nz)
    for j in range(4):
        s_s[0, 2 + j] = src[j]
        put_rim(s_s.at[0], 2 + j, rim[j], nz)
    for j in range(5):
        s_s[1, j] = src[ny - 5 + j]
        put_rim(s_s.at[1], j, rim[ny - 5 + j], nz)
    put_rim(s_s.at[0], 1, corner[0:8], nz)
    put_rim(s_s.at[1], 4, corner[8:16], nz)
    for b in range(2):
        y0 = 0 if b == 0 else ny - 3

        def finish(j, p3):
            amp[2 * b + j] = jnp.sqrt(jnp.maximum(-p3 * dens[y0 + j], 0.0))

        edges = (flags[0], 1) if b == 0 else (1, flags[1])
        filter_block(s_s.at[b], d_s.at[b], 6 + b, (flags[2], flags[3]), edges, finish, True)
    table(5, nz, nx, amp, low, high, outer_row(ny), fine_s, vol, vol_i, 10)

    def lanes(ref, count):
        total = ref[pl.ds(0, count, stride=8), :]
        for s in range(1, 8):
            total = total + ref[pl.ds(s, count, stride=8), :]
        return total

    volumes, present = lanes(vol, POINTS), lanes(tgt, COARSE)
    over = [volumes[FINE * i : FINE * i + FINE] - present[i : i + 1] for i in range(COARSE)]
    excess[...] = jnp.sum(jnp.transpose(jnp.concatenate(over, axis=0)), axis=0, keepdims=True)


def outer_call(flags, src, rim, nodes, got_even, got_odd, mat, dens, low, high, vol_i, tgt):
    ny, nz, nx = dens.shape
    rows = nz + 2 * OFF
    return pl.pallas_call(
        outer_kernel,
        in_specs=[SMEM] + [VMEM] * 11,
        out_shape=(jax.ShapeDtypeStruct((5, nz, nx), f32), jax.ShapeDtypeStruct((1, POINTS), f32)),
        scratch_shapes=[
            pltpu.VMEM((2, 7, rows, nx), f32),
            pltpu.VMEM((2, 5, rows, nx), f32),
            pltpu.VMEM((FINE, 5, nz, nx), f32),
            pltpu.VMEM((8 * POINTS, nx), f32),
            pltpu.VMEM(got_odd.shape, f32),
            pltpu.VMEM(got_odd.shape, f32),
        ]
        + workspace(2, 2, nx),
        compiler_params=pltpu.CompilerParams(vmem_limit_bytes=20 * 2**20),
        cost_estimate=estimate(3),
        name="filter_outer",
    )(flags, src, rim, nodes, got_even, got_odd, mat, dens, low, high, vol_i, tgt)


def update_kernel(tables, amp_i, amp_o, low, high, new, logm):
    inner = amp_i.shape[0]
    nx = amp_i.shape[-1]
    total = jnp.sum(tables[...], axis=0, keepdims=True)
    lane = lax.broadcasted_iota(jnp.int32, total.shape, 1)
    above = jnp.where((total > 0.0) & (lane > 0), 1.0, 0.0)
    middle = -bracket_end + (2.0 * bracket_end / POINTS) * (jnp.sum(above) + 0.5)
    logm[0] = middle
    scale = jnp.exp(jnp.full((1, nx), -0.5 * middle, f32))

    def new_row(y, amp):
        new[y] = jnp.minimum(jnp.maximum(amp * scale, low[y]), high[y])

    def body(j, _):
        new_row(inner_row(j), amp_i[j])
        return 0

    lax.fori_loop(0, inner, body, 0, unroll=4)
    for j in range(5):
        new_row(j if j < 2 else inner + j, amp_o[j])


def update_call(tables, amp_i, amp_o, low, high):
    return pl.pallas_call(
        update_kernel,
        in_specs=[VMEM] * 5,
        out_specs=(VMEM, SMEM),
        out_shape=(jax.ShapeDtypeStruct(low.shape, f32), jax.ShapeDtypeStruct((1,), f32)),
        compiler_params=pltpu.CompilerParams(vmem_limit_bytes=8 * 2**20),
        cost_estimate=estimate(1),
        name="update",
    )(tables, amp_i, amp_o, low, high)


def to_lower(value, axis):
    count = lax.axis_size(axis)
    return lax.ppermute(value, axis, [(i + 1, i) for i in range(count - 1)])


def swap(value, axis, start):
    pairs = []
    for i in range(start, lax.axis_size(axis) - 1, 2):
        pairs += [(i, i + 1), (i + 1, i)]
    return lax.ppermute(value, axis, pairs)


def on_device(displacement, density, passive, solid, stiffness):
    ny, nz, nx = density.shape
    gy, gz = lax.axis_size("gy"), lax.axis_size("gz")
    iy, iz = lax.axis_index("gy"), lax.axis_index("gz")
    flags = jnp.stack([iy > 0, iy < gy - 1, iz > 0, iz < gz - 1, iy % 2 == 1, iz % 2 == 1]).astype(jnp.int32)

    disp_hbm = pltpu.with_memory_space_constraint(displacement, pltpu.HBM)
    stiff_hbm = pltpu.with_memory_space_constraint(stiffness, pltpu.HBM)

    face, mat = start_call(disp_hbm, stiff_hbm)
    fy = to_lower(face, "gy")
    ends, up, down, z_even, z_odd = ends_call(flags, displacement, density, mat)

    z_got_even = swap(z_even, "gz", 0)
    z_got_odd = swap(z_odd, "gz", 1)
    src, low, high, tgt, mat_y = middle_call(displacement, density, fy, mat, ends, passive, solid, stiffness)
    rim, nodes, msg_even, msg_odd = rim_call(flags, z_got_even, z_got_odd, up, down, displacement, density, mat_y, src)

    got_even = swap(msg_even, "gy", 0)
    got_odd = swap(msg_odd, "gy", 1)
    amp_i, vol = inner_call(flags, src, rim, density, low, high)
    amp_o, excess = outer_call(flags, src, rim, nodes, got_even, got_odd, mat, density, low, high, vol, tgt)

    everyone = jnp.broadcast_to(excess, (gz * gy, POINTS))
    tables = lax.all_to_all(everyone, ("gz", "gy"), 0, 0, tiled=True)
    new, logm = update_call(tables, amp_i, amp_o, low, high)
    return new, logm.reshape(())


def solution(mesh):
    placed = (
        P(None, "gy", "gz", None),
        P("gy", "gz", None),
        P("gy", "gz", None),
        P("gy", "gz", None),
        P(),
    )
    return jax.shard_map(
        on_device, mesh=mesh, in_specs=placed, out_specs=(P("gy", "gz", None), P()), check_vma=False
    )
```

```python
import math

import jax
import jax.numpy as jnp
from jax import lax
from jax.experimental import pallas as pl
from jax.experimental.pallas import tpu as pltpu
from jax.sharding import PartitionSpec as P

ITERS = 8
POINTS = 2**ITERS
OFF = 8

smoothing = 0.52
move_limit = 0.2
floor_density = 0.001
bracket_end = 12.0

f32 = jnp.float32
bf16 = jnp.bfloat16
VMEM = pl.BlockSpec(memory_space=pltpu.VMEM)
SMEM = pl.BlockSpec(memory_space=pltpu.SMEM)
HBM = pl.BlockSpec(memory_space=pltpu.HBM)


def cheb_weights():
    spectrum_top = 1.0 + 12.0 * smoothing
    centre_value = (spectrum_top + 1.0) / 2.0
    half_width = (spectrum_top - 1.0) / 2.0
    ratio_value = centre_value / half_width
    first_rho = 1.0 / ratio_value
    second_rho = 1.0 / (2.0 * ratio_value - first_rho)
    third_rho = 1.0 / (2.0 * ratio_value - second_rho)
    return (
        centre_value,
        second_rho * first_rho,
        2.0 * second_rho / half_width,
        third_rho * second_rho,
        2.0 * third_rho / half_width,
    )


def filter_weights():
    t, w1, w2, w3, w4 = cheb_weights()
    diag = 1.0 + 6.0 * smoothing
    alpha = w1 / t + w2 * (1.0 - diag / t)
    beta = w2 * smoothing / t
    gamma = 1.0 / t - w4 * w1 / (t * w2)
    delta = 1.0 + w3 + w4 / w2 - w4 * diag
    eps = w4 * smoothing
    return alpha, beta, gamma, delta, eps


def lane_up(v):
    n = v.shape[-1]
    lane = lax.broadcasted_iota(jnp.int32, v.shape, v.ndim - 1)
    return jnp.where(lane < n - 1, pltpu.roll(v, n - 1, v.ndim - 1), 0.0)


def lane_down(v):
    n = v.shape[-1]
    lane = lax.broadcasted_iota(jnp.int32, v.shape, v.ndim - 1)
    return jnp.where(lane > 0, pltpu.roll(v, 1, v.ndim - 1), 0.0)


def estimate(us):
    return pl.CostEstimate(flops=int(us * 1e9), bytes_accessed=1 << 20, transcendentals=0)


def build_matrices(k, mats):
    shape = (24, 128)
    col = lax.broadcasted_iota(jnp.int32, shape, 1)
    row = lax.broadcasted_iota(jnp.int32, shape, 0)
    main = col < 96
    q = jnp.where(main, jnp.where(col >= 48, 1, 0), jnp.where(col >= 104, 1, 0))
    m = col - 48 * q
    e = col - 96 - 8 * q
    c = jnp.where(main, m >> 4, e >> 1)
    dx = jnp.where(main, (m >> 3) & 1, e & 1)
    valid = main | (e < 6)
    picks = []
    for _, plane, band in mats:
        dof0 = 3 * (plane * q + dx) + c
        picks.append(jnp.where(main & (row == dof0), 1.0, 0.0))
        picks.append(jnp.where(valid & (row == dof0 + 3 * band), 1.0, 0.0))
    picked = jnp.dot(
        k, jnp.concatenate(picks, axis=1), precision=lax.Precision.HIGHEST, preferred_element_type=f32
    )
    col8 = lax.broadcasted_iota(jnp.int32, (8, 128), 1)
    row8 = lax.broadcasted_iota(jnp.int32, (8, 128), 0)
    main8 = col8 < 96
    rc = col8 & 7
    m0 = main8 & (rc == row8)
    m1 = jnp.where(main8, rc, 8) == row8 + 1
    for n, (mat, plane, band) in enumerate(mats):
        k0 = picked[:, 256 * n : 256 * n + 128]
        k1 = picked[:, 256 * n + 128 : 256 * n + 256]
        rows = []
        for b in range(2):
            for q_ in range(2):
                for c_ in range(3):
                    for dx_ in range(2):
                        r = 3 * (plane * q_ + band * b + dx_) + c_
                        rows.append(jnp.where(m0, k0[r : r + 1], 0.0) + jnp.where(m1, k1[r : r + 1], 0.0))
        full = jnp.concatenate(rows, axis=0)
        hi = full.astype(bf16)
        lo = (full - hi.astype(f32)).astype(bf16)
        mat[:, 0:112] = hi[:, 0:112]
        mat[:, 112:224] = lo[:, 0:112]


def prepare(segments, p, work):
    main_s, ext_s, mul_s = work
    for l in range(3):
        for c in range(3):
            w0 = 0
            for u, x in segments(3 * l + c):
                size, nx = u.shape
                n = size // 8
                last = lax.broadcasted_iota(jnp.int32, u.shape, 0) == size - 1
                both = (u, lane_up(u))
                after = (None, None) if x is None else (x, lane_up(x))
                for w in range(n):
                    sl = slice(8 * w, 8 * w + 8)
                    main_s[p, l, 16 * c : 16 * c + 16, (w0 + w) * nx : (w0 + w + 1) * nx] = jnp.concatenate(
                        [both[0][sl], both[1][sl]], axis=0
                    ).astype(bf16)
                for dx in range(2):
                    v, vx = both[dx], after[dx]
                    k = 2 * c + dx
                    for w in range(n):
                        nxt = v[8 * w + 8 : 8 * w + 9] if w < n - 1 else vx
                        if nxt is not None:
                            ext_s[p, l, k : k + 1, (w0 + w) * nx : (w0 + w + 1) * nx] = nxt
                    m = 2.0 * v - v.astype(bf16).astype(f32)
                    mx = 0.0 if vx is None else jnp.broadcast_to(2.0 * vx - vx.astype(bf16).astype(f32), v.shape)
                    at = slice(8 * w0, 8 * (w0 + n))
                    mul_s[p, l, k, 0, at] = m
                    mul_s[p, l, k, 1, at] = jnp.where(last, mx, pltpu.roll(m, size - 1, 0))
                w0 += n


def energy_rows(p, mat, work, density):
    main_s, ext_s, mul_s = work
    rows, nx = density.shape
    count = rows // 8
    acc = [None] * count
    for l in range(3):
        ext = jnp.concatenate([ext_s[p, l], ext_s[p + 1, l]], axis=0).astype(bf16)
        one = jnp.concatenate([main_s[p, l], main_s[p + 1, l], ext], axis=0)
        force = jnp.dot(mat[...], jnp.concatenate([one, one], axis=0), preferred_element_type=f32)
        i = 0
        for b in range(2):
            for q in range(2):
                for k in range(6):
                    for w in range(count):
                        at = slice(8 * w, 8 * w + 8)
                        term = force[8 * i : 8 * i + 8, w * nx : (w + 1) * nx] * mul_s[p + q, l, k, b, at]
                        acc[w] = term if acc[w] is None else acc[w] + term
                    i += 1
    return density * (-3.0 * density * density * jnp.concatenate(acc, axis=0))


def workspace(planes, windows, nx):
    return [
        pltpu.VMEM((planes, 3, 48, windows * nx), bf16),
        pltpu.VMEM((planes, 3, 8, windows * nx), f32),
        pltpu.VMEM((planes, 3, 6, 2, 8 * windows, nx), f32),
    ]


def sweep(rows, segments, put, work):
    work[1][...] = jnp.zeros_like(work[1])
    for p in range(2):
        prepare(segments(p), p, work)

    def body(y, _):
        put(y)
        prepare(segments(y + 2), y + 2, work)
        return 0

    lax.fori_loop(0, rows - 1, body, 0, unroll=7)
    put(rows - 1)


def start_kernel(disp, stiff, face, mat, stiff_s, sems):
    copies = [
        pltpu.make_async_copy(stiff, stiff_s, sems.at[0]),
        pltpu.make_async_copy(disp.at[:, 0], face, sems.at[1]),
    ]
    for copy in copies:
        copy.start()
    copies[0].wait()
    build_matrices(stiff_s[...], ((mat, 4, 2),))
    copies[1].wait()


def start_call(disp, stiff):
    _, _, nz, nx = disp.shape
    matrix = jax.ShapeDtypeStruct((192, 224), bf16)
    return pl.pallas_call(
        start_kernel,
        in_specs=[HBM, HBM],
        out_shape=(jax.ShapeDtypeStruct((9, nz, nx), f32), matrix),
        scratch_shapes=[pltpu.VMEM((24, 24), f32), pltpu.SemaphoreType.DMA((2,))],
        compiler_params=pltpu.CompilerParams(vmem_limit_bytes=4 * 2**20),
        cost_estimate=estimate(10),
        name="start",
    )(disp, stiff)


def extra(ref, row):
    ny = ref.shape[1]
    return 11 + row // ny, slice(row % ny, row % ny + 1)


def ends_kernel(flags, disp, dens, mat, ends, up, down, msg_even, msg_odd, *work):
    _, ny, nz, nx = disp.shape

    def segments(p):
        return lambda i: [(disp[i, p, 0:8], disp[i, p, 8:9]), (disp[i, p, nz - 8 : nz], None)]

    for ref in (up, down):
        ref[9:] = jnp.zeros((ref.shape[0] - 9, ny, nx), f32)

    def pack(y):
        row = pl.ds(y, 1)
        for i in range(9):
            up[i, row] = disp[i, y, nz - 1 : nz]
            down[i, row] = disp[i, y, 0:1]
        up[9, row] = dens[y, nz - 1 : nz]

    def put(y):
        d = jnp.concatenate([dens[y, 0:8], dens[y, nz - 8 : nz]], axis=0)
        s = energy_rows(y, mat, work, d)
        ends[y] = s
        row = pl.ds(y, 1)
        up[10, row] = s[14:15]
        down[9, row] = s[0:1]
        down[10, row] = s[1:2]
        pack(y)

    sweep(ny - 1, segments, put, work)
    pack(ny - 1)
    for n, y in enumerate((0, ny - 1)):
        for i in range(9):
            up[extra(up, 9 * n + i)] = disp[i, y, nz - 2 : nz - 1]
            down[extra(down, 9 * n + i)] = disp[i, y, 1:2]
            down[extra(down, 18 + 9 * n + i)] = disp[i, y, 2:3]
    up[extra(up, 36)] = dens[ny - 1, nz - 2 : nz - 1]
    down[extra(down, 36)] = dens[ny - 1, 0:1]
    down[extra(down, 37)] = dens[ny - 1, 1:2]
    odd = flags[5] == 1
    msg_even[...] = jnp.where(odd, down[...], up[...])
    msg_odd[...] = jnp.where(odd, up[...], down[...])


def ends_call(flags, disp, dens, mat):
    _, ny, nz, nx = disp.shape
    message = jax.ShapeDtypeStruct((11 + -(-38 // ny), ny, nx), f32)
    return pl.pallas_call(
        ends_kernel,
        in_specs=[SMEM] + [VMEM] * 3,
        out_shape=(jax.ShapeDtypeStruct((ny, 16, nx), f32),) + (message,) * 4,
        scratch_shapes=workspace(ny, 2, nx),
        compiler_params=pltpu.CompilerParams(vmem_limit_bytes=16 * 2**20),
        cost_estimate=estimate(4),
        name="energy_ends",
    )(flags, disp, dens, mat)


def middle_kernel(disp, dens, fy, mat, ends, passive, solid, stiff, src, low, high, tgt, mat_y, now_s, *work):
    _, ny, nz, nx = disp.shape
    work, last = work[:3], work[3:]

    def segments(p):
        return lambda i: [(disp[i, p, 8 : nz - 8], disp[i, p, nz - 8 : nz - 7])]

    def frame(y):
        src[y, 0:OFF] = jnp.zeros((OFF, nx), f32)
        src[y, OFF + nz :] = jnp.zeros((src.shape[1] - OFF - nz, nx), f32)

    def put(y):
        frame(y)
        src[y, OFF : OFF + 8] = ends[y, 0:8]
        src[y, OFF + 8 : OFF + nz - 8] = energy_rows(y, mat, work, dens[y, 8 : nz - 8])
        src[y, OFF + nz - 8 : OFF + nz] = ends[y, 8:16]

    sweep(ny - 1, segments, put, work)
    last[1][...] = jnp.zeros_like(last[1])
    prepare(lambda i: [(disp[i, ny - 1], None)], 0, last)
    prepare(lambda i: [(fy[i], None)], 1, last)
    frame(ny - 1)
    src[ny - 1, OFF : OFF + nz] = energy_rows(0, mat, last, dens[ny - 1])

    def bound(y, _):
        low[y], high[y], now_s[y] = limits(dens[y], passive[y] == 1, solid[y] == 1)
        return 0

    lax.fori_loop(0, ny, bound, 0, unroll=4)
    build_matrices(stiff[...], ((mat_y, 2, 4),))
    targets(((ny - 5, inner_row), (5, outer_row(ny))), nz, nx, now_s, tgt)


def middle_call(disp, dens, fy, mat, ends, passive, solid, stiff):
    _, ny, nz, nx = disp.shape
    field = jax.ShapeDtypeStruct((ny, nz, nx), f32)
    return pl.pallas_call(
        middle_kernel,
        in_specs=[VMEM] * 8,
        out_shape=(
            jax.ShapeDtypeStruct((ny, nz + 2 * OFF, nx), f32),
            field,
            field,
            jax.ShapeDtypeStruct((8 * COARSE, nx), f32),
            jax.ShapeDtypeStruct((192, 224), bf16),
        ),
        scratch_shapes=[pltpu.VMEM((ny, nz, nx), f32)]
        + workspace(ny, nz // 8 - 2, nx)
        + workspace(2, nz // 8, nx),
        compiler_params=pltpu.CompilerParams(vmem_limit_bytes=24 * 2**20),
        cost_estimate=estimate(4),
        name="energy_middle",
    )(disp, dens, fy, mat, ends, passive, solid, stiff)


def rim_kernel(
    flags, got_even, got_odd, up, down, disp, dens, mat_y, src,
    rim, nodes, msg_even, msg_odd, low_s, high_s, t_s, *work,
):
    ny, rows, nx = src.shape
    nz = rows - 2 * OFF
    odd = flags[5] == 1
    low_s[...] = jnp.where(odd, got_even[...], got_odd[...])
    high_s[...] = jnp.where(odd, got_odd[...], got_even[...])
    work[1][...] = jnp.zeros_like(work[1])
    prepare(lambda i: [(low_s[i], None), (up[i], None)], 0, work)
    prepare(lambda i: [(down[i], None), (high_s[i], None)], 1, work)
    s = energy_rows(0, mat_y, work, jnp.concatenate([low_s[9], up[9]], axis=0))
    columns = ((0, low_s[10]), (1, s[0:ny]), (3, s[ny : 2 * ny]), (4, high_s[9]), (5, high_s[10]))
    for y in range(ny):
        rim[y] = jnp.zeros((8, nx), f32)
        for r, column in columns:
            rim[y, r : r + 1] = column[y : y + 1]
    half = 2 * (nz + 8)
    zero = jnp.zeros((1, nx), f32)
    for n, y in enumerate((0, ny - 1)):
        row = slice(y, y + 1)
        for i in range(9):
            window = jnp.concatenate(
                [
                    low_s[extra(low_s, 9 * n + i)],
                    low_s[i, row],
                    disp[i, y, 0:1],
                    disp[i, y, nz - 1 : nz],
                    high_s[i, row],
                    high_s[extra(high_s, 9 * n + i)],
                    high_s[extra(high_s, 18 + 9 * n + i)],
                    zero,
                ],
                axis=0,
            )
            nodes[n, i] = window
            t_s[n, half + 8 * i : half + 8 * i + 8] = window
        nodes[n, 9] = jnp.concatenate(
            [
                low_s[extra(low_s, 36)],
                low_s[9, ny - 1 : ny],
                zero,
                dens[ny - 1, nz - 1 : nz],
                high_s[extra(high_s, 36)],
                high_s[extra(high_s, 37)],
                zero,
                zero,
            ],
            axis=0,
        )
        t_s[n, half + 72 : half + 80] = nodes[n, 9]
        for j in range(2):
            at = j * (nz + 8)
            yy = j if n == 0 else ny - 2 + j
            t_s[n, at : at + nz] = src[yy, OFF : OFF + nz]
            t_s[n, at + nz : at + nz + 8] = rim[yy]
    odd = flags[4] == 1
    msg_even[...] = jnp.where(odd, t_s[0], t_s[1])
    msg_odd[...] = jnp.where(odd, t_s[1], t_s[0])


def put_rim(s, y, rim, nz):
    s[y, OFF - 2 : OFF] = rim[0:2]
    s[y, OFF + nz - 1 : OFF + nz + 2] = rim[3:6]


def rim_call(flags, got_even, got_odd, up, down, disp, dens, mat_y, src):
    ny, rows, nx = src.shape
    nz = rows - 2 * OFF
    size = 2 * (nz + 8) + 80
    return pl.pallas_call(
        rim_kernel,
        in_specs=[SMEM] + [VMEM] * 8,
        out_shape=(
            jax.ShapeDtypeStruct((ny, 8, nx), f32),
            jax.ShapeDtypeStruct((2, 10, 8, nx), f32),
            jax.ShapeDtypeStruct((size, nx), f32),
            jax.ShapeDtypeStruct((size, nx), f32),
        ),
        scratch_shapes=[
            pltpu.VMEM(up.shape, f32),
            pltpu.VMEM(up.shape, f32),
            pltpu.VMEM((2, size, nx), f32),
        ]
        + workspace(2, 2 * (ny // 8), nx),
        compiler_params=pltpu.CompilerParams(vmem_limit_bytes=16 * 2**20),
        cost_estimate=estimate(2),
        name="energy_rim",
    )(flags, got_even, got_odd, up, down, disp, dens, mat_y, src)


def filter_block(s_s, d_s, n, z_edges, y_edges, finish, unroll):
    rows, nx = s_s.shape[1:]
    nz = rows - 2 * OFF
    alpha, beta, gamma, delta, eps = filter_weights()
    row = lax.broadcasted_iota(jnp.int32, (rows, nx), 0)
    keep = jnp.where(row < OFF, z_edges[0], jnp.where(row >= OFF + nz, z_edges[1], 1)) == 1

    def beside(v):
        return pltpu.roll(v, 1, 0) + pltpu.roll(v, rows - 1, 0) + lane_up(v) + lane_down(v)

    def second(j, _):
        c = s_s[j + 1]
        d2 = alpha * c + beta * (beside(c) + s_s[j] + s_s[j + 2])
        ok = keep
        if y_edges is not None:
            ok = keep & (jnp.where(j == 0, y_edges[0], jnp.where(j == n - 3, y_edges[1], 1)) == 1)
        d_s[j] = jnp.where(ok, d2, 0.0)
        return 0

    def third(j, _):
        d2 = d_s[j + 1]
        p3 = gamma * s_s[j + 2] + delta * d2 + eps * (beside(d2) + d_s[j] + d_s[j + 2])
        finish(j, p3[OFF : OFF + nz])
        return 0

    lax.fori_loop(0, n - 2, second, 0, unroll=unroll)
    lax.fori_loop(0, n - 4, third, 0, unroll=unroll)


def limits(d, pas, sol):
    lower = jnp.maximum(d - move_limit, floor_density)
    upper = jnp.minimum(d + move_limit, 1.0)
    return tuple(jnp.where(sol, 1.0, jnp.where(pas, floor_density, v)) for v in (lower, upper, d))


FINE = 16
COARSE = POINTS // FINE


SPACING = 2.0 * bracket_end / POINTS


def inverse_coarse(i):
    return math.exp(0.5 * (-bracket_end + SPACING * FINE * i))


def targets(rows, nz, nx, now, tgt):
    acc = tuple(jnp.zeros((8, nx), f32) for _ in range(COARSE))
    for n, row in rows:

        def add(j, acc):
            acc = list(acc)
            for w in range(nz // 8):
                d = now[row(j), 8 * w : 8 * w + 8]
                for i in range(COARSE):
                    acc[i] = acc[i] + d * inverse_coarse(i)
            return tuple(acc)

        acc = lax.fori_loop(0, n, add, acc, unroll=2)
    for i in range(COARSE):
        tgt[8 * i : 8 * i + 8] = acc[i]


def table(n, nz, nx, amp, low, high, row, fine_s, vol, start, unroll):
    pair = 2

    def run(first, make):
        inverse = []
        for i in range(pair):
            c = inverse_coarse(i)
            if not make:
                c = jnp.float32(inverse_coarse(pair + i))
                for other in range(2 * pair, COARSE, pair):
                    c = jnp.where(first == other, jnp.float32(inverse_coarse(other + i)), c)
            inverse.append(c)

        def volume(j, acc):
            acc = list(acc)
            y = row(j)
            for w in range(nz // 8):
                at = slice(8 * w, 8 * w + 8)
                lo, hi = low[y, at], high[y, at]
                los, his = [lo * c for c in inverse], [hi * c for c in inverse]
                for f in range(FINE):
                    if make:
                        t = amp[j, at] * math.exp(-0.5 * SPACING * f)
                        fine_s[f, j, at] = t
                    else:
                        t = fine_s[f, j, at]
                    for i in range(pair):
                        acc[i * FINE + f] = acc[i * FINE + f] + jnp.minimum(jnp.maximum(t, los[i]), his[i])
            return tuple(acc)

        places = [pl.ds(pl.multiple_of(8 * FINE * first + 8 * e, 8), 8) for e in range(pair * FINE)]
        begin = tuple(jnp.zeros((8, nx), f32) if start is None else start[at] for at in places)
        acc = lax.fori_loop(0, n, volume, begin, unroll=unroll)
        for at, value in zip(places, acc):
            vol[at] = value

    run(0, True)

    def later(q, _):
        run(pair * q, False)
        return 0

    lax.fori_loop(1, COARSE // pair, later, 0)


def inner_row(j):
    return j + 2


def outer_row(ny):
    return lambda j: jnp.where(j < 2, j, j + ny - 5)


def inner_kernel(flags, src, rim, dens, low, high, amp, vol, s_s, d_s, fine_s):
    ny, nz, nx = dens.shape
    s_s[...] = src[0 : ny - 1]

    def fix(y, _):
        put_rim(s_s, y, rim[y], nz)
        return 0

    lax.fori_loop(0, ny - 1, fix, 0, unroll=5)

    def finish(j, p3):
        amp[j] = jnp.sqrt(jnp.maximum(-p3 * dens[inner_row(j)], 0.0))

    filter_block(s_s, d_s, ny - 1, (flags[2], flags[3]), None, finish, True)
    table(ny - 5, nz, nx, amp, low, high, inner_row, fine_s, vol, None, 4)


def inner_call(flags, src, rim, dens, low, high):
    ny, nz, nx = dens.shape
    rows = nz + 2 * OFF
    return pl.pallas_call(
        inner_kernel,
        in_specs=[SMEM] + [VMEM] * 5,
        out_shape=(
            jax.ShapeDtypeStruct((ny - 5, nz, nx), f32),
            jax.ShapeDtypeStruct((8 * POINTS, nx), f32),
        ),
        scratch_shapes=[
            pltpu.VMEM((ny - 1, rows, nx), f32),
            pltpu.VMEM((ny - 3, rows, nx), f32),
            pltpu.VMEM((FINE, ny - 5, nz, nx), f32),
        ],
        compiler_params=pltpu.CompilerParams(vmem_limit_bytes=24 * 2**20),
        cost_estimate=estimate(9),
        name="filter_inner",
    )(flags, src, rim, dens, low, high)


def outer_kernel(
    flags, src, rim, nodes, got_even, got_odd, mat, dens, low, high, vol_i, tgt,
    amp, excess, s_s, d_s, fine_s, vol, below, above, *work,
):
    ny, nz, nx = dens.shape
    odd = flags[4] == 1
    below[...] = jnp.where(odd, got_even[...], got_odd[...])
    above[...] = jnp.where(odd, got_odd[...], got_even[...])
    half = 2 * (nz + 8)

    def window(ref, i):
        return ref[half + 8 * i : half + 8 * i + 8]

    work[1][...] = jnp.zeros_like(work[1])
    prepare(lambda i: [(window(below, i), None), (nodes[1, i], None)], 0, work)
    prepare(lambda i: [(nodes[0, i], None), (window(above, i), None)], 1, work)
    corner = energy_rows(0, mat, work, jnp.concatenate([window(below, 9), nodes[1, 9]], axis=0))
    for b, ref in enumerate((below, above)):
        for j in range(2):
            at = j if b == 0 else 5 + j
            start = j * (nz + 8)
            s_s[b, at, 0:OFF] = jnp.zeros((OFF, nx), f32)
            s_s[b, at, OFF : OFF + nz] = ref[start : start + nz]
            s_s[b, at, OFF + nz :] = jnp.zeros((OFF, nx), f32)
            put_rim(s_s.at[b], at, ref[start + nz : start + nz + 8], nz)
    for j in range(4):
        s_s[0, 2 + j] = src[j]
        put_rim(s_s.at[0], 2 + j, rim[j], nz)
    for j in range(5):
        s_s[1, j] = src[ny - 5 + j]
        put_rim(s_s.at[1], j, rim[ny - 5 + j], nz)
    put_rim(s_s.at[0], 1, corner[0:8], nz)
    put_rim(s_s.at[1], 4, corner[8:16], nz)
    for b in range(2):
        y0 = 0 if b == 0 else ny - 3

        def finish(j, p3):
            amp[2 * b + j] = jnp.sqrt(jnp.maximum(-p3 * dens[y0 + j], 0.0))

        edges = (flags[0], 1) if b == 0 else (1, flags[1])
        filter_block(s_s.at[b], d_s.at[b], 6 + b, (flags[2], flags[3]), edges, finish, True)
    table(5, nz, nx, amp, low, high, outer_row(ny), fine_s, vol, vol_i, 2)

    def lanes(ref, count):
        total = ref[pl.ds(0, count, stride=8), :]
        for s in range(1, 8):
            total = total + ref[pl.ds(s, count, stride=8), :]
        return total

    volumes, present = lanes(vol, POINTS), lanes(tgt, COARSE)
    over = [volumes[FINE * i : FINE * i + FINE] - present[i : i + 1] for i in range(COARSE)]
    excess[...] = jnp.sum(jnp.transpose(jnp.concatenate(over, axis=0)), axis=0, keepdims=True)


def outer_call(flags, src, rim, nodes, got_even, got_odd, mat, dens, low, high, vol_i, tgt):
    ny, nz, nx = dens.shape
    rows = nz + 2 * OFF
    return pl.pallas_call(
        outer_kernel,
        in_specs=[SMEM] + [VMEM] * 11,
        out_shape=(jax.ShapeDtypeStruct((5, nz, nx), f32), jax.ShapeDtypeStruct((1, POINTS), f32)),
        scratch_shapes=[
            pltpu.VMEM((2, 7, rows, nx), f32),
            pltpu.VMEM((2, 5, rows, nx), f32),
            pltpu.VMEM((FINE, 5, nz, nx), f32),
            pltpu.VMEM((8 * POINTS, nx), f32),
            pltpu.VMEM(got_odd.shape, f32),
            pltpu.VMEM(got_odd.shape, f32),
        ]
        + workspace(2, 2, nx),
        compiler_params=pltpu.CompilerParams(vmem_limit_bytes=20 * 2**20),
        cost_estimate=estimate(3),
        name="filter_outer",
    )(flags, src, rim, nodes, got_even, got_odd, mat, dens, low, high, vol_i, tgt)


def update_kernel(tables, amp_i, amp_o, low, high, new, logm):
    inner = amp_i.shape[0]
    nx = amp_i.shape[-1]
    total = jnp.sum(tables[...], axis=0, keepdims=True)
    lane = lax.broadcasted_iota(jnp.int32, total.shape, 1)
    above = jnp.where((total > 0.0) & (lane > 0), 1.0, 0.0)
    middle = -bracket_end + (2.0 * bracket_end / POINTS) * (jnp.sum(above) + 0.5)
    logm[0] = middle
    scale = jnp.exp(jnp.full((1, nx), -0.5 * middle, f32))

    def new_row(y, amp):
        new[y] = jnp.minimum(jnp.maximum(amp * scale, low[y]), high[y])

    def body(j, _):
        new_row(inner_row(j), amp_i[j])
        return 0

    lax.fori_loop(0, inner, body, 0, unroll=4)
    for j in range(5):
        new_row(j if j < 2 else inner + j, amp_o[j])


def update_call(tables, amp_i, amp_o, low, high):
    return pl.pallas_call(
        update_kernel,
        in_specs=[VMEM] * 5,
        out_specs=(VMEM, SMEM),
        out_shape=(jax.ShapeDtypeStruct(low.shape, f32), jax.ShapeDtypeStruct((1,), f32)),
        compiler_params=pltpu.CompilerParams(vmem_limit_bytes=8 * 2**20),
        cost_estimate=estimate(1),
        name="update",
    )(tables, amp_i, amp_o, low, high)


def to_lower(value, axis):
    count = lax.axis_size(axis)
    return lax.ppermute(value, axis, [(i + 1, i) for i in range(count - 1)])


def swap(value, axis, start):
    pairs = []
    for i in range(start, lax.axis_size(axis) - 1, 2):
        pairs += [(i, i + 1), (i + 1, i)]
    return lax.ppermute(value, axis, pairs)


def on_device(displacement, density, passive, solid, stiffness):
    ny, nz, nx = density.shape
    gy, gz = lax.axis_size("gy"), lax.axis_size("gz")
    iy, iz = lax.axis_index("gy"), lax.axis_index("gz")
    flags = jnp.stack([iy > 0, iy < gy - 1, iz > 0, iz < gz - 1, iy % 2 == 1, iz % 2 == 1]).astype(jnp.int32)

    disp_hbm = pltpu.with_memory_space_constraint(displacement, pltpu.HBM)
    stiff_hbm = pltpu.with_memory_space_constraint(stiffness, pltpu.HBM)

    face, mat = start_call(disp_hbm, stiff_hbm)
    fy = to_lower(face, "gy")
    ends, up, down, z_even, z_odd = ends_call(flags, displacement, density, mat)

    z_got_even = swap(z_even, "gz", 0)
    z_got_odd = swap(z_odd, "gz", 1)
    src, low, high, tgt, mat_y = middle_call(displacement, density, fy, mat, ends, passive, solid, stiffness)
    rim, nodes, msg_even, msg_odd = rim_call(flags, z_got_even, z_got_odd, up, down, displacement, density, mat_y, src)

    got_even = swap(msg_even, "gy", 0)
    got_odd = swap(msg_odd, "gy", 1)
    amp_i, vol = inner_call(flags, src, rim, density, low, high)
    amp_o, excess = outer_call(flags, src, rim, nodes, got_even, got_odd, mat, density, low, high, vol, tgt)

    everyone = jnp.broadcast_to(excess, (gz * gy, POINTS))
    tables = lax.all_to_all(everyone, ("gz", "gy"), 0, 0, tiled=True)
    new, logm = update_call(tables, amp_i, amp_o, low, high)
    return new, logm.reshape(())


def solution(mesh):
    placed = (
        P(None, "gy", "gz", None),
        P("gy", "gz", None),
        P("gy", "gz", None),
        P("gy", "gz", None),
        P(),
    )
    return jax.shard_map(
        on_device, mesh=mesh, in_specs=placed, out_specs=(P("gy", "gz", None), P()), check_vma=False
    )
```

```python
import math

import jax
import jax.numpy as jnp
from jax import lax
from jax.experimental import pallas as pl
from jax.experimental.pallas import tpu as pltpu
from jax.sharding import PartitionSpec as P

ITERS = 8
POINTS = 2**ITERS
OFF = 8

smoothing = 0.52
move_limit = 0.2
floor_density = 0.001
bracket_end = 12.0

f32 = jnp.float32
bf16 = jnp.bfloat16
VMEM = pl.BlockSpec(memory_space=pltpu.VMEM)
SMEM = pl.BlockSpec(memory_space=pltpu.SMEM)
HBM = pl.BlockSpec(memory_space=pltpu.HBM)


def cheb_weights():
    spectrum_top = 1.0 + 12.0 * smoothing
    centre_value = (spectrum_top + 1.0) / 2.0
    half_width = (spectrum_top - 1.0) / 2.0
    ratio_value = centre_value / half_width
    first_rho = 1.0 / ratio_value
    second_rho = 1.0 / (2.0 * ratio_value - first_rho)
    third_rho = 1.0 / (2.0 * ratio_value - second_rho)
    return (
        centre_value,
        second_rho * first_rho,
        2.0 * second_rho / half_width,
        third_rho * second_rho,
        2.0 * third_rho / half_width,
    )


def filter_weights():
    t, w1, w2, w3, w4 = cheb_weights()
    diag = 1.0 + 6.0 * smoothing
    alpha = w1 / t + w2 * (1.0 - diag / t)
    beta = w2 * smoothing / t
    gamma = 1.0 / t - w4 * w1 / (t * w2)
    delta = 1.0 + w3 + w4 / w2 - w4 * diag
    eps = w4 * smoothing
    return alpha, beta, gamma, delta, eps


def lane_up(v):
    n = v.shape[-1]
    lane = lax.broadcasted_iota(jnp.int32, v.shape, v.ndim - 1)
    return jnp.where(lane < n - 1, pltpu.roll(v, n - 1, v.ndim - 1), 0.0)


def lane_down(v):
    n = v.shape[-1]
    lane = lax.broadcasted_iota(jnp.int32, v.shape, v.ndim - 1)
    return jnp.where(lane > 0, pltpu.roll(v, 1, v.ndim - 1), 0.0)


def estimate(us):
    return pl.CostEstimate(flops=int(us * 1e9), bytes_accessed=1 << 20, transcendentals=0)


def build_matrices(k, mats):
    shape = (24, 128)
    col = lax.broadcasted_iota(jnp.int32, shape, 1)
    row = lax.broadcasted_iota(jnp.int32, shape, 0)
    main = col < 96
    q = jnp.where(main, jnp.where(col >= 48, 1, 0), jnp.where(col >= 104, 1, 0))
    m = col - 48 * q
    e = col - 96 - 8 * q
    c = jnp.where(main, m >> 4, e >> 1)
    dx = jnp.where(main, (m >> 3) & 1, e & 1)
    valid = main | (e < 6)
    picks = []
    for _, plane, band in mats:
        dof0 = 3 * (plane * q + dx) + c
        picks.append(jnp.where(main & (row == dof0), 1.0, 0.0))
        picks.append(jnp.where(valid & (row == dof0 + 3 * band), 1.0, 0.0))
    picked = jnp.dot(
        k, jnp.concatenate(picks, axis=1), precision=lax.Precision.HIGHEST, preferred_element_type=f32
    )
    col8 = lax.broadcasted_iota(jnp.int32, (8, 128), 1)
    row8 = lax.broadcasted_iota(jnp.int32, (8, 128), 0)
    main8 = col8 < 96
    rc = col8 & 7
    m0 = main8 & (rc == row8)
    m1 = jnp.where(main8, rc, 8) == row8 + 1
    for n, (mat, plane, band) in enumerate(mats):
        k0 = picked[:, 256 * n : 256 * n + 128]
        k1 = picked[:, 256 * n + 128 : 256 * n + 256]
        rows = []
        for b in range(2):
            for q_ in range(2):
                for c_ in range(3):
                    for dx_ in range(2):
                        r = 3 * (plane * q_ + band * b + dx_) + c_
                        rows.append(jnp.where(m0, k0[r : r + 1], 0.0) + jnp.where(m1, k1[r : r + 1], 0.0))
        full = jnp.concatenate(rows, axis=0)
        hi = full.astype(bf16)
        lo = (full - hi.astype(f32)).astype(bf16)
        mat[:, 0:112] = hi[:, 0:112]
        mat[:, 112:224] = lo[:, 0:112]


def prepare(segments, p, work):
    main_s, ext_s, mul_s = work
    for l in range(3):
        for c in range(3):
            w0 = 0
            for u, x in segments(3 * l + c):
                size, nx = u.shape
                n = size // 8
                last = lax.broadcasted_iota(jnp.int32, u.shape, 0) == size - 1
                both = (u, lane_up(u))
                after = (None, None) if x is None else (x, lane_up(x))
                for w in range(n):
                    sl = slice(8 * w, 8 * w + 8)
                    main_s[p, l, 16 * c : 16 * c + 16, (w0 + w) * nx : (w0 + w + 1) * nx] = jnp.concatenate(
                        [both[0][sl], both[1][sl]], axis=0
                    ).astype(bf16)
                for dx in range(2):
                    v, vx = both[dx], after[dx]
                    k = 2 * c + dx
                    for w in range(n):
                        nxt = v[8 * w + 8 : 8 * w + 9] if w < n - 1 else vx
                        if nxt is not None:
                            ext_s[p, l, k : k + 1, (w0 + w) * nx : (w0 + w + 1) * nx] = nxt
                    m = 2.0 * v - v.astype(bf16).astype(f32)
                    mx = 0.0 if vx is None else jnp.broadcast_to(2.0 * vx - vx.astype(bf16).astype(f32), v.shape)
                    at = slice(8 * w0, 8 * (w0 + n))
                    mul_s[p, l, k, 0, at] = m
                    mul_s[p, l, k, 1, at] = jnp.where(last, mx, pltpu.roll(m, size - 1, 0))
                w0 += n


def energy_rows(p, mat, work, density):
    main_s, ext_s, mul_s = work
    rows, nx = density.shape
    count = rows // 8
    acc = [None] * count
    for l in range(3):
        ext = jnp.concatenate([ext_s[p, l], ext_s[p + 1, l]], axis=0).astype(bf16)
        one = jnp.concatenate([main_s[p, l], main_s[p + 1, l], ext], axis=0)
        force = jnp.dot(mat[...], jnp.concatenate([one, one], axis=0), preferred_element_type=f32)
        i = 0
        for b in range(2):
            for q in range(2):
                for k in range(6):
                    for w in range(count):
                        at = slice(8 * w, 8 * w + 8)
                        term = force[8 * i : 8 * i + 8, w * nx : (w + 1) * nx] * mul_s[p + q, l, k, b, at]
                        acc[w] = term if acc[w] is None else acc[w] + term
                    i += 1
    return density * (-3.0 * density * density * jnp.concatenate(acc, axis=0))


def workspace(planes, windows, nx):
    return [
        pltpu.VMEM((planes, 3, 48, windows * nx), bf16),
        pltpu.VMEM((planes, 3, 8, windows * nx), f32),
        pltpu.VMEM((planes, 3, 6, 2, 8 * windows, nx), f32),
    ]


def sweep(rows, segments, put, work):
    work[1][...] = jnp.zeros_like(work[1])
    for p in range(2):
        prepare(segments(p), p, work)

    def body(y, _):
        put(y)
        prepare(segments(y + 2), y + 2, work)
        return 0

    lax.fori_loop(0, rows - 1, body, 0, unroll=7)
    put(rows - 1)


def start_kernel(disp, stiff, face, mat, stiff_s, sems):
    copies = [
        pltpu.make_async_copy(stiff, stiff_s, sems.at[0]),
        pltpu.make_async_copy(disp.at[:, 0], face, sems.at[1]),
    ]
    for copy in copies:
        copy.start()
    copies[0].wait()
    build_matrices(stiff_s[...], ((mat, 4, 2),))
    copies[1].wait()


def start_call(disp, stiff):
    _, _, nz, nx = disp.shape
    matrix = jax.ShapeDtypeStruct((192, 224), bf16)
    return pl.pallas_call(
        start_kernel,
        in_specs=[HBM, HBM],
        out_shape=(jax.ShapeDtypeStruct((9, nz, nx), f32), matrix),
        scratch_shapes=[pltpu.VMEM((24, 24), f32), pltpu.SemaphoreType.DMA((2,))],
        compiler_params=pltpu.CompilerParams(vmem_limit_bytes=4 * 2**20),
        cost_estimate=estimate(10),
        name="start",
    )(disp, stiff)


def extra(ref, row):
    ny = ref.shape[1]
    return 11 + row // ny, slice(row % ny, row % ny + 1)


def ends_kernel(flags, disp, dens, mat, ends, up, down, msg_even, msg_odd, *work):
    _, ny, nz, nx = disp.shape

    def segments(p):
        return lambda i: [(disp[i, p, 0:8], disp[i, p, 8:9]), (disp[i, p, nz - 8 : nz], None)]

    for ref in (up, down):
        ref[9:] = jnp.zeros((ref.shape[0] - 9, ny, nx), f32)

    def pack(y):
        row = pl.ds(y, 1)
        for i in range(9):
            up[i, row] = disp[i, y, nz - 1 : nz]
            down[i, row] = disp[i, y, 0:1]
        up[9, row] = dens[y, nz - 1 : nz]

    def put(y):
        d = jnp.concatenate([dens[y, 0:8], dens[y, nz - 8 : nz]], axis=0)
        s = energy_rows(y, mat, work, d)
        ends[y] = s
        row = pl.ds(y, 1)
        up[10, row] = s[14:15]
        down[9, row] = s[0:1]
        down[10, row] = s[1:2]
        pack(y)

    sweep(ny - 1, segments, put, work)
    pack(ny - 1)
    for n, y in enumerate((0, ny - 1)):
        for i in range(9):
            up[extra(up, 9 * n + i)] = disp[i, y, nz - 2 : nz - 1]
            down[extra(down, 9 * n + i)] = disp[i, y, 1:2]
            down[extra(down, 18 + 9 * n + i)] = disp[i, y, 2:3]
    up[extra(up, 36)] = dens[ny - 1, nz - 2 : nz - 1]
    down[extra(down, 36)] = dens[ny - 1, 0:1]
    down[extra(down, 37)] = dens[ny - 1, 1:2]
    odd = flags[5] == 1
    msg_even[...] = jnp.where(odd, down[...], up[...])
    msg_odd[...] = jnp.where(odd, up[...], down[...])


def ends_call(flags, disp, dens, mat):
    _, ny, nz, nx = disp.shape
    message = jax.ShapeDtypeStruct((11 + -(-38 // ny), ny, nx), f32)
    return pl.pallas_call(
        ends_kernel,
        in_specs=[SMEM] + [VMEM] * 3,
        out_shape=(jax.ShapeDtypeStruct((ny, 16, nx), f32),) + (message,) * 4,
        scratch_shapes=workspace(ny, 2, nx),
        compiler_params=pltpu.CompilerParams(vmem_limit_bytes=16 * 2**20),
        cost_estimate=estimate(4),
        name="energy_ends",
    )(flags, disp, dens, mat)


def middle_kernel(disp, dens, fy, mat, ends, passive, solid, stiff, src, low, high, tgt, mat_y, now_s, *work):
    _, ny, nz, nx = disp.shape
    work, last = work[:3], work[3:]

    def segments(p):
        return lambda i: [(disp[i, p, 8 : nz - 8], disp[i, p, nz - 8 : nz - 7])]

    def frame(y):
        src[y, 0:OFF] = jnp.zeros((OFF, nx), f32)
        src[y, OFF + nz :] = jnp.zeros((src.shape[1] - OFF - nz, nx), f32)

    def put(y):
        frame(y)
        src[y, OFF : OFF + 8] = ends[y, 0:8]
        src[y, OFF + 8 : OFF + nz - 8] = energy_rows(y, mat, work, dens[y, 8 : nz - 8])
        src[y, OFF + nz - 8 : OFF + nz] = ends[y, 8:16]

    sweep(ny - 1, segments, put, work)
    last[1][...] = jnp.zeros_like(last[1])
    prepare(lambda i: [(disp[i, ny - 1], None)], 0, last)
    prepare(lambda i: [(fy[i], None)], 1, last)
    frame(ny - 1)
    src[ny - 1, OFF : OFF + nz] = energy_rows(0, mat, last, dens[ny - 1])

    def bound(y, _):
        low[y], high[y], now_s[y] = limits(dens[y], passive[y] == 1, solid[y] == 1)
        return 0

    lax.fori_loop(0, ny, bound, 0, unroll=4)
    build_matrices(stiff[...], ((mat_y, 2, 4),))
    targets(((ny - 5, inner_row), (5, outer_row(ny))), nz, nx, now_s, tgt)


def middle_call(disp, dens, fy, mat, ends, passive, solid, stiff):
    _, ny, nz, nx = disp.shape
    field = jax.ShapeDtypeStruct((ny, nz, nx), f32)
    return pl.pallas_call(
        middle_kernel,
        in_specs=[VMEM] * 8,
        out_shape=(
            jax.ShapeDtypeStruct((ny, nz + 2 * OFF, nx), f32),
            field,
            field,
            jax.ShapeDtypeStruct((8 * COARSE, nx), f32),
            jax.ShapeDtypeStruct((192, 224), bf16),
        ),
        scratch_shapes=[pltpu.VMEM((ny, nz, nx), f32)]
        + workspace(ny, nz // 8 - 2, nx)
        + workspace(2, nz // 8, nx),
        compiler_params=pltpu.CompilerParams(vmem_limit_bytes=24 * 2**20),
        cost_estimate=estimate(4),
        name="energy_middle",
    )(disp, dens, fy, mat, ends, passive, solid, stiff)


def rim_kernel(
    flags, got_even, got_odd, up, down, disp, dens, mat_y, src,
    rim, nodes, msg_even, msg_odd, low_s, high_s, t_s, *work,
):
    ny, rows, nx = src.shape
    nz = rows - 2 * OFF
    odd = flags[5] == 1
    low_s[...] = jnp.where(odd, got_even[...], got_odd[...])
    high_s[...] = jnp.where(odd, got_odd[...], got_even[...])
    work[1][...] = jnp.zeros_like(work[1])
    prepare(lambda i: [(low_s[i], None), (up[i], None)], 0, work)
    prepare(lambda i: [(down[i], None), (high_s[i], None)], 1, work)
    s = energy_rows(0, mat_y, work, jnp.concatenate([low_s[9], up[9]], axis=0))
    columns = ((0, low_s[10]), (1, s[0:ny]), (3, s[ny : 2 * ny]), (4, high_s[9]), (5, high_s[10]))
    for y in range(ny):
        rim[y] = jnp.zeros((8, nx), f32)
        for r, column in columns:
            rim[y, r : r + 1] = column[y : y + 1]
    half = 2 * (nz + 8)
    zero = jnp.zeros((1, nx), f32)
    for n, y in enumerate((0, ny - 1)):
        row = slice(y, y + 1)
        for i in range(9):
            window = jnp.concatenate(
                [
                    low_s[extra(low_s, 9 * n + i)],
                    low_s[i, row],
                    disp[i, y, 0:1],
                    disp[i, y, nz - 1 : nz],
                    high_s[i, row],
                    high_s[extra(high_s, 9 * n + i)],
                    high_s[extra(high_s, 18 + 9 * n + i)],
                    zero,
                ],
                axis=0,
            )
            nodes[n, i] = window
            t_s[n, half + 8 * i : half + 8 * i + 8] = window
        nodes[n, 9] = jnp.concatenate(
            [
                low_s[extra(low_s, 36)],
                low_s[9, ny - 1 : ny],
                zero,
                dens[ny - 1, nz - 1 : nz],
                high_s[extra(high_s, 36)],
                high_s[extra(high_s, 37)],
                zero,
                zero,
            ],
            axis=0,
        )
        t_s[n, half + 72 : half + 80] = nodes[n, 9]
        for j in range(2):
            at = j * (nz + 8)
            yy = j if n == 0 else ny - 2 + j
            t_s[n, at : at + nz] = src[yy, OFF : OFF + nz]
            t_s[n, at + nz : at + nz + 8] = rim[yy]
    odd = flags[4] == 1
    msg_even[...] = jnp.where(odd, t_s[0], t_s[1])
    msg_odd[...] = jnp.where(odd, t_s[1], t_s[0])


def put_rim(s, y, rim, nz):
    s[y, OFF - 2 : OFF] = rim[0:2]
    s[y, OFF + nz - 1 : OFF + nz + 2] = rim[3:6]


def rim_call(flags, got_even, got_odd, up, down, disp, dens, mat_y, src):
    ny, rows, nx = src.shape
    nz = rows - 2 * OFF
    size = 2 * (nz + 8) + 80
    return pl.pallas_call(
        rim_kernel,
        in_specs=[SMEM] + [VMEM] * 8,
        out_shape=(
            jax.ShapeDtypeStruct((ny, 8, nx), f32),
            jax.ShapeDtypeStruct((2, 10, 8, nx), f32),
            jax.ShapeDtypeStruct((size, nx), f32),
            jax.ShapeDtypeStruct((size, nx), f32),
        ),
        scratch_shapes=[
            pltpu.VMEM(up.shape, f32),
            pltpu.VMEM(up.shape, f32),
            pltpu.VMEM((2, size, nx), f32),
        ]
        + workspace(2, 2 * (ny // 8), nx),
        compiler_params=pltpu.CompilerParams(vmem_limit_bytes=16 * 2**20),
        cost_estimate=estimate(2),
        name="energy_rim",
    )(flags, got_even, got_odd, up, down, disp, dens, mat_y, src)


def filter_block(s_s, d_s, n, z_edges, y_edges, finish, unroll):
    rows, nx = s_s.shape[1:]
    nz = rows - 2 * OFF
    alpha, beta, gamma, delta, eps = filter_weights()
    row = lax.broadcasted_iota(jnp.int32, (rows, nx), 0)
    keep = jnp.where(row < OFF, z_edges[0], jnp.where(row >= OFF + nz, z_edges[1], 1)) == 1

    def beside(v):
        return pltpu.roll(v, 1, 0) + pltpu.roll(v, rows - 1, 0) + lane_up(v) + lane_down(v)

    def second(j, _):
        c = s_s[j + 1]
        d2 = alpha * c + beta * (beside(c) + s_s[j] + s_s[j + 2])
        ok = keep
        if y_edges is not None:
            ok = keep & (jnp.where(j == 0, y_edges[0], jnp.where(j == n - 3, y_edges[1], 1)) == 1)
        d_s[j] = jnp.where(ok, d2, 0.0)
        return 0

    def third(j, _):
        d2 = d_s[j + 1]
        p3 = gamma * s_s[j + 2] + delta * d2 + eps * (beside(d2) + d_s[j] + d_s[j + 2])
        finish(j, p3[OFF : OFF + nz])
        return 0

    lax.fori_loop(0, n - 2, second, 0, unroll=unroll)
    lax.fori_loop(0, n - 4, third, 0, unroll=unroll)


def limits(d, pas, sol):
    lower = jnp.maximum(d - move_limit, floor_density)
    upper = jnp.minimum(d + move_limit, 1.0)
    return tuple(jnp.where(sol, 1.0, jnp.where(pas, floor_density, v)) for v in (lower, upper, d))


FINE = 16
COARSE = POINTS // FINE


SPACING = 2.0 * bracket_end / POINTS


def inverse_coarse(i):
    return math.exp(0.5 * (-bracket_end + SPACING * FINE * i))


def targets(rows, nz, nx, now, tgt):
    acc = tuple(jnp.zeros((8, nx), f32) for _ in range(COARSE))
    for n, row in rows:

        def add(j, acc):
            acc = list(acc)
            for w in range(nz // 8):
                d = now[row(j), 8 * w : 8 * w + 8]
                for i in range(COARSE):
                    acc[i] = acc[i] + d * inverse_coarse(i)
            return tuple(acc)

        acc = lax.fori_loop(0, n, add, acc, unroll=2)
    for i in range(COARSE):
        tgt[8 * i : 8 * i + 8] = acc[i]


def table(n, nz, nx, amp, low, high, row, fine_s, vol, start, unroll):
    pair = 2

    def run(first, make):
        inverse = []
        for i in range(pair):
            c = inverse_coarse(i)
            if not make:
                c = jnp.float32(inverse_coarse(pair + i))
                for other in range(2 * pair, COARSE, pair):
                    c = jnp.where(first == other, jnp.float32(inverse_coarse(other + i)), c)
            inverse.append(c)

        def volume(j, acc):
            acc = list(acc)
            y = row(j)
            for w in range(nz // 8):
                at = slice(8 * w, 8 * w + 8)
                lo, hi = low[y, at], high[y, at]
                los, his = [lo * c for c in inverse], [hi * c for c in inverse]
                for f in range(FINE):
                    if make:
                        t = amp[j, at] * math.exp(-0.5 * SPACING * f)
                        fine_s[f, j, at] = t
                    else:
                        t = fine_s[f, j, at]
                    for i in range(pair):
                        acc[i * FINE + f] = acc[i * FINE + f] + jnp.minimum(jnp.maximum(t, los[i]), his[i])
            return tuple(acc)

        places = [pl.ds(pl.multiple_of(8 * FINE * first + 8 * e, 8), 8) for e in range(pair * FINE)]
        begin = tuple(jnp.zeros((8, nx), f32) if start is None else start[at] for at in places)
        acc = lax.fori_loop(0, n, volume, begin, unroll=unroll)
        for at, value in zip(places, acc):
            vol[at] = value

    run(0, True)

    def later(q, _):
        run(pair * q, False)
        return 0

    lax.fori_loop(1, COARSE // pair, later, 0)


def inner_row(j):
    return j + 2


def outer_row(ny):
    return lambda j: jnp.where(j < 2, j, j + ny - 5)


def inner_kernel(flags, src, rim, dens, low, high, amp, vol, s_s, d_s, fine_s):
    ny, nz, nx = dens.shape
    s_s[...] = src[0 : ny - 1]

    def fix(y, _):
        put_rim(s_s, y, rim[y], nz)
        return 0

    lax.fori_loop(0, ny - 1, fix, 0, unroll=5)

    def finish(j, p3):
        amp[j] = jnp.sqrt(jnp.maximum(-p3 * dens[inner_row(j)], 0.0))

    filter_block(s_s, d_s, ny - 1, (flags[2], flags[3]), None, finish, True)
    table(ny - 5, nz, nx, amp, low, high, inner_row, fine_s, vol, None, 4)


def inner_call(flags, src, rim, dens, low, high):
    ny, nz, nx = dens.shape
    rows = nz + 2 * OFF
    return pl.pallas_call(
        inner_kernel,
        in_specs=[SMEM] + [VMEM] * 5,
        out_shape=(
            jax.ShapeDtypeStruct((ny - 5, nz, nx), f32),
            jax.ShapeDtypeStruct((8 * POINTS, nx), f32),
        ),
        scratch_shapes=[
            pltpu.VMEM((ny - 1, rows, nx), f32),
            pltpu.VMEM((ny - 3, rows, nx), f32),
            pltpu.VMEM((FINE, ny - 5, nz, nx), f32),
        ],
        compiler_params=pltpu.CompilerParams(vmem_limit_bytes=24 * 2**20),
        cost_estimate=estimate(9),
        name="filter_inner",
    )(flags, src, rim, dens, low, high)


def outer_kernel(
    flags, src, rim, nodes, got_even, got_odd, mat, dens, low, high, vol_i, tgt,
    amp, excess, s_s, d_s, fine_s, vol, below, above, *work,
):
    ny, nz, nx = dens.shape
    odd = flags[4] == 1
    below[...] = jnp.where(odd, got_even[...], got_odd[...])
    above[...] = jnp.where(odd, got_odd[...], got_even[...])
    half = 2 * (nz + 8)

    def window(ref, i):
        return ref[half + 8 * i : half + 8 * i + 8]

    work[1][...] = jnp.zeros_like(work[1])
    prepare(lambda i: [(window(below, i), None), (nodes[1, i], None)], 0, work)
    prepare(lambda i: [(nodes[0, i], None), (window(above, i), None)], 1, work)
    corner = energy_rows(0, mat, work, jnp.concatenate([window(below, 9), nodes[1, 9]], axis=0))
    for b, ref in enumerate((below, above)):
        for j in range(2):
            at = j if b == 0 else 5 + j
            start = j * (nz + 8)
            s_s[b, at, 0:OFF] = jnp.zeros((OFF, nx), f32)
            s_s[b, at, OFF : OFF + nz] = ref[start : start + nz]
            s_s[b, at, OFF + nz :] = jnp.zeros((OFF, nx), f32)
            put_rim(s_s.at[b], at, ref[start + nz : start + nz + 8], nz)
    for j in range(4):
        s_s[0, 2 + j] = src[j]
        put_rim(s_s.at[0], 2 + j, rim[j], nz)
    for j in range(5):
        s_s[1, j] = src[ny - 5 + j]
        put_rim(s_s.at[1], j, rim[ny - 5 + j], nz)
    put_rim(s_s.at[0], 1, corner[0:8], nz)
    put_rim(s_s.at[1], 4, corner[8:16], nz)
    for b in range(2):
        y0 = 0 if b == 0 else ny - 3

        def finish(j, p3):
            amp[2 * b + j] = jnp.sqrt(jnp.maximum(-p3 * dens[y0 + j], 0.0))

        edges = (flags[0], 1) if b == 0 else (1, flags[1])
        filter_block(s_s.at[b], d_s.at[b], 6 + b, (flags[2], flags[3]), edges, finish, True)
    table(5, nz, nx, amp, low, high, outer_row(ny), fine_s, vol, vol_i, True)

    def lanes(ref, count):
        total = ref[pl.ds(0, count, stride=8), :]
        for s in range(1, 8):
            total = total + ref[pl.ds(s, count, stride=8), :]
        return total

    volumes, present = lanes(vol, POINTS), lanes(tgt, COARSE)
    over = [volumes[FINE * i : FINE * i + FINE] - present[i : i + 1] for i in range(COARSE)]
    excess[...] = jnp.sum(jnp.transpose(jnp.concatenate(over, axis=0)), axis=0, keepdims=True)


def outer_call(flags, src, rim, nodes, got_even, got_odd, mat, dens, low, high, vol_i, tgt):
    ny, nz, nx = dens.shape
    rows = nz + 2 * OFF
    return pl.pallas_call(
        outer_kernel,
        in_specs=[SMEM] + [VMEM] * 11,
        out_shape=(jax.ShapeDtypeStruct((5, nz, nx), f32), jax.ShapeDtypeStruct((1, POINTS), f32)),
        scratch_shapes=[
            pltpu.VMEM((2, 7, rows, nx), f32),
            pltpu.VMEM((2, 5, rows, nx), f32),
            pltpu.VMEM((FINE, 5, nz, nx), f32),
            pltpu.VMEM((8 * POINTS, nx), f32),
            pltpu.VMEM(got_odd.shape, f32),
            pltpu.VMEM(got_odd.shape, f32),
        ]
        + workspace(2, 2, nx),
        compiler_params=pltpu.CompilerParams(vmem_limit_bytes=20 * 2**20),
        cost_estimate=estimate(3),
        name="filter_outer",
    )(flags, src, rim, nodes, got_even, got_odd, mat, dens, low, high, vol_i, tgt)


def update_kernel(tables, amp_i, amp_o, low, high, new, logm):
    inner = amp_i.shape[0]
    nx = amp_i.shape[-1]
    total = jnp.sum(tables[...], axis=0, keepdims=True)
    lane = lax.broadcasted_iota(jnp.int32, total.shape, 1)
    above = jnp.where((total > 0.0) & (lane > 0), 1.0, 0.0)
    middle = -bracket_end + (2.0 * bracket_end / POINTS) * (jnp.sum(above) + 0.5)
    logm[0] = middle
    scale = jnp.exp(jnp.full((1, nx), -0.5 * middle, f32))

    def new_row(y, amp):
        new[y] = jnp.minimum(jnp.maximum(amp * scale, low[y]), high[y])

    def body(j, _):
        new_row(inner_row(j), amp_i[j])
        return 0

    lax.fori_loop(0, inner, body, 0, unroll=4)
    for j in range(5):
        new_row(j if j < 2 else inner + j, amp_o[j])


def update_call(tables, amp_i, amp_o, low, high):
    return pl.pallas_call(
        update_kernel,
        in_specs=[VMEM] * 5,
        out_specs=(VMEM, SMEM),
        out_shape=(jax.ShapeDtypeStruct(low.shape, f32), jax.ShapeDtypeStruct((1,), f32)),
        compiler_params=pltpu.CompilerParams(vmem_limit_bytes=8 * 2**20),
        cost_estimate=estimate(1),
        name="update",
    )(tables, amp_i, amp_o, low, high)


def to_lower(value, axis):
    count = lax.axis_size(axis)
    return lax.ppermute(value, axis, [(i + 1, i) for i in range(count - 1)])


def swap(value, axis, start):
    pairs = []
    for i in range(start, lax.axis_size(axis) - 1, 2):
        pairs += [(i, i + 1), (i + 1, i)]
    return lax.ppermute(value, axis, pairs)


def on_device(displacement, density, passive, solid, stiffness):
    ny, nz, nx = density.shape
    gy, gz = lax.axis_size("gy"), lax.axis_size("gz")
    iy, iz = lax.axis_index("gy"), lax.axis_index("gz")
    flags = jnp.stack([iy > 0, iy < gy - 1, iz > 0, iz < gz - 1, iy % 2 == 1, iz % 2 == 1]).astype(jnp.int32)

    disp_hbm = pltpu.with_memory_space_constraint(displacement, pltpu.HBM)
    stiff_hbm = pltpu.with_memory_space_constraint(stiffness, pltpu.HBM)

    face, mat = start_call(disp_hbm, stiff_hbm)
    fy = to_lower(face, "gy")
    ends, up, down, z_even, z_odd = ends_call(flags, displacement, density, mat)

    z_got_even = swap(z_even, "gz", 0)
    z_got_odd = swap(z_odd, "gz", 1)
    src, low, high, tgt, mat_y = middle_call(displacement, density, fy, mat, ends, passive, solid, stiffness)
    rim, nodes, msg_even, msg_odd = rim_call(flags, z_got_even, z_got_odd, up, down, displacement, density, mat_y, src)

    got_even = swap(msg_even, "gy", 0)
    got_odd = swap(msg_odd, "gy", 1)
    amp_i, vol = inner_call(flags, src, rim, density, low, high)
    amp_o, excess = outer_call(flags, src, rim, nodes, got_even, got_odd, mat, density, low, high, vol, tgt)

    everyone = jnp.broadcast_to(excess, (gz * gy, POINTS))
    tables = lax.all_to_all(everyone, ("gz", "gy"), 0, 0, tiled=True)
    new, logm = update_call(tables, amp_i, amp_o, low, high)
    return new, logm.reshape(())


def solution(mesh):
    placed = (
        P(None, "gy", "gz", None),
        P("gy", "gz", None),
        P("gy", "gz", None),
        P("gy", "gz", None),
        P(),
    )
    return jax.shard_map(
        on_device, mesh=mesh, in_specs=placed, out_specs=(P("gy", "gz", None), P()), check_vma=False
    )
```
